32 devices in a mesh: parts: 2 (over y), az: 4 (over z), date: 2 (over x), rg: 2 (over core).
Axes of the slice: x: 2, y: 2, z: 4, core: 2. Of those that a mesh axis runs over, the one named last changes fastest.
Arguments:
- image_stack: float32 [2, 4, 256, 512], P(None, ('parts', 'date'), 'az', 'rg'), parts along dimension 1, may hold values from -6 to 6
- tap_weights: float32 [8, 4, 256], P(None, ('parts', 'date'), 'az'), parts along dimension 1, may hold values from -0.25 to 0.75
- offsets: int32 [4, 256], P(('parts', 'date'), 'az'), parts along dimension 0, may hold values from -12 to 12, as said below
- matchings: int32 [3, 2], replicated, may hold values from 0 to 1, each once within a row
Outputs:
- filtered: float32 [3, 2, 4, 256, 512], P(None, None, ('parts', 'date'), 'az', 'rg'), parts along dimension 2
The draws below stay inside these ranges and needn't reach their ends.
There are 2 independent parts, one for each index of `parts`. The reference program is written for one: setup_inputs(seed, part) draws one part's arguments, and reference() takes and returns one part's arrays. A program takes and returns all parts, laid end to end along the dimension named above; an argument that names none is the same for every part. Nothing has to cross between parts.
Inputs may be any that keep to these rules, and one draw needn't show every extreme that they name: `offsets`: both ends of the range occur in every draw. `matchings`: each row names every date once.
All inputs are finite; a program needn't handle non-finite values.
Results may differ from the reference program's by a relative error of at most 0.0045.
Values may be sent and summed in bfloat16 or wider, within the bound.
No kernel may reach another device: no remote copies, remote signals or barrier semaphores. Data moves between devices by JAX's collectives and lax.ppermute only.
A program may use at most 64 MiB of HBM per device.

```python
import math
import jax
import jax.numpy as jnp
from jax import lax

TAPS = 8
SHIFT_MAX = 12
MATCHES = 3
PATCH = 64
DATES = 2
LINES = 256
SAMPLES = 512


def draw_offsets(key, part):
    random_base = jax.random.randint(jax.random.fold_in(key, 11), (DATES * LINES,), -SHIFT_MAX, SHIFT_MAX + 1, dtype=jnp.int32)
    spot_first = jax.random.randint(jax.random.fold_in(key, 12), (), 0, DATES * LINES, dtype=jnp.int32)
    spot_step = jax.random.randint(jax.random.fold_in(key, 13), (), 1, DATES * LINES, dtype=jnp.int32)
    spot_second = (spot_first + spot_step) % (DATES * LINES)
    flat_values = random_base.at[spot_first].set(SHIFT_MAX)
    flat_values = flat_values.at[spot_second].set(-SHIFT_MAX)
    return flat_values.reshape(DATES, LINES)


def steps_of(stream_key, dims, pieces, low, largest):
    factor_of, own = 1.0, jax.random.fold_in(stream_key, 6)
    for axis_at, shards_of in pieces:
        draws = jnp.exp(jax.random.uniform(jax.random.fold_in(own, axis_at), (shards_of,), jnp.float32, low / len(pieces), largest / len(pieces)))
        factor_of = factor_of * jnp.repeat(draws, dims[axis_at] // shards_of).reshape([-1 if axis == axis_at else 1 for axis in range(len(dims))])
    return factor_of


def noise(stream_key, shape, spread, limit, pieces=(), held_as=jnp.bfloat16):
    level = steps_of(stream_key, shape, pieces, -0.22, 0.18) if pieces else 1.0
    values = jax.random.normal(stream_key, shape, jnp.float32) * spread * level
    return jnp.minimum(jnp.maximum(values, -limit), limit).astype(held_as)


def setup_inputs(seed: int = 0, part: int = 0) -> dict:
    streams_of = jax.random.split(jax.random.key(seed), 5)
    own_keys = jax.random.split(jax.random.fold_in(streams_of[4], part), 5)
    return {
        "image_stack": noise(own_keys[0], (2, DATES, LINES, SAMPLES), 1.0, 6.0, ((1, 2), (2, 4), (3, 2)), jnp.float32),
        "tap_weights": jnp.clip(-0.25 + 1.0 * jax.random.uniform(own_keys[1], (TAPS, DATES, LINES), jnp.float32) ** steps_of(own_keys[1], (TAPS, DATES, LINES), ((1, 2), (2, 4)), -0.2, 0.2), -0.25, 0.75),
        "offsets": draw_offsets(jax.random.fold_in(jax.random.fold_in(streams_of[4], part), 71), part),
        "matchings": jax.vmap(lambda own: jax.random.permutation(own, DATES))(jax.random.split(streams_of[3], MATCHES)).reshape((MATCHES, DATES)).astype(jnp.int32),
    }


def fourier_table(sine_sign, table_scale):
    freq_ids = jnp.arange(PATCH, dtype=jnp.int32)
    phase_ids = (freq_ids[:, None] * freq_ids[None, :]) % PATCH
    angles = phase_ids.astype(jnp.float32) * (2.0 * math.pi / PATCH)
    cosine = jnp.cos(angles) * table_scale
    sine_part = jnp.sin(angles) * (sine_sign * table_scale)
    upper_rows = jnp.concatenate([cosine, -sine_part], axis=1)
    bottom = jnp.concatenate([sine_part, cosine], axis=1)
    return jnp.concatenate([upper_rows, bottom], axis=0).astype(jnp.bfloat16)


def patch_window():
    return jnp.sin(math.pi * (jnp.arange(PATCH, dtype=jnp.float32) + 0.5) / PATCH) ** 2


def filter_rows(band_rows, forward_table, inverse_table, window):
    half_patch = PATCH // 2
    width = band_rows.shape[1]
    line_spectra = jnp.dot(forward_table.T, band_rows, preferred_element_type=jnp.float32).astype(jnp.bfloat16)
    blocks = line_spectra.reshape(2, PATCH, width // half_patch, half_patch)
    patches = jnp.concatenate([blocks[:, :, :-1], blocks[:, :, 1:]], axis=3)
    patches = patches.transpose(1, 2, 0, 3).reshape(PATCH, -1, 2 * PATCH)
    spectrum = jnp.dot(patches, forward_table, preferred_element_type=jnp.float32)
    spec_real = spectrum[..., :PATCH]
    spec_imag = spectrum[..., PATCH:]
    power_spec = spec_real * spec_real + spec_imag * spec_imag
    smooth = power_spec + jnp.roll(power_spec, 1, 0) + jnp.roll(power_spec, -1, 0)
    smooth = smooth + jnp.roll(smooth, 1, 2) + jnp.roll(smooth, -1, 2)
    ref_power = PATCH * PATCH * 1.0
    gain_map = jnp.power((smooth / 9.0 + ref_power) / ref_power, 0.25)
    shaped = jnp.concatenate([spec_real * gain_map, spec_imag * gain_map], axis=-1).astype(jnp.bfloat16)
    range_back = jnp.dot(shaped, inverse_table, preferred_element_type=jnp.float32).astype(jnp.bfloat16)
    range_back = range_back.reshape(PATCH, -1, 2, PATCH)
    lines_back = jnp.einsum('lqcs,cldm->mqds', range_back.astype(jnp.float32), inverse_table.reshape(2, PATCH, 2, PATCH).astype(jnp.float32))
    weighted = lines_back * window[:, None, None, None] * window[None, None, None, :]
    joined = weighted[:, :-1, :, half_patch:] + weighted[:, 1:, :, :half_patch]
    return joined.transpose(2, 0, 1, 3).reshape(2, PATCH, -1)


def filter_item(item_slab, forward_table, inverse_table, window):
    half_patch = PATCH // 2
    width = item_slab.shape[2]
    row_count = item_slab.shape[1] // half_patch - 1

    def single_row(row_index):
        band_rows = lax.dynamic_slice_in_dim(item_slab, row_index * half_patch, PATCH, 1).reshape(2 * PATCH, width)
        return filter_rows(band_rows, forward_table, inverse_table, window)

    row_results = lax.map(single_row, jnp.arange(row_count, dtype=jnp.int32))
    joined = row_results[:-1, :, half_patch:] + row_results[1:, :, :half_patch]
    return joined.transpose(1, 0, 2, 3).reshape(2, (row_count - 1) * half_patch, -1)


def reference(image_stack, tap_weights, offsets, matchings):
    rim_width = SHIFT_MAX + TAPS // 2
    padded = jnp.pad(image_stack, ((0, 0), (0, 0), (rim_width, rim_width), (0, 0)))
    line_ids = jnp.arange(LINES, dtype=jnp.int32)
    summed = jnp.zeros(image_stack.shape, jnp.float32)
    for tap_index in range(TAPS):
        source_rows = (line_ids[None, :] + offsets + (tap_index - (TAPS // 2 - 1) + rim_width)).astype(jnp.int32)
        picked = jax.vmap(lambda slab_one, rows_one: jnp.take(slab_one, rows_one, axis=1), in_axes=(1, 0), out_axes=1)(padded, source_rows)
        summed = summed + tap_weights[tap_index][None, :, :, None] * picked
    resampled = summed.astype(jnp.bfloat16)
    own_real = resampled[0].astype(jnp.float32)
    own_imag = resampled[1].astype(jnp.float32)
    products = []
    for match_index in range(MATCHES):
        partner = jnp.take(resampled, matchings[match_index], axis=1)
        other_real = partner[0].astype(jnp.float32)
        other_imag = partner[1].astype(jnp.float32)
        real_part = own_real * other_real + own_imag * other_imag
        imag_part = own_imag * other_real - own_real * other_imag
        products.append(jnp.stack([real_part, imag_part], axis=0))
    interferogram = jnp.stack(products, axis=0).astype(jnp.bfloat16)
    half_patch = PATCH // 2
    padded_ifg = jnp.pad(interferogram, ((0, 0), (0, 0), (0, 0), (half_patch, half_patch), (half_patch, half_patch)))
    items = padded_ifg.transpose(0, 2, 1, 3, 4).reshape(MATCHES * DATES, 2, LINES + PATCH, SAMPLES + PATCH)
    forward_table = fourier_table(1.0, 1.0)
    inverse_table = fourier_table(-1.0, 1.0 / PATCH)
    window = patch_window()
    results = lax.map(lambda item_slab: filter_item(item_slab, forward_table, inverse_table, window), items)
    return results.reshape(MATCHES, DATES, 2, LINES, SAMPLES).transpose(0, 2, 1, 3, 4)
```

```python
import math

import jax
import jax.numpy as jnp
import numpy as np
from jax import lax
from jax.experimental import pallas as pl
from jax.experimental.pallas import tpu as pltpu
from jax.sharding import PartitionSpec as P

TAPS = 8
SHIFT_MAX = 12
PATCH = 64
HALF = PATCH // 2
RIM = SHIFT_MAX + TAPS // 2
REACH = HALF + RIM
LANES = 128
VMEM_LIMIT = 48 * 1024 * 1024

VMEM = pl.BlockSpec(memory_space=pltpu.VMEM)
SMEM = pl.BlockSpec(memory_space=pltpu.SMEM)
PARAMS = pltpu.CompilerParams(vmem_limit_bytes=VMEM_LIMIT)


def fourier_table(sine_sign, table_scale):
    freq_ids = np.arange(PATCH)
    phase_ids = (freq_ids[:, None] * freq_ids[None, :]) % PATCH
    angles = phase_ids * (2.0 * math.pi / PATCH)
    cosine = np.cos(angles) * table_scale
    sine_part = np.sin(angles) * (sine_sign * table_scale)
    top = np.concatenate([cosine, -sine_part], axis=1)
    bottom = np.concatenate([sine_part, cosine], axis=1)
    return np.concatenate([top, bottom], axis=0).astype(np.float32)


def paired(table):
    split = table.reshape(2, PATCH, 2, PATCH)
    wide = np.zeros((2, 2, PATCH, 2, 2, PATCH), np.float32)
    for slot in range(2):
        wide[:, slot, :, :, slot, :] = split
    return wide.reshape(4 * PATCH, 4 * PATCH)


def line_table(forward, row_patches):
    wide_lines = (row_patches + 1) * HALF
    table = np.zeros((row_patches, 2 * PATCH, 2, wide_lines), np.float32)
    transposed = forward.T.reshape(2 * PATCH, 2, PATCH)
    for row in range(row_patches):
        table[row, :, :, row * HALF : row * HALF + PATCH] = transposed
    return table.reshape(row_patches * 2 * PATCH, 2 * wide_lines)


def window_table():
    window = np.sin(math.pi * (np.arange(PATCH) + 0.5) / PATCH) ** 2
    return np.tile(np.outer(window, window), (2, 2)).astype(np.float32)


def ring_table():
    ring = np.zeros((LANES, LANES), np.float32)
    for lane in range(LANES):
        base = lane // PATCH * PATCH
        for step in (-1, 0, 1):
            ring[base + (lane + step) % PATCH, lane] = 1.0
    return ring


def pack_kernel(image_ref, taps_ref, offsets_ref, first_ref, last_ref):
    lines = image_ref.shape[1]
    width = image_ref.shape[2]
    taps = taps_ref[...]
    taps_high = taps.astype(jnp.bfloat16).astype(jnp.float32)
    taps_low = taps - taps_high
    shifts = jnp.broadcast_to(offsets_ref[...].astype(jnp.float32), (TAPS, lines))

    def write(out_ref, line_start, tap_start):
        for part in range(2):
            rows = image_ref[part, line_start : line_start + REACH, :]
            out_ref[part * REACH : (part + 1) * REACH, :] = rows.astype(jnp.bfloat16)
        cut = slice(tap_start, tap_start + HALF)
        filler = jnp.zeros((TAPS, width - 3 * HALF), jnp.float32)
        block = jnp.concatenate([taps_high[:, cut], taps_low[:, cut], shifts[:, cut], filler], axis=1)
        block = jnp.concatenate([block, jnp.zeros_like(block)], axis=0)
        out_ref[2 * REACH :, :] = block.astype(jnp.bfloat16)

    write(first_ref, 0, 0)
    write(last_ref, lines - REACH, lines - HALF)


def resample_kernel(image_ref, taps_ref, offsets_ref, above_ref, below_ref, tile_ref, edge_ref):
    lines = image_ref.shape[1]
    width = image_ref.shape[2]
    wide = lines + 2 * HALF

    def unpacked(ref):
        block = ref[2 * REACH :, : LANES].astype(jnp.float32)[:TAPS]
        return block[:, :HALF] + block[:, HALF : 2 * HALF], block[:1, 2 * HALF : 3 * HALF]

    above_taps, above_shift = unpacked(above_ref)
    below_taps, below_shift = unpacked(below_ref)
    taps = jnp.concatenate([above_taps, taps_ref[...], below_taps], axis=1)
    own_shift = offsets_ref[...].astype(jnp.float32)
    shift = jnp.concatenate([above_shift, own_shift, below_shift], axis=1).astype(jnp.int32)

    def band(source_lines):
        count = source_lines.shape[0]
        place = lax.broadcasted_iota(jnp.int32, (count, wide), 1) - HALF
        tap_ids = source_lines - place - shift + (TAPS // 2 - 1)
        total = jnp.zeros((count, wide), jnp.float32)
        for tap in range(TAPS):
            total = jnp.where(tap_ids == tap, taps[tap : tap + 1, :], total)
        return total

    own_ids = lax.broadcasted_iota(jnp.int32, (lines, wide), 0)
    rim_ids = lax.broadcasted_iota(jnp.int32, (2 * REACH, wide), 0)
    rim_ids = jnp.where(rim_ids < REACH, rim_ids - REACH, rim_ids - REACH + lines)
    own_band = band(own_ids)
    rim_band = band(rim_ids)
    rim_high = rim_band.astype(jnp.bfloat16)
    rim_low = (rim_band - rim_high.astype(jnp.float32)).astype(jnp.bfloat16)
    rim_both = jnp.concatenate([rim_high, rim_low], axis=0)
    over_rows = (((0,), (0,)), ((), ()))
    side = lax.axis_index("rg")
    edges = []
    for part in range(2):
        own = lax.dot_general(
            own_band,
            image_ref[part],
            over_rows,
            precision=lax.Precision.HIGHEST,
            preferred_element_type=jnp.float32,
        )
        cut = slice(part * REACH, (part + 1) * REACH)
        rim = jnp.concatenate([above_ref[cut, :], below_ref[cut, :]], axis=0)
        rim = jnp.concatenate([rim, rim], axis=0)
        total = own + lax.dot_general(rim_both, rim, over_rows, preferred_element_type=jnp.float32)
        tile_ref[part * wide : (part + 1) * wide, :] = total.astype(jnp.bfloat16)
        edge = jnp.where(side == 0, total[:, width - HALF :], total[:, :HALF])
        edges += [edge[: wide // 2], edge[wide // 2 :]]
    edge_ref[...] = jnp.concatenate(edges, axis=1).astype(jnp.bfloat16)


def cross(own_parts, other_parts):
    own_real, own_imag = own_parts
    other_real, other_imag = other_parts
    real = own_real * other_real + own_imag * other_imag
    imag = own_imag * other_real - own_real * other_imag
    return real, imag


def filter_kernel(
    match_ref,
    line_ref,
    forward_ref,
    inverse_ref,
    back_ref,
    window_ref,
    ring_ref,
    *refs,
):
    slots = (len(refs) - 3) // 2
    out_ref, spectrum_ref, filtered_ref = refs[-3:]
    match_count, _, _, lines, width = out_ref.shape
    wide = lines + 2 * HALF
    row_patches = lines // HALF + 1
    side = lax.axis_index("rg")
    date = lax.axis_index("date")
    dates = match_ref.shape[1]
    window = window_ref[...]
    back = back_ref[...]

    def tile_parts(slot):
        tile = refs[2 * slot][...].astype(jnp.float32)
        edge = refs[2 * slot + 1][...].astype(jnp.float32)
        cuts = [edge[:, i * HALF : (i + 1) * HALF] for i in range(4)]
        edge_real = jnp.concatenate(cuts[:2], axis=0)
        edge_imag = jnp.concatenate(cuts[2:], axis=0)
        return (tile[:wide], tile[wide:]), (edge_real, edge_imag)

    own_tile, own_edge = tile_parts(0)
    for slot in range(slots):
        other_tile, other_edge = (own_tile, own_edge) if slot == 0 else tile_parts(slot)
        mid = jnp.concatenate(cross(own_tile, other_tile), axis=0)
        rim = jnp.concatenate(cross(own_edge, other_edge), axis=0)
        before = jnp.where(side == 0, 0.0, rim)
        after = jnp.where(side == 0, rim, 0.0)
        filler = jnp.zeros((2 * wide, LANES - 2 * HALF), jnp.float32)
        shifted = jnp.concatenate([before, mid, after, filler], axis=1).astype(jnp.bfloat16)
        both = jnp.concatenate([mid.astype(jnp.bfloat16), shifted], axis=1)
        chunks = both.shape[1] // LANES
        line_spectra = jnp.dot(
            line_ref[...], both, preferred_element_type=jnp.float32
        ).astype(jnp.bfloat16)
        pieces = []
        for row in range(row_patches):
            top = row * 2 * PATCH
            for chunk in range(chunks):
                cut = slice(chunk * LANES, (chunk + 1) * LANES)
                pieces.append(
                    jnp.concatenate(
                        [
                            line_spectra[top : top + PATCH, cut],
                            line_spectra[top + PATCH : top + 2 * PATCH, cut],
                        ],
                        axis=1,
                    )
                )
        patches = jnp.concatenate(pieces, axis=0)
        spectrum_ref[...] = jnp.dot(
            patches, forward_ref[...], preferred_element_type=jnp.float32
        )
        pieces = []
        for block in range(row_patches * chunks):
            rows = slice(block * PATCH, (block + 1) * PATCH)
            real = spectrum_ref[rows, :LANES]
            imag = spectrum_ref[rows, LANES:]
            power = real * real + imag * imag
            power = power + pltpu.roll(power, 1, 0) + pltpu.roll(power, PATCH - 1, 0)
            smooth = jnp.dot(
                power.astype(jnp.bfloat16), ring_ref[...], preferred_element_type=jnp.float32
            )
            gain = lax.rsqrt(lax.rsqrt(smooth * (1.0 / (9.0 * PATCH * PATCH)) + 1.0))
            pieces.append(
                jnp.concatenate([real * gain, imag * gain], axis=1).astype(jnp.bfloat16)
            )
        shaped = jnp.concatenate(pieces, axis=0)
        range_back = jnp.dot(
            shaped, inverse_ref[...], preferred_element_type=jnp.float32
        ).astype(jnp.bfloat16)
        for chunk in range(chunks):
            totals = [[None] * (row_patches - 1) for _ in range(2)]
            for row in range(row_patches):
                top = (row * chunks + chunk) * PATCH
                block = range_back[top : top + PATCH]
                stacked = jnp.concatenate([block[:, :LANES], block[:, LANES:]], axis=0)
                patch_out = jnp.dot(back, stacked, preferred_element_type=jnp.float32) * window
                for part in range(2):
                    upper = patch_out[part * PATCH : part * PATCH + HALF]
                    lower = patch_out[part * PATCH + HALF : (part + 1) * PATCH]
                    if row > 0:
                        totals[part][row - 1] = totals[part][row - 1] + upper
                    if row < row_patches - 1:
                        totals[part][row] = lower
            for part in range(2):
                spectrum_ref[part * lines : (part + 1) * lines, :LANES] = jnp.concatenate(
                    totals[part], axis=0
                )
            filtered_ref[chunk] = spectrum_ref[: 2 * lines, :LANES]
        mids = width // LANES
        mid = jnp.concatenate([filtered_ref[i] for i in range(mids)], axis=1)
        moved = jnp.concatenate([filtered_ref[i] for i in range(mids, chunks)], axis=1)
        result = mid + moved[:, HALF : HALF + width]
        for match in range(match_count):
            wanted = match_ref[match, date]
            here = lax.rem(wanted - date + dates, dates) == slot

            @pl.when(here)
            def _():
                for part in range(2):
                    out_ref[match, part, 0] = result[part * lines : (part + 1) * lines]


def per_device(image_stack, tap_weights, offsets, matchings):
    _, _, lines, width = image_stack.shape
    match_count = matchings.shape[0]
    image = image_stack.reshape(2, lines, width)
    taps = tap_weights.reshape(TAPS, lines)
    message = jax.ShapeDtypeStruct((2 * REACH + 16, width), jnp.bfloat16)
    first, last = pl.pallas_call(
        pack_kernel,
        out_shape=(message, message),
        in_specs=[VMEM] * 3,
        out_specs=(VMEM, VMEM),
        compiler_params=PARAMS,
        name="pack",
    )(image, taps, offsets)
    peers = lax.axis_size("az")
    up = [(i, i + 1) for i in range(peers - 1)]
    down = [(j, i) for i, j in up]
    above = lax.ppermute(last, "az", up)
    below = lax.ppermute(first, "az", down)
    wide = lines + 2 * HALF
    tile, edge = pl.pallas_call(
        resample_kernel,
        out_shape=(
            jax.ShapeDtypeStruct((2 * wide, width), jnp.bfloat16),
            jax.ShapeDtypeStruct((wide // 2, 4 * HALF), jnp.bfloat16),
        ),
        in_specs=[VMEM] * 5,
        out_specs=(VMEM, VMEM),
        compiler_params=PARAMS,
        name="resample",
    )(image, taps, offsets, above, below)
    dates = lax.axis_size("date")
    received = []
    for slot in range(dates):
        if slot > 0:
            pairs = [((i + slot) % dates, i) for i in range(dates)]
            received.append(lax.ppermute(tile, "date", pairs))
        else:
            received.append(tile)
        crossed = [
            (((i + slot) % dates) * 2 + 1 - j, i * 2 + j) for i in range(dates) for j in range(2)
        ]
        received.append(lax.ppermute(edge, ("date", "rg"), crossed))
    row_patches = lines // HALF + 1
    forward = fourier_table(1.0, 1.0)
    inverse = fourier_table(-1.0, 1.0 / PATCH)
    chunks = (width + width + LANES) // LANES
    back = inverse.reshape(2, PATCH, 2, PATCH).transpose(2, 3, 0, 1).reshape(2 * PATCH, 2 * PATCH)
    tables = [
        jnp.asarray(line_table(forward, row_patches), jnp.bfloat16),
        jnp.asarray(paired(forward), jnp.bfloat16),
        jnp.asarray(paired(inverse), jnp.bfloat16),
        jnp.asarray(back, jnp.bfloat16),
        jnp.asarray(window_table()),
        jnp.asarray(ring_table(), jnp.bfloat16),
    ]
    return pl.pallas_call(
        filter_kernel,
        out_shape=jax.ShapeDtypeStruct((match_count, 2, 1, lines, width), jnp.float32),
        in_specs=[SMEM] + [VMEM] * (len(tables) + len(received)),
        out_specs=VMEM,
        scratch_shapes=[
            pltpu.VMEM((row_patches * chunks * PATCH, 2 * LANES), jnp.float32),
            pltpu.VMEM((chunks, 2 * lines, LANES), jnp.float32),
        ],
        compiler_params=PARAMS,
        name="goldstein",
    )(matchings, *tables, *received)


def solution(mesh):
    placed = (
        P(None, ("parts", "date"), "az", "rg"),
        P(None, ("parts", "date"), "az"),
        P(("parts", "date"), "az"),
        P(),
    )
    return jax.shard_map(
        per_device,
        mesh=mesh,
        in_specs=placed,
        out_specs=P(None, None, ("parts", "date"), "az", "rg"),
        check_vma=False,
    )
```

```python
import math

import jax
import jax.numpy as jnp
import numpy as np
from jax import lax
from jax.experimental import pallas as pl
from jax.experimental.pallas import tpu as pltpu
from jax.sharding import PartitionSpec as P

TAPS = 8
SHIFT_MAX = 12
PATCH = 64
HALF = PATCH // 2
RIM = SHIFT_MAX + TAPS // 2
REACH = HALF + RIM
LANES = 128
VMEM_LIMIT = 48 * 1024 * 1024

VMEM = pl.BlockSpec(memory_space=pltpu.VMEM)
SMEM = pl.BlockSpec(memory_space=pltpu.SMEM)
PARAMS = pltpu.CompilerParams(vmem_limit_bytes=VMEM_LIMIT)


def fourier_table(sine_sign, table_scale):
    freq_ids = np.arange(PATCH)
    phase_ids = (freq_ids[:, None] * freq_ids[None, :]) % PATCH
    angles = phase_ids * (2.0 * math.pi / PATCH)
    cosine = np.cos(angles) * table_scale
    sine_part = np.sin(angles) * (sine_sign * table_scale)
    top = np.concatenate([cosine, -sine_part], axis=1)
    bottom = np.concatenate([sine_part, cosine], axis=1)
    return np.concatenate([top, bottom], axis=0).astype(np.float32)


def paired(table):
    split = table.reshape(2, PATCH, 2, PATCH)
    wide = np.zeros((2, 2, PATCH, 2, 2, PATCH), np.float32)
    for slot in range(2):
        wide[:, slot, :, :, slot, :] = split
    return wide.reshape(4 * PATCH, 4 * PATCH)


def line_table(forward, row_patches):
    wide_lines = (row_patches + 1) * HALF
    table = np.zeros((row_patches, 2 * PATCH, 2, wide_lines), np.float32)
    transposed = forward.T.reshape(2 * PATCH, 2, PATCH)
    for row in range(row_patches):
        table[row, :, :, row * HALF : row * HALF + PATCH] = transposed
    return table.reshape(row_patches * 2 * PATCH, 2 * wide_lines)


def window_table():
    window = np.sin(math.pi * (np.arange(PATCH) + 0.5) / PATCH) ** 2
    return np.tile(np.outer(window, window), (2, 2)).astype(np.float32)


def ring_table():
    ring = np.zeros((LANES, LANES), np.float32)
    for lane in range(LANES):
        base = lane // PATCH * PATCH
        for step in (-1, 0, 1):
            ring[base + (lane + step) % PATCH, lane] = 1.0
    return ring


def edge_of(other_ref, part, side, lines):
    width = other_ref.shape[2]
    return jnp.where(
        side == 0, other_ref[part, lines, :HALF], other_ref[part, lines, width - HALF :]
    )


def pack_kernel(image_ref, other_ref, taps_ref, offsets_ref, first_ref, last_ref):
    lines = image_ref.shape[1]
    width = image_ref.shape[2]
    side = lax.axis_index("rg")
    taps = taps_ref[...]
    taps_high = taps.astype(jnp.bfloat16).astype(jnp.float32)
    taps_low = taps - taps_high
    shifts = jnp.broadcast_to(offsets_ref[...].astype(jnp.float32), (TAPS, lines))

    def write(out_ref, line_start, tap_start):
        rows = slice(line_start, line_start + REACH)
        for part in range(2):
            cut = slice(part * REACH, (part + 1) * REACH)
            out_ref[cut, :] = image_ref[part, rows, :].astype(jnp.bfloat16)
        edges = jnp.concatenate([edge_of(other_ref, part, side, rows) for part in range(2)], axis=0)
        cut = slice(tap_start, tap_start + HALF)
        block = jnp.concatenate([taps_high[:, cut], taps_low[:, cut], shifts[:, cut]], axis=1)
        block = jnp.concatenate([block, jnp.zeros((HALF - TAPS, 3 * HALF), jnp.float32)], axis=0)
        cuts = [edges[i * HALF : (i + 1) * HALF] for i in range(3)]
        filler = jnp.zeros((HALF, width - 6 * HALF), jnp.float32)
        block = jnp.concatenate([block, *cuts, filler], axis=1)
        out_ref[2 * REACH :, :] = block.astype(jnp.bfloat16)

    write(first_ref, 0, 0)
    write(last_ref, lines - REACH, lines - HALF)


def resample_kernel(
    image_ref, other_ref, taps_ref, offsets_ref, above_ref, below_ref, tile_ref
):
    lines = image_ref.shape[1]
    width = image_ref.shape[2]
    wide = lines + 2 * HALF
    side = lax.axis_index("rg")

    def unpacked(ref):
        block = ref[2 * REACH :, :].astype(jnp.float32)
        head = block[:TAPS]
        edges = [block[:, i * HALF : (i + 1) * HALF] for i in range(3, 6)]
        return (
            head[:, :HALF] + head[:, HALF : 2 * HALF],
            head[:1, 2 * HALF : 3 * HALF],
            jnp.concatenate(edges, axis=0),
        )

    above_taps, above_shift, above_edge = unpacked(above_ref)
    below_taps, below_shift, below_edge = unpacked(below_ref)
    taps = jnp.concatenate([above_taps, taps_ref[...], below_taps], axis=1)
    own_shift = offsets_ref[...].astype(jnp.float32)
    shift = jnp.concatenate([above_shift, own_shift, below_shift], axis=1).astype(jnp.int32)

    def band(source_lines):
        count = source_lines.shape[0]
        place = lax.broadcasted_iota(jnp.int32, (count, wide), 1) - HALF
        tap_ids = source_lines - place - shift + (TAPS // 2 - 1)
        total = jnp.zeros((count, wide), jnp.float32)
        for tap in range(TAPS):
            total = jnp.where(tap_ids == tap, taps[tap : tap + 1, :], total)
        return total

    own_ids = lax.broadcasted_iota(jnp.int32, (lines, wide), 0)
    rim_ids = lax.broadcasted_iota(jnp.int32, (2 * REACH, wide), 0)
    rim_ids = jnp.where(rim_ids < REACH, rim_ids - REACH, rim_ids - REACH + lines)
    own_band = band(own_ids)
    rim_band = band(rim_ids)
    rim_high = rim_band.astype(jnp.bfloat16)
    rim_low = (rim_band - rim_high.astype(jnp.float32)).astype(jnp.bfloat16)
    rim_both = jnp.concatenate([rim_high, rim_low], axis=0)
    over_rows = (((0,), (0,)), ((), ()))
    edges = []
    for part in range(2):
        edge = edge_of(other_ref, part, side, slice(0, lines))
        own = lax.dot_general(
            own_band,
            jnp.concatenate([image_ref[part], edge], axis=1),
            over_rows,
            precision=lax.Precision.HIGHEST,
            preferred_element_type=jnp.float32,
        )
        cut = slice(part * REACH, (part + 1) * REACH)
        rim = jnp.concatenate([above_ref[cut, :], below_ref[cut, :]], axis=0)
        rim_edge = jnp.concatenate([above_edge[cut], below_edge[cut]], axis=0).astype(jnp.bfloat16)
        rim = jnp.concatenate([rim, rim_edge], axis=1)
        rim = jnp.concatenate([rim, rim], axis=0)
        total = own + lax.dot_general(rim_both, rim, over_rows, preferred_element_type=jnp.float32)
        tile_ref[part * wide : (part + 1) * wide, :] = total[:, :width].astype(jnp.bfloat16)
        rows = wide // 4
        edges += [total[i * rows : (i + 1) * rows, width:] for i in range(4)]
    tile_ref[2 * wide :, :] = jnp.concatenate(edges, axis=1).astype(jnp.bfloat16)


def cross(own_parts, other_parts):
    own_real, own_imag = own_parts
    other_real, other_imag = other_parts
    real = own_real * other_real + own_imag * other_imag
    imag = own_imag * other_real - own_real * other_imag
    return real, imag


def tile_parts(tile_ref, wide):
    tile = tile_ref[: 2 * wide, :].astype(jnp.float32)
    edge = tile_ref[2 * wide :, :].astype(jnp.float32)
    cuts = [edge[:, i * HALF : (i + 1) * HALF] for i in range(8)]
    edge_real = jnp.concatenate(cuts[:4], axis=0)
    edge_imag = jnp.concatenate(cuts[4:], axis=0)
    return (tile[:wide], tile[wide:]), (edge_real, edge_imag)


def filtered_of(own_ref, other_ref, table_ref, spectrum_ref, filtered_ref, lines):
    width = own_ref.shape[1]
    wide = lines + 2 * HALF
    row_patches = lines // HALF + 1
    side = lax.axis_index("rg")
    tables = split_tables(table_ref, row_patches)
    line_table_of, forward, inverse, back, ring, window = tables
    own_tile, own_edge = tile_parts(own_ref, wide)
    other_tile, other_edge = tile_parts(other_ref, wide)
    mid = jnp.concatenate(cross(own_tile, other_tile), axis=0)
    rim = jnp.concatenate(cross(own_edge, other_edge), axis=0)
    before = jnp.where(side == 0, 0.0, rim)
    after = jnp.where(side == 0, rim, 0.0)
    filler = jnp.zeros((2 * wide, LANES - 2 * HALF), jnp.float32)
    shifted = jnp.concatenate([before, mid, after, filler], axis=1).astype(jnp.bfloat16)
    both = jnp.concatenate([mid.astype(jnp.bfloat16), shifted], axis=1)
    chunks = both.shape[1] // LANES
    line_spectra = jnp.dot(line_table_of, both, preferred_element_type=jnp.float32)
    line_spectra = line_spectra.astype(jnp.bfloat16)
    pieces = []
    for row in range(row_patches):
        top = row * 2 * PATCH
        for chunk in range(chunks):
            cut = slice(chunk * LANES, (chunk + 1) * LANES)
            real = line_spectra[top : top + PATCH, cut]
            imag = line_spectra[top + PATCH : top + 2 * PATCH, cut]
            pieces.append(jnp.concatenate([real, imag], axis=1))
    patches = jnp.concatenate(pieces, axis=0)
    spectrum_ref[...] = jnp.dot(patches, forward, preferred_element_type=jnp.float32)
    pieces = []
    for block in range(row_patches * chunks):
        rows = slice(block * PATCH, (block + 1) * PATCH)
        real = spectrum_ref[rows, :LANES]
        imag = spectrum_ref[rows, LANES:]
        power = real * real + imag * imag
        power = power + pltpu.roll(power, 1, 0) + pltpu.roll(power, PATCH - 1, 0)
        smooth = jnp.dot(power.astype(jnp.bfloat16), ring, preferred_element_type=jnp.float32)
        gain = lax.rsqrt(lax.rsqrt(smooth * (1.0 / (9.0 * PATCH * PATCH)) + 1.0))
        pieces.append(jnp.concatenate([real * gain, imag * gain], axis=1).astype(jnp.bfloat16))
    shaped = jnp.concatenate(pieces, axis=0)
    range_back = jnp.dot(shaped, inverse, preferred_element_type=jnp.float32)
    range_back = range_back.astype(jnp.bfloat16)
    for chunk in range(chunks):
        totals = [[None] * (row_patches - 1) for _ in range(2)]
        for row in range(row_patches):
            top = (row * chunks + chunk) * PATCH
            block = range_back[top : top + PATCH]
            stacked = jnp.concatenate([block[:, :LANES], block[:, LANES:]], axis=0)
            patch_out = jnp.dot(back, stacked, preferred_element_type=jnp.float32) * window
            for part in range(2):
                upper = patch_out[part * PATCH : part * PATCH + HALF]
                lower = patch_out[part * PATCH + HALF : (part + 1) * PATCH]
                if row > 0:
                    totals[part][row - 1] = totals[part][row - 1] + upper
                if row < row_patches - 1:
                    totals[part][row] = lower
        for part in range(2):
            for row in range(row_patches - 1):
                top = part * lines + row * HALF
                filtered_ref[chunk, top : top + HALF] = totals[part][row]
    mids = width // LANES
    mid = jnp.concatenate([filtered_ref[i] for i in range(mids)], axis=1)
    moved = jnp.concatenate([filtered_ref[i] for i in range(mids, chunks)], axis=1)
    return mid + moved[:, HALF : HALF + width]


def own_kernel(table_ref, own_ref, out_ref, spectrum_ref, filtered_ref):
    lines = out_ref.shape[0] // 2
    out_ref[...] = filtered_of(own_ref, own_ref, table_ref, spectrum_ref, filtered_ref, lines)


def other_kernel(match_ref, table_ref, filtered_own_ref, own_ref, *refs):
    out_ref, spectrum_ref, filtered_ref = refs[-3:]
    match_count, _, _, lines, _ = out_ref.shape
    date = lax.axis_index("date")
    dates = match_ref.shape[1]

    def store(slot, result):
        for match in range(match_count):
            here = lax.rem(match_ref[match, date] - date + dates, dates) == slot

            @pl.when(here)
            def _():
                for part in range(2):
                    out_ref[match, part, 0] = result[part * lines : (part + 1) * lines]

    store(0, filtered_own_ref[...])
    for slot, other_ref in enumerate(refs[:-3], 1):
        store(slot, filtered_of(own_ref, other_ref, table_ref, spectrum_ref, filtered_ref, lines))


def all_tables(row_patches):
    forward = fourier_table(1.0, 1.0)
    inverse = fourier_table(-1.0, 1.0 / PATCH)
    back = inverse.reshape(2, PATCH, 2, PATCH).transpose(2, 3, 0, 1).reshape(2 * PATCH, 2 * PATCH)
    window = window_table()[:PATCH, :PATCH]
    splits = []
    for _ in range(3):
        splits.append(window.astype(jnp.bfloat16).astype(np.float32))
        window = window - splits[-1]
    rows = [
        line_table(forward, row_patches),
        paired(forward),
        paired(inverse),
        np.concatenate([back, ring_table()], axis=1),
        np.concatenate([*splits, np.zeros_like(window)], axis=1),
    ]
    return np.concatenate(rows, axis=0).astype(jnp.bfloat16)


def split_tables(table_ref, row_patches):
    at = row_patches * 2 * PATCH
    line_table_of = table_ref[:at, :]
    forward = table_ref[at : at + 4 * PATCH, :]
    at += 4 * PATCH
    inverse = table_ref[at : at + 4 * PATCH, :]
    at += 4 * PATCH
    back = table_ref[at : at + LANES, :LANES]
    ring = table_ref[at : at + LANES, LANES:]
    at += LANES
    splits = table_ref[at : at + PATCH, :].astype(jnp.float32)
    window = splits[:, :PATCH] + splits[:, PATCH : 2 * PATCH] + splits[:, 2 * PATCH : 3 * PATCH]
    window = jnp.concatenate([window, window], axis=1)
    window = jnp.concatenate([window, window], axis=0)
    return line_table_of, forward, inverse, back, ring, window


def per_device(image_stack, tap_weights, offsets, matchings):
    _, _, lines, width = image_stack.shape
    match_count = matchings.shape[0]
    wide = lines + 2 * HALF
    row_patches = lines // HALF + 1
    other = lax.ppermute(image_stack, "rg", [(0, 1), (1, 0)]).reshape(2, lines, width)
    image = image_stack.reshape(2, lines, width)
    taps = tap_weights.reshape(TAPS, lines)
    message = jax.ShapeDtypeStruct((2 * REACH + HALF, width), jnp.bfloat16)
    first, last = pl.pallas_call(
        pack_kernel,
        out_shape=(message, message),
        in_specs=[VMEM] * 4,
        out_specs=(VMEM, VMEM),
        compiler_params=PARAMS,
        name="pack",
    )(image, other, taps, offsets)
    peers = lax.axis_size("az")
    up = [(i, i + 1) for i in range(peers - 1)]
    down = [(j, i) for i, j in up]
    above = lax.ppermute(last, "az", up)
    below = lax.ppermute(first, "az", down)
    tile = pl.pallas_call(
        resample_kernel,
        out_shape=jax.ShapeDtypeStruct((2 * wide + wide // 4, width), jnp.bfloat16),
        in_specs=[VMEM] * 6,
        out_specs=VMEM,
        compiler_params=PARAMS,
        name="resample",
    )(image, other, taps, offsets, above, below)
    dates = lax.axis_size("date")
    others = [
        lax.ppermute(tile, "date", [((i + slot) % dates, i) for i in range(dates)])
        for slot in range(1, dates)
    ]
    chunks = (width + width + LANES) // LANES
    tables = jnp.asarray(all_tables(row_patches))
    scratch = [
        pltpu.VMEM((row_patches * chunks * PATCH, 2 * LANES), jnp.float32),
        pltpu.VMEM((chunks, 2 * lines, LANES), jnp.float32),
    ]
    filtered_own = pl.pallas_call(
        own_kernel,
        out_shape=jax.ShapeDtypeStruct((2 * lines, width), jnp.float32),
        in_specs=[VMEM] * 2,
        out_specs=VMEM,
        scratch_shapes=scratch,
        compiler_params=PARAMS,
        name="filter_own",
    )(tables, tile)
    return pl.pallas_call(
        other_kernel,
        out_shape=jax.ShapeDtypeStruct((match_count, 2, 1, lines, width), jnp.float32),
        in_specs=[SMEM] + [VMEM] * (3 + len(others)),
        out_specs=VMEM,
        scratch_shapes=scratch,
        compiler_params=PARAMS,
        name="filter_other",
    )(matchings, tables, filtered_own, tile, *others)


def solution(mesh):
    placed = (
        P(None, ("parts", "date"), "az", "rg"),
        P(None, ("parts", "date"), "az"),
        P(("parts", "date"), "az"),
        P(),
    )
    return jax.shard_map(
        per_device,
        mesh=mesh,
        in_specs=placed,
        out_specs=P(None, None, ("parts", "date"), "az", "rg"),
        check_vma=False,
    )
```

```python
import math

import jax
import jax.numpy as jnp
import numpy as np
from jax import lax
from jax.experimental import pallas as pl
from jax.experimental.pallas import tpu as pltpu
from jax.sharding import PartitionSpec as P

TAPS = 8
SHIFT_MAX = 12
PATCH = 64
HALF = PATCH // 2
RIM = SHIFT_MAX + TAPS // 2
REACH = HALF + RIM
LANES = 128
VMEM_LIMIT = 48 * 1024 * 1024

VMEM = pl.BlockSpec(memory_space=pltpu.VMEM)
SMEM = pl.BlockSpec(memory_space=pltpu.SMEM)
HBM = pl.BlockSpec(memory_space=pltpu.HBM)
PARAMS = pltpu.CompilerParams(vmem_limit_bytes=VMEM_LIMIT)


def fourier_table(sine_sign, table_scale):
    freq_ids = np.arange(PATCH)
    phase_ids = (freq_ids[:, None] * freq_ids[None, :]) % PATCH
    angles = phase_ids * (2.0 * math.pi / PATCH)
    cosine = np.cos(angles) * table_scale
    sine_part = np.sin(angles) * (sine_sign * table_scale)
    top = np.concatenate([cosine, -sine_part], axis=1)
    bottom = np.concatenate([sine_part, cosine], axis=1)
    return np.concatenate([top, bottom], axis=0).astype(np.float32)


def paired(table):
    split = table.reshape(2, PATCH, 2, PATCH)
    wide = np.zeros((2, 2, PATCH, 2, 2, PATCH), np.float32)
    for slot in range(2):
        wide[:, slot, :, :, slot, :] = split
    return wide.reshape(4 * PATCH, 4 * PATCH)


def line_table(forward, row_patches):
    wide_lines = (row_patches + 1) * HALF
    table = np.zeros((row_patches, 2 * PATCH, 2, wide_lines), np.float32)
    transposed = forward.T.reshape(2 * PATCH, 2, PATCH)
    for row in range(row_patches):
        table[row, :, :, row * HALF : row * HALF + PATCH] = transposed
    return table.reshape(row_patches * 2 * PATCH, 2 * wide_lines)


def window_table():
    window = np.sin(math.pi * (np.arange(PATCH) + 0.5) / PATCH) ** 2
    return np.tile(np.outer(window, window), (2, 2)).astype(np.float32)


def ring_table():
    ring = np.zeros((LANES, LANES), np.float32)
    for lane in range(LANES):
        base = lane // PATCH * PATCH
        for step in (-1, 0, 1):
            ring[base + (lane + step) % PATCH, lane] = 1.0
    return ring


def edge_of(other_ref, part, side, lines):
    width = other_ref.shape[2]
    return jnp.where(
        side == 0, other_ref[part, lines, :HALF], other_ref[part, lines, width - HALF :]
    )


def load_kernel(*refs):
    count = (len(refs) - 1) // 2
    copies = [
        pltpu.make_async_copy(refs[i], refs[count + i], refs[-1].at[i]) for i in range(count)
    ]
    for copy in copies:
        copy.start()
    for copy in copies:
        copy.wait()


def pack_kernel(image_ref, other_ref, taps_ref, offsets_ref, even_ref, odd_ref):
    lines = image_ref.shape[1]
    width = image_ref.shape[2]
    side = lax.axis_index("rg")
    taps = taps_ref[...]
    taps_high = taps.astype(jnp.bfloat16).astype(jnp.float32)
    taps_low = taps - taps_high
    shifts = jnp.broadcast_to(offsets_ref[...].astype(jnp.float32), (TAPS, lines))

    def write(out_ref, line_start, tap_start):
        rows = slice(line_start, line_start + REACH)
        for part in range(2):
            cut = slice(part * REACH, (part + 1) * REACH)
            out_ref[cut, :] = image_ref[part, rows, :].astype(jnp.bfloat16)
        edges = jnp.concatenate([edge_of(other_ref, part, side, rows) for part in range(2)], axis=0)
        cut = slice(tap_start, tap_start + HALF)
        block = jnp.concatenate([taps_high[:, cut], taps_low[:, cut], shifts[:, cut]], axis=1)
        block = jnp.concatenate([block, jnp.zeros((HALF - TAPS, 3 * HALF), jnp.float32)], axis=0)
        cuts = [edges[i * HALF : (i + 1) * HALF] for i in range(3)]
        filler = jnp.zeros((HALF, width - 6 * HALF), jnp.float32)
        block = jnp.concatenate([block, *cuts, filler], axis=1)
        out_ref[2 * REACH :, :] = block.astype(jnp.bfloat16)

    parity = lax.rem(lax.axis_index("az"), 2)

    @pl.when(parity == 0)
    def _():
        write(even_ref, lines - REACH, lines - HALF)
        write(odd_ref, 0, 0)

    @pl.when(parity == 1)
    def _():
        write(even_ref, 0, 0)
        write(odd_ref, lines - REACH, lines - HALF)


def resample_kernel(
    image_ref, other_ref, taps_ref, offsets_ref, even_ref, odd_ref, tile_ref
):
    lines = image_ref.shape[1]
    width = image_ref.shape[2]
    wide = lines + 2 * HALF
    side = lax.axis_index("rg")

    parity = lax.rem(lax.axis_index("az"), 2)
    above = jnp.where(parity == 0, odd_ref[...], even_ref[...])
    below = jnp.where(parity == 0, even_ref[...], odd_ref[...])

    def unpacked(message):
        block = message[2 * REACH :, :].astype(jnp.float32)
        head = block[:TAPS]
        edges = [block[:, i * HALF : (i + 1) * HALF] for i in range(3, 6)]
        return (
            head[:, :HALF] + head[:, HALF : 2 * HALF],
            head[:1, 2 * HALF : 3 * HALF],
            jnp.concatenate(edges, axis=0),
        )

    above_taps, above_shift, above_edge = unpacked(above)
    below_taps, below_shift, below_edge = unpacked(below)
    taps = jnp.concatenate([above_taps, taps_ref[...], below_taps], axis=1)
    own_shift = offsets_ref[...].astype(jnp.float32)
    shift = jnp.concatenate([above_shift, own_shift, below_shift], axis=1).astype(jnp.int32)

    def band(source_lines):
        count = source_lines.shape[0]
        place = lax.broadcasted_iota(jnp.int32, (count, wide), 1) - HALF
        tap_ids = source_lines - place - shift + (TAPS // 2 - 1)
        total = jnp.zeros((count, wide), jnp.float32)
        for tap in range(TAPS):
            total = jnp.where(tap_ids == tap, taps[tap : tap + 1, :], total)
        return total

    own_ids = lax.broadcasted_iota(jnp.int32, (lines, wide), 0)
    rim_ids = lax.broadcasted_iota(jnp.int32, (2 * REACH, wide), 0)
    rim_ids = jnp.where(rim_ids < REACH, rim_ids - REACH, rim_ids - REACH + lines)
    own_band = band(own_ids)
    rim_band = band(rim_ids)
    rim_high = rim_band.astype(jnp.bfloat16)
    rim_low = (rim_band - rim_high.astype(jnp.float32)).astype(jnp.bfloat16)
    rim_both = jnp.concatenate([rim_high, rim_low], axis=0)
    over_rows = (((0,), (0,)), ((), ()))
    edges = []
    for part in range(2):
        edge = edge_of(other_ref, part, side, slice(0, lines))
        own = lax.dot_general(
            own_band,
            jnp.concatenate([image_ref[part], edge], axis=1),
            over_rows,
            precision=lax.Precision.HIGHEST,
            preferred_element_type=jnp.float32,
        )
        cut = slice(part * REACH, (part + 1) * REACH)
        rim = jnp.concatenate([above[cut, :], below[cut, :]], axis=0)
        rim_edge = jnp.concatenate([above_edge[cut], below_edge[cut]], axis=0).astype(jnp.bfloat16)
        rim = jnp.concatenate([rim, rim_edge], axis=1)
        rim = jnp.concatenate([rim, rim], axis=0)
        total = own + lax.dot_general(rim_both, rim, over_rows, preferred_element_type=jnp.float32)
        tile_ref[part * wide : (part + 1) * wide, :] = total[:, :width].astype(jnp.bfloat16)
        rows = wide // 4
        edges += [total[i * rows : (i + 1) * rows, width:] for i in range(4)]
    tile_ref[2 * wide :, :] = jnp.concatenate(edges, axis=1).astype(jnp.bfloat16)


def cross(own_parts, other_parts):
    own_real, own_imag = own_parts
    other_real, other_imag = other_parts
    real = own_real * other_real + own_imag * other_imag
    imag = own_imag * other_real - own_real * other_imag
    return real, imag


def tile_parts(tile_ref, wide):
    tile = tile_ref[: 2 * wide, :].astype(jnp.float32)
    edge = tile_ref[2 * wide :, :].astype(jnp.float32)
    cuts = [edge[:, i * HALF : (i + 1) * HALF] for i in range(8)]
    edge_real = jnp.concatenate(cuts[:4], axis=0)
    edge_imag = jnp.concatenate(cuts[4:], axis=0)
    return (tile[:wide], tile[wide:]), (edge_real, edge_imag)


def filtered_of(own_ref, other_ref, table_ref, spectrum_ref, filtered_ref, lines):
    width = own_ref.shape[1]
    wide = lines + 2 * HALF
    row_patches = lines // HALF + 1
    side = lax.axis_index("rg")
    tables = split_tables(table_ref, row_patches)
    line_table_of, forward, inverse, back, ring, window = tables
    own_tile, own_edge = tile_parts(own_ref, wide)
    other_tile, other_edge = tile_parts(other_ref, wide)
    mid = jnp.concatenate(cross(own_tile, other_tile), axis=0)
    rim = jnp.concatenate(cross(own_edge, other_edge), axis=0)
    before = jnp.where(side == 0, 0.0, rim)
    after = jnp.where(side == 0, rim, 0.0)
    filler = jnp.zeros((2 * wide, LANES - 2 * HALF), jnp.float32)
    shifted = jnp.concatenate([before, mid, after, filler], axis=1).astype(jnp.bfloat16)
    both = jnp.concatenate([mid.astype(jnp.bfloat16), shifted], axis=1)
    chunks = both.shape[1] // LANES
    line_spectra = jnp.dot(line_table_of, both, preferred_element_type=jnp.float32)
    line_spectra = line_spectra.astype(jnp.bfloat16)
    pieces = []
    for row in range(row_patches):
        top = row * 2 * PATCH
        for chunk in range(chunks):
            cut = slice(chunk * LANES, (chunk + 1) * LANES)
            real = line_spectra[top : top + PATCH, cut]
            imag = line_spectra[top + PATCH : top + 2 * PATCH, cut]
            pieces.append(jnp.concatenate([real, imag], axis=1))
    patches = jnp.concatenate(pieces, axis=0)
    spectrum_ref[...] = jnp.dot(patches, forward, preferred_element_type=jnp.float32)
    pieces = []
    for block in range(row_patches * chunks):
        rows = slice(block * PATCH, (block + 1) * PATCH)
        real = spectrum_ref[rows, :LANES]
        imag = spectrum_ref[rows, LANES:]
        power = real * real + imag * imag
        power = power + pltpu.roll(power, 1, 0) + pltpu.roll(power, PATCH - 1, 0)
        smooth = jnp.dot(power.astype(jnp.bfloat16), ring, preferred_element_type=jnp.float32)
        gain = lax.rsqrt(lax.rsqrt(smooth * (1.0 / (9.0 * PATCH * PATCH)) + 1.0))
        pieces.append(jnp.concatenate([real * gain, imag * gain], axis=1).astype(jnp.bfloat16))
    shaped = jnp.concatenate(pieces, axis=0)
    range_back = jnp.dot(shaped, inverse, preferred_element_type=jnp.float32)
    range_back = range_back.astype(jnp.bfloat16)
    for chunk in range(chunks):
        totals = [[None] * (row_patches - 1) for _ in range(2)]
        for row in range(row_patches):
            top = (row * chunks + chunk) * PATCH
            block = range_back[top : top + PATCH]
            stacked = jnp.concatenate([block[:, :LANES], block[:, LANES:]], axis=0)
            patch_out = jnp.dot(back, stacked, preferred_element_type=jnp.float32) * window
            for part in range(2):
                upper = patch_out[part * PATCH : part * PATCH + HALF]
                lower = patch_out[part * PATCH + HALF : (part + 1) * PATCH]
                if row > 0:
                    totals[part][row - 1] = totals[part][row - 1] + upper
                if row < row_patches - 1:
                    totals[part][row] = lower
        for part in range(2):
            for row in range(row_patches - 1):
                top = part * lines + row * HALF
                filtered_ref[chunk, top : top + HALF] = totals[part][row]
    mids = width // LANES
    mid = jnp.concatenate([filtered_ref[i] for i in range(mids)], axis=1)
    moved = jnp.concatenate([filtered_ref[i] for i in range(mids, chunks)], axis=1)
    return mid + moved[:, HALF : HALF + width]


def own_kernel(table_ref, own_ref, out_ref, spectrum_ref, filtered_ref):
    lines = out_ref.shape[0] // 2
    out_ref[...] = filtered_of(own_ref, own_ref, table_ref, spectrum_ref, filtered_ref, lines)


def other_kernel(match_ref, table_ref, filtered_own_ref, own_ref, *refs):
    out_ref, result_ref, spectrum_ref, filtered_ref, sems = refs[-5:]
    match_count, _, _, lines, _ = out_ref.shape
    date = lax.axis_index("date")
    dates = match_ref.shape[1]

    def keep(slot, result):
        for part in range(2):
            result_ref[slot, part] = result[part * lines : (part + 1) * lines]

    keep(0, filtered_own_ref[...])
    for slot, other_ref in enumerate(refs[:-5], 1):
        keep(slot, filtered_of(own_ref, other_ref, table_ref, spectrum_ref, filtered_ref, lines))
    copies = []
    for match in range(match_count):
        slot = lax.rem(match_ref[match, date] - date + dates, dates)
        copies.append(
            pltpu.make_async_copy(result_ref.at[slot], out_ref.at[match, :, 0], sems.at[match])
        )
    for copy in copies:
        copy.start()
    for copy in copies:
        copy.wait()


def all_tables(row_patches):
    forward = fourier_table(1.0, 1.0)
    inverse = fourier_table(-1.0, 1.0 / PATCH)
    back = inverse.reshape(2, PATCH, 2, PATCH).transpose(2, 3, 0, 1).reshape(2 * PATCH, 2 * PATCH)
    window = window_table()[:PATCH, :PATCH]
    splits = []
    for _ in range(3):
        splits.append(window.astype(jnp.bfloat16).astype(np.float32))
        window = window - splits[-1]
    rows = [
        line_table(forward, row_patches),
        paired(forward),
        paired(inverse),
        np.concatenate([back, ring_table()], axis=1),
        np.concatenate([*splits, np.zeros_like(window)], axis=1),
    ]
    return np.concatenate(rows, axis=0).astype(jnp.bfloat16)


def split_tables(table_ref, row_patches):
    at = row_patches * 2 * PATCH
    line_table_of = table_ref[:at, :]
    forward = table_ref[at : at + 4 * PATCH, :]
    at += 4 * PATCH
    inverse = table_ref[at : at + 4 * PATCH, :]
    at += 4 * PATCH
    back = table_ref[at : at + LANES, :LANES]
    ring = table_ref[at : at + LANES, LANES:]
    at += LANES
    splits = table_ref[at : at + PATCH, :].astype(jnp.float32)
    window = splits[:, :PATCH] + splits[:, PATCH : 2 * PATCH] + splits[:, 2 * PATCH : 3 * PATCH]
    window = jnp.concatenate([window, window], axis=1)
    window = jnp.concatenate([window, window], axis=0)
    return line_table_of, forward, inverse, back, ring, window


def per_device(image_stack, tap_weights, offsets, matchings):
    _, _, lines, width = image_stack.shape
    match_count = matchings.shape[0]
    wide = lines + 2 * HALF
    row_patches = lines // HALF + 1
    other = lax.ppermute(image_stack, "rg", [(0, 1), (1, 0)]).reshape(2, lines, width)
    arguments = (
        image_stack.reshape(2, lines, width),
        tap_weights.reshape(TAPS, lines),
        offsets,
    )
    loaded = pl.pallas_call(
        load_kernel,
        out_shape=tuple(jax.ShapeDtypeStruct(a.shape, a.dtype) for a in arguments),
        in_specs=[HBM] * 3,
        out_specs=(VMEM,) * 3,
        scratch_shapes=[pltpu.SemaphoreType.DMA((3,))],
        compiler_params=PARAMS,
        name="load",
    )(*arguments)
    image, taps, offsets = loaded
    message = jax.ShapeDtypeStruct((2 * REACH + HALF, width), jnp.bfloat16)
    even, odd = pl.pallas_call(
        pack_kernel,
        out_shape=(message, message),
        in_specs=[VMEM] * 4,
        out_specs=(VMEM, VMEM),
        compiler_params=PARAMS,
        name="pack",
    )(image, other, taps, offsets)
    peers = lax.axis_size("az")

    def swapped(value, start):
        pairs = [(i, i + 1) for i in range(start, peers - 1, 2)]
        return lax.ppermute(value, "az", pairs + [(j, i) for i, j in pairs])

    even, odd = swapped(even, 0), swapped(odd, 1)
    tile = pl.pallas_call(
        resample_kernel,
        out_shape=jax.ShapeDtypeStruct((2 * wide + wide // 4, width), jnp.bfloat16),
        in_specs=[VMEM] * 6,
        out_specs=VMEM,
        compiler_params=PARAMS,
        name="resample",
    )(image, other, taps, offsets, even, odd)
    dates = lax.axis_size("date")
    others = [
        lax.ppermute(tile, "date", [((i + slot) % dates, i) for i in range(dates)])
        for slot in range(1, dates)
    ]
    chunks = (width + width + LANES) // LANES
    tables = jnp.asarray(all_tables(row_patches))
    scratch = [
        pltpu.VMEM((row_patches * chunks * PATCH, 2 * LANES), jnp.float32),
        pltpu.VMEM((chunks, 2 * lines, LANES), jnp.float32),
    ]
    filtered_own = pl.pallas_call(
        own_kernel,
        out_shape=jax.ShapeDtypeStruct((2 * lines, width), jnp.float32),
        in_specs=[VMEM] * 2,
        out_specs=VMEM,
        scratch_shapes=scratch,
        compiler_params=PARAMS,
        name="filter_own",
    )(tables, tile)
    return pl.pallas_call(
        other_kernel,
        out_shape=jax.ShapeDtypeStruct((match_count, 2, 1, lines, width), jnp.float32),
        in_specs=[SMEM] + [VMEM] * (3 + len(others)),
        out_specs=HBM,
        scratch_shapes=[
            pltpu.VMEM((dates, 2, lines, width), jnp.float32),
            *scratch,
            pltpu.SemaphoreType.DMA((match_count,)),
        ],
        compiler_params=PARAMS,
        name="filter_other",
    )(matchings, tables, filtered_own, tile, *others)


def solution(mesh):
    placed = (
        P(None, ("parts", "date"), "az", "rg"),
        P(None, ("parts", "date"), "az"),
        P(("parts", "date"), "az"),
        P(),
    )
    return jax.shard_map(
        per_device,
        mesh=mesh,
        in_specs=placed,
        out_specs=P(None, None, ("parts", "date"), "az", "rg"),
        check_vma=False,
    )
```

```python
import math

import jax
import jax.numpy as jnp
import numpy as np
from jax import lax
from jax.experimental import pallas as pl
from jax.experimental.pallas import tpu as pltpu
from jax.sharding import PartitionSpec as P

TAPS = 8
SHIFT_MAX = 12
PATCH = 64
HALF = PATCH // 2
RIM = SHIFT_MAX + TAPS // 2
REACH = HALF + RIM
LANES = 128
VMEM_LIMIT = 48 * 1024 * 1024

VMEM = pl.BlockSpec(memory_space=pltpu.VMEM)
SMEM = pl.BlockSpec(memory_space=pltpu.SMEM)
HBM = pl.BlockSpec(memory_space=pltpu.HBM)
PARAMS = pltpu.CompilerParams(vmem_limit_bytes=VMEM_LIMIT)


def fourier_table(sine_sign, table_scale):
    freq_ids = np.arange(PATCH)
    phase_ids = (freq_ids[:, None] * freq_ids[None, :]) % PATCH
    angles = phase_ids * (2.0 * math.pi / PATCH)
    cosine = np.cos(angles) * table_scale
    sine_part = np.sin(angles) * (sine_sign * table_scale)
    top = np.concatenate([cosine, -sine_part], axis=1)
    bottom = np.concatenate([sine_part, cosine], axis=1)
    return np.concatenate([top, bottom], axis=0).astype(np.float32)


def paired(table):
    split = table.reshape(2, PATCH, 2, PATCH)
    wide = np.zeros((2, 2, PATCH, 2, 2, PATCH), np.float32)
    for slot in range(2):
        wide[:, slot, :, :, slot, :] = split
    return wide.reshape(4 * PATCH, 4 * PATCH)


def line_table(forward, row_patches):
    wide_lines = (row_patches + 1) * HALF
    table = np.zeros((row_patches, 2 * PATCH, 2, wide_lines), np.float32)
    transposed = forward.T.reshape(2 * PATCH, 2, PATCH)
    for row in range(row_patches):
        table[row, :, :, row * HALF : row * HALF + PATCH] = transposed
    return table.reshape(row_patches * 2 * PATCH, 2 * wide_lines)


def window_table():
    window = np.sin(math.pi * (np.arange(PATCH) + 0.5) / PATCH) ** 2
    return np.tile(np.outer(window, window), (2, 2)).astype(np.float32)


def ring_table():
    ring = np.zeros((LANES, LANES), np.float32)
    for lane in range(LANES):
        base = lane // PATCH * PATCH
        for step in (-1, 0, 1):
            ring[base + (lane + step) % PATCH, lane] = 1.0
    return ring


def load_kernel(image_ref, kernel_ref, image_out, kernel_out):
    image_out[...] = image_ref[...]
    kernel_out[...] = kernel_ref[...]


def faces_below():
    return lax.rem(lax.axis_index("az") + lax.axis_index("rg"), 2) == 0


def all_samples(image_ref, other_ref, part, lines):
    mine = image_ref[part, lines, :]
    other = other_ref[part, lines, :]
    side = lax.axis_index("rg")
    left = jnp.where(side == 0, mine, other)
    right = jnp.where(side == 0, other, mine)
    return jnp.concatenate([left, right], axis=1)


def pack_kernel(image_ref, other_ref, kernel_ref, out_ref):
    lines = image_ref.shape[1]
    samples = 2 * image_ref.shape[2]
    below = faces_below()
    taps = kernel_ref[:TAPS, :]
    shifts = jnp.broadcast_to(kernel_ref[TAPS : TAPS + 1, :], taps.shape)
    taps_high = taps.astype(jnp.bfloat16).astype(jnp.float32)
    taps_low = taps - taps_high

    def write(line_start, tap_start):
        for part in range(2):
            rows = all_samples(image_ref, other_ref, part, slice(line_start, line_start + REACH))
            out_ref[part * REACH : (part + 1) * REACH, :] = rows.astype(jnp.bfloat16)
        cut = slice(tap_start, tap_start + HALF)
        filler = jnp.zeros((TAPS, samples - 3 * HALF), jnp.float32)
        block = jnp.concatenate([taps_high[:, cut], taps_low[:, cut], shifts[:, cut], filler], axis=1)
        block = jnp.concatenate([block, jnp.zeros_like(block)], axis=0)
        out_ref[2 * REACH :, :] = block.astype(jnp.bfloat16)

    @pl.when(below)
    def _():
        write(lines - REACH, lines - HALF)

    @pl.when(jnp.logical_not(below))
    def _():
        write(0, 0)


def resample_kernel(image_ref, other_ref, kernel_ref, message_ref, keep_ref, send_ref):
    lines = image_ref.shape[1]
    width = image_ref.shape[2]
    half = lines // 2 + HALF
    below = faces_below()
    side = lax.axis_index("rg")
    head = message_ref[2 * REACH :, :LANES].astype(jnp.float32)[:TAPS]
    rim_taps = head[:, :HALF] + head[:, HALF : 2 * HALF]
    rim_shift = head[:1, 2 * HALF : 3 * HALF]

    def per_line(own, rim):
        lower = jnp.concatenate([own[:, lines - (half - HALF) :], rim], axis=1)
        upper = jnp.concatenate([rim, own[:, : half - HALF]], axis=1)
        return jnp.where(below, lower, upper)

    taps = per_line(kernel_ref[:TAPS, :], rim_taps)
    shift = per_line(kernel_ref[TAPS : TAPS + 1, :], rim_shift).astype(jnp.int32)
    first_line = jnp.where(below, lines + HALF - half, -HALF)
    first_rim = jnp.where(below, lines, -REACH)

    def band(count, first_source):
        source = lax.broadcasted_iota(jnp.int32, (count, half), 0) + first_source
        place = lax.broadcasted_iota(jnp.int32, (count, half), 1) + first_line
        tap_ids = source - place - shift + (TAPS // 2 - 1)
        total = jnp.zeros((count, half), jnp.float32)
        for tap in range(TAPS):
            total = jnp.where(tap_ids == tap, taps[tap : tap + 1, :], total)
        return total

    own_band = band(lines, 0)
    rim_band = band(REACH, first_rim)
    rim_high = rim_band.astype(jnp.bfloat16)
    rim_low = (rim_band - rim_high.astype(jnp.float32)).astype(jnp.bfloat16)
    rim_both = jnp.concatenate([rim_high, rim_low], axis=0)
    over_rows = (((0,), (0,)), ((), ()))
    mine, others = [], []
    for part in range(2):
        own = lax.dot_general(
            own_band,
            all_samples(image_ref, other_ref, part, slice(0, lines)),
            over_rows,
            precision=lax.Precision.HIGHEST,
            preferred_element_type=jnp.float32,
        )
        rim = message_ref[part * REACH : (part + 1) * REACH, :]
        rim = jnp.concatenate([rim, rim], axis=0)
        total = own + lax.dot_general(rim_both, rim, over_rows, preferred_element_type=jnp.float32)
        left, right = total[:, :width], total[:, width:]
        left_edge, right_edge = right[:, :HALF], left[:, width - HALF :]
        mine.append((jnp.where(side == 0, left, right), jnp.where(side == 0, left_edge, right_edge)))
        others.append((jnp.where(side == 0, right, left), jnp.where(side == 0, right_edge, left_edge)))
    rows = half // 4
    for out_ref, parts in ((keep_ref, mine), (send_ref, others)):
        edges = []
        for part, (tile, edge) in enumerate(parts):
            out_ref[part * half : (part + 1) * half, :] = tile.astype(jnp.bfloat16)
            edges += [edge[i * rows : (i + 1) * rows] for i in range(4)]
        out_ref[2 * half :, :] = jnp.concatenate(edges, axis=1).astype(jnp.bfloat16)


def join_kernel(mine_ref, other_ref, tile_ref):
    rows = mine_ref.shape[0]
    below = faces_below()

    @pl.when(below)
    def _():
        tile_ref[:rows, :] = other_ref[...]
        tile_ref[rows:, :] = mine_ref[...]

    @pl.when(jnp.logical_not(below))
    def _():
        tile_ref[:rows, :] = mine_ref[...]
        tile_ref[rows:, :] = other_ref[...]


def cross(own_parts, other_parts):
    own_real, own_imag = own_parts
    other_real, other_imag = other_parts
    real = own_real * other_real + own_imag * other_imag
    imag = own_imag * other_real - own_real * other_imag
    return real, imag


def tile_parts(tile_ref, wide):
    half = wide // 2
    step = tile_ref.shape[0] // 2
    parts, edges = [], []
    for part in range(2):
        tops = [at * step + part * half for at in range(2)]
        pieces = [tile_ref[top : top + half, :].astype(jnp.float32) for top in tops]
        parts.append(jnp.concatenate(pieces, axis=0))
        pieces = []
        for at in range(2):
            block = tile_ref[at * step + 2 * half : (at + 1) * step, :].astype(jnp.float32)
            for i in range(4 * part, 4 * part + 4):
                pieces.append(block[:, i * HALF : (i + 1) * HALF])
        edges.append(jnp.concatenate(pieces, axis=0))
    return parts, edges


def filtered_of(own_ref, other_ref, table_ref, spectrum_ref, filtered_ref, lines):
    width = own_ref.shape[1]
    wide = lines + 2 * HALF
    row_patches = lines // HALF + 1
    side = lax.axis_index("rg")
    tables = split_tables(table_ref, row_patches)
    line_table_of, forward, inverse, back, ring, window = tables
    own_tile, own_edge = tile_parts(own_ref, wide)
    other_tile, other_edge = tile_parts(other_ref, wide)
    mid = jnp.concatenate(cross(own_tile, other_tile), axis=0)
    rim = jnp.concatenate(cross(own_edge, other_edge), axis=0)
    before = jnp.where(side == 0, 0.0, rim)
    after = jnp.where(side == 0, rim, 0.0)
    filler = jnp.zeros((2 * wide, LANES - 2 * HALF), jnp.float32)
    shifted = jnp.concatenate([before, mid, after, filler], axis=1).astype(jnp.bfloat16)
    both = jnp.concatenate([mid.astype(jnp.bfloat16), shifted], axis=1)
    chunks = both.shape[1] // LANES
    line_spectra = jnp.dot(line_table_of, both, preferred_element_type=jnp.float32)
    line_spectra = line_spectra.astype(jnp.bfloat16)
    pieces = []
    for row in range(row_patches):
        top = row * 2 * PATCH
        for chunk in range(chunks):
            cut = slice(chunk * LANES, (chunk + 1) * LANES)
            real = line_spectra[top : top + PATCH, cut]
            imag = line_spectra[top + PATCH : top + 2 * PATCH, cut]
            pieces.append(jnp.concatenate([real, imag], axis=1))
    patches = jnp.concatenate(pieces, axis=0)
    spectrum_ref[...] = jnp.dot(patches, forward, preferred_element_type=jnp.float32)
    pieces = []
    for block in range(row_patches * chunks):
        rows = slice(block * PATCH, (block + 1) * PATCH)
        real = spectrum_ref[rows, :LANES]
        imag = spectrum_ref[rows, LANES:]
        power = real * real + imag * imag
        power = power + pltpu.roll(power, 1, 0) + pltpu.roll(power, PATCH - 1, 0)
        smooth = jnp.dot(power.astype(jnp.bfloat16), ring, preferred_element_type=jnp.float32)
        gain = lax.rsqrt(lax.rsqrt(smooth * (1.0 / (9.0 * PATCH * PATCH)) + 1.0))
        pieces.append(jnp.concatenate([real * gain, imag * gain], axis=1).astype(jnp.bfloat16))
    shaped = jnp.concatenate(pieces, axis=0)
    range_back = jnp.dot(shaped, inverse, preferred_element_type=jnp.float32)
    range_back = range_back.astype(jnp.bfloat16)
    for chunk in range(chunks):
        totals = [[None] * (row_patches - 1) for _ in range(2)]
        for row in range(row_patches):
            top = (row * chunks + chunk) * PATCH
            block = range_back[top : top + PATCH]
            stacked = jnp.concatenate([block[:, :LANES], block[:, LANES:]], axis=0)
            patch_out = jnp.dot(back, stacked, preferred_element_type=jnp.float32) * window
            for part in range(2):
                upper = patch_out[part * PATCH : part * PATCH + HALF]
                lower = patch_out[part * PATCH + HALF : (part + 1) * PATCH]
                if row > 0:
                    totals[part][row - 1] = totals[part][row - 1] + upper
                if row < row_patches - 1:
                    totals[part][row] = lower
        for part in range(2):
            for row in range(row_patches - 1):
                top = part * lines + row * HALF
                filtered_ref[chunk, top : top + HALF] = totals[part][row]
    mids = width // LANES
    mid = jnp.concatenate([filtered_ref[i] for i in range(mids)], axis=1)
    moved = jnp.concatenate([filtered_ref[i] for i in range(mids, chunks)], axis=1)
    return mid + moved[:, HALF : HALF + width]


def own_kernel(table_ref, own_ref, out_ref, spectrum_ref, filtered_ref):
    lines = out_ref.shape[0] // 2
    out_ref[...] = filtered_of(own_ref, own_ref, table_ref, spectrum_ref, filtered_ref, lines)


def other_kernel(match_ref, table_ref, filtered_own_ref, own_ref, *refs):
    out_ref, result_ref, spectrum_ref, filtered_ref, sems = refs[-5:]
    match_count, _, _, lines, _ = out_ref.shape
    date = lax.axis_index("date")
    dates = match_ref.shape[1]

    def keep(slot, result):
        for part in range(2):
            result_ref[slot, part] = result[part * lines : (part + 1) * lines]

    keep(0, filtered_own_ref[...])
    for slot, other_ref in enumerate(refs[:-5], 1):
        keep(slot, filtered_of(own_ref, other_ref, table_ref, spectrum_ref, filtered_ref, lines))
    copies = []
    for match in range(match_count):
        slot = lax.rem(match_ref[match, date] - date + dates, dates)
        copies.append(
            pltpu.make_async_copy(result_ref.at[slot], out_ref.at[match, :, 0], sems.at[match])
        )
    for copy in copies:
        copy.start()
    for copy in copies:
        copy.wait()


def all_tables(row_patches):
    forward = fourier_table(1.0, 1.0)
    inverse = fourier_table(-1.0, 1.0 / PATCH)
    back = inverse.reshape(2, PATCH, 2, PATCH).transpose(2, 3, 0, 1).reshape(2 * PATCH, 2 * PATCH)
    window = window_table()[:PATCH, :PATCH]
    splits = []
    for _ in range(3):
        splits.append(window.astype(jnp.bfloat16).astype(np.float32))
        window = window - splits[-1]
    rows = [
        line_table(forward, row_patches),
        paired(forward),
        paired(inverse),
        np.concatenate([back, ring_table()], axis=1),
        np.concatenate([*splits, np.zeros_like(window)], axis=1),
    ]
    return np.concatenate(rows, axis=0).astype(jnp.bfloat16)


def split_tables(table_ref, row_patches):
    at = row_patches * 2 * PATCH
    line_table_of = table_ref[:at, :]
    forward = table_ref[at : at + 4 * PATCH, :]
    at += 4 * PATCH
    inverse = table_ref[at : at + 4 * PATCH, :]
    at += 4 * PATCH
    back = table_ref[at : at + LANES, :LANES]
    ring = table_ref[at : at + LANES, LANES:]
    at += LANES
    splits = table_ref[at : at + PATCH, :].astype(jnp.float32)
    window = splits[:, :PATCH] + splits[:, PATCH : 2 * PATCH] + splits[:, 2 * PATCH : 3 * PATCH]
    window = jnp.concatenate([window, window], axis=1)
    window = jnp.concatenate([window, window], axis=0)
    return line_table_of, forward, inverse, back, ring, window


def per_device(image_stack, tap_weights, offsets, matchings):
    _, _, lines, width = image_stack.shape
    match_count = matchings.shape[0]
    wide = lines + 2 * HALF
    row_patches = lines // HALF + 1
    other = lax.ppermute(image_stack, "rg", [(0, 1), (1, 0)]).reshape(2, lines, width)
    image = image_stack.reshape(2, lines, width)
    kernel = jnp.concatenate(
        [
            tap_weights.reshape(TAPS, lines),
            offsets.astype(jnp.float32),
            jnp.zeros((TAPS - 1, lines), jnp.float32),
        ],
        axis=0,
    )
    image, kernel = pl.pallas_call(
        load_kernel,
        out_shape=tuple(jax.ShapeDtypeStruct(a.shape, a.dtype) for a in (image, kernel)),
        in_specs=[VMEM] * 2,
        out_specs=(VMEM,) * 2,
        compiler_params=PARAMS,
        name="load",
    )(image, kernel)
    message = pl.pallas_call(
        pack_kernel,
        out_shape=jax.ShapeDtypeStruct((2 * REACH + 2 * TAPS, 2 * width), jnp.bfloat16),
        in_specs=[VMEM] * 3,
        out_specs=VMEM,
        compiler_params=PARAMS,
        name="pack",
    )(image, other, kernel)
    peers = lax.axis_size("az")
    pairs = [
        (2 * i + core, 2 * (i + 1) + core) for core in range(2) for i in range(core, peers - 1, 2)
    ]
    message = lax.ppermute(message, ("az", "rg"), pairs + [(j, i) for i, j in pairs])
    half = jax.ShapeDtypeStruct((wide + wide // 8, width), jnp.bfloat16)
    mine, theirs = pl.pallas_call(
        resample_kernel,
        out_shape=(half, half),
        in_specs=[VMEM] * 4,
        out_specs=(VMEM, VMEM),
        compiler_params=PARAMS,
        name="resample",
    )(image, other, kernel, message)
    theirs = lax.ppermute(theirs, "rg", [(0, 1), (1, 0)])
    tile = pl.pallas_call(
        join_kernel,
        out_shape=jax.ShapeDtypeStruct((2 * half.shape[0], width), jnp.bfloat16),
        in_specs=[VMEM] * 2,
        out_specs=VMEM,
        compiler_params=PARAMS,
        name="join",
    )(mine, theirs)
    dates = lax.axis_size("date")
    others = [
        lax.ppermute(tile, "date", [((i + slot) % dates, i) for i in range(dates)])
        for slot in range(1, dates)
    ]
    chunks = (width + width + LANES) // LANES
    tables = jnp.asarray(all_tables(row_patches))
    scratch = [
        pltpu.VMEM((row_patches * chunks * PATCH, 2 * LANES), jnp.float32),
        pltpu.VMEM((chunks, 2 * lines, LANES), jnp.float32),
    ]
    filtered_own = pl.pallas_call(
        own_kernel,
        out_shape=jax.ShapeDtypeStruct((2 * lines, width), jnp.float32),
        in_specs=[VMEM] * 2,
        out_specs=VMEM,
        scratch_shapes=scratch,
        compiler_params=PARAMS,
        name="filter_own",
    )(tables, tile)
    return pl.pallas_call(
        other_kernel,
        out_shape=jax.ShapeDtypeStruct((match_count, 2, 1, lines, width), jnp.float32),
        in_specs=[SMEM] + [VMEM] * (3 + len(others)),
        out_specs=HBM,
        scratch_shapes=[
            pltpu.VMEM((dates, 2, lines, width), jnp.float32),
            *scratch,
            pltpu.SemaphoreType.DMA((match_count,)),
        ],
        compiler_params=PARAMS,
        name="filter_other",
    )(matchings, tables, filtered_own, tile, *others)


def solution(mesh):
    placed = (
        P(None, ("parts", "date"), "az", "rg"),
        P(None, ("parts", "date"), "az"),
        P(("parts", "date"), "az"),
        P(),
    )
    return jax.shard_map(
        per_device,
        mesh=mesh,
        in_specs=placed,
        out_specs=P(None, None, ("parts", "date"), "az", "rg"),
        check_vma=False,
    )
```

```python
import math

import jax
import jax.numpy as jnp
import numpy as np
from jax import lax
from jax.experimental import pallas as pl
from jax.experimental.pallas import tpu as pltpu
from jax.sharding import PartitionSpec as P

TAPS = 8
SHIFT_MAX = 12
PATCH = 64
HALF = PATCH // 2
RIM = SHIFT_MAX + TAPS // 2
REACH = HALF + RIM
LANES = 128
VMEM_LIMIT = 48 * 1024 * 1024

VMEM = pl.BlockSpec(memory_space=pltpu.VMEM)
SMEM = pl.BlockSpec(memory_space=pltpu.SMEM)
HBM = pl.BlockSpec(memory_space=pltpu.HBM)
PARAMS = pltpu.CompilerParams(vmem_limit_bytes=VMEM_LIMIT)


def fourier_table(sine_sign, table_scale):
    freq_ids = np.arange(PATCH)
    phase_ids = (freq_ids[:, None] * freq_ids[None, :]) % PATCH
    angles = phase_ids * (2.0 * math.pi / PATCH)
    cosine = np.cos(angles) * table_scale
    sine_part = np.sin(angles) * (sine_sign * table_scale)
    top = np.concatenate([cosine, -sine_part], axis=1)
    bottom = np.concatenate([sine_part, cosine], axis=1)
    return np.concatenate([top, bottom], axis=0).astype(np.float32)


def paired(table):
    split = table.reshape(2, PATCH, 2, PATCH)
    wide = np.zeros((2, 2, PATCH, 2, 2, PATCH), np.float32)
    for slot in range(2):
        wide[:, slot, :, :, slot, :] = split
    return wide.reshape(4 * PATCH, 4 * PATCH)


def line_table(forward, row_patches):
    wide_lines = (row_patches + 1) * HALF
    table = np.zeros((row_patches, 2 * PATCH, 2, wide_lines), np.float32)
    transposed = forward.T.reshape(2 * PATCH, 2, PATCH)
    for row in range(row_patches):
        table[row, :, :, row * HALF : row * HALF + PATCH] = transposed
    return table.reshape(row_patches * 2 * PATCH, 2 * wide_lines)


def window_table():
    window = np.sin(math.pi * (np.arange(PATCH) + 0.5) / PATCH) ** 2
    return np.tile(np.outer(window, window), (2, 2)).astype(np.float32)


def ring_table():
    ring = np.zeros((LANES, LANES), np.float32)
    for lane in range(LANES):
        base = lane // PATCH * PATCH
        for step in (-1, 0, 1):
            ring[base + (lane + step) % PATCH, lane] = 1.0
    return ring


def edge_of(other_ref, part, side, lines):
    width = other_ref.shape[2]
    return jnp.where(
        side == 0, other_ref[part, lines, :HALF], other_ref[part, lines, width - HALF :]
    )


def load_kernel(image_ref, kernel_ref, image_out, kernel_out):
    image_out[...] = image_ref[...]
    kernel_out[...] = kernel_ref[...]


def pack_kernel(image_ref, other_ref, kernel_ref, even_ref, odd_ref):
    lines = image_ref.shape[1]
    width = image_ref.shape[2]
    side = lax.axis_index("rg")
    taps = kernel_ref[:TAPS, :]
    taps_high = taps.astype(jnp.bfloat16).astype(jnp.float32)
    taps_low = taps - taps_high
    shifts = jnp.broadcast_to(kernel_ref[TAPS : TAPS + 1, :], (TAPS, lines))

    def write(out_ref, line_start, tap_start):
        rows = slice(line_start, line_start + REACH)
        for part in range(2):
            cut = slice(part * REACH, (part + 1) * REACH)
            out_ref[cut, :] = image_ref[part, rows, :].astype(jnp.bfloat16)
        edges = jnp.concatenate([edge_of(other_ref, part, side, rows) for part in range(2)], axis=0)
        cut = slice(tap_start, tap_start + HALF)
        block = jnp.concatenate([taps_high[:, cut], taps_low[:, cut], shifts[:, cut]], axis=1)
        block = jnp.concatenate([block, jnp.zeros((HALF - TAPS, 3 * HALF), jnp.float32)], axis=0)
        cuts = [edges[i * HALF : (i + 1) * HALF] for i in range(3)]
        filler = jnp.zeros((HALF, width - 6 * HALF), jnp.float32)
        block = jnp.concatenate([block, *cuts, filler], axis=1)
        out_ref[2 * REACH :, :] = block.astype(jnp.bfloat16)

    parity = lax.rem(lax.axis_index("az"), 2)

    @pl.when(parity == 0)
    def _():
        write(even_ref, lines - REACH, lines - HALF)
        write(odd_ref, 0, 0)

    @pl.when(parity == 1)
    def _():
        write(even_ref, 0, 0)
        write(odd_ref, lines - REACH, lines - HALF)


def resample_kernel(image_ref, other_ref, kernel_ref, even_ref, odd_ref, tile_ref):
    lines = image_ref.shape[1]
    width = image_ref.shape[2]
    wide = lines + 2 * HALF
    side = lax.axis_index("rg")

    place = lax.axis_index("az")
    parity = lax.rem(place, 2)
    above = jnp.where(parity == 0, odd_ref[...], even_ref[...])
    below = jnp.where(parity == 0, even_ref[...], odd_ref[...])
    above = jnp.where(place == 0, jnp.zeros_like(above), above)
    below = jnp.where(place == lax.axis_size("az") - 1, jnp.zeros_like(below), below)

    def unpacked(message):
        block = message[2 * REACH :, :].astype(jnp.float32)
        head = block[:TAPS]
        edges = [block[:, i * HALF : (i + 1) * HALF] for i in range(3, 6)]
        return (
            head[:, :HALF] + head[:, HALF : 2 * HALF],
            head[:1, 2 * HALF : 3 * HALF],
            jnp.concatenate(edges, axis=0),
        )

    above_taps, above_shift, above_edge = unpacked(above)
    below_taps, below_shift, below_edge = unpacked(below)
    taps = jnp.concatenate([above_taps, kernel_ref[:TAPS, :], below_taps], axis=1)
    own_shift = kernel_ref[TAPS : TAPS + 1, :]
    shift = jnp.concatenate([above_shift, own_shift, below_shift], axis=1).astype(jnp.int32)

    def band(source_lines):
        count = source_lines.shape[0]
        place = lax.broadcasted_iota(jnp.int32, (count, wide), 1) - HALF
        tap_ids = source_lines - place - shift + (TAPS // 2 - 1)
        total = jnp.zeros((count, wide), jnp.float32)
        for tap in range(TAPS):
            total = jnp.where(tap_ids == tap, taps[tap : tap + 1, :], total)
        return total

    own_ids = lax.broadcasted_iota(jnp.int32, (lines, wide), 0)
    rim_ids = lax.broadcasted_iota(jnp.int32, (2 * REACH, wide), 0)
    rim_ids = jnp.where(rim_ids < REACH, rim_ids - REACH, rim_ids - REACH + lines)
    own_band = band(own_ids)
    rim_band = band(rim_ids)
    rim_high = rim_band.astype(jnp.bfloat16)
    rim_low = (rim_band - rim_high.astype(jnp.float32)).astype(jnp.bfloat16)
    rim_both = jnp.concatenate([rim_high, rim_low], axis=0)
    over_rows = (((0,), (0,)), ((), ()))
    edges = []
    for part in range(2):
        edge = edge_of(other_ref, part, side, slice(0, lines))
        own = lax.dot_general(
            own_band,
            jnp.concatenate([image_ref[part], edge], axis=1),
            over_rows,
            precision=lax.Precision.HIGHEST,
            preferred_element_type=jnp.float32,
        )
        cut = slice(part * REACH, (part + 1) * REACH)
        rim = jnp.concatenate([above[cut, :], below[cut, :]], axis=0)
        rim_edge = jnp.concatenate([above_edge[cut], below_edge[cut]], axis=0).astype(jnp.bfloat16)
        rim = jnp.concatenate([rim, rim_edge], axis=1)
        rim = jnp.concatenate([rim, rim], axis=0)
        total = own + lax.dot_general(rim_both, rim, over_rows, preferred_element_type=jnp.float32)
        tile_ref[part * wide : (part + 1) * wide, :] = total[:, :width].astype(jnp.bfloat16)
        rows = wide // 4
        edges += [total[i * rows : (i + 1) * rows, width:] for i in range(4)]
    tile_ref[2 * wide :, :] = jnp.concatenate(edges, axis=1).astype(jnp.bfloat16)


def cross(own_parts, other_parts):
    own_real, own_imag = own_parts
    other_real, other_imag = other_parts
    real = own_real * other_real + own_imag * other_imag
    imag = own_imag * other_real - own_real * other_imag
    return real, imag


def tile_parts(tile_ref, wide):
    tile = tile_ref[: 2 * wide, :].astype(jnp.float32)
    edge = tile_ref[2 * wide :, :].astype(jnp.float32)
    cuts = [edge[:, i * HALF : (i + 1) * HALF] for i in range(8)]
    edge_real = jnp.concatenate(cuts[:4], axis=0)
    edge_imag = jnp.concatenate(cuts[4:], axis=0)
    return (tile[:wide], tile[wide:]), (edge_real, edge_imag)


def filtered_of(own_ref, other_ref, table_ref, spectrum_ref, filtered_ref, lines):
    width = own_ref.shape[1]
    wide = lines + 2 * HALF
    row_patches = lines // HALF + 1
    side = lax.axis_index("rg")
    tables = split_tables(table_ref, row_patches)
    line_table_of, forward, inverse, back, ring, window = tables
    own_tile, own_edge = tile_parts(own_ref, wide)
    other_tile, other_edge = tile_parts(other_ref, wide)
    mid = jnp.concatenate(cross(own_tile, other_tile), axis=0)
    rim = jnp.concatenate(cross(own_edge, other_edge), axis=0)
    before = jnp.where(side == 0, 0.0, rim)
    after = jnp.where(side == 0, rim, 0.0)
    filler = jnp.zeros((2 * wide, LANES - 2 * HALF), jnp.float32)
    shifted = jnp.concatenate([before, mid, after, filler], axis=1).astype(jnp.bfloat16)
    both = jnp.concatenate([mid.astype(jnp.bfloat16), shifted], axis=1)
    chunks = both.shape[1] // LANES
    line_spectra = jnp.dot(line_table_of, both, preferred_element_type=jnp.float32)
    line_spectra = line_spectra.astype(jnp.bfloat16)
    pieces = []
    for row in range(row_patches):
        top = row * 2 * PATCH
        for chunk in range(chunks):
            cut = slice(chunk * LANES, (chunk + 1) * LANES)
            real = line_spectra[top : top + PATCH, cut]
            imag = line_spectra[top + PATCH : top + 2 * PATCH, cut]
            pieces.append(jnp.concatenate([real, imag], axis=1))
    patches = jnp.concatenate(pieces, axis=0)
    spectrum_ref[...] = jnp.dot(patches, forward, preferred_element_type=jnp.float32)
    pieces = []
    for block in range(row_patches * chunks):
        rows = slice(block * PATCH, (block + 1) * PATCH)
        real = spectrum_ref[rows, :LANES]
        imag = spectrum_ref[rows, LANES:]
        power = real * real + imag * imag
        power = power + pltpu.roll(power, 1, 0) + pltpu.roll(power, PATCH - 1, 0)
        smooth = jnp.dot(power.astype(jnp.bfloat16), ring, preferred_element_type=jnp.float32)
        gain = lax.rsqrt(lax.rsqrt(smooth * (1.0 / (9.0 * PATCH * PATCH)) + 1.0))
        pieces.append(jnp.concatenate([real * gain, imag * gain], axis=1).astype(jnp.bfloat16))
    shaped = jnp.concatenate(pieces, axis=0)
    range_back = jnp.dot(shaped, inverse, preferred_element_type=jnp.float32)
    range_back = range_back.astype(jnp.bfloat16)
    for chunk in range(chunks):
        totals = [[None] * (row_patches - 1) for _ in range(2)]
        for row in range(row_patches):
            top = (row * chunks + chunk) * PATCH
            block = range_back[top : top + PATCH]
            stacked = jnp.concatenate([block[:, :LANES], block[:, LANES:]], axis=0)
            patch_out = jnp.dot(back, stacked, preferred_element_type=jnp.float32) * window
            for part in range(2):
                upper = patch_out[part * PATCH : part * PATCH + HALF]
                lower = patch_out[part * PATCH + HALF : (part + 1) * PATCH]
                if row > 0:
                    totals[part][row - 1] = totals[part][row - 1] + upper
                if row < row_patches - 1:
                    totals[part][row] = lower
        for part in range(2):
            for row in range(row_patches - 1):
                top = part * lines + row * HALF
                filtered_ref[chunk, top : top + HALF] = totals[part][row]
    mids = width // LANES
    mid = jnp.concatenate([filtered_ref[i] for i in range(mids)], axis=1)
    moved = jnp.concatenate([filtered_ref[i] for i in range(mids, chunks)], axis=1)
    return mid + moved[:, HALF : HALF + width]


def own_kernel(table_ref, own_ref, out_ref, spectrum_ref, filtered_ref):
    lines = out_ref.shape[0] // 2
    out_ref[...] = filtered_of(own_ref, own_ref, table_ref, spectrum_ref, filtered_ref, lines)


def other_kernel(match_ref, table_ref, filtered_own_ref, own_ref, *refs):
    out_ref, result_ref, spectrum_ref, filtered_ref, sems = refs[-5:]
    match_count, _, _, lines, _ = out_ref.shape
    date = lax.axis_index("date")
    dates = match_ref.shape[1]

    def keep(slot, result):
        for part in range(2):
            result_ref[slot, part] = result[part * lines : (part + 1) * lines]

    keep(0, filtered_own_ref[...])
    for slot, other_ref in enumerate(refs[:-5], 1):
        keep(slot, filtered_of(own_ref, other_ref, table_ref, spectrum_ref, filtered_ref, lines))
    copies = []
    for match in range(match_count):
        slot = lax.rem(match_ref[match, date] - date + dates, dates)
        copies.append(
            pltpu.make_async_copy(result_ref.at[slot], out_ref.at[match, :, 0], sems.at[match])
        )
    for copy in copies:
        copy.start()
    for copy in copies:
        copy.wait()


def all_tables(row_patches):
    forward = fourier_table(1.0, 1.0)
    inverse = fourier_table(-1.0, 1.0 / PATCH)
    back = inverse.reshape(2, PATCH, 2, PATCH).transpose(2, 3, 0, 1).reshape(2 * PATCH, 2 * PATCH)
    window = window_table()[:PATCH, :PATCH]
    splits = []
    for _ in range(3):
        splits.append(window.astype(jnp.bfloat16).astype(np.float32))
        window = window - splits[-1]
    rows = [
        line_table(forward, row_patches),
        paired(forward),
        paired(inverse),
        np.concatenate([back, ring_table()], axis=1),
        np.concatenate([*splits, np.zeros_like(window)], axis=1),
    ]
    return np.concatenate(rows, axis=0).astype(jnp.bfloat16)


def split_tables(table_ref, row_patches):
    at = row_patches * 2 * PATCH
    line_table_of = table_ref[:at, :]
    forward = table_ref[at : at + 4 * PATCH, :]
    at += 4 * PATCH
    inverse = table_ref[at : at + 4 * PATCH, :]
    at += 4 * PATCH
    back = table_ref[at : at + LANES, :LANES]
    ring = table_ref[at : at + LANES, LANES:]
    at += LANES
    splits = table_ref[at : at + PATCH, :].astype(jnp.float32)
    window = splits[:, :PATCH] + splits[:, PATCH : 2 * PATCH] + splits[:, 2 * PATCH : 3 * PATCH]
    window = jnp.concatenate([window, window], axis=1)
    window = jnp.concatenate([window, window], axis=0)
    return line_table_of, forward, inverse, back, ring, window


def per_device(image_stack, tap_weights, offsets, matchings):
    _, _, lines, width = image_stack.shape
    match_count = matchings.shape[0]
    wide = lines + 2 * HALF
    row_patches = lines // HALF + 1
    other = lax.ppermute(image_stack, "rg", [(0, 1), (1, 0)]).reshape(2, lines, width)
    image = image_stack.reshape(2, lines, width)
    kernel = jnp.concatenate(
        [
            tap_weights.reshape(TAPS, lines),
            offsets.astype(jnp.float32),
            jnp.zeros((TAPS - 1, lines), jnp.float32),
        ],
        axis=0,
    )
    image, kernel = pl.pallas_call(
        load_kernel,
        out_shape=tuple(jax.ShapeDtypeStruct(a.shape, a.dtype) for a in (image, kernel)),
        in_specs=[VMEM] * 2,
        out_specs=(VMEM,) * 2,
        compiler_params=PARAMS,
        name="load",
    )(image, kernel)
    message = jax.ShapeDtypeStruct((2 * REACH + HALF, width), jnp.bfloat16)
    even, odd = pl.pallas_call(
        pack_kernel,
        out_shape=(message, message),
        in_specs=[VMEM] * 3,
        out_specs=(VMEM, VMEM),
        compiler_params=PARAMS,
        name="pack",
    )(image, other, kernel)
    peers = lax.axis_size("az")

    def swapped(value, start):
        pairs = [(i, i + 1) for i in range(start, peers - 1, 2)]
        paired_up = {i for pair in pairs for i in pair}
        alone = [(i, i) for i in range(peers) if i not in paired_up]
        return lax.ppermute(value, "az", pairs + [(j, i) for i, j in pairs] + alone)

    even, odd = swapped(even, 0), swapped(odd, 1)
    tile = pl.pallas_call(
        resample_kernel,
        out_shape=jax.ShapeDtypeStruct((2 * wide + wide // 4, width), jnp.bfloat16),
        in_specs=[VMEM] * 5,
        out_specs=VMEM,
        compiler_params=PARAMS,
        name="resample",
    )(image, other, kernel, even, odd)
    dates = lax.axis_size("date")
    others = [
        lax.ppermute(tile, "date", [((i + slot) % dates, i) for i in range(dates)])
        for slot in range(1, dates)
    ]
    chunks = (width + width + LANES) // LANES
    tables = jnp.asarray(all_tables(row_patches))
    scratch = [
        pltpu.VMEM((row_patches * chunks * PATCH, 2 * LANES), jnp.float32),
        pltpu.VMEM((chunks, 2 * lines, LANES), jnp.float32),
    ]
    filtered_own = pl.pallas_call(
        own_kernel,
        out_shape=jax.ShapeDtypeStruct((2 * lines, width), jnp.float32),
        in_specs=[VMEM] * 2,
        out_specs=VMEM,
        scratch_shapes=scratch,
        compiler_params=PARAMS,
        name="filter_own",
    )(tables, tile)
    return pl.pallas_call(
        other_kernel,
        out_shape=jax.ShapeDtypeStruct((match_count, 2, 1, lines, width), jnp.float32),
        in_specs=[SMEM] + [VMEM] * (3 + len(others)),
        out_specs=HBM,
        scratch_shapes=[
            pltpu.VMEM((dates, 2, lines, width), jnp.float32),
            *scratch,
            pltpu.SemaphoreType.DMA((match_count,)),
        ],
        compiler_params=PARAMS,
        name="filter_other",
    )(matchings, tables, filtered_own, tile, *others)


def solution(mesh):
    placed = (
        P(None, ("parts", "date"), "az", "rg"),
        P(None, ("parts", "date"), "az"),
        P(("parts", "date"), "az"),
        P(),
    )
    return jax.shard_map(
        per_device,
        mesh=mesh,
        in_specs=placed,
        out_specs=P(None, None, ("parts", "date"), "az", "rg"),
        check_vma=False,
    )
```

```python
import math

import jax
import jax.numpy as jnp
import numpy as np
from jax import lax
from jax.experimental import pallas as pl
from jax.experimental.pallas import tpu as pltpu
from jax.sharding import PartitionSpec as P

TAPS = 8
SHIFT_MAX = 12
PATCH = 64
HALF = PATCH // 2
RIM = SHIFT_MAX + TAPS // 2
REACH = HALF + RIM
LANES = 128
VMEM_LIMIT = 48 * 1024 * 1024

VMEM = pl.BlockSpec(memory_space=pltpu.VMEM)
SMEM = pl.BlockSpec(memory_space=pltpu.SMEM)
HBM = pl.BlockSpec(memory_space=pltpu.HBM)
PARAMS = pltpu.CompilerParams(vmem_limit_bytes=VMEM_LIMIT)


def fourier_table(sine_sign, table_scale):
    freq_ids = np.arange(PATCH)
    phase_ids = (freq_ids[:, None] * freq_ids[None, :]) % PATCH
    angles = phase_ids * (2.0 * math.pi / PATCH)
    cosine = np.cos(angles) * table_scale
    sine_part = np.sin(angles) * (sine_sign * table_scale)
    top = np.concatenate([cosine, -sine_part], axis=1)
    bottom = np.concatenate([sine_part, cosine], axis=1)
    return np.concatenate([top, bottom], axis=0).astype(np.float32)


def paired(table):
    split = table.reshape(2, PATCH, 2, PATCH)
    wide = np.zeros((2, 2, PATCH, 2, 2, PATCH), np.float32)
    for slot in range(2):
        wide[:, slot, :, :, slot, :] = split
    return wide.reshape(4 * PATCH, 4 * PATCH)


def line_table(forward, row_patches):
    wide_lines = (row_patches + 1) * HALF
    table = np.zeros((row_patches, 2 * PATCH, 2, wide_lines), np.float32)
    transposed = forward.T.reshape(2 * PATCH, 2, PATCH)
    for row in range(row_patches):
        table[row, :, :, row * HALF : row * HALF + PATCH] = transposed
    return table.reshape(row_patches * 2 * PATCH, 2 * wide_lines)


def window_table():
    window = np.sin(math.pi * (np.arange(PATCH) + 0.5) / PATCH) ** 2
    return np.tile(np.outer(window, window), (2, 2)).astype(np.float32)


def ring_table():
    ring = np.zeros((LANES, LANES), np.float32)
    for lane in range(LANES):
        base = lane // PATCH * PATCH
        for step in (-1, 0, 1):
            ring[base + (lane + step) % PATCH, lane] = 1.0
    return ring


def edge_of(other_ref, part, side, lines):
    width = other_ref.shape[2]
    return jnp.where(
        side == 0, other_ref[part, lines, :HALF], other_ref[part, lines, width - HALF :]
    )


def load_kernel(*refs):
    count = (len(refs) - 1) // 2
    copies = [
        pltpu.make_async_copy(refs[i], refs[count + i], refs[-1].at[i]) for i in range(count)
    ]
    for copy in copies:
        copy.start()
    for copy in copies:
        copy.wait()


def pack_kernel(image_ref, other_ref, taps_ref, offsets_ref, even_ref, odd_ref):
    lines = image_ref.shape[1]
    width = image_ref.shape[2]
    side = lax.axis_index("rg")
    taps = taps_ref[...]
    taps_high = taps.astype(jnp.bfloat16).astype(jnp.float32)
    taps_low = taps - taps_high
    shifts = jnp.broadcast_to(offsets_ref[...].astype(jnp.float32), (TAPS, lines))

    def write(out_ref, line_start, tap_start):
        rows = slice(line_start, line_start + REACH)
        for part in range(2):
            cut = slice(part * REACH, (part + 1) * REACH)
            out_ref[cut, :] = image_ref[part, rows, :].astype(jnp.bfloat16)
        edges = jnp.concatenate([edge_of(other_ref, part, side, rows) for part in range(2)], axis=0)
        cut = slice(tap_start, tap_start + HALF)
        block = jnp.concatenate([taps_high[:, cut], taps_low[:, cut], shifts[:, cut]], axis=1)
        block = jnp.concatenate([block, jnp.zeros((HALF - TAPS, 3 * HALF), jnp.float32)], axis=0)
        cuts = [edges[i * HALF : (i + 1) * HALF] for i in range(3)]
        filler = jnp.zeros((HALF, width - 6 * HALF), jnp.float32)
        block = jnp.concatenate([block, *cuts, filler], axis=1)
        out_ref[2 * REACH :, :] = block.astype(jnp.bfloat16)

    parity = lax.rem(lax.axis_index("az"), 2)

    @pl.when(parity == 0)
    def _():
        write(even_ref, lines - REACH, lines - HALF)
        write(odd_ref, 0, 0)

    @pl.when(parity == 1)
    def _():
        write(even_ref, 0, 0)
        write(odd_ref, lines - REACH, lines - HALF)


def resample_kernel(
    image_ref, other_ref, taps_ref, offsets_ref, even_ref, odd_ref, tile_ref
):
    lines = image_ref.shape[1]
    width = image_ref.shape[2]
    wide = lines + 2 * HALF
    side = lax.axis_index("rg")

    place = lax.axis_index("az")
    parity = lax.rem(place, 2)
    above = jnp.where(parity == 0, odd_ref[...], even_ref[...])
    below = jnp.where(parity == 0, even_ref[...], odd_ref[...])
    above = jnp.where(place == 0, jnp.zeros_like(above), above)
    below = jnp.where(place == lax.axis_size("az") - 1, jnp.zeros_like(below), below)

    def unpacked(message):
        block = message[2 * REACH :, :].astype(jnp.float32)
        head = block[:TAPS]
        edges = [block[:, i * HALF : (i + 1) * HALF] for i in range(3, 6)]
        return (
            head[:, :HALF] + head[:, HALF : 2 * HALF],
            head[:1, 2 * HALF : 3 * HALF],
            jnp.concatenate(edges, axis=0),
        )

    above_taps, above_shift, above_edge = unpacked(above)
    below_taps, below_shift, below_edge = unpacked(below)
    taps = jnp.concatenate([above_taps, taps_ref[...], below_taps], axis=1)
    own_shift = offsets_ref[...].astype(jnp.float32)
    shift = jnp.concatenate([above_shift, own_shift, below_shift], axis=1).astype(jnp.int32)

    def band(source_lines):
        count = source_lines.shape[0]
        place = lax.broadcasted_iota(jnp.int32, (count, wide), 1) - HALF
        tap_ids = source_lines - place - shift + (TAPS // 2 - 1)
        total = jnp.zeros((count, wide), jnp.float32)
        for tap in range(TAPS):
            total = jnp.where(tap_ids == tap, taps[tap : tap + 1, :], total)
        return total

    own_ids = lax.broadcasted_iota(jnp.int32, (lines, wide), 0)
    rim_ids = lax.broadcasted_iota(jnp.int32, (2 * REACH, wide), 0)
    rim_ids = jnp.where(rim_ids < REACH, rim_ids - REACH, rim_ids - REACH + lines)
    own_band = band(own_ids)
    rim_band = band(rim_ids)
    rim_high = rim_band.astype(jnp.bfloat16)
    rim_low = (rim_band - rim_high.astype(jnp.float32)).astype(jnp.bfloat16)
    rim_both = jnp.concatenate([rim_high, rim_low], axis=0)
    over_rows = (((0,), (0,)), ((), ()))
    edges = []
    for part in range(2):
        edge = edge_of(other_ref, part, side, slice(0, lines))
        own = lax.dot_general(
            own_band,
            jnp.concatenate([image_ref[part], edge], axis=1),
            over_rows,
            precision=lax.Precision.HIGHEST,
            preferred_element_type=jnp.float32,
        )
        cut = slice(part * REACH, (part + 1) * REACH)
        rim = jnp.concatenate([above[cut, :], below[cut, :]], axis=0)
        rim_edge = jnp.concatenate([above_edge[cut], below_edge[cut]], axis=0).astype(jnp.bfloat16)
        rim = jnp.concatenate([rim, rim_edge], axis=1)
        rim = jnp.concatenate([rim, rim], axis=0)
        total = own + lax.dot_general(rim_both, rim, over_rows, preferred_element_type=jnp.float32)
        tile_ref[part * wide : (part + 1) * wide, :] = total[:, :width].astype(jnp.bfloat16)
        rows = wide // 4
        edges += [total[i * rows : (i + 1) * rows, width:] for i in range(4)]
    tile_ref[2 * wide :, :] = jnp.concatenate(edges, axis=1).astype(jnp.bfloat16)


def cross(own_parts, other_parts):
    own_real, own_imag = own_parts
    other_real, other_imag = other_parts
    real = own_real * other_real + own_imag * other_imag
    imag = own_imag * other_real - own_real * other_imag
    return real, imag


def tile_parts(tile_ref, wide):
    tile = tile_ref[: 2 * wide, :].astype(jnp.float32)
    edge = tile_ref[2 * wide :, :].astype(jnp.float32)
    cuts = [edge[:, i * HALF : (i + 1) * HALF] for i in range(8)]
    edge_real = jnp.concatenate(cuts[:4], axis=0)
    edge_imag = jnp.concatenate(cuts[4:], axis=0)
    return (tile[:wide], tile[wide:]), (edge_real, edge_imag)


def filtered_of(own_ref, other_ref, table_ref, spectrum_ref, filtered_ref, lines):
    width = own_ref.shape[1]
    wide = lines + 2 * HALF
    row_patches = lines // HALF + 1
    side = lax.axis_index("rg")
    tables = split_tables(table_ref, row_patches)
    line_table_of, forward, inverse, back, ring, window = tables
    own_tile, own_edge = tile_parts(own_ref, wide)
    other_tile, other_edge = tile_parts(other_ref, wide)
    mid = jnp.concatenate(cross(own_tile, other_tile), axis=0)
    rim = jnp.concatenate(cross(own_edge, other_edge), axis=0)
    before = jnp.where(side == 0, 0.0, rim)
    after = jnp.where(side == 0, rim, 0.0)
    filler = jnp.zeros((2 * wide, LANES - 2 * HALF), jnp.float32)
    shifted = jnp.concatenate([before, mid, after, filler], axis=1).astype(jnp.bfloat16)
    both = jnp.concatenate([mid.astype(jnp.bfloat16), shifted], axis=1)
    chunks = both.shape[1] // LANES
    line_spectra = jnp.dot(line_table_of, both, preferred_element_type=jnp.float32)
    line_spectra = line_spectra.astype(jnp.bfloat16)
    pieces = []
    for row in range(row_patches):
        top = row * 2 * PATCH
        for chunk in range(chunks):
            cut = slice(chunk * LANES, (chunk + 1) * LANES)
            real = line_spectra[top : top + PATCH, cut]
            imag = line_spectra[top + PATCH : top + 2 * PATCH, cut]
            pieces.append(jnp.concatenate([real, imag], axis=1))
    patches = jnp.concatenate(pieces, axis=0)
    spectrum_ref[...] = jnp.dot(patches, forward, preferred_element_type=jnp.float32)
    pieces = []
    for block in range(row_patches * chunks):
        rows = slice(block * PATCH, (block + 1) * PATCH)
        real = spectrum_ref[rows, :LANES]
        imag = spectrum_ref[rows, LANES:]
        power = real * real + imag * imag
        power = power + pltpu.roll(power, 1, 0) + pltpu.roll(power, PATCH - 1, 0)
        smooth = jnp.dot(power.astype(jnp.bfloat16), ring, preferred_element_type=jnp.float32)
        gain = lax.rsqrt(lax.rsqrt(smooth * (1.0 / (9.0 * PATCH * PATCH)) + 1.0))
        pieces.append(jnp.concatenate([real * gain, imag * gain], axis=1).astype(jnp.bfloat16))
    shaped = jnp.concatenate(pieces, axis=0)
    range_back = jnp.dot(shaped, inverse, preferred_element_type=jnp.float32)
    range_back = range_back.astype(jnp.bfloat16)
    for chunk in range(chunks):
        totals = [[None] * (row_patches - 1) for _ in range(2)]
        for row in range(row_patches):
            top = (row * chunks + chunk) * PATCH
            block = range_back[top : top + PATCH]
            stacked = jnp.concatenate([block[:, :LANES], block[:, LANES:]], axis=0)
            patch_out = jnp.dot(back, stacked, preferred_element_type=jnp.float32) * window
            for part in range(2):
                upper = patch_out[part * PATCH : part * PATCH + HALF]
                lower = patch_out[part * PATCH + HALF : (part + 1) * PATCH]
                if row > 0:
                    totals[part][row - 1] = totals[part][row - 1] + upper
                if row < row_patches - 1:
                    totals[part][row] = lower
        for part in range(2):
            for row in range(row_patches - 1):
                top = part * lines + row * HALF
                filtered_ref[chunk, top : top + HALF] = totals[part][row]
    mids = width // LANES
    mid = jnp.concatenate([filtered_ref[i] for i in range(mids)], axis=1)
    moved = jnp.concatenate([filtered_ref[i] for i in range(mids, chunks)], axis=1)
    return mid + moved[:, HALF : HALF + width]


def own_kernel(table_ref, own_ref, out_ref, spectrum_ref, filtered_ref):
    lines = out_ref.shape[0] // 2
    out_ref[...] = filtered_of(own_ref, own_ref, table_ref, spectrum_ref, filtered_ref, lines)


def other_kernel(match_ref, table_ref, filtered_own_ref, own_ref, *refs):
    out_ref, result_ref, spectrum_ref, filtered_ref, sems = refs[-5:]
    match_count, _, _, lines, _ = out_ref.shape
    date = lax.axis_index("date")
    dates = match_ref.shape[1]

    def keep(slot, result):
        for part in range(2):
            result_ref[slot, part] = result[part * lines : (part + 1) * lines]

    keep(0, filtered_own_ref[...])
    for slot, other_ref in enumerate(refs[:-5], 1):
        keep(slot, filtered_of(own_ref, other_ref, table_ref, spectrum_ref, filtered_ref, lines))
    copies = []
    for match in range(match_count):
        slot = lax.rem(match_ref[match, date] - date + dates, dates)
        copies.append(
            pltpu.make_async_copy(result_ref.at[slot], out_ref.at[match, :, 0], sems.at[match])
        )
    for copy in copies:
        copy.start()
    for copy in copies:
        copy.wait()


def all_tables(row_patches):
    forward = fourier_table(1.0, 1.0)
    inverse = fourier_table(-1.0, 1.0 / PATCH)
    back = inverse.reshape(2, PATCH, 2, PATCH).transpose(2, 3, 0, 1).reshape(2 * PATCH, 2 * PATCH)
    window = window_table()[:PATCH, :PATCH]
    splits = []
    for _ in range(3):
        splits.append(window.astype(jnp.bfloat16).astype(np.float32))
        window = window - splits[-1]
    rows = [
        line_table(forward, row_patches),
        paired(forward),
        paired(inverse),
        np.concatenate([back, ring_table()], axis=1),
        np.concatenate([*splits, np.zeros_like(window)], axis=1),
    ]
    return np.concatenate(rows, axis=0).astype(jnp.bfloat16)


def split_tables(table_ref, row_patches):
    at = row_patches * 2 * PATCH
    line_table_of = table_ref[:at, :]
    forward = table_ref[at : at + 4 * PATCH, :]
    at += 4 * PATCH
    inverse = table_ref[at : at + 4 * PATCH, :]
    at += 4 * PATCH
    back = table_ref[at : at + LANES, :LANES]
    ring = table_ref[at : at + LANES, LANES:]
    at += LANES
    splits = table_ref[at : at + PATCH, :].astype(jnp.float32)
    window = splits[:, :PATCH] + splits[:, PATCH : 2 * PATCH] + splits[:, 2 * PATCH : 3 * PATCH]
    window = jnp.concatenate([window, window], axis=1)
    window = jnp.concatenate([window, window], axis=0)
    return line_table_of, forward, inverse, back, ring, window


def per_device(image_stack, tap_weights, offsets, matchings):
    _, _, lines, width = image_stack.shape
    match_count = matchings.shape[0]
    wide = lines + 2 * HALF
    row_patches = lines // HALF + 1
    other = lax.ppermute(image_stack, "rg", [(0, 1), (1, 0)]).reshape(2, lines, width)
    arguments = (
        image_stack.reshape(2, lines, width),
        tap_weights.reshape(TAPS, lines),
        offsets,
    )
    image, taps, offsets = pl.pallas_call(
        load_kernel,
        out_shape=tuple(pltpu.VMEM(a.shape, a.dtype) for a in arguments),
        in_specs=[HBM] * 3,
        out_specs=(VMEM,) * 3,
        scratch_shapes=[pltpu.SemaphoreType.DMA((3,))],
        compiler_params=PARAMS,
        name="load",
    )(*(pltpu.with_memory_space_constraint(a, pltpu.HBM) for a in arguments))
    message = jax.ShapeDtypeStruct((2 * REACH + HALF, width), jnp.bfloat16)
    even, odd = pl.pallas_call(
        pack_kernel,
        out_shape=(message, message),
        in_specs=[VMEM] * 4,
        out_specs=(VMEM, VMEM),
        compiler_params=PARAMS,
        name="pack",
    )(image, other, taps, offsets)
    peers = lax.axis_size("az")

    def swapped(value, start):
        pairs = [(i, (i + 1) % peers) for i in range(start, peers, 2)]
        return lax.ppermute(value, "az", pairs + [(j, i) for i, j in pairs])

    even, odd = swapped(even, 0), swapped(odd, 1)
    tile = pl.pallas_call(
        resample_kernel,
        out_shape=jax.ShapeDtypeStruct((2 * wide + wide // 4, width), jnp.bfloat16),
        in_specs=[VMEM] * 6,
        out_specs=VMEM,
        compiler_params=PARAMS,
        name="resample",
    )(image, other, taps, offsets, even, odd)
    dates = lax.axis_size("date")
    others = [
        lax.ppermute(tile, "date", [((i + slot) % dates, i) for i in range(dates)])
        for slot in range(1, dates)
    ]
    chunks = (width + width + LANES) // LANES
    tables = jnp.asarray(all_tables(row_patches))
    scratch = [
        pltpu.VMEM((row_patches * chunks * PATCH, 2 * LANES), jnp.float32),
        pltpu.VMEM((chunks, 2 * lines, LANES), jnp.float32),
    ]
    filtered_own = pl.pallas_call(
        own_kernel,
        out_shape=jax.ShapeDtypeStruct((2 * lines, width), jnp.float32),
        in_specs=[VMEM] * 2,
        out_specs=VMEM,
        scratch_shapes=scratch,
        compiler_params=PARAMS,
        name="filter_own",
    )(tables, tile)
    return pl.pallas_call(
        other_kernel,
        out_shape=jax.ShapeDtypeStruct((match_count, 2, 1, lines, width), jnp.float32),
        in_specs=[SMEM] + [VMEM] * (3 + len(others)),
        out_specs=HBM,
        scratch_shapes=[
            pltpu.VMEM((dates, 2, lines, width), jnp.float32),
            *scratch,
            pltpu.SemaphoreType.DMA((match_count,)),
        ],
        compiler_params=PARAMS,
        name="filter_other",
    )(matchings, tables, filtered_own, tile, *others)


def solution(mesh):
    placed = (
        P(None, ("parts", "date"), "az", "rg"),
        P(None, ("parts", "date"), "az"),
        P(("parts", "date"), "az"),
        P(),
    )
    return jax.shard_map(
        per_device,
        mesh=mesh,
        in_specs=placed,
        out_specs=P(None, None, ("parts", "date"), "az", "rg"),
        check_vma=False,
    )
```

```python
import math

import jax
import jax.numpy as jnp
import numpy as np
from jax import lax
from jax.experimental import pallas as pl
from jax.experimental.pallas import tpu as pltpu
from jax.sharding import PartitionSpec as P

TAPS = 8
SHIFT_MAX = 12
PATCH = 64
HALF = PATCH // 2
RIM = SHIFT_MAX + TAPS // 2
REACH = HALF + RIM
LANES = 128
VMEM_LIMIT = 48 * 1024 * 1024

VMEM = pl.BlockSpec(memory_space=pltpu.VMEM)
SMEM = pl.BlockSpec(memory_space=pltpu.SMEM)
HBM = pl.BlockSpec(memory_space=pltpu.HBM)
PARAMS = pltpu.CompilerParams(vmem_limit_bytes=VMEM_LIMIT)


def fourier_table(sine_sign, table_scale):
    freq_ids = np.arange(PATCH)
    phase_ids = (freq_ids[:, None] * freq_ids[None, :]) % PATCH
    angles = phase_ids * (2.0 * math.pi / PATCH)
    cosine = np.cos(angles) * table_scale
    sine_part = np.sin(angles) * (sine_sign * table_scale)
    top = np.concatenate([cosine, -sine_part], axis=1)
    bottom = np.concatenate([sine_part, cosine], axis=1)
    return np.concatenate([top, bottom], axis=0).astype(np.float32)


def paired(table):
    split = table.reshape(2, PATCH, 2, PATCH)
    wide = np.zeros((2, 2, PATCH, 2, 2, PATCH), np.float32)
    for slot in range(2):
        wide[:, slot, :, :, slot, :] = split
    return wide.reshape(4 * PATCH, 4 * PATCH)


def line_table(forward, row_patches):
    wide_lines = (row_patches + 1) * HALF
    table = np.zeros((row_patches, 2 * PATCH, 2, wide_lines), np.float32)
    transposed = forward.T.reshape(2 * PATCH, 2, PATCH)
    for row in range(row_patches):
        table[row, :, :, row * HALF : row * HALF + PATCH] = transposed
    return table.reshape(row_patches * 2 * PATCH, 2 * wide_lines)


def window_table():
    window = np.sin(math.pi * (np.arange(PATCH) + 0.5) / PATCH) ** 2
    return np.tile(np.outer(window, window), (2, 2)).astype(np.float32)


def ring_table():
    ring = np.zeros((LANES, LANES), np.float32)
    for lane in range(LANES):
        base = lane // PATCH * PATCH
        for step in (-1, 0, 1):
            ring[base + (lane + step) % PATCH, lane] = 1.0
    return ring


def edge_of(other_ref, part, side, lines):
    width = other_ref.shape[2]
    return jnp.where(
        side == 0, other_ref[part, lines, :HALF], other_ref[part, lines, width - HALF :]
    )


def load_kernel(*refs):
    count = (len(refs) - 1) // 2
    copies = [
        pltpu.make_async_copy(refs[i], refs[count + i], refs[-1].at[i]) for i in range(count)
    ]
    for copy in copies:
        copy.start()
    for copy in copies:
        copy.wait()


def pack_kernel(image_ref, other_ref, taps_ref, offsets_ref, even_ref, odd_ref):
    lines = image_ref.shape[1]
    width = image_ref.shape[2]
    side = lax.axis_index("rg")
    taps = taps_ref[...]
    taps_high = taps.astype(jnp.bfloat16).astype(jnp.float32)
    taps_low = taps - taps_high
    shifts = jnp.broadcast_to(offsets_ref[...].astype(jnp.float32), (TAPS, lines))

    def write(out_ref, line_start, tap_start):
        rows = slice(line_start, line_start + REACH)
        for part in range(2):
            cut = slice(part * REACH, (part + 1) * REACH)
            out_ref[cut, :] = image_ref[part, rows, :].astype(jnp.bfloat16)
        edges = jnp.concatenate([edge_of(other_ref, part, side, rows) for part in range(2)], axis=0)
        cut = slice(tap_start, tap_start + HALF)
        block = jnp.concatenate([taps_high[:, cut], taps_low[:, cut], shifts[:, cut]], axis=1)
        block = jnp.concatenate([block, jnp.zeros((HALF - TAPS, 3 * HALF), jnp.float32)], axis=0)
        cuts = [edges[i * HALF : (i + 1) * HALF] for i in range(3)]
        filler = jnp.zeros((HALF, width - 6 * HALF), jnp.float32)
        block = jnp.concatenate([block, *cuts, filler], axis=1)
        out_ref[2 * REACH :, :] = block.astype(jnp.bfloat16)

    parity = lax.rem(lax.axis_index("az"), 2)

    @pl.when(parity == 0)
    def _():
        write(even_ref, lines - REACH, lines - HALF)
        write(odd_ref, 0, 0)

    @pl.when(parity == 1)
    def _():
        write(even_ref, 0, 0)
        write(odd_ref, lines - REACH, lines - HALF)


def resample_kernel(
    image_ref, other_ref, taps_ref, offsets_ref, even_ref, odd_ref, tile_ref
):
    lines = image_ref.shape[1]
    width = image_ref.shape[2]
    wide = lines + 2 * HALF
    side = lax.axis_index("rg")

    place = lax.axis_index("az")
    parity = lax.rem(place, 2)
    above = jnp.where(parity == 0, odd_ref[...], even_ref[...])
    below = jnp.where(parity == 0, even_ref[...], odd_ref[...])
    above = jnp.where(place == 0, jnp.zeros_like(above), above)
    below = jnp.where(place == lax.axis_size("az") - 1, jnp.zeros_like(below), below)

    def unpacked(message):
        block = message[2 * REACH :, :].astype(jnp.float32)
        head = block[:TAPS]
        edges = [block[:, i * HALF : (i + 1) * HALF] for i in range(3, 6)]
        return (
            head[:, :HALF] + head[:, HALF : 2 * HALF],
            head[:1, 2 * HALF : 3 * HALF],
            jnp.concatenate(edges, axis=0),
        )

    above_taps, above_shift, above_edge = unpacked(above)
    below_taps, below_shift, below_edge = unpacked(below)
    taps = jnp.concatenate([above_taps, taps_ref[...], below_taps], axis=1)
    own_shift = offsets_ref[...].astype(jnp.float32)
    shift = jnp.concatenate([above_shift, own_shift, below_shift], axis=1).astype(jnp.int32)

    def band(source_lines):
        count = source_lines.shape[0]
        place = lax.broadcasted_iota(jnp.int32, (count, wide), 1) - HALF
        tap_ids = source_lines - place - shift + (TAPS // 2 - 1)
        total = jnp.zeros((count, wide), jnp.float32)
        for tap in range(TAPS):
            total = jnp.where(tap_ids == tap, taps[tap : tap + 1, :], total)
        return total

    own_ids = lax.broadcasted_iota(jnp.int32, (lines, wide), 0)
    rim_ids = lax.broadcasted_iota(jnp.int32, (2 * REACH, wide), 0)
    rim_ids = jnp.where(rim_ids < REACH, rim_ids - REACH, rim_ids - REACH + lines)
    own_band = band(own_ids)
    rim_band = band(rim_ids)
    rim_high = rim_band.astype(jnp.bfloat16)
    rim_low = (rim_band - rim_high.astype(jnp.float32)).astype(jnp.bfloat16)
    rim_both = jnp.concatenate([rim_high, rim_low], axis=0)
    over_rows = (((0,), (0,)), ((), ()))
    edges = []
    for part in range(2):
        edge = edge_of(other_ref, part, side, slice(0, lines))
        own = lax.dot_general(
            own_band,
            jnp.concatenate([image_ref[part], edge], axis=1),
            over_rows,
            precision=lax.Precision.HIGHEST,
            preferred_element_type=jnp.float32,
        )
        cut = slice(part * REACH, (part + 1) * REACH)
        rim = jnp.concatenate([above[cut, :], below[cut, :]], axis=0)
        rim_edge = jnp.concatenate([above_edge[cut], below_edge[cut]], axis=0).astype(jnp.bfloat16)
        rim = jnp.concatenate([rim, rim_edge], axis=1)
        rim = jnp.concatenate([rim, rim], axis=0)
        total = own + lax.dot_general(rim_both, rim, over_rows, preferred_element_type=jnp.float32)
        tile_ref[part * wide : (part + 1) * wide, :] = total[:, :width].astype(jnp.bfloat16)
        rows = wide // 4
        edges += [total[i * rows : (i + 1) * rows, width:] for i in range(4)]
    tile_ref[2 * wide :, :] = jnp.concatenate(edges, axis=1).astype(jnp.bfloat16)


def cross(own_parts, other_parts):
    own_real, own_imag = own_parts
    other_real, other_imag = other_parts
    real = own_real * other_real + own_imag * other_imag
    imag = own_imag * other_real - own_real * other_imag
    return real, imag


def tile_parts(tile_ref, wide):
    tile = tile_ref[: 2 * wide, :].astype(jnp.float32)
    edge = tile_ref[2 * wide :, :].astype(jnp.float32)
    cuts = [edge[:, i * HALF : (i + 1) * HALF] for i in range(8)]
    edge_real = jnp.concatenate(cuts[:4], axis=0)
    edge_imag = jnp.concatenate(cuts[4:], axis=0)
    return (tile[:wide], tile[wide:]), (edge_real, edge_imag)


def filtered_of(own_ref, other_ref, table_ref, spectrum_ref, filtered_ref, lines):
    width = own_ref.shape[1]
    wide = lines + 2 * HALF
    row_patches = lines // HALF + 1
    side = lax.axis_index("rg")
    tables = split_tables(table_ref, row_patches)
    line_table_of, forward, inverse, back, ring, window = tables
    own_tile, own_edge = tile_parts(own_ref, wide)
    other_tile, other_edge = tile_parts(other_ref, wide)
    mid = jnp.concatenate(cross(own_tile, other_tile), axis=0)
    rim = jnp.concatenate(cross(own_edge, other_edge), axis=0)
    before = jnp.where(side == 0, 0.0, rim)
    after = jnp.where(side == 0, rim, 0.0)
    filler = jnp.zeros((2 * wide, LANES - 2 * HALF), jnp.float32)
    shifted = jnp.concatenate([before, mid, after, filler], axis=1).astype(jnp.bfloat16)
    both = jnp.concatenate([mid.astype(jnp.bfloat16), shifted], axis=1)
    chunks = both.shape[1] // LANES
    line_spectra = jnp.dot(line_table_of, both, preferred_element_type=jnp.float32)
    line_spectra = line_spectra.astype(jnp.bfloat16)
    pieces = []
    for row in range(row_patches):
        top = row * 2 * PATCH
        for chunk in range(chunks):
            cut = slice(chunk * LANES, (chunk + 1) * LANES)
            real = line_spectra[top : top + PATCH, cut]
            imag = line_spectra[top + PATCH : top + 2 * PATCH, cut]
            pieces.append(jnp.concatenate([real, imag], axis=1))
    patches = jnp.concatenate(pieces, axis=0)
    spectrum_ref[...] = jnp.dot(patches, forward, preferred_element_type=jnp.float32)
    pieces = []
    for block in range(row_patches * chunks):
        rows = slice(block * PATCH, (block + 1) * PATCH)
        real = spectrum_ref[rows, :LANES]
        imag = spectrum_ref[rows, LANES:]
        power = real * real + imag * imag
        power = power + pltpu.roll(power, 1, 0) + pltpu.roll(power, PATCH - 1, 0)
        smooth = jnp.dot(power.astype(jnp.bfloat16), ring, preferred_element_type=jnp.float32)
        gain = lax.rsqrt(lax.rsqrt(smooth * (1.0 / (9.0 * PATCH * PATCH)) + 1.0))
        pieces.append(jnp.concatenate([real * gain, imag * gain], axis=1).astype(jnp.bfloat16))
    shaped = jnp.concatenate(pieces, axis=0)
    range_back = jnp.dot(shaped, inverse, preferred_element_type=jnp.float32)
    range_back = range_back.astype(jnp.bfloat16)
    for chunk in range(chunks):
        totals = [[None] * (row_patches - 1) for _ in range(2)]
        for row in range(row_patches):
            top = (row * chunks + chunk) * PATCH
            block = range_back[top : top + PATCH]
            stacked = jnp.concatenate([block[:, :LANES], block[:, LANES:]], axis=0)
            patch_out = jnp.dot(back, stacked, preferred_element_type=jnp.float32) * window
            for part in range(2):
                upper = patch_out[part * PATCH : part * PATCH + HALF]
                lower = patch_out[part * PATCH + HALF : (part + 1) * PATCH]
                if row > 0:
                    totals[part][row - 1] = totals[part][row - 1] + upper
                if row < row_patches - 1:
                    totals[part][row] = lower
        for part in range(2):
            for row in range(row_patches - 1):
                top = part * lines + row * HALF
                filtered_ref[chunk, top : top + HALF] = totals[part][row]
    mids = width // LANES
    mid = jnp.concatenate([filtered_ref[i] for i in range(mids)], axis=1)
    moved = jnp.concatenate([filtered_ref[i] for i in range(mids, chunks)], axis=1)
    return mid + moved[:, HALF : HALF + width]


def own_kernel(table_ref, own_ref, out_ref, spectrum_ref, filtered_ref):
    lines = out_ref.shape[0] // 2
    out_ref[...] = filtered_of(own_ref, own_ref, table_ref, spectrum_ref, filtered_ref, lines)


def other_kernel(match_ref, table_ref, filtered_own_ref, own_ref, *refs):
    out_ref, result_ref, spectrum_ref, filtered_ref, sems = refs[-5:]
    match_count, _, _, lines, _ = out_ref.shape
    date = lax.axis_index("date")
    dates = match_ref.shape[1]

    def keep(slot, result):
        for part in range(2):
            result_ref[slot, part] = result[part * lines : (part + 1) * lines]

    keep(0, filtered_own_ref[...])
    for slot, other_ref in enumerate(refs[:-5], 1):
        keep(slot, filtered_of(own_ref, other_ref, table_ref, spectrum_ref, filtered_ref, lines))
    copies = []
    for match in range(match_count):
        slot = lax.rem(match_ref[match, date] - date + dates, dates)
        copies.append(
            pltpu.make_async_copy(result_ref.at[slot], out_ref.at[match, :, 0], sems.at[match])
        )
    for copy in copies:
        copy.start()
    for copy in copies:
        copy.wait()


def all_tables(row_patches):
    forward = fourier_table(1.0, 1.0)
    inverse = fourier_table(-1.0, 1.0 / PATCH)
    back = inverse.reshape(2, PATCH, 2, PATCH).transpose(2, 3, 0, 1).reshape(2 * PATCH, 2 * PATCH)
    window = window_table()[:PATCH, :PATCH]
    splits = []
    for _ in range(3):
        splits.append(window.astype(jnp.bfloat16).astype(np.float32))
        window = window - splits[-1]
    rows = [
        line_table(forward, row_patches),
        paired(forward),
        paired(inverse),
        np.concatenate([back, ring_table()], axis=1),
        np.concatenate([*splits, np.zeros_like(window)], axis=1),
    ]
    return np.concatenate(rows, axis=0).astype(jnp.bfloat16)


def split_tables(table_ref, row_patches):
    at = row_patches * 2 * PATCH
    line_table_of = table_ref[:at, :]
    forward = table_ref[at : at + 4 * PATCH, :]
    at += 4 * PATCH
    inverse = table_ref[at : at + 4 * PATCH, :]
    at += 4 * PATCH
    back = table_ref[at : at + LANES, :LANES]
    ring = table_ref[at : at + LANES, LANES:]
    at += LANES
    splits = table_ref[at : at + PATCH, :].astype(jnp.float32)
    window = splits[:, :PATCH] + splits[:, PATCH : 2 * PATCH] + splits[:, 2 * PATCH : 3 * PATCH]
    window = jnp.concatenate([window, window], axis=1)
    window = jnp.concatenate([window, window], axis=0)
    return line_table_of, forward, inverse, back, ring, window


def per_device(image_stack, tap_weights, offsets, matchings):
    _, _, lines, width = image_stack.shape
    match_count = matchings.shape[0]
    wide = lines + 2 * HALF
    row_patches = lines // HALF + 1
    other = lax.ppermute(image_stack, "rg", [(0, 1), (1, 0)]).reshape(2, lines, width)
    arguments = (
        image_stack.reshape(2, lines, width),
        tap_weights.reshape(TAPS, lines),
        offsets,
    )
    image, taps, offsets = pl.pallas_call(
        load_kernel,
        out_shape=tuple(pltpu.VMEM(a.shape, a.dtype) for a in arguments),
        in_specs=[HBM] * 3,
        out_specs=(VMEM,) * 3,
        scratch_shapes=[pltpu.SemaphoreType.DMA((3,))],
        compiler_params=PARAMS,
        name="load",
    )(*(pltpu.with_memory_space_constraint(a, pltpu.HBM) for a in arguments))
    message = jax.ShapeDtypeStruct((2 * REACH + HALF, width), jnp.bfloat16)
    even, odd = pl.pallas_call(
        pack_kernel,
        out_shape=(message, message),
        in_specs=[VMEM] * 4,
        out_specs=(VMEM, VMEM),
        compiler_params=PARAMS,
        name="pack",
    )(image, other, taps, offsets)
    peers = lax.axis_size("az")

    def swapped(value, start):
        paired = {i: i + 1 for i in range(start, peers - 1, 2)}
        paired.update({j: i for i, j in paired.items()})
        pairs = [
            (2 * i + core, 2 * paired[i] + core if i in paired else 2 * i + 1 - core)
            for i in range(peers)
            for core in range(2)
        ]
        return lax.ppermute(value, ("az", "rg"), pairs)

    even, odd = swapped(even, 0), swapped(odd, 1)
    tile = pl.pallas_call(
        resample_kernel,
        out_shape=jax.ShapeDtypeStruct((2 * wide + wide // 4, width), jnp.bfloat16),
        in_specs=[VMEM] * 6,
        out_specs=VMEM,
        compiler_params=PARAMS,
        name="resample",
    )(image, other, taps, offsets, even, odd)
    dates = lax.axis_size("date")
    others = [
        lax.ppermute(tile, "date", [((i + slot) % dates, i) for i in range(dates)])
        for slot in range(1, dates)
    ]
    chunks = (width + width + LANES) // LANES
    tables = jnp.asarray(all_tables(row_patches))
    scratch = [
        pltpu.VMEM((row_patches * chunks * PATCH, 2 * LANES), jnp.float32),
        pltpu.VMEM((chunks, 2 * lines, LANES), jnp.float32),
    ]
    filtered_own = pl.pallas_call(
        own_kernel,
        out_shape=jax.ShapeDtypeStruct((2 * lines, width), jnp.float32),
        in_specs=[VMEM] * 2,
        out_specs=VMEM,
        scratch_shapes=scratch,
        compiler_params=PARAMS,
        name="filter_own",
    )(tables, tile)
    return pl.pallas_call(
        other_kernel,
        out_shape=jax.ShapeDtypeStruct((match_count, 2, 1, lines, width), jnp.float32),
        in_specs=[SMEM] + [VMEM] * (3 + len(others)),
        out_specs=HBM,
        scratch_shapes=[
            pltpu.VMEM((dates, 2, lines, width), jnp.float32),
            *scratch,
            pltpu.SemaphoreType.DMA((match_count,)),
        ],
        compiler_params=PARAMS,
        name="filter_other",
    )(matchings, tables, filtered_own, tile, *others)


def solution(mesh):
    placed = (
        P(None, ("parts", "date"), "az", "rg"),
        P(None, ("parts", "date"), "az"),
        P(("parts", "date"), "az"),
        P(),
    )
    return jax.shard_map(
        per_device,
        mesh=mesh,
        in_specs=placed,
        out_specs=P(None, None, ("parts", "date"), "az", "rg"),
        check_vma=False,
    )
```

```python
import functools
import math

import jax
import jax.numpy as jnp
import numpy as np
from jax import lax
from jax.experimental import pallas as pl
from jax.experimental.pallas import tpu as pltpu
from jax.sharding import PartitionSpec as P

TAPS = 8
SHIFT_MAX = 12
PATCH = 64
HALF = PATCH // 2
RIM = SHIFT_MAX + TAPS // 2
REACH = HALF + RIM
LANES = 128
EDGE_ROWS = 16
VMEM_LIMIT = 48 * 1024 * 1024

VMEM = pl.BlockSpec(memory_space=pltpu.VMEM)
SMEM = pl.BlockSpec(memory_space=pltpu.SMEM)
HBM = pl.BlockSpec(memory_space=pltpu.HBM)
PARAMS = pltpu.CompilerParams(vmem_limit_bytes=VMEM_LIMIT)


def fourier_table(sine_sign, table_scale):
    freq_ids = np.arange(PATCH)
    phase_ids = (freq_ids[:, None] * freq_ids[None, :]) % PATCH
    angles = phase_ids * (2.0 * math.pi / PATCH)
    cosine = np.cos(angles) * table_scale
    sine_part = np.sin(angles) * (sine_sign * table_scale)
    top = np.concatenate([cosine, -sine_part], axis=1)
    bottom = np.concatenate([sine_part, cosine], axis=1)
    return np.concatenate([top, bottom], axis=0).astype(np.float32)


def paired(table):
    split = table.reshape(2, PATCH, 2, PATCH)
    wide = np.zeros((2, 2, PATCH, 2, 2, PATCH), np.float32)
    for slot in range(2):
        wide[:, slot, :, :, slot, :] = split
    return wide.reshape(4 * PATCH, 4 * PATCH)


def line_table(forward, order):
    return forward.T.reshape(2 * PATCH, 2, PATCH)[:, :, order].reshape(2 * PATCH, 2 * PATCH)


def window_table():
    window = np.sin(math.pi * (np.arange(PATCH) + 0.5) / PATCH) ** 2
    return np.tile(np.outer(window, window), (2, 2)).astype(np.float32)


def ring_table():
    ring = np.zeros((LANES, LANES), np.float32)
    for lane in range(LANES):
        base = lane // PATCH * PATCH
        for step in (-1, 0, 1):
            ring[base + (lane + step) % PATCH, lane] = 1.0
    return ring


def edge_of(other_ref, part, side, lines):
    width = other_ref.shape[2]
    return jnp.where(
        side == 0, other_ref[part, lines, :HALF], other_ref[part, lines, width - HALF :]
    )


def load_kernel(*refs):
    count = (len(refs) - 1) // 2
    copies = [
        pltpu.make_async_copy(refs[i], refs[count + i], refs[-1].at[i]) for i in range(count)
    ]
    for copy in copies:
        copy.start()
    for copy in copies:
        copy.wait()


def pack_kernel(image_ref, other_ref, taps_ref, offsets_ref, even_ref, odd_ref):
    lines = image_ref.shape[1]
    width = image_ref.shape[2]
    side = lax.axis_index("rg")
    taps = taps_ref[...]
    taps_high = taps.astype(jnp.bfloat16).astype(jnp.float32)
    taps_low = taps - taps_high
    shifts = jnp.broadcast_to(offsets_ref[...].astype(jnp.float32), (TAPS, lines))

    def write(out_ref, line_start, tap_start):
        rows = slice(line_start, line_start + REACH)
        for part in range(2):
            cut = slice(part * REACH, (part + 1) * REACH)
            out_ref[cut, :] = image_ref[part, rows, :].astype(jnp.bfloat16)
        edges = jnp.concatenate([edge_of(other_ref, part, side, rows) for part in range(2)], axis=0)
        cut = slice(tap_start, tap_start + HALF)
        block = jnp.concatenate([taps_high[:, cut], taps_low[:, cut], shifts[:, cut]], axis=1)
        block = jnp.concatenate([block, jnp.zeros((HALF - TAPS, 3 * HALF), jnp.float32)], axis=0)
        cuts = [edges[i * HALF : (i + 1) * HALF] for i in range(3)]
        filler = jnp.zeros((HALF, width - 6 * HALF), jnp.float32)
        block = jnp.concatenate([block, *cuts, filler], axis=1)
        out_ref[2 * REACH :, :] = block.astype(jnp.bfloat16)

    parity = lax.rem(lax.axis_index("az"), 2)

    @pl.when(parity == 0)
    def _():
        write(even_ref, lines - REACH, lines - HALF)
        write(odd_ref, 0, 0)

    @pl.when(parity == 1)
    def _():
        write(even_ref, 0, 0)
        write(odd_ref, lines - REACH, lines - HALF)


def is_above(turn):
    return lax.rem(lax.axis_index("az") + turn, 2) == 1


def band(taps, shift, first_line, source):
    count, lines = source.shape
    tap_ids = source - (lax.broadcasted_iota(jnp.int32, (count, lines), 1) + first_line)
    tap_ids = tap_ids - shift + (TAPS // 2 - 1)
    total = jnp.zeros((count, lines), jnp.float32)
    for tap in range(TAPS):
        total = jnp.where(tap_ids == tap, taps[tap : tap + 1, :], total)
    return total


def high_low(value):
    high = value.astype(jnp.bfloat16)
    low = (value - high.astype(jnp.float32)).astype(jnp.bfloat16)
    return jnp.concatenate([high, low], axis=0)


def apply_band(weights, rows):
    over_rows = (((0,), (0,)), ((), ()))
    rows = jnp.concatenate([rows, rows], axis=0)
    return lax.dot_general(high_low(weights), rows, over_rows, preferred_element_type=jnp.float32)


def write_piece(out_ref, parts, width):
    lines = parts[0].shape[0]
    edges = []
    for part, value in enumerate(parts):
        out_ref[part * lines : (part + 1) * lines, :] = value[:, :width].astype(jnp.bfloat16)
        for at in range(0, lines, EDGE_ROWS):
            edges.append(value[at : at + EDGE_ROWS, width:])
    edges.append(jnp.zeros((EDGE_ROWS, width - len(edges) * HALF), jnp.float32))
    out_ref[2 * lines :, :] = jnp.concatenate(edges, axis=1).astype(jnp.bfloat16)


def read_piece(ref):
    lines = (ref.shape[0] - EDGE_ROWS) // 2
    block = ref[2 * lines :, :].astype(jnp.float32)
    steps = lines // EDGE_ROWS
    parts = []
    for part in range(2):
        tile = ref[part * lines : (part + 1) * lines, :].astype(jnp.float32)
        slots = range(part * steps, (part + 1) * steps)
        edge = jnp.concatenate([block[:, i * HALF : (i + 1) * HALF] for i in slots], axis=0)
        parts.append((tile, edge))
    return parts


def inner_kernel(image_ref, other_ref, taps_ref, offsets_ref, out_ref):
    lines = image_ref.shape[1]
    width = image_ref.shape[2]
    side = lax.axis_index("rg")
    cut = slice(RIM, lines - RIM)
    source = lax.broadcasted_iota(jnp.int32, (lines, lines - 2 * RIM), 0)
    weights = band(taps_ref[:, cut], offsets_ref[:, cut], RIM, source)
    weights = jnp.concatenate([weights, weights], axis=0)
    parts = []
    for part in range(2):
        edge = edge_of(other_ref, part, side, slice(0, lines))
        rows = high_low(jnp.concatenate([image_ref[part], edge], axis=1))
        parts.append(apply_band(weights, rows))
    write_piece(out_ref, parts, width)


def side_kernel(turn, image_ref, other_ref, taps_ref, offsets_ref, message_ref, *refs):
    out_ref = refs[-1]
    lines = image_ref.shape[1]
    width = image_ref.shape[2]
    side = lax.axis_index("rg")
    place = lax.axis_index("az")
    above = is_above(turn)
    alone = jnp.where(above, place == 0, place == lax.axis_size("az") - 1)
    message = message_ref[...]
    message = jnp.where(alone, jnp.zeros_like(message), message)
    block = message[2 * REACH :, :].astype(jnp.float32)
    head = block[:TAPS]
    rim_taps = head[:, :HALF] + head[:, HALF : 2 * HALF]
    rim_shift = head[:1, 2 * HALF : 3 * HALF]
    rim_edges = [block[:, i * HALF : (i + 1) * HALF] for i in range(3, 6)]
    rim_edges = jnp.concatenate(rim_edges, axis=0).astype(jnp.bfloat16)

    def per_line(own, rim):
        upper = jnp.concatenate([rim, own[:, :RIM]], axis=1)
        lower = jnp.concatenate([own[:, lines - RIM :], rim], axis=1)
        return jnp.where(above, upper, lower)

    taps = per_line(taps_ref[...], rim_taps)
    shift = per_line(offsets_ref[...].astype(jnp.float32), rim_shift).astype(jnp.int32)
    first_line = jnp.where(above, -HALF, lines - RIM)
    near = 2 * RIM
    first_own = jnp.where(above, 0, lines - near)
    first_rim = jnp.where(above, -REACH, lines)
    source = lax.broadcasted_iota(jnp.int32, (REACH + near, REACH), 0)
    source = jnp.where(source < REACH, source + first_rim, source - REACH + first_own)
    weights = band(taps, shift, first_line, source)
    weights = jnp.concatenate([weights, weights[REACH:]], axis=0)
    parts = []
    for part in range(2):
        upper, lower = slice(0, near), slice(lines - near, lines)
        edge = jnp.where(
            above, edge_of(other_ref, part, side, upper), edge_of(other_ref, part, side, lower)
        )
        own = jnp.where(above, image_ref[part, upper, :], image_ref[part, lower, :])
        own = high_low(jnp.concatenate([own, edge], axis=1))
        cut = slice(part * REACH, (part + 1) * REACH)
        rim = jnp.concatenate([message[cut, :], rim_edges[cut]], axis=1)
        parts.append(apply_band(weights, jnp.concatenate([rim, own], axis=0)))
    write_piece(out_ref, parts, width)


def cross(own_parts, other_parts):
    own_real, own_imag = own_parts
    other_real, other_imag = other_parts
    real = own_real * other_real + own_imag * other_imag
    imag = own_imag * other_real - own_real * other_imag
    return real, imag


def interferogram(own_pieces, other_pieces, cuts):
    side = lax.axis_index("rg")

    def lines_of(pieces, part, which):
        return jnp.concatenate([cut(piece[part][which]) for piece, cut in zip(pieces, cuts)], axis=0)

    def both(which):
        own = [lines_of(own_pieces, part, which) for part in range(2)]
        other = [lines_of(other_pieces, part, which) for part in range(2)]
        return jnp.concatenate(cross(own, other), axis=0)

    mid, rim = both(0), both(1)
    before = jnp.where(side == 0, 0.0, rim)
    after = jnp.where(side == 0, rim, 0.0)
    filler = jnp.zeros((mid.shape[0], LANES - 2 * HALF), jnp.float32)
    shifted = jnp.concatenate([before, mid, after, filler], axis=1).astype(jnp.bfloat16)
    return jnp.concatenate([mid.astype(jnp.bfloat16), shifted], axis=1)


def side_cuts(above):
    return [
        lambda value: value,
        lambda value: jnp.where(above, value[:RIM], value[value.shape[0] - RIM :]),
    ]


def middle_cuts(above):
    def near(flag):
        return lambda value: jnp.where(flag, value[value.shape[0] - RIM :], value[:RIM])

    return [near(above), lambda value: value, near(jnp.logical_not(above))]


def patch_row(both, line_table_of, tables, spectrum_ref):
    forward, inverse, ring = tables
    chunks = both.shape[1] // LANES
    line_spectra = jnp.dot(line_table_of, both, preferred_element_type=jnp.float32)
    line_spectra = line_spectra.astype(jnp.bfloat16)
    pieces = []
    for chunk in range(chunks):
        cut = slice(chunk * LANES, (chunk + 1) * LANES)
        pieces.append(jnp.concatenate([line_spectra[:PATCH, cut], line_spectra[PATCH:, cut]], axis=1))
    patches = jnp.concatenate(pieces, axis=0)
    spectrum_ref[...] = jnp.dot(patches, forward, preferred_element_type=jnp.float32)
    pieces = []
    for chunk in range(chunks):
        rows = slice(chunk * PATCH, (chunk + 1) * PATCH)
        real = spectrum_ref[rows, :LANES]
        imag = spectrum_ref[rows, LANES:]
        power = real * real + imag * imag
        power = power + pltpu.roll(power, 1, 0) + pltpu.roll(power, PATCH - 1, 0)
        smooth = jnp.dot(power.astype(jnp.bfloat16), ring, preferred_element_type=jnp.float32)
        gain = lax.rsqrt(lax.rsqrt(smooth * (1.0 / (9.0 * PATCH * PATCH)) + 1.0))
        pieces.append(jnp.concatenate([real * gain, imag * gain], axis=1).astype(jnp.bfloat16))
    shaped = jnp.concatenate(pieces, axis=0)
    range_back = jnp.dot(shaped, inverse, preferred_element_type=jnp.float32)
    range_back = range_back.astype(jnp.bfloat16)
    stacked = []
    for chunk in range(chunks):
        block = range_back[chunk * PATCH : (chunk + 1) * PATCH]
        stacked.append(jnp.concatenate([block[:, :LANES], block[:, LANES:]], axis=0))
    return stacked


def lines_back(stacked, back, window, width):
    pieces = [jnp.dot(back, s, preferred_element_type=jnp.float32) * window for s in stacked]
    mids = width // LANES
    mid = jnp.concatenate(pieces[:mids], axis=1)
    moved = jnp.concatenate(pieces[mids:], axis=1)
    return mid + moved[:, HALF : HALF + width]


def all_tables():
    forward = fourier_table(1.0, 1.0)
    inverse = fourier_table(-1.0, 1.0 / PATCH)
    back = inverse.reshape(2, PATCH, 2, PATCH).transpose(2, 3, 0, 1)
    back = back.reshape(2, 2, HALF, 2 * PATCH).transpose(1, 0, 2, 3).reshape(2 * PATCH, 2 * PATCH)
    window = window_table()[:PATCH, :PATCH]
    splits = []
    for _ in range(3):
        splits.append(window.astype(jnp.bfloat16).astype(np.float32))
        window = window - splits[-1]
    natural = np.arange(PATCH)
    rotated = np.concatenate([natural[RIM:], natural[:RIM]])
    swapped = np.concatenate([natural[PATCH - RIM :], natural[RIM : PATCH - RIM], natural[:RIM]])
    side = [line_table(forward, order) for order in (natural, rotated)]
    middle = [line_table(forward, order) for order in (natural, swapped)]
    rows = [
        np.concatenate([np.concatenate(side, axis=0), np.concatenate(middle, axis=0)], axis=1),
        paired(forward),
        paired(inverse),
        np.concatenate([back, ring_table()], axis=1),
        np.concatenate([*splits, np.zeros_like(window)], axis=1),
    ]
    return np.concatenate(rows, axis=0).astype(jnp.bfloat16)


class Tables:
    def __init__(self, ref):
        self.ref = ref
        size = 4 * PATCH
        self.back_at, self.window_at = 3 * size, 3 * size + LANES
        ring = ref[self.back_at : self.back_at + LANES, LANES:]
        self.core = ref[size : 2 * size, :], ref[2 * size : 3 * size, :], ring

    def line(self, above, lanes):
        start = pl.multiple_of(jnp.where(above, 0, 2 * PATCH), 2 * PATCH)
        return self.ref[pl.ds(start, 2 * PATCH), lanes * LANES : (lanes + 1) * LANES]

    def back(self, half):
        start = pl.multiple_of(self.back_at + half * PATCH, PATCH)
        return self.ref[pl.ds(start, PATCH), :LANES]

    def window(self, half):
        start = pl.multiple_of(self.window_at + half * HALF, HALF)
        splits = self.ref[pl.ds(start, HALF), :].astype(jnp.float32)
        window = splits[:, :PATCH] + splits[:, PATCH : 2 * PATCH] + splits[:, 2 * PATCH : 3 * PATCH]
        window = jnp.concatenate([window, window], axis=1)
        return jnp.concatenate([window, window], axis=0)


def half_of(turn):
    return jnp.where(is_above(turn), 0, 1)


def side_row(turn, own, other, tables, spectrum_ref, width):
    above = is_above(turn)
    both = interferogram(own, other, side_cuts(above))
    stacked = patch_row(both, tables.line(above, 0), tables.core, spectrum_ref)
    half = 1 - half_of(turn)
    return lines_back(stacked, tables.back(half), tables.window(half), width)


def middle_row(own, other, tables, spectrum_ref, width):
    above = is_above(0)
    both = interferogram(own, other, middle_cuts(above))
    stacked = patch_row(both, tables.line(above, 1), tables.core, spectrum_ref)
    back = jnp.concatenate([tables.back(half_of(turn)) for turn in range(2)], axis=0)
    window = jnp.concatenate([tables.window(half_of(turn)) for turn in range(2)], axis=0)
    return lines_back(stacked, back, window, width)


def keep(result_ref, result, turn):
    start = pl.multiple_of(half_of(turn) * HALF, HALF)
    for part in range(2):
        result_ref[part, pl.ds(start, HALF), :] = result[part * HALF : (part + 1) * HALF]


def rest_of(own, other, first, tables, spectrum_ref, result_ref, width):
    middle = middle_row(own, other, tables, spectrum_ref, width)
    keep(result_ref, middle[: 2 * HALF] + first, 0)
    second = side_row(1, [own[2], own[1]], [other[2], other[1]], tables, spectrum_ref, width)
    keep(result_ref, middle[2 * HALF :] + second, 1)


def own_kernel(table_ref, first_ref, inner_ref, second_ref, out_ref, spectrum_ref):
    width = first_ref.shape[1]
    own = [read_piece(ref) for ref in (first_ref, inner_ref, second_ref)]
    tables = Tables(table_ref)
    first = side_row(0, own[:2], own[:2], tables, spectrum_ref, width)
    rest_of(own, own, first, tables, spectrum_ref, out_ref, width)


def other_first_kernel(table_ref, first_ref, inner_ref, *refs):
    count = (len(refs) - 1) // 3
    spectrum_ref = refs[-1]
    own = [read_piece(ref) for ref in (first_ref, inner_ref)]
    tables = Tables(table_ref)
    for at in range(count):
        other = [read_piece(ref) for ref in refs[2 * at : 2 * at + 2]]
        result = side_row(0, own, other, tables, spectrum_ref, first_ref.shape[1])
        refs[2 * count + at][...] = result


def other_rest_kernel(
    match_ref, table_ref, filtered_own_ref, first_ref, inner_ref, second_ref, *refs
):
    out_ref, result_ref, spectrum_ref, sems = refs[-4:]
    match_count = out_ref.shape[0]
    date = lax.axis_index("date")
    dates = match_ref.shape[1]
    own = [read_piece(ref) for ref in (first_ref, inner_ref, second_ref)]
    tables = Tables(table_ref)
    result_ref[0] = filtered_own_ref[...]
    for slot in range(1, dates):
        *pieces, done_ref = refs[4 * slot - 4 : 4 * slot]
        other = [read_piece(ref) for ref in pieces]
        rest_of(
            own,
            other,
            done_ref[...],
            tables,
            spectrum_ref,
            result_ref.at[slot],
            first_ref.shape[1],
        )
    copies = []
    for match in range(match_count):
        slot = lax.rem(match_ref[match, date] - date + dates, dates)
        copies.append(
            pltpu.make_async_copy(result_ref.at[slot], out_ref.at[match, :, 0], sems.at[match])
        )
    for copy in copies:
        copy.start()
    for copy in copies:
        copy.wait()


def per_device(image_stack, tap_weights, offsets, matchings):
    _, _, lines, width = image_stack.shape
    match_count = matchings.shape[0]
    other = lax.ppermute(image_stack, "rg", [(0, 1), (1, 0)]).reshape(2, lines, width)
    arguments = (
        image_stack.reshape(2, lines, width),
        tap_weights.reshape(TAPS, lines),
        offsets,
    )
    raw = pl.pallas_call(
        load_kernel,
        out_shape=tuple(pltpu.VMEM(a.shape, a.dtype) for a in arguments),
        in_specs=[HBM] * 3,
        out_specs=(VMEM,) * 3,
        scratch_shapes=[pltpu.SemaphoreType.DMA((3,))],
        compiler_params=PARAMS,
        name="load",
    )(*(pltpu.with_memory_space_constraint(a, pltpu.HBM) for a in arguments))
    raw = (raw[0], other, *raw[1:])
    message = jax.ShapeDtypeStruct((2 * REACH + HALF, width), jnp.bfloat16)
    messages = pl.pallas_call(
        pack_kernel,
        out_shape=(message, message),
        in_specs=[VMEM] * 4,
        out_specs=(VMEM, VMEM),
        compiler_params=PARAMS,
        name="pack",
    )(*raw)
    peers = lax.axis_size("az")

    def swapped(value, start):
        paired_with = {i: i + 1 for i in range(start, peers - 1, 2)}
        paired_with.update({j: i for i, j in paired_with.items()})
        pairs = [
            (2 * i + core, 2 * paired_with[i] + core if i in paired_with else 2 * i + 1 - core)
            for i in range(peers)
            for core in range(2)
        ]
        return lax.ppermute(value, ("az", "rg"), pairs)

    messages = [swapped(messages[turn], turn) for turn in range(2)]
    inner = pl.pallas_call(
        inner_kernel,
        out_shape=jax.ShapeDtypeStruct((2 * (lines - 2 * RIM) + EDGE_ROWS, width), jnp.bfloat16),
        in_specs=[VMEM] * 4,
        out_specs=VMEM,
        compiler_params=PARAMS,
        name="inner",
    )(*raw)
    dates = lax.axis_size("date")

    def from_date(piece, slot):
        return lax.ppermute(piece, "date", [((i + slot) % dates, i) for i in range(dates)])

    slots = range(1, dates)
    inners = [from_date(inner, slot) for slot in slots]
    sides = []
    for turn in range(2):
        made = (*inners, *sides) if turn else (inner,)
        call = pl.pallas_call(
            functools.partial(side_kernel, turn),
            out_shape=jax.ShapeDtypeStruct((2 * REACH + EDGE_ROWS, width), jnp.bfloat16),
            in_specs=[VMEM] * (5 + len(made)),
            out_specs=VMEM,
            compiler_params=PARAMS,
            name="side_" + "ab"[turn],
        )
        sides.append(call(*raw, messages[turn], *made))
    own = (sides[0], inner, sides[1])
    firsts = [from_date(sides[0], slot) for slot in slots]
    seconds = [from_date(sides[1], slot) for slot in slots]
    tables = jnp.asarray(all_tables())
    chunks = (width + width + LANES) // LANES
    spectrum = pltpu.VMEM((chunks * PATCH, 2 * LANES), jnp.float32)
    filtered_own = pl.pallas_call(
        own_kernel,
        out_shape=jax.ShapeDtypeStruct((2, lines, width), jnp.float32),
        in_specs=[VMEM] * 4,
        out_specs=VMEM,
        scratch_shapes=[spectrum],
        compiler_params=PARAMS,
        name="filter_own",
    )(tables, *own)
    pieces = [piece for pair in zip(firsts, inners) for piece in pair]
    done = pl.pallas_call(
        other_first_kernel,
        out_shape=[jax.ShapeDtypeStruct((2 * HALF, width), jnp.float32)] * len(firsts),
        in_specs=[VMEM] * (3 + len(pieces)),
        out_specs=[VMEM] * len(firsts),
        scratch_shapes=[spectrum],
        compiler_params=PARAMS,
        name="filter_first",
    )(tables, *own[:2], *pieces)
    pieces = [piece for group in zip(firsts, inners, seconds, done) for piece in group]
    return pl.pallas_call(
        other_rest_kernel,
        out_shape=jax.ShapeDtypeStruct((match_count, 2, 1, lines, width), jnp.float32),
        in_specs=[SMEM] + [VMEM] * (5 + len(pieces)),
        out_specs=HBM,
        scratch_shapes=[
            pltpu.VMEM((dates, 2, lines, width), jnp.float32),
            spectrum,
            pltpu.SemaphoreType.DMA((match_count,)),
        ],
        compiler_params=PARAMS,
        name="filter_rest",
    )(matchings, tables, filtered_own, *own, *pieces)


def solution(mesh):
    placed = (
        P(None, ("parts", "date"), "az", "rg"),
        P(None, ("parts", "date"), "az"),
        P(("parts", "date"), "az"),
        P(),
    )
    return jax.shard_map(
        per_device,
        mesh=mesh,
        in_specs=placed,
        out_specs=P(None, None, ("parts", "date"), "az", "rg"),
        check_vma=False,
    )
```

```python
import functools
import math

import jax
import jax.numpy as jnp
import numpy as np
from jax import lax
from jax.experimental import pallas as pl
from jax.experimental.pallas import tpu as pltpu
from jax.sharding import PartitionSpec as P

TAPS = 8
SHIFT_MAX = 12
PATCH = 64
HALF = PATCH // 2
RIM = SHIFT_MAX + TAPS // 2
REACH = HALF + RIM
LANES = 128
EDGE_STEP = 16
VMEM_LIMIT = 48 * 1024 * 1024

VMEM = pl.BlockSpec(memory_space=pltpu.VMEM)
SMEM = pl.BlockSpec(memory_space=pltpu.SMEM)
HBM = pl.BlockSpec(memory_space=pltpu.HBM)
PARAMS = pltpu.CompilerParams(vmem_limit_bytes=VMEM_LIMIT)


def fourier_table(sine_sign, table_scale):
    freq_ids = np.arange(PATCH)
    phase_ids = (freq_ids[:, None] * freq_ids[None, :]) % PATCH
    angles = phase_ids * (2.0 * math.pi / PATCH)
    cosine = np.cos(angles) * table_scale
    sine_part = np.sin(angles) * (sine_sign * table_scale)
    top = np.concatenate([cosine, -sine_part], axis=1)
    bottom = np.concatenate([sine_part, cosine], axis=1)
    return np.concatenate([top, bottom], axis=0).astype(np.float32)


def paired(table):
    split = table.reshape(2, PATCH, 2, PATCH)
    wide = np.zeros((2, 2, PATCH, 2, 2, PATCH), np.float32)
    for slot in range(2):
        wide[:, slot, :, :, slot, :] = split
    return wide.reshape(4 * PATCH, 4 * PATCH)


def line_table(forward, row_patches):
    wide_lines = (row_patches + 1) * HALF
    table = np.zeros((row_patches, 2 * PATCH, 2, wide_lines), np.float32)
    transposed = forward.T.reshape(2 * PATCH, 2, PATCH)
    for row in range(row_patches):
        table[row, :, :, row * HALF : row * HALF + PATCH] = transposed
    return table.reshape(row_patches * 2 * PATCH, 2 * wide_lines)


def window_table():
    window = np.sin(math.pi * (np.arange(PATCH) + 0.5) / PATCH) ** 2
    return np.tile(np.outer(window, window), (2, 2)).astype(np.float32)


def ring_table():
    ring = np.zeros((LANES, LANES), np.float32)
    for lane in range(LANES):
        base = lane // PATCH * PATCH
        for step in (-1, 0, 1):
            ring[base + (lane + step) % PATCH, lane] = 1.0
    return ring


def edge_of(other_ref, part, side, lines):
    width = other_ref.shape[2]
    return jnp.where(
        side == 0, other_ref[part, lines, :HALF], other_ref[part, lines, width - HALF :]
    )


def load_kernel(*refs):
    count = (len(refs) - 1) // 2
    copies = [
        pltpu.make_async_copy(refs[i], refs[count + i], refs[-1].at[i]) for i in range(count)
    ]
    for copy in copies:
        copy.start()
    for copy in copies:
        copy.wait()


def pack_kernel(image_ref, other_ref, taps_ref, offsets_ref, even_ref, odd_ref):
    lines = image_ref.shape[1]
    width = image_ref.shape[2]
    side = lax.axis_index("rg")
    taps = taps_ref[...]
    taps_high = taps.astype(jnp.bfloat16).astype(jnp.float32)
    taps_low = taps - taps_high
    shifts = jnp.broadcast_to(offsets_ref[...].astype(jnp.float32), (TAPS, lines))

    def write(out_ref, line_start, tap_start):
        rows = slice(line_start, line_start + REACH)
        for part in range(2):
            cut = slice(part * REACH, (part + 1) * REACH)
            out_ref[cut, :] = image_ref[part, rows, :].astype(jnp.bfloat16)
        edges = jnp.concatenate([edge_of(other_ref, part, side, rows) for part in range(2)], axis=0)
        cut = slice(tap_start, tap_start + HALF)
        block = jnp.concatenate([taps_high[:, cut], taps_low[:, cut], shifts[:, cut]], axis=1)
        block = jnp.concatenate([block, jnp.zeros((HALF - TAPS, 3 * HALF), jnp.float32)], axis=0)
        cuts = [edges[i * HALF : (i + 1) * HALF] for i in range(3)]
        filler = jnp.zeros((HALF, width - 6 * HALF), jnp.float32)
        block = jnp.concatenate([block, *cuts, filler], axis=1)
        out_ref[2 * REACH :, :] = block.astype(jnp.bfloat16)

    parity = lax.rem(lax.axis_index("az"), 2)

    @pl.when(parity == 0)
    def _():
        write(even_ref, lines - REACH, lines - HALF)
        write(odd_ref, 0, 0)

    @pl.when(parity == 1)
    def _():
        write(even_ref, 0, 0)
        write(odd_ref, lines - REACH, lines - HALF)


def is_above(turn):
    return lax.rem(lax.axis_index("az") + turn, 2) == 1


def band(taps, shift, first_line, source):
    count, lines = source.shape
    tap_ids = source - (lax.broadcasted_iota(jnp.int32, (count, lines), 1) + first_line)
    tap_ids = tap_ids - shift + (TAPS // 2 - 1)
    total = jnp.zeros((count, lines), jnp.float32)
    for tap in range(TAPS):
        total = jnp.where(tap_ids == tap, taps[tap : tap + 1, :], total)
    return total


def high_low(value):
    high = value.astype(jnp.bfloat16)
    low = (value - high.astype(jnp.float32)).astype(jnp.bfloat16)
    return jnp.concatenate([high, low], axis=0)


def apply_band(weights, rows):
    over_rows = (((0,), (0,)), ((), ()))
    rows = jnp.concatenate([rows, rows], axis=0)
    return lax.dot_general(high_low(weights), rows, over_rows, preferred_element_type=jnp.float32)


def edge_rows(lines, width):
    rows = EDGE_STEP
    while 2 * lines // rows * HALF > width:
        rows *= 2
    return rows


def piece_shape(lines, width):
    return jax.ShapeDtypeStruct((2 * lines + edge_rows(lines, width), width), jnp.bfloat16)


def write_piece(out_ref, parts, width):
    lines = parts[0].shape[0]
    rows = edge_rows(lines, width)
    for part, value in enumerate(parts):
        out_ref[part * lines : (part + 1) * lines, :] = value[:, :width].astype(jnp.bfloat16)
    edges = jnp.concatenate([value[:, width:] for value in parts], axis=0)
    slots = [edges[at : at + rows] for at in range(0, 2 * lines, rows)]
    slots.append(jnp.zeros((rows, width - len(slots) * HALF), jnp.float32))
    out_ref[2 * lines :, :] = jnp.concatenate(slots, axis=1).astype(jnp.bfloat16)


def read_piece(ref, lines):
    rows = ref.shape[0] - 2 * lines
    block = ref[2 * lines :, :].astype(jnp.float32)
    slots = [block[:, i * HALF : (i + 1) * HALF] for i in range(2 * lines // rows)]
    edges = jnp.concatenate(slots, axis=0)
    tiles = ref[: 2 * lines, :].astype(jnp.float32)
    return [(v[:lines], v[lines:]) for v in (tiles, edges)]


def inner_kernel(image_ref, other_ref, taps_ref, offsets_ref, out_ref):
    lines = image_ref.shape[1]
    width = image_ref.shape[2]
    side = lax.axis_index("rg")
    cut = slice(RIM, lines - RIM)
    source = lax.broadcasted_iota(jnp.int32, (lines, lines - 2 * RIM), 0)
    weights = band(taps_ref[:, cut], offsets_ref[:, cut], RIM, source)
    weights = jnp.concatenate([weights, weights], axis=0)
    for part in range(2):
        edge = edge_of(other_ref, part, side, slice(0, lines))
        rows = high_low(jnp.concatenate([image_ref[part], edge], axis=1))
        out_ref[part] = apply_band(weights, rows)


def side_kernel(turn, image_ref, other_ref, taps_ref, offsets_ref, message_ref, *refs):
    out_ref = refs[-1]
    lines = image_ref.shape[1]
    width = image_ref.shape[2]
    side = lax.axis_index("rg")
    place = lax.axis_index("az")
    above = is_above(turn)
    alone = jnp.where(above, place == 0, place == lax.axis_size("az") - 1)
    message = message_ref[...]
    message = jnp.where(alone, jnp.zeros_like(message), message)
    block = message[2 * REACH :, :].astype(jnp.float32)
    head = block[:TAPS]
    rim_taps = head[:, :HALF] + head[:, HALF : 2 * HALF]
    rim_shift = head[:1, 2 * HALF : 3 * HALF]
    rim_edges = [block[:, i * HALF : (i + 1) * HALF] for i in range(3, 6)]
    rim_edges = jnp.concatenate(rim_edges, axis=0).astype(jnp.bfloat16)

    def per_line(own, rim):
        upper = jnp.concatenate([rim, own[:, :RIM]], axis=1)
        lower = jnp.concatenate([own[:, lines - RIM :], rim], axis=1)
        return jnp.where(above, upper, lower)

    taps = per_line(taps_ref[...], rim_taps)
    shift = per_line(offsets_ref[...].astype(jnp.float32), rim_shift).astype(jnp.int32)
    first_line = jnp.where(above, -HALF, lines - RIM)
    near = 2 * RIM
    first_own = jnp.where(above, 0, lines - near)
    first_rim = jnp.where(above, -REACH, lines)
    source = lax.broadcasted_iota(jnp.int32, (REACH + near, REACH), 0)
    source = jnp.where(source < REACH, source + first_rim, source - REACH + first_own)
    weights = band(taps, shift, first_line, source)
    weights = jnp.concatenate([weights, weights[REACH:]], axis=0)
    parts = []
    for part in range(2):
        upper, lower = slice(0, near), slice(lines - near, lines)
        edge = jnp.where(
            above, edge_of(other_ref, part, side, upper), edge_of(other_ref, part, side, lower)
        )
        own = jnp.where(above, image_ref[part, upper, :], image_ref[part, lower, :])
        own = high_low(jnp.concatenate([own, edge], axis=1))
        cut = slice(part * REACH, (part + 1) * REACH)
        rim = jnp.concatenate([message[cut, :], rim_edges[cut]], axis=1)
        total = apply_band(weights, jnp.concatenate([rim, own], axis=0))
        if turn == 0:
            total = jnp.concatenate([total, refs[0][part]], axis=0)
        parts.append(total)
    write_piece(out_ref, parts, width)


def cross(own_parts, other_parts):
    own_real, own_imag = own_parts
    other_real, other_imag = other_parts
    real = own_real * other_real + own_imag * other_imag
    imag = own_imag * other_real - own_real * other_imag
    return real, imag


def tile_of(first_ref, second_ref, lines):
    first = read_piece(first_ref, REACH + lines - 2 * RIM)
    second = read_piece(second_ref, REACH)
    return [
        tuple(jnp.concatenate([a, b], axis=0) for a, b in zip(*which))
        for which in zip(first, second)
    ]


def filtered_of(own_refs, other_refs, table_ref, spectrum_ref, lines):
    width = own_refs[0].shape[1]
    wide = lines + 2 * HALF
    row_patches = lines // HALF + 1
    side = lax.axis_index("rg")
    line_table_of, forward, inverse, back, ring, window = split_tables(table_ref, row_patches)
    own_tile, own_edge = tile_of(*own_refs, lines)
    other_tile, other_edge = tile_of(*other_refs, lines)
    mid = jnp.concatenate(cross(own_tile, other_tile), axis=0)
    rim = jnp.concatenate(cross(own_edge, other_edge), axis=0)
    before = jnp.where(side == 0, 0.0, rim)
    after = jnp.where(side == 0, rim, 0.0)
    filler = jnp.zeros((2 * wide, LANES - 2 * HALF), jnp.float32)
    shifted = jnp.concatenate([before, mid, after, filler], axis=1).astype(jnp.bfloat16)
    both = jnp.concatenate([mid.astype(jnp.bfloat16), shifted], axis=1)
    chunks = both.shape[1] // LANES
    line_spectra = jnp.dot(line_table_of, both, preferred_element_type=jnp.float32)
    line_spectra = line_spectra.astype(jnp.bfloat16)
    pieces = []
    for row in range(row_patches):
        top = row * 2 * PATCH
        for chunk in range(chunks):
            cut = slice(chunk * LANES, (chunk + 1) * LANES)
            real = line_spectra[top : top + PATCH, cut]
            imag = line_spectra[top + PATCH : top + 2 * PATCH, cut]
            pieces.append(jnp.concatenate([real, imag], axis=1))
    patches = jnp.concatenate(pieces, axis=0)
    spectrum_ref[...] = jnp.dot(patches, forward, preferred_element_type=jnp.float32)
    powers = []
    for block in range(row_patches * chunks):
        rows = slice(block * PATCH, (block + 1) * PATCH)
        real = spectrum_ref[rows, :LANES]
        imag = spectrum_ref[rows, LANES:]
        power = real * real + imag * imag
        power = power + pltpu.roll(power, 1, 0) + pltpu.roll(power, PATCH - 1, 0)
        powers.append(power.astype(jnp.bfloat16))
    smooth = jnp.dot(jnp.concatenate(powers, axis=0), ring, preferred_element_type=jnp.float32)
    gain = lax.rsqrt(lax.rsqrt(smooth * (1.0 / (9.0 * PATCH * PATCH)) + 1.0))
    shaped = jnp.concatenate(
        [spectrum_ref[:, :LANES] * gain, spectrum_ref[:, LANES:] * gain], axis=1
    ).astype(jnp.bfloat16)
    range_back = jnp.dot(shaped, inverse, preferred_element_type=jnp.float32)
    range_back = range_back.astype(jnp.bfloat16)
    window = jnp.concatenate([window] * chunks, axis=1)
    totals = [[None] * (row_patches - 1) for _ in range(2)]
    for row in range(row_patches):
        stacked = []
        for chunk in range(chunks):
            top = (row * chunks + chunk) * PATCH
            block = range_back[top : top + PATCH]
            stacked.append(jnp.concatenate([block[:, :LANES], block[:, LANES:]], axis=0))
        stacked = jnp.concatenate(stacked, axis=1)
        patch_out = jnp.dot(back, stacked, preferred_element_type=jnp.float32) * window
        for part in range(2):
            upper = patch_out[part * PATCH : part * PATCH + HALF]
            lower = patch_out[part * PATCH + HALF : (part + 1) * PATCH]
            if row > 0:
                totals[part][row - 1] = totals[part][row - 1] + upper
            if row < row_patches - 1:
                totals[part][row] = lower
    total = jnp.concatenate([block for part in totals for block in part], axis=0)
    return total[:, :width] + total[:, width + HALF : 2 * width + HALF]


def own_kernel(table_ref, first_ref, second_ref, out_ref, spectrum_ref):
    own = (first_ref, second_ref)
    lines = out_ref.shape[1]
    result = filtered_of(own, own, table_ref, spectrum_ref, lines)
    for part in range(2):
        out_ref[part] = result[part * lines : (part + 1) * lines]


def other_kernel(match_ref, table_ref, filtered_own_ref, first_ref, second_ref, *refs):
    out_ref, result_ref, spectrum_ref, sems = refs[-4:]
    match_count, _, _, lines, _ = out_ref.shape
    date = lax.axis_index("date")
    dates = match_ref.shape[1]

    def slot_of(match):
        return lax.rem(match_ref[match, date] - date + dates, dates)

    def copy_of(match, source):
        return pltpu.make_async_copy(source, out_ref.at[match, :, 0], sems.at[match])

    for match in range(match_count):

        @pl.when(slot_of(match) == 0)
        def _():
            copy_of(match, filtered_own_ref).start()

    for slot in range(1, dates):
        other = refs[2 * slot - 2 : 2 * slot]
        result = filtered_of((first_ref, second_ref), other, table_ref, spectrum_ref, lines)
        for part in range(2):
            result_ref[slot - 1, part] = result[part * lines : (part + 1) * lines]
    for match in range(match_count):
        slot = slot_of(match)

        @pl.when(slot > 0)
        def _():
            copy_of(match, result_ref.at[lax.max(slot - 1, 0)]).start()

    for match in range(match_count):
        copy_of(match, filtered_own_ref).wait()


def all_tables(row_patches):
    forward = fourier_table(1.0, 1.0)
    inverse = fourier_table(-1.0, 1.0 / PATCH)
    back = inverse.reshape(2, PATCH, 2, PATCH).transpose(2, 3, 0, 1).reshape(2 * PATCH, 2 * PATCH)
    window = window_table()[:PATCH, :PATCH]
    splits = []
    for _ in range(3):
        splits.append(window.astype(jnp.bfloat16).astype(np.float32))
        window = window - splits[-1]
    natural = np.arange((row_patches + 1) * HALF)
    wide = len(natural)
    inner = natural[REACH : wide - REACH]
    orders = [
        np.concatenate([natural[:REACH], inner, natural[wide - REACH :]]),
        np.concatenate([natural[wide - REACH :], inner, natural[:REACH]]),
    ]
    lines = line_table(forward, row_patches).reshape(-1, 2, wide)
    rows = [lines[:, :, order].reshape(-1, 2 * wide) for order in orders] + [
        paired(forward),
        paired(inverse),
        np.concatenate([back, ring_table()], axis=1),
        np.concatenate([*splits, np.zeros_like(window)], axis=1),
    ]
    return np.concatenate(rows, axis=0).astype(jnp.bfloat16)


def split_tables(table_ref, row_patches):
    size = row_patches * 2 * PATCH
    start = pl.multiple_of(jnp.where(is_above(0), 0, size), size)
    line_table_of = table_ref[pl.ds(start, size), :]
    at = 2 * size
    forward = table_ref[at : at + 4 * PATCH, :]
    at += 4 * PATCH
    inverse = table_ref[at : at + 4 * PATCH, :]
    at += 4 * PATCH
    back = table_ref[at : at + LANES, :LANES]
    ring = table_ref[at : at + LANES, LANES:]
    at += LANES
    splits = table_ref[at : at + PATCH, :].astype(jnp.float32)
    window = splits[:, :PATCH] + splits[:, PATCH : 2 * PATCH] + splits[:, 2 * PATCH : 3 * PATCH]
    window = jnp.concatenate([window, window], axis=1)
    window = jnp.concatenate([window, window], axis=0)
    return line_table_of, forward, inverse, back, ring, window


def per_device(image_stack, tap_weights, offsets, matchings):
    _, _, lines, width = image_stack.shape
    match_count = matchings.shape[0]
    other = lax.ppermute(image_stack, "rg", [(0, 1), (1, 0)]).reshape(2, lines, width)
    arguments = (
        image_stack.reshape(2, lines, width),
        tap_weights.reshape(TAPS, lines),
        offsets,
    )
    raw = pl.pallas_call(
        load_kernel,
        out_shape=tuple(pltpu.VMEM(a.shape, a.dtype) for a in arguments),
        in_specs=[HBM] * 3,
        out_specs=(VMEM,) * 3,
        scratch_shapes=[pltpu.SemaphoreType.DMA((3,))],
        compiler_params=PARAMS,
        name="load",
    )(*(pltpu.with_memory_space_constraint(a, pltpu.HBM) for a in arguments))
    raw = (raw[0], other, *raw[1:])
    message = jax.ShapeDtypeStruct((2 * REACH + HALF, width), jnp.bfloat16)
    messages = pl.pallas_call(
        pack_kernel,
        out_shape=(message, message),
        in_specs=[VMEM] * 4,
        out_specs=(VMEM, VMEM),
        compiler_params=PARAMS,
        name="pack",
    )(*raw)
    peers = lax.axis_size("az")

    def swapped(value, start):
        paired_with = {i: i + 1 for i in range(start, peers - 1, 2)}
        paired_with.update({j: i for i, j in paired_with.items()})
        pairs = [
            (2 * i + core, 2 * paired_with[i] + core if i in paired_with else 2 * i + 1 - core)
            for i in range(peers)
            for core in range(2)
        ]
        return lax.ppermute(value, ("az", "rg"), pairs)

    messages = [swapped(messages[turn], turn) for turn in range(2)]
    inner = pl.pallas_call(
        inner_kernel,
        out_shape=jax.ShapeDtypeStruct((2, lines - 2 * RIM, width + HALF), jnp.float32),
        in_specs=[VMEM] * 4,
        out_specs=VMEM,
        compiler_params=PARAMS,
        name="inner",
    )(*raw)
    own = []
    for turn in range(2):
        made = (*own, inner)[:1] if turn else (inner,)
        call = pl.pallas_call(
            functools.partial(side_kernel, turn),
            out_shape=piece_shape(REACH + (0 if turn else lines - 2 * RIM), width),
            in_specs=[VMEM] * (5 + len(made)),
            out_specs=VMEM,
            compiler_params=PARAMS,
            name="side_" + "ab"[turn],
        )
        own.append(call(*raw, messages[turn], *made))
    dates = lax.axis_size("date")

    def from_date(piece, slot):
        return lax.ppermute(piece, "date", [((i + slot) % dates, i) for i in range(dates)])

    others = [from_date(piece, slot) for slot in range(1, dates) for piece in own]
    row_patches = lines // HALF + 1
    chunks = (width + width + LANES) // LANES
    tables = jnp.asarray(all_tables(row_patches))
    spectrum = pltpu.VMEM((row_patches * chunks * PATCH, 2 * LANES), jnp.float32)
    filtered_own = pl.pallas_call(
        own_kernel,
        out_shape=jax.ShapeDtypeStruct((2, lines, width), jnp.float32),
        in_specs=[VMEM] * 3,
        out_specs=VMEM,
        scratch_shapes=[spectrum],
        compiler_params=PARAMS,
        name="filter_own",
    )(tables, *own)
    return pl.pallas_call(
        other_kernel,
        out_shape=jax.ShapeDtypeStruct((match_count, 2, 1, lines, width), jnp.float32),
        in_specs=[SMEM] + [VMEM] * (4 + len(others)),
        out_specs=HBM,
        scratch_shapes=[
            pltpu.VMEM((dates - 1, 2, lines, width), jnp.float32),
            spectrum,
            pltpu.SemaphoreType.DMA((match_count,)),
        ],
        compiler_params=PARAMS,
        name="filter_other",
    )(matchings, tables, filtered_own, *own, *others)


def solution(mesh):
    placed = (
        P(None, ("parts", "date"), "az", "rg"),
        P(None, ("parts", "date"), "az"),
        P(("parts", "date"), "az"),
        P(),
    )
    return jax.shard_map(
        per_device,
        mesh=mesh,
        in_specs=placed,
        out_specs=P(None, None, ("parts", "date"), "az", "rg"),
        check_vma=False,
    )
```

```python
import functools
import math

import jax
import jax.numpy as jnp
import numpy as np
from jax import lax
from jax.experimental import pallas as pl
from jax.experimental.pallas import tpu as pltpu
from jax.sharding import PartitionSpec as P

TAPS = 8
SHIFT_MAX = 12
PATCH = 64
HALF = PATCH // 2
RIM = SHIFT_MAX + TAPS // 2
REACH = HALF + RIM
LANES = 128
STEP = 16
VMEM_LIMIT = 48 * 1024 * 1024

VMEM = pl.BlockSpec(memory_space=pltpu.VMEM)
SMEM = pl.BlockSpec(memory_space=pltpu.SMEM)
HBM = pl.BlockSpec(memory_space=pltpu.HBM)
PARAMS = pltpu.CompilerParams(vmem_limit_bytes=VMEM_LIMIT)


def fourier_table(sine_sign, table_scale):
    freq_ids = np.arange(PATCH)
    phase_ids = (freq_ids[:, None] * freq_ids[None, :]) % PATCH
    angles = phase_ids * (2.0 * math.pi / PATCH)
    cosine = np.cos(angles) * table_scale
    sine_part = np.sin(angles) * (sine_sign * table_scale)
    top = np.concatenate([cosine, -sine_part], axis=1)
    bottom = np.concatenate([sine_part, cosine], axis=1)
    return np.concatenate([top, bottom], axis=0).astype(np.float32)


def paired(table):
    split = table.reshape(2, PATCH, 2, PATCH)
    wide = np.zeros((2, 2, PATCH, 2, 2, PATCH), np.float32)
    for slot in range(2):
        wide[:, slot, :, :, slot, :] = split
    return wide.reshape(4 * PATCH, 4 * PATCH)


def line_table(forward, row_patches):
    wide_lines = (row_patches + 1) * HALF
    table = np.zeros((row_patches, 2 * PATCH, 2, wide_lines), np.float32)
    transposed = forward.T.reshape(2 * PATCH, 2, PATCH)
    for row in range(row_patches):
        table[row, :, :, row * HALF : row * HALF + PATCH] = transposed
    return table.reshape(row_patches * 2 * PATCH, 2 * wide_lines)


def window_table():
    window = np.sin(math.pi * (np.arange(PATCH) + 0.5) / PATCH) ** 2
    return np.tile(np.outer(window, window), (2, 2)).astype(np.float32)


def ring_table():
    ring = np.zeros((LANES, LANES), np.float32)
    for lane in range(LANES):
        base = lane // PATCH * PATCH
        for step in (-1, 0, 1):
            ring[base + (lane + step) % PATCH, lane] = 1.0
    return ring


def edge_of(other_ref, part, side, lines):
    width = other_ref.shape[2]
    return jnp.where(
        side == 0, other_ref[part, lines, :HALF], other_ref[part, lines, width - HALF :]
    )


def side_by_side(values):
    values = jnp.concatenate(values, axis=0)
    return jnp.concatenate([values[i : i + STEP] for i in range(0, values.shape[0], STEP)], axis=1)


def one_below(block, first, last):
    return jnp.concatenate([block[:, i * HALF : (i + 1) * HALF] for i in range(first, last)], axis=0)


def load_kernel(*refs):
    count = (len(refs) - 1) // 2
    copies = [
        pltpu.make_async_copy(refs[i], refs[count + i], refs[-1].at[i]) for i in range(count)
    ]
    for copy in copies:
        copy.start()
    for copy in copies:
        copy.wait()


def pack_kernel(image_ref, other_ref, taps_ref, offsets_ref, even_ref, odd_ref):
    lines = image_ref.shape[1]
    side = lax.axis_index("rg")
    taps = taps_ref[...]
    taps_high = taps.astype(jnp.bfloat16).astype(jnp.float32)
    taps = jnp.concatenate([taps_high, taps - taps_high], axis=0)
    shifts = jnp.broadcast_to(offsets_ref[...].astype(jnp.float32), taps.shape)

    def write(out_ref, line_start, tap_start):
        rows = slice(line_start, line_start + REACH)
        for part in range(2):
            cut = slice(part * REACH, (part + 1) * REACH)
            out_ref[cut, :] = image_ref[part, rows, :].astype(jnp.bfloat16)
        edges = [edge_of(other_ref, part, side, rows) for part in range(2)]
        cut = slice(tap_start, tap_start + HALF)
        block = side_by_side([*edges, taps[:, cut], shifts[:, cut]])
        out_ref[2 * REACH :, :] = block.astype(jnp.bfloat16)

    parity = lax.rem(lax.axis_index("az"), 2)

    @pl.when(parity == 0)
    def _():
        write(even_ref, lines - REACH, lines - HALF)
        write(odd_ref, 0, 0)

    @pl.when(parity == 1)
    def _():
        write(even_ref, 0, 0)
        write(odd_ref, lines - REACH, lines - HALF)


def is_above(turn):
    return lax.rem(lax.axis_index("az") + turn, 2) == 1


def band(taps, shift, first_line, source):
    count, lines = source.shape
    tap_ids = source - (lax.broadcasted_iota(jnp.int32, (count, lines), 1) + first_line)
    tap_ids = tap_ids - shift + (TAPS // 2 - 1)
    total = jnp.zeros((count, lines), jnp.float32)
    for tap in range(TAPS):
        total = jnp.where(tap_ids == tap, taps[tap : tap + 1, :], total)
    return total


def high_low(value):
    high = value.astype(jnp.bfloat16)
    low = (value - high.astype(jnp.float32)).astype(jnp.bfloat16)
    return jnp.concatenate([high, low], axis=0)


def apply_band(weights, rows):
    over_rows = (((0,), (0,)), ((), ()))
    rows = jnp.concatenate([rows, rows], axis=0)
    return lax.dot_general(high_low(weights), rows, over_rows, preferred_element_type=jnp.float32)


def write_piece(out_ref, parts, more_edge, width):
    lines = parts[0].shape[0]
    for part, value in enumerate(parts):
        out_ref[part * lines : (part + 1) * lines, :] = value[:, :width].astype(jnp.bfloat16)
    edges = side_by_side([value[:REACH, width:] for value in parts] + [more_edge])
    out_ref[2 * lines :, :] = edges.astype(jnp.bfloat16)


def inner_kernel(image_ref, other_ref, taps_ref, offsets_ref, out_ref):
    lines = image_ref.shape[1]
    width = image_ref.shape[2]
    side = lax.axis_index("rg")
    cut = slice(RIM, lines - RIM)
    source = lax.broadcasted_iota(jnp.int32, (lines, lines - 2 * RIM), 0)
    weights = band(taps_ref[:, cut], offsets_ref[:, cut], RIM, source)
    weights = jnp.concatenate([weights, weights], axis=0)
    for part in range(2):
        edge = edge_of(other_ref, part, side, slice(0, lines))
        rows = high_low(jnp.concatenate([image_ref[part], edge], axis=1))
        out_ref[part] = apply_band(weights, rows)


def side_kernel(
    turn, image_ref, other_ref, taps_ref, offsets_ref, message_ref, inner_ref, *refs
):
    out_ref = refs[-1]
    lines = image_ref.shape[1]
    width = image_ref.shape[2]
    side = lax.axis_index("rg")
    place = lax.axis_index("az")
    above = is_above(turn)
    alone = jnp.where(above, place == 0, place == lax.axis_size("az") - 1)
    message = message_ref[...]
    message = jnp.where(alone, jnp.zeros_like(message), message)
    block = message[2 * REACH :, :].astype(jnp.float32)
    steps = 2 * REACH // STEP
    rim_edges = one_below(block, 0, steps).astype(jnp.bfloat16)
    rim_taps = one_below(block, steps, steps + 1)
    rim_taps = rim_taps[:TAPS] + rim_taps[TAPS:]
    rim_shift = one_below(block, steps + 1, steps + 2)[:1]

    def per_line(own, rim):
        upper = jnp.concatenate([rim, own[:, :RIM]], axis=1)
        lower = jnp.concatenate([own[:, lines - RIM :], rim], axis=1)
        return jnp.where(above, upper, lower)

    taps = per_line(taps_ref[...], rim_taps)
    shift = per_line(offsets_ref[...].astype(jnp.float32), rim_shift).astype(jnp.int32)
    first_line = jnp.where(above, -HALF, lines - RIM)
    near = 2 * RIM
    first_own = jnp.where(above, 0, lines - near)
    first_rim = jnp.where(above, -REACH, lines)
    source = lax.broadcasted_iota(jnp.int32, (REACH + near, REACH), 0)
    source = jnp.where(source < REACH, source + first_rim, source - REACH + first_own)
    weights = band(taps, shift, first_line, source)
    weights = jnp.concatenate([weights, weights[REACH:]], axis=0)
    parts = []
    for part in range(2):
        upper, lower = slice(0, near), slice(lines - near, lines)
        edge = jnp.where(
            above, edge_of(other_ref, part, side, upper), edge_of(other_ref, part, side, lower)
        )
        own = jnp.where(above, image_ref[part, upper, :], image_ref[part, lower, :])
        own = high_low(jnp.concatenate([own, edge], axis=1))
        cut = slice(part * REACH, (part + 1) * REACH)
        rim = jnp.concatenate([message[cut, :], rim_edges[cut]], axis=1)
        total = apply_band(weights, jnp.concatenate([rim, own], axis=0))
        if turn == 0:
            total = jnp.concatenate([total, inner_ref[part]], axis=0)
        parts.append(total)
    write_piece(out_ref, parts, inner_ref[turn, :, width:], width)


def cross(own_parts, other_parts):
    own_real, own_imag = own_parts
    other_real, other_imag = other_parts
    real = own_real * other_real + own_imag * other_imag
    imag = own_imag * other_real - own_real * other_imag
    return real, imag


def tile_of(first_ref, second_ref, lines):
    inner = lines - 2 * RIM
    step, more = REACH // STEP, inner // STEP

    def split(ref, count):
        tiles = ref[: 2 * count, :].astype(jnp.float32)
        block = ref[2 * count :, :].astype(jnp.float32)
        edges = [one_below(block, part * step, (part + 1) * step) for part in range(2)]
        return (tiles[:count], tiles[count:]), edges, one_below(block, 2 * step, 2 * step + more)

    first = split(first_ref, REACH + inner)
    second = split(second_ref, REACH)
    tiles, edges = [], []
    for part, middle in enumerate((first[2], second[2])):
        tiles.append(jnp.concatenate([first[0][part], second[0][part]], axis=0))
        edges.append(jnp.concatenate([first[1][part], middle, second[1][part]], axis=0))
    return tiles, edges


def filtered_of(own_refs, other_refs, table_ref, spectrum_ref, lines, emit):
    width = own_refs[0].shape[1]
    wide = lines + 2 * HALF
    row_patches = lines // HALF + 1
    side = lax.axis_index("rg")
    line_table_of, forward, inverse, back, ring, window = split_tables(table_ref, row_patches)
    own_tile, own_edge = tile_of(*own_refs, lines)
    other_tile, other_edge = tile_of(*other_refs, lines)
    mid = jnp.concatenate(cross(own_tile, other_tile), axis=0)
    rim = jnp.concatenate(cross(own_edge, other_edge), axis=0)
    before = jnp.where(side == 0, 0.0, rim)
    after = jnp.where(side == 0, rim, 0.0)
    filler = jnp.zeros((2 * wide, LANES - 2 * HALF), jnp.float32)
    shifted = jnp.concatenate([before, mid, after, filler], axis=1).astype(jnp.bfloat16)
    both = jnp.concatenate([mid.astype(jnp.bfloat16), shifted], axis=1)
    chunks = both.shape[1] // LANES
    line_spectra = jnp.dot(line_table_of, both, preferred_element_type=jnp.float32)
    line_spectra = line_spectra.astype(jnp.bfloat16)
    pieces = []
    for row in range(row_patches):
        top = row * 2 * PATCH
        for chunk in range(chunks):
            cut = slice(chunk * LANES, (chunk + 1) * LANES)
            real = line_spectra[top : top + PATCH, cut]
            imag = line_spectra[top + PATCH : top + 2 * PATCH, cut]
            pieces.append(jnp.concatenate([real, imag], axis=1))
    patches = jnp.concatenate(pieces, axis=0)
    spectrum_ref[...] = jnp.dot(patches, forward, preferred_element_type=jnp.float32)
    powers = []
    for block in range(row_patches * chunks):
        rows = slice(block * PATCH, (block + 1) * PATCH)
        real = spectrum_ref[rows, :LANES]
        imag = spectrum_ref[rows, LANES:]
        power = real * real + imag * imag
        power = power + pltpu.roll(power, 1, 0) + pltpu.roll(power, PATCH - 1, 0)
        powers.append(power.astype(jnp.bfloat16))
    smooth = jnp.dot(jnp.concatenate(powers, axis=0), ring, preferred_element_type=jnp.float32)
    gain = lax.rsqrt(lax.rsqrt(smooth * (1.0 / (9.0 * PATCH * PATCH)) + 1.0))
    shaped = jnp.concatenate(
        [spectrum_ref[:, :LANES] * gain, spectrum_ref[:, LANES:] * gain], axis=1
    ).astype(jnp.bfloat16)
    range_back = jnp.dot(shaped, inverse, preferred_element_type=jnp.float32)
    range_back = range_back.astype(jnp.bfloat16)
    window = jnp.concatenate([window] * chunks, axis=1)
    earlier = None
    for row in range(row_patches):
        stacked = []
        for chunk in range(chunks):
            top = (row * chunks + chunk) * PATCH
            block = range_back[top : top + PATCH]
            stacked.append(jnp.concatenate([block[:, :LANES], block[:, LANES:]], axis=0))
        stacked = jnp.concatenate(stacked, axis=1)
        patch_out = jnp.dot(back, stacked, preferred_element_type=jnp.float32) * window
        uppers = [patch_out[part * PATCH : part * PATCH + HALF] for part in range(2)]
        if row > 0:
            total = jnp.concatenate(uppers, axis=0) + earlier
            total = total[:, :width] + total[:, width + HALF : 2 * width + HALF]
            emit(row - 1, total)
        lowers = [patch_out[part * PATCH + HALF : (part + 1) * PATCH] for part in range(2)]
        earlier = jnp.concatenate(lowers, axis=0)


def keep(ref, row, total):
    for part in range(2):
        ref[part, row * HALF : (row + 1) * HALF] = total[part * HALF : (part + 1) * HALF]


def own_kernel(table_ref, first_ref, second_ref, out_ref, spectrum_ref):
    own = (first_ref, second_ref)
    lines = out_ref.shape[1]
    filtered_of(own, own, table_ref, spectrum_ref, lines, functools.partial(keep, out_ref))


def other_kernel(match_ref, table_ref, filtered_own_ref, first_ref, second_ref, *refs):
    out_ref, result_ref, spectrum_ref, sems = refs[-4:]
    match_count, _, _, lines, _ = out_ref.shape
    date = lax.axis_index("date")
    dates = match_ref.shape[1]
    rows = lines // HALF

    def copy_of(match, row, source_ref):
        cut = slice(row * HALF, (row + 1) * HALF)
        target = out_ref.at[match, :, 0, cut]
        return pltpu.make_async_copy(source_ref.at[:, cut], target, sems.at[match, row])

    def send(slot, row, source_ref):
        for match in range(match_count):
            wanted = lax.rem(match_ref[match, date] - date + dates, dates)

            @pl.when(wanted == slot)
            def _():
                copy_of(match, row, source_ref).start()

    for row in range(rows):
        send(0, row, filtered_own_ref)
    for slot in range(1, dates):
        other = refs[2 * slot - 2 : 2 * slot]
        target_ref = result_ref.at[slot - 1]

        def emit(row, total):
            keep(target_ref, row, total)
            send(slot, row, target_ref)

        filtered_of((first_ref, second_ref), other, table_ref, spectrum_ref, lines, emit)
    for match in range(match_count):
        for row in range(rows):
            copy_of(match, row, filtered_own_ref).wait()


def all_tables(row_patches):
    forward = fourier_table(1.0, 1.0)
    inverse = fourier_table(-1.0, 1.0 / PATCH)
    back = inverse.reshape(2, PATCH, 2, PATCH).transpose(2, 3, 0, 1).reshape(2 * PATCH, 2 * PATCH)
    window = window_table()[:PATCH, :PATCH]
    splits = []
    for _ in range(3):
        splits.append(window.astype(jnp.bfloat16).astype(np.float32))
        window = window - splits[-1]
    natural = np.arange((row_patches + 1) * HALF)
    wide = len(natural)
    inner = natural[REACH : wide - REACH]
    orders = [
        np.concatenate([natural[:REACH], inner, natural[wide - REACH :]]),
        np.concatenate([natural[wide - REACH :], inner, natural[:REACH]]),
    ]
    lines = line_table(forward, row_patches).reshape(-1, 2, wide)
    rows = [lines[:, :, order].reshape(-1, 2 * wide) for order in orders] + [
        paired(forward),
        paired(inverse),
        np.concatenate([back, ring_table()], axis=1),
        np.concatenate([*splits, np.zeros_like(window)], axis=1),
    ]
    return np.concatenate(rows, axis=0).astype(jnp.bfloat16)


def split_tables(table_ref, row_patches):
    size = row_patches * 2 * PATCH
    start = pl.multiple_of(jnp.where(is_above(0), 0, size), size)
    line_table_of = table_ref[pl.ds(start, size), :]
    at = 2 * size
    forward = table_ref[at : at + 4 * PATCH, :]
    at += 4 * PATCH
    inverse = table_ref[at : at + 4 * PATCH, :]
    at += 4 * PATCH
    back = table_ref[at : at + LANES, :LANES]
    ring = table_ref[at : at + LANES, LANES:]
    at += LANES
    splits = table_ref[at : at + PATCH, :].astype(jnp.float32)
    window = splits[:, :PATCH] + splits[:, PATCH : 2 * PATCH] + splits[:, 2 * PATCH : 3 * PATCH]
    window = jnp.concatenate([window, window], axis=1)
    window = jnp.concatenate([window, window], axis=0)
    return line_table_of, forward, inverse, back, ring, window


def per_device(image_stack, tap_weights, offsets, matchings):
    _, _, lines, width = image_stack.shape
    match_count = matchings.shape[0]
    other = lax.ppermute(image_stack, "rg", [(0, 1), (1, 0)]).reshape(2, lines, width)
    arguments = (
        image_stack.reshape(2, lines, width),
        tap_weights.reshape(TAPS, lines),
        offsets,
    )
    raw = pl.pallas_call(
        load_kernel,
        out_shape=tuple(pltpu.VMEM(a.shape, a.dtype) for a in arguments),
        in_specs=[HBM] * 3,
        out_specs=(VMEM,) * 3,
        scratch_shapes=[pltpu.SemaphoreType.DMA((3,))],
        compiler_params=PARAMS,
        name="load",
    )(*(pltpu.with_memory_space_constraint(a, pltpu.HBM) for a in arguments))
    raw = (raw[0], other, *raw[1:])
    message = jax.ShapeDtypeStruct((2 * REACH + STEP, width), jnp.bfloat16)
    messages = pl.pallas_call(
        pack_kernel,
        out_shape=(message, message),
        in_specs=[VMEM] * 4,
        out_specs=(VMEM, VMEM),
        compiler_params=PARAMS,
        name="pack",
    )(*raw)
    peers = lax.axis_size("az")

    def swapped(value, start):
        paired_with = {i: i + 1 for i in range(start, peers - 1, 2)}
        paired_with.update({j: i for i, j in paired_with.items()})
        pairs = [
            (2 * i + core, 2 * paired_with[i] + core if i in paired_with else 2 * i + 1 - core)
            for i in range(peers)
            for core in range(2)
        ]
        return lax.ppermute(value, ("az", "rg"), pairs)

    messages = [swapped(messages[turn], turn) for turn in range(2)]
    inner = pl.pallas_call(
        inner_kernel,
        out_shape=jax.ShapeDtypeStruct((2, lines - 2 * RIM, width + HALF), jnp.float32),
        in_specs=[VMEM] * 4,
        out_specs=VMEM,
        compiler_params=PARAMS,
        name="inner",
    )(*raw)
    own = []
    for turn in range(2):
        count = REACH + (0 if turn else lines - 2 * RIM)
        call = pl.pallas_call(
            functools.partial(side_kernel, turn),
            out_shape=jax.ShapeDtypeStruct((2 * count + STEP, width), jnp.bfloat16),
            in_specs=[VMEM] * (6 + len(own)),
            out_specs=VMEM,
            compiler_params=PARAMS,
            name="side_" + "ab"[turn],
        )
        own.append(call(*raw, messages[turn], inner, *own))
    dates = lax.axis_size("date")

    def from_date(piece, slot):
        return lax.ppermute(piece, "date", [((i + slot) % dates, i) for i in range(dates)])

    others = [from_date(piece, slot) for slot in range(1, dates) for piece in own]
    row_patches = lines // HALF + 1
    chunks = (width + width + LANES) // LANES
    tables = jnp.asarray(all_tables(row_patches))
    spectrum = pltpu.VMEM((row_patches * chunks * PATCH, 2 * LANES), jnp.float32)
    filtered_own = pl.pallas_call(
        own_kernel,
        out_shape=jax.ShapeDtypeStruct((2, lines, width), jnp.float32),
        in_specs=[VMEM] * 3,
        out_specs=VMEM,
        scratch_shapes=[spectrum],
        compiler_params=PARAMS,
        name="filter_own",
    )(tables, *own)
    return pl.pallas_call(
        other_kernel,
        out_shape=jax.ShapeDtypeStruct((match_count, 2, 1, lines, width), jnp.float32),
        in_specs=[SMEM] + [VMEM] * (4 + len(others)),
        out_specs=HBM,
        scratch_shapes=[
            pltpu.VMEM((dates - 1, 2, lines, width), jnp.float32),
            spectrum,
            pltpu.SemaphoreType.DMA((match_count, lines // HALF)),
        ],
        compiler_params=PARAMS,
        name="filter_other",
    )(matchings, tables, filtered_own, *own, *others)


def solution(mesh):
    placed = (
        P(None, ("parts", "date"), "az", "rg"),
        P(None, ("parts", "date"), "az"),
        P(("parts", "date"), "az"),
        P(),
    )
    return jax.shard_map(
        per_device,
        mesh=mesh,
        in_specs=placed,
        out_specs=P(None, None, ("parts", "date"), "az", "rg"),
        check_vma=False,
    )
```

```python
import functools
import math

import jax
import jax.numpy as jnp
import numpy as np
from jax import lax
from jax.experimental import pallas as pl
from jax.experimental.pallas import tpu as pltpu
from jax.sharding import PartitionSpec as P

TAPS = 8
SHIFT_MAX = 12
PATCH = 64
HALF = PATCH // 2
RIM = SHIFT_MAX + TAPS // 2
REACH = HALF + RIM
LANES = 128
STEP = 16
VMEM_LIMIT = 48 * 1024 * 1024

VMEM = pl.BlockSpec(memory_space=pltpu.VMEM)
SMEM = pl.BlockSpec(memory_space=pltpu.SMEM)
HBM = pl.BlockSpec(memory_space=pltpu.HBM)
PARAMS = pltpu.CompilerParams(vmem_limit_bytes=VMEM_LIMIT)


def fourier_table(sine_sign, table_scale):
    freq_ids = np.arange(PATCH)
    phase_ids = (freq_ids[:, None] * freq_ids[None, :]) % PATCH
    angles = phase_ids * (2.0 * math.pi / PATCH)
    cosine = np.cos(angles) * table_scale
    sine_part = np.sin(angles) * (sine_sign * table_scale)
    top = np.concatenate([cosine, -sine_part], axis=1)
    bottom = np.concatenate([sine_part, cosine], axis=1)
    return np.concatenate([top, bottom], axis=0).astype(np.float32)


def paired(table):
    split = table.reshape(2, PATCH, 2, PATCH)
    wide = np.zeros((2, 2, PATCH, 2, 2, PATCH), np.float32)
    for slot in range(2):
        wide[:, slot, :, :, slot, :] = split
    return wide.reshape(4 * PATCH, 4 * PATCH)


def line_table(forward, row_patches):
    wide_lines = (row_patches + 1) * HALF
    table = np.zeros((row_patches, 2 * PATCH, 2, wide_lines), np.float32)
    transposed = forward.T.reshape(2 * PATCH, 2, PATCH)
    for row in range(row_patches):
        table[row, :, :, row * HALF : row * HALF + PATCH] = transposed
    return table.reshape(row_patches * 2 * PATCH, 2 * wide_lines)


def window_table():
    window = np.sin(math.pi * (np.arange(PATCH) + 0.5) / PATCH) ** 2
    return np.tile(np.outer(window, window), (2, 2)).astype(np.float32)


def ring_table():
    ring = np.zeros((LANES, LANES), np.float32)
    for lane in range(LANES):
        base = lane // PATCH * PATCH
        for step in (-1, 0, 1):
            ring[base + (lane + step) % PATCH, lane] = 1.0
    return ring


def edge_of(other_ref, part, side, lines):
    width = other_ref.shape[2]
    return jnp.where(
        side == 0, other_ref[part, lines, :HALF], other_ref[part, lines, width - HALF :]
    )


def side_by_side(values):
    values = jnp.concatenate(values, axis=0)
    return jnp.concatenate([values[i : i + STEP] for i in range(0, values.shape[0], STEP)], axis=1)


def one_below(block, first, last):
    return jnp.concatenate([block[:, i * HALF : (i + 1) * HALF] for i in range(first, last)], axis=0)


def load_kernel(*refs):
    count = (len(refs) - 1) // 2
    copies = [
        pltpu.make_async_copy(refs[i], refs[count + i], refs[-1].at[i]) for i in range(count)
    ]
    for copy in copies:
        copy.start()
    for copy in copies:
        copy.wait()


def pack_kernel(image_ref, other_ref, taps_ref, offsets_ref, even_ref, odd_ref, own_ref):
    lines = image_ref.shape[1]
    width = image_ref.shape[2]
    side = lax.axis_index("rg")
    taps = taps_ref[...]
    taps_high = taps.astype(jnp.bfloat16).astype(jnp.float32)
    taps = jnp.concatenate([taps_high, taps - taps_high], axis=0)
    shifts = jnp.broadcast_to(offsets_ref[...].astype(jnp.float32), taps.shape)

    def write(out_ref, line_start, count, weights):
        rows = slice(line_start, line_start + count)
        for part in range(2):
            cut = slice(part * count, (part + 1) * count)
            out_ref[cut, :] = image_ref[part, rows, :].astype(jnp.bfloat16)
        edges = side_by_side([edge_of(other_ref, part, side, rows) for part in range(2)])
        block = jnp.concatenate([edges, *weights], axis=1)
        for at in range(0, block.shape[1], width):
            top = 2 * count + at // width * STEP
            out_ref[top : top + STEP, :] = block[:, at : at + width].astype(jnp.bfloat16)

    def write_side(out_ref, first):
        cut = slice(0, HALF) if first else slice(lines - HALF, lines)
        start = 0 if first else lines - REACH
        write(out_ref, start, REACH, [taps[:, cut], shifts[:, cut]])

    parity = lax.rem(lax.axis_index("az"), 2)

    @pl.when(parity == 0)
    def _():
        write_side(even_ref, False)
        write_side(odd_ref, True)

    @pl.when(parity == 1)
    def _():
        write_side(even_ref, True)
        write_side(odd_ref, False)

    filler = jnp.zeros((STEP, width - 2 * lines), jnp.float32)
    write(own_ref, 0, lines, [taps, shifts, filler])


def is_above(turn):
    return lax.rem(lax.axis_index("az") + turn, 2) == 1


def band(taps, shift, first_line, source):
    count, lines = source.shape
    tap_ids = source - (lax.broadcasted_iota(jnp.int32, (count, lines), 1) + first_line)
    tap_ids = tap_ids - shift + (TAPS // 2 - 1)
    total = jnp.zeros((count, lines), jnp.float32)
    for tap in range(TAPS):
        total = jnp.where(tap_ids == tap, taps[tap : tap + 1, :], total)
    return total


def high_low(value):
    high = value.astype(jnp.bfloat16)
    low = (value - high.astype(jnp.float32)).astype(jnp.bfloat16)
    return jnp.concatenate([high, low], axis=0)


def apply_band(weights, rows):
    over_rows = (((0,), (0,)), ((), ()))
    rows = jnp.concatenate([rows, rows], axis=0)
    return lax.dot_general(high_low(weights), rows, over_rows, preferred_element_type=jnp.float32)


class Own:
    def __init__(self, image_ref, other_ref, taps_ref, offsets_ref):
        self.image_ref, self.other_ref = image_ref, other_ref
        self.lines, self.width = image_ref.shape[1:]
        self.taps = taps_ref[...]
        self.shift = offsets_ref[...].astype(jnp.float32)

    def rows(self, part, cut):
        edge = edge_of(self.other_ref, part, lax.axis_index("rg"), cut)
        return high_low(jnp.concatenate([self.image_ref[part, cut, :], edge], axis=1))


class Partner:
    def __init__(self, ref):
        self.ref = ref
        self.width = ref.shape[1]
        self.lines = lines = (ref.shape[0] - 2 * STEP) // 2
        steps = 2 * lines // STEP
        self.edges = one_below(ref[2 * lines : 2 * lines + STEP, :].astype(jnp.float32), 0, steps)
        block = ref[2 * lines + STEP :, :].astype(jnp.float32)
        self.taps = block[:TAPS, :lines] + block[TAPS : 2 * TAPS, :lines]
        self.shift = block[:1, lines : 2 * lines]

    def rows(self, part, cut):
        rows = slice(part * self.lines + cut.start, part * self.lines + cut.stop)
        edge = self.edges[rows].astype(jnp.bfloat16)
        return jnp.concatenate([self.ref[rows, :], edge], axis=1)


def inner_lines(source):
    lines = source.lines
    cut = slice(RIM, lines - RIM)
    ids = lax.broadcasted_iota(jnp.int32, (lines, lines - 2 * RIM), 0)
    weights = band(source.taps[:, cut], source.shift[:, cut].astype(jnp.int32), RIM, ids)
    parts = []
    for part in range(2):
        rows = source.rows(part, slice(0, lines))
        repeats = rows.shape[0] // lines
        parts.append(apply_band(jnp.concatenate([weights] * repeats, axis=0), rows))
    return parts


def side_lines(turn, source, message_ref):
    lines = source.lines
    place = lax.axis_index("az")
    above = is_above(turn)
    alone = jnp.where(above, place == 0, place == lax.axis_size("az") - 1)
    message = message_ref[...]
    message = jnp.where(alone, jnp.zeros_like(message), message)
    block = message[2 * REACH :, :].astype(jnp.float32)
    steps = 2 * REACH // STEP
    rim_edges = one_below(block, 0, steps).astype(jnp.bfloat16)
    rim_taps = one_below(block, steps, steps + 1)
    rim_taps = rim_taps[:TAPS] + rim_taps[TAPS:]
    rim_shift = one_below(block, steps + 1, steps + 2)[:1]

    def per_line(own, rim):
        upper = jnp.concatenate([rim, own[:, :RIM]], axis=1)
        lower = jnp.concatenate([own[:, lines - RIM :], rim], axis=1)
        return jnp.where(above, upper, lower)

    taps = per_line(source.taps, rim_taps)
    shift = per_line(source.shift, rim_shift).astype(jnp.int32)
    first_line = jnp.where(above, -HALF, lines - RIM)
    near = 2 * RIM
    first_own = jnp.where(above, 0, lines - near)
    first_rim = jnp.where(above, -REACH, lines)
    ids = lax.broadcasted_iota(jnp.int32, (REACH + near, REACH), 0)
    ids = jnp.where(ids < REACH, ids + first_rim, ids - REACH + first_own)
    weights = band(taps, shift, first_line, ids)
    parts = []
    for part in range(2):
        upper = source.rows(part, slice(0, near))
        own = jnp.where(above, upper, source.rows(part, slice(lines - near, lines)))
        repeats = own.shape[0] // near
        both = jnp.concatenate([weights] + [weights[REACH:]] * (repeats - 1), axis=0)
        cut = slice(part * REACH, (part + 1) * REACH)
        rim = jnp.concatenate([message[cut, :], rim_edges[cut]], axis=1)
        parts.append(apply_band(both, jnp.concatenate([rim, own], axis=0)))
    return parts


def inner_kernel(make, *refs):
    for part, value in enumerate(inner_lines(make(*refs[:-1]))):
        refs[-1][part] = value.astype(jnp.bfloat16)


def side_kernel(turn, make, *refs):
    for part, value in enumerate(side_lines(turn, make(*refs[:-2]), refs[-2])):
        refs[-1][part] = value.astype(jnp.bfloat16)


def pass_kernel(message_ref, *refs):
    refs[-1][...] = message_ref[...]


def cross(own_parts, other_parts):
    own_real, own_imag = own_parts
    other_real, other_imag = other_parts
    real = own_real * other_real + own_imag * other_imag
    imag = own_imag * other_real - own_real * other_imag
    return real, imag


def tile_of(pieces, width):
    parts = [
        jnp.concatenate([piece[part].astype(jnp.float32) for piece in pieces], axis=0)
        for part in range(2)
    ]
    return [part[:, :width] for part in parts], [part[:, width:] for part in parts]


def filtered_of(own_pieces, other_pieces, table_ref, spectrum_ref, lines, width):
    wide = lines + 2 * HALF
    row_patches = lines // HALF + 1
    side = lax.axis_index("rg")
    line_table_of, forward, inverse, back, ring, window = split_tables(table_ref, row_patches)
    own_tile, own_edge = tile_of(own_pieces, width)
    other_tile, other_edge = tile_of(other_pieces, width)
    mid = jnp.concatenate(cross(own_tile, other_tile), axis=0)
    rim = jnp.concatenate(cross(own_edge, other_edge), axis=0)
    before = jnp.where(side == 0, 0.0, rim)
    after = jnp.where(side == 0, rim, 0.0)
    filler = jnp.zeros((2 * wide, LANES - 2 * HALF), jnp.float32)
    shifted = jnp.concatenate([before, mid, after, filler], axis=1).astype(jnp.bfloat16)
    both = jnp.concatenate([mid.astype(jnp.bfloat16), shifted], axis=1)
    chunks = both.shape[1] // LANES
    line_spectra = jnp.dot(line_table_of, both, preferred_element_type=jnp.float32)
    line_spectra = line_spectra.astype(jnp.bfloat16)
    pieces = []
    for row in range(row_patches):
        top = row * 2 * PATCH
        for chunk in range(chunks):
            cut = slice(chunk * LANES, (chunk + 1) * LANES)
            real = line_spectra[top : top + PATCH, cut]
            imag = line_spectra[top + PATCH : top + 2 * PATCH, cut]
            pieces.append(jnp.concatenate([real, imag], axis=1))
    patches = jnp.concatenate(pieces, axis=0)
    spectrum_ref[...] = jnp.dot(patches, forward, preferred_element_type=jnp.float32)
    powers = []
    for block in range(row_patches * chunks):
        rows = slice(block * PATCH, (block + 1) * PATCH)
        real = spectrum_ref[rows, :LANES]
        imag = spectrum_ref[rows, LANES:]
        power = real * real + imag * imag
        power = power + pltpu.roll(power, 1, 0) + pltpu.roll(power, PATCH - 1, 0)
        powers.append(power.astype(jnp.bfloat16))
    smooth = jnp.dot(jnp.concatenate(powers, axis=0), ring, preferred_element_type=jnp.float32)
    gain = lax.rsqrt(lax.rsqrt(smooth * (1.0 / (9.0 * PATCH * PATCH)) + 1.0))
    shaped = jnp.concatenate(
        [spectrum_ref[:, :LANES] * gain, spectrum_ref[:, LANES:] * gain], axis=1
    ).astype(jnp.bfloat16)
    range_back = jnp.dot(shaped, inverse, preferred_element_type=jnp.float32)
    range_back = range_back.astype(jnp.bfloat16)
    window = jnp.concatenate([window] * chunks, axis=1)
    totals = [[None] * (row_patches - 1) for _ in range(2)]
    for row in range(row_patches):
        stacked = []
        for chunk in range(chunks):
            top = (row * chunks + chunk) * PATCH
            block = range_back[top : top + PATCH]
            stacked.append(jnp.concatenate([block[:, :LANES], block[:, LANES:]], axis=0))
        stacked = jnp.concatenate(stacked, axis=1)
        patch_out = jnp.dot(back, stacked, preferred_element_type=jnp.float32) * window
        for part in range(2):
            upper = patch_out[part * PATCH : part * PATCH + HALF]
            lower = patch_out[part * PATCH + HALF : (part + 1) * PATCH]
            if row > 0:
                totals[part][row - 1] = totals[part][row - 1] + upper
            if row < row_patches - 1:
                totals[part][row] = lower
    total = jnp.concatenate([block for part in totals for block in part], axis=0)
    return total[:, :width] + total[:, width + HALF : 2 * width + HALF]


def own_kernel(table_ref, first_ref, inner_ref, second_ref, out_ref, spectrum_ref):
    own = (first_ref, inner_ref, second_ref)
    _, lines, width = out_ref.shape
    result = filtered_of(own, own, table_ref, spectrum_ref, lines, width)
    for part in range(2):
        out_ref[part] = result[part * lines : (part + 1) * lines]


def other_kernel(
    match_ref, table_ref, filtered_own_ref, first_ref, inner_ref, second_ref, *refs
):
    out_ref, result_ref, spectrum_ref, sems = refs[-4:]
    match_count, _, _, lines, width = out_ref.shape
    date = lax.axis_index("date")
    dates = match_ref.shape[1]

    def send(slot, source_ref):
        for match in range(match_count):
            wanted = lax.rem(match_ref[match, date] - date + dates, dates)

            @pl.when(wanted == slot)
            def _():
                copy_of(match, source_ref).start()

    def copy_of(match, source_ref):
        return pltpu.make_async_copy(source_ref, out_ref.at[match, :, 0], sems.at[match])

    send(0, filtered_own_ref)
    own = (first_ref, inner_ref, second_ref)
    for slot in range(1, dates):
        near_ref, middle_ref, raw_ref, message_ref = refs[4 * slot - 4 : 4 * slot]
        last = [v.astype(jnp.bfloat16) for v in side_lines(1, Partner(raw_ref), message_ref)]
        other = (near_ref, middle_ref, last)
        result = filtered_of(own, other, table_ref, spectrum_ref, lines, width)
        for part in range(2):
            result_ref[slot - 1, part] = result[part * lines : (part + 1) * lines]
        send(slot, result_ref.at[slot - 1])
    for match in range(match_count):
        copy_of(match, filtered_own_ref).wait()


def all_tables(row_patches):
    forward = fourier_table(1.0, 1.0)
    inverse = fourier_table(-1.0, 1.0 / PATCH)
    back = inverse.reshape(2, PATCH, 2, PATCH).transpose(2, 3, 0, 1).reshape(2 * PATCH, 2 * PATCH)
    window = window_table()[:PATCH, :PATCH]
    splits = []
    for _ in range(3):
        splits.append(window.astype(jnp.bfloat16).astype(np.float32))
        window = window - splits[-1]
    natural = np.arange((row_patches + 1) * HALF)
    wide = len(natural)
    inner = natural[REACH : wide - REACH]
    orders = [
        np.concatenate([natural[:REACH], inner, natural[wide - REACH :]]),
        np.concatenate([natural[wide - REACH :], inner, natural[:REACH]]),
    ]
    lines = line_table(forward, row_patches).reshape(-1, 2, wide)
    rows = [lines[:, :, order].reshape(-1, 2 * wide) for order in orders] + [
        paired(forward),
        paired(inverse),
        np.concatenate([back, ring_table()], axis=1),
        np.concatenate([*splits, np.zeros_like(window)], axis=1),
    ]
    return np.concatenate(rows, axis=0).astype(jnp.bfloat16)


def split_tables(table_ref, row_patches):
    size = row_patches * 2 * PATCH
    start = pl.multiple_of(jnp.where(is_above(0), 0, size), size)
    line_table_of = table_ref[pl.ds(start, size), :]
    at = 2 * size
    forward = table_ref[at : at + 4 * PATCH, :]
    at += 4 * PATCH
    inverse = table_ref[at : at + 4 * PATCH, :]
    at += 4 * PATCH
    back = table_ref[at : at + LANES, :LANES]
    ring = table_ref[at : at + LANES, LANES:]
    at += LANES
    splits = table_ref[at : at + PATCH, :].astype(jnp.float32)
    window = splits[:, :PATCH] + splits[:, PATCH : 2 * PATCH] + splits[:, 2 * PATCH : 3 * PATCH]
    window = jnp.concatenate([window, window], axis=1)
    window = jnp.concatenate([window, window], axis=0)
    return line_table_of, forward, inverse, back, ring, window


def per_device(image_stack, tap_weights, offsets, matchings):
    _, _, lines, width = image_stack.shape
    match_count = matchings.shape[0]
    other = lax.ppermute(image_stack, "rg", [(0, 1), (1, 0)]).reshape(2, lines, width)
    arguments = (
        image_stack.reshape(2, lines, width),
        tap_weights.reshape(TAPS, lines),
        offsets,
    )
    raw = pl.pallas_call(
        load_kernel,
        out_shape=tuple(pltpu.VMEM(a.shape, a.dtype) for a in arguments),
        in_specs=[HBM] * 3,
        out_specs=(VMEM,) * 3,
        scratch_shapes=[pltpu.SemaphoreType.DMA((3,))],
        compiler_params=PARAMS,
        name="load",
    )(*(pltpu.with_memory_space_constraint(a, pltpu.HBM) for a in arguments))
    raw = (raw[0], other, *raw[1:])
    message = jax.ShapeDtypeStruct((2 * REACH + STEP, width), jnp.bfloat16)
    *messages, own_raw = pl.pallas_call(
        pack_kernel,
        out_shape=(
            message,
            message,
            jax.ShapeDtypeStruct((2 * lines + 2 * STEP, width), jnp.bfloat16),
        ),
        in_specs=[VMEM] * 4,
        out_specs=(VMEM,) * 3,
        compiler_params=PARAMS,
        name="pack",
    )(*raw)
    dates = lax.axis_size("date")

    def from_date(piece, slot):
        return lax.ppermute(piece, "date", [((i + slot) % dates, i) for i in range(dates)])

    slots = range(1, dates)
    raws = [from_date(own_raw, slot) for slot in slots]
    peers = lax.axis_size("az")

    def swapped(value, start):
        paired_with = {i: i + 1 for i in range(start, peers - 1, 2)}
        paired_with.update({j: i for i, j in paired_with.items()})
        pairs = [
            (2 * i + core, 2 * paired_with[i] + core if i in paired_with else 2 * i + 1 - core)
            for i in range(peers)
            for core in range(2)
        ]
        return lax.ppermute(value, ("az", "rg"), pairs)

    messages = [swapped(messages[turn], turn) for turn in range(2)]
    def resampled(kernel, count, name, *args):
        return pl.pallas_call(
            kernel,
            out_shape=jax.ShapeDtypeStruct((2, count, width + HALF), jnp.bfloat16),
            in_specs=[VMEM] * len(args),
            out_specs=VMEM,
            compiler_params=PARAMS,
            name=name,
        )(*args)

    between = lines - 2 * RIM
    inner = resampled(functools.partial(inner_kernel, Own), between, "own_inner", *raw)

    def own_side(turn):
        name = "own_side_" + "ab"[turn]
        kernel = functools.partial(side_kernel, turn, Own)
        return resampled(kernel, REACH, name, *raw, messages[turn])

    def forwarded(turn, *made):
        message = pl.pallas_call(
            pass_kernel,
            out_shape=jax.ShapeDtypeStruct(messages[turn].shape, jnp.bfloat16),
            in_specs=[VMEM] * (1 + len(made)),
            out_specs=VMEM,
            compiler_params=PARAMS,
            name="pass_" + "ab"[turn],
        )(messages[turn], *made)
        return [from_date(message, slot) for slot in slots]

    nears = forwarded(0, inner)
    first = own_side(0)
    middles = [
        resampled(functools.partial(inner_kernel, Partner), between, "partner_inner", partner)
        for partner in raws
    ]
    fars = forwarded(1, first, *middles)
    second = own_side(1)
    own = (first, inner, second)
    others = []
    for partner, near, middle, far in zip(raws, nears, middles, fars):
        near = resampled(
            functools.partial(side_kernel, 0, Partner), REACH, "partner_side_a", partner, near
        )
        others += [near, middle, partner, far]
    row_patches = lines // HALF + 1
    chunks = (width + width + LANES) // LANES
    tables = jnp.asarray(all_tables(row_patches))
    spectrum = pltpu.VMEM((row_patches * chunks * PATCH, 2 * LANES), jnp.float32)
    filtered_own = pl.pallas_call(
        own_kernel,
        out_shape=jax.ShapeDtypeStruct((2, lines, width), jnp.float32),
        in_specs=[VMEM] * 4,
        out_specs=VMEM,
        scratch_shapes=[spectrum],
        compiler_params=PARAMS,
        name="filter_own",
    )(tables, *own)
    return pl.pallas_call(
        other_kernel,
        out_shape=jax.ShapeDtypeStruct((match_count, 2, 1, lines, width), jnp.float32),
        in_specs=[SMEM] + [VMEM] * (5 + len(others)),
        out_specs=HBM,
        scratch_shapes=[
            pltpu.VMEM((dates - 1, 2, lines, width), jnp.float32),
            spectrum,
            pltpu.SemaphoreType.DMA((match_count,)),
        ],
        compiler_params=PARAMS,
        name="filter_other",
    )(matchings, tables, filtered_own, *own, *others)


def solution(mesh):
    placed = (
        P(None, ("parts", "date"), "az", "rg"),
        P(None, ("parts", "date"), "az"),
        P(("parts", "date"), "az"),
        P(),
    )
    return jax.shard_map(
        per_device,
        mesh=mesh,
        in_specs=placed,
        out_specs=P(None, None, ("parts", "date"), "az", "rg"),
        check_vma=False,
    )
```

```python
import functools
import math

import jax
import jax.numpy as jnp
import numpy as np
from jax import lax
from jax.experimental import pallas as pl
from jax.experimental.pallas import tpu as pltpu
from jax.sharding import PartitionSpec as P

TAPS = 8
SHIFT_MAX = 12
PATCH = 64
HALF = PATCH // 2
RIM = SHIFT_MAX + TAPS // 2
REACH = HALF + RIM
LANES = 128
STEP = 16
VMEM_LIMIT = 48 * 1024 * 1024

VMEM = pl.BlockSpec(memory_space=pltpu.VMEM)
HBM = pl.BlockSpec(memory_space=pltpu.HBM)
PARAMS = pltpu.CompilerParams(vmem_limit_bytes=VMEM_LIMIT)


def fourier_table(sine_sign, table_scale):
    freq_ids = np.arange(PATCH)
    phase_ids = (freq_ids[:, None] * freq_ids[None, :]) % PATCH
    angles = phase_ids * (2.0 * math.pi / PATCH)
    cosine = np.cos(angles) * table_scale
    sine_part = np.sin(angles) * (sine_sign * table_scale)
    top = np.concatenate([cosine, -sine_part], axis=1)
    bottom = np.concatenate([sine_part, cosine], axis=1)
    return np.concatenate([top, bottom], axis=0).astype(np.float32)


def paired(table):
    split = table.reshape(2, PATCH, 2, PATCH)
    wide = np.zeros((2, 2, PATCH, 2, 2, PATCH), np.float32)
    for slot in range(2):
        wide[:, slot, :, :, slot, :] = split
    return wide.reshape(4 * PATCH, 4 * PATCH)


def line_table(forward, row_patches):
    wide_lines = (row_patches + 1) * HALF
    table = np.zeros((row_patches, 2 * PATCH, 2, wide_lines), np.float32)
    transposed = forward.T.reshape(2 * PATCH, 2, PATCH)
    for row in range(row_patches):
        table[row, :, :, row * HALF : row * HALF + PATCH] = transposed
    return table.reshape(row_patches * 2 * PATCH, 2 * wide_lines)


def window_table():
    window = np.sin(math.pi * (np.arange(PATCH) + 0.5) / PATCH) ** 2
    return np.tile(np.outer(window, window), (2, 2)).astype(np.float32)


def ring_table():
    ring = np.zeros((LANES, LANES), np.float32)
    for lane in range(LANES):
        base = lane // PATCH * PATCH
        for step in (-1, 0, 1):
            ring[base + (lane + step) % PATCH, lane] = 1.0
    return ring


def edge_of(other_ref, part, side, lines):
    width = other_ref.shape[2]
    return jnp.where(
        side == 0, other_ref[part, lines, :HALF], other_ref[part, lines, width - HALF :]
    )


def side_by_side(values):
    values = jnp.concatenate(values, axis=0)
    return jnp.concatenate([values[i : i + STEP] for i in range(0, values.shape[0], STEP)], axis=1)


def one_below(block, first, last):
    return jnp.concatenate([block[:, i * HALF : (i + 1) * HALF] for i in range(first, last)], axis=0)


def load_kernel(*refs):
    count = (len(refs) - 1) // 2
    copies = [
        pltpu.make_async_copy(refs[i], refs[count + i], refs[-1].at[i]) for i in range(count)
    ]
    for copy in copies:
        copy.start()
    for copy in copies:
        copy.wait()


def pack_kernel(image_ref, other_ref, taps_ref, offsets_ref, even_ref, odd_ref):
    lines = image_ref.shape[1]
    side = lax.axis_index("rg")
    taps = taps_ref[...]
    taps_high = taps.astype(jnp.bfloat16).astype(jnp.float32)
    taps = jnp.concatenate([taps_high, taps - taps_high], axis=0)
    shifts = jnp.broadcast_to(offsets_ref[...].astype(jnp.float32), taps.shape)

    def write(out_ref, line_start, tap_start):
        rows = slice(line_start, line_start + REACH)
        for part in range(2):
            cut = slice(part * REACH, (part + 1) * REACH)
            out_ref[cut, :] = image_ref[part, rows, :].astype(jnp.bfloat16)
        edges = [edge_of(other_ref, part, side, rows) for part in range(2)]
        cut = slice(tap_start, tap_start + HALF)
        block = side_by_side([*edges, taps[:, cut], shifts[:, cut]])
        out_ref[2 * REACH :, :] = block.astype(jnp.bfloat16)

    parity = lax.rem(lax.axis_index("az"), 2)

    @pl.when(parity == 0)
    def _():
        write(even_ref, lines - REACH, lines - HALF)
        write(odd_ref, 0, 0)

    @pl.when(parity == 1)
    def _():
        write(even_ref, 0, 0)
        write(odd_ref, lines - REACH, lines - HALF)


def is_above(turn):
    return lax.rem(lax.axis_index("az") + turn, 2) == 1


def band(taps, shift, first_line, source):
    count, lines = source.shape
    tap_ids = source - (lax.broadcasted_iota(jnp.int32, (count, lines), 1) + first_line)
    tap_ids = tap_ids - shift + (TAPS // 2 - 1)
    total = jnp.zeros((count, lines), jnp.float32)
    for tap in range(TAPS):
        total = jnp.where(tap_ids == tap, taps[tap : tap + 1, :], total)
    return total


def high_low(value):
    high = value.astype(jnp.bfloat16)
    low = (value - high.astype(jnp.float32)).astype(jnp.bfloat16)
    return jnp.concatenate([high, low], axis=0)


def apply_band(weights, rows):
    over_rows = (((0,), (0,)), ((), ()))
    rows = jnp.concatenate([rows, rows], axis=0)
    return lax.dot_general(high_low(weights), rows, over_rows, preferred_element_type=jnp.float32)


def write_piece(out_ref, parts, more_edge, width):
    lines = parts[0].shape[0]
    for part, value in enumerate(parts):
        out_ref[part * lines : (part + 1) * lines, :] = value[:, :width].astype(jnp.bfloat16)
    edges = side_by_side([value[:REACH, width:] for value in parts] + [more_edge])
    out_ref[2 * lines :, :] = edges.astype(jnp.bfloat16)


def inner_kernel(image_ref, other_ref, taps_ref, offsets_ref, out_ref):
    lines = image_ref.shape[1]
    width = image_ref.shape[2]
    side = lax.axis_index("rg")
    cut = slice(RIM, lines - RIM)
    source = lax.broadcasted_iota(jnp.int32, (lines, lines - 2 * RIM), 0)
    weights = band(taps_ref[:, cut], offsets_ref[:, cut], RIM, source)
    weights = jnp.concatenate([weights, weights], axis=0)
    for part in range(2):
        edge = edge_of(other_ref, part, side, slice(0, lines))
        rows = high_low(jnp.concatenate([image_ref[part], edge], axis=1))
        out_ref[part] = apply_band(weights, rows)


def side_kernel(
    turn, image_ref, other_ref, taps_ref, offsets_ref, message_ref, inner_ref, *refs
):
    out_ref = refs[-1]
    lines = image_ref.shape[1]
    width = image_ref.shape[2]
    side = lax.axis_index("rg")
    place = lax.axis_index("az")
    above = is_above(turn)
    alone = jnp.where(above, place == 0, place == lax.axis_size("az") - 1)
    message = message_ref[...]
    message = jnp.where(alone, jnp.zeros_like(message), message)
    block = message[2 * REACH :, :].astype(jnp.float32)
    steps = 2 * REACH // STEP
    rim_edges = one_below(block, 0, steps).astype(jnp.bfloat16)
    rim_taps = one_below(block, steps, steps + 1)
    rim_taps = rim_taps[:TAPS] + rim_taps[TAPS:]
    rim_shift = one_below(block, steps + 1, steps + 2)[:1]

    def per_line(own, rim):
        upper = jnp.concatenate([rim, own[:, :RIM]], axis=1)
        lower = jnp.concatenate([own[:, lines - RIM :], rim], axis=1)
        return jnp.where(above, upper, lower)

    taps = per_line(taps_ref[...], rim_taps)
    shift = per_line(offsets_ref[...].astype(jnp.float32), rim_shift).astype(jnp.int32)
    first_line = jnp.where(above, -HALF, lines - RIM)
    near = 2 * RIM
    first_own = jnp.where(above, 0, lines - near)
    first_rim = jnp.where(above, -REACH, lines)
    source = lax.broadcasted_iota(jnp.int32, (REACH + near, REACH), 0)
    source = jnp.where(source < REACH, source + first_rim, source - REACH + first_own)
    weights = band(taps, shift, first_line, source)
    weights = jnp.concatenate([weights, weights[REACH:]], axis=0)
    parts = []
    for part in range(2):
        upper, lower = slice(0, near), slice(lines - near, lines)
        edge = jnp.where(
            above, edge_of(other_ref, part, side, upper), edge_of(other_ref, part, side, lower)
        )
        own = jnp.where(above, image_ref[part, upper, :], image_ref[part, lower, :])
        own = high_low(jnp.concatenate([own, edge], axis=1))
        cut = slice(part * REACH, (part + 1) * REACH)
        rim = jnp.concatenate([message[cut, :], rim_edges[cut]], axis=1)
        total = apply_band(weights, jnp.concatenate([rim, own], axis=0))
        if turn == 0:
            total = jnp.concatenate([total, inner_ref[part]], axis=0)
        parts.append(total)
    write_piece(out_ref, parts, inner_ref[turn, :, width:], width)


def cross(own_parts, other_parts):
    own_real, own_imag = own_parts
    other_real, other_imag = other_parts
    real = own_real * other_real + own_imag * other_imag
    imag = own_imag * other_real - own_real * other_imag
    return real, imag


def tile_of(first_ref, second_ref, lines):
    inner = lines - 2 * RIM
    step, more = REACH // STEP, inner // STEP

    def split(ref, count):
        tiles = ref[: 2 * count, :].astype(jnp.float32)
        block = ref[2 * count :, :].astype(jnp.float32)
        edges = [one_below(block, part * step, (part + 1) * step) for part in range(2)]
        return (tiles[:count], tiles[count:]), edges, one_below(block, 2 * step, 2 * step + more)

    first = split(first_ref, REACH + inner)
    second = split(second_ref, REACH)
    tiles, edges = [], []
    for part, middle in enumerate((first[2], second[2])):
        tiles.append(jnp.concatenate([first[0][part], second[0][part]], axis=0))
        edges.append(jnp.concatenate([first[1][part], middle, second[1][part]], axis=0))
    return tiles, edges


def filtered_of(own_refs, other_refs, table_ref, spectrum_ref, lines, meanwhile=None):
    width = own_refs[0].shape[1]
    wide = lines + 2 * HALF
    row_patches = lines // HALF + 1
    side = lax.axis_index("rg")
    line_table_of, forward, inverse, back, ring, window = split_tables(table_ref, row_patches)
    own_tile, own_edge = tile_of(*own_refs, lines)
    other_tile, other_edge = tile_of(*other_refs, lines)
    mid = jnp.concatenate(cross(own_tile, other_tile), axis=0)
    rim = jnp.concatenate(cross(own_edge, other_edge), axis=0)
    before = jnp.where(side == 0, 0.0, rim)
    after = jnp.where(side == 0, rim, 0.0)
    filler = jnp.zeros((2 * wide, LANES - 2 * HALF), jnp.float32)
    shifted = jnp.concatenate([before, mid, after, filler], axis=1).astype(jnp.bfloat16)
    both = jnp.concatenate([mid.astype(jnp.bfloat16), shifted], axis=1)
    chunks = both.shape[1] // LANES
    line_spectra = jnp.dot(line_table_of, both, preferred_element_type=jnp.float32)
    line_spectra = line_spectra.astype(jnp.bfloat16)
    pieces = []
    for row in range(row_patches):
        top = row * 2 * PATCH
        for chunk in range(chunks):
            cut = slice(chunk * LANES, (chunk + 1) * LANES)
            real = line_spectra[top : top + PATCH, cut]
            imag = line_spectra[top + PATCH : top + 2 * PATCH, cut]
            pieces.append(jnp.concatenate([real, imag], axis=1))
    patches = jnp.concatenate(pieces, axis=0)
    spectrum_ref[...] = jnp.dot(patches, forward, preferred_element_type=jnp.float32)
    if meanwhile is not None:
        meanwhile()
    powers = []
    for block in range(row_patches * chunks):
        rows = slice(block * PATCH, (block + 1) * PATCH)
        real = spectrum_ref[rows, :LANES]
        imag = spectrum_ref[rows, LANES:]
        power = real * real + imag * imag
        power = power + pltpu.roll(power, 1, 0) + pltpu.roll(power, PATCH - 1, 0)
        powers.append(power.astype(jnp.bfloat16))
    smooth = jnp.dot(jnp.concatenate(powers, axis=0), ring, preferred_element_type=jnp.float32)
    gain = lax.rsqrt(lax.rsqrt(smooth * (1.0 / (9.0 * PATCH * PATCH)) + 1.0))
    shaped = jnp.concatenate(
        [spectrum_ref[:, :LANES] * gain, spectrum_ref[:, LANES:] * gain], axis=1
    ).astype(jnp.bfloat16)
    range_back = jnp.dot(shaped, inverse, preferred_element_type=jnp.float32)
    range_back = range_back.astype(jnp.bfloat16)
    window = jnp.concatenate([window] * chunks, axis=1)
    totals = [[None] * (row_patches - 1) for _ in range(2)]
    for row in range(row_patches):
        stacked = []
        for chunk in range(chunks):
            top = (row * chunks + chunk) * PATCH
            block = range_back[top : top + PATCH]
            stacked.append(jnp.concatenate([block[:, :LANES], block[:, LANES:]], axis=0))
        stacked = jnp.concatenate(stacked, axis=1)
        patch_out = jnp.dot(back, stacked, preferred_element_type=jnp.float32) * window
        for part in range(2):
            upper = patch_out[part * PATCH : part * PATCH + HALF]
            lower = patch_out[part * PATCH + HALF : (part + 1) * PATCH]
            if row > 0:
                totals[part][row - 1] = totals[part][row - 1] + upper
            if row < row_patches - 1:
                totals[part][row] = lower
    total = jnp.concatenate([block for part in totals for block in part], axis=0)
    return total[:, :width] + total[:, width + HALF : 2 * width + HALF]


def keep(ref, result):
    lines = ref.shape[1]
    for part in range(2):
        ref[part] = result[part * lines : (part + 1) * lines]


def own_kernel(table_ref, first_ref, second_ref, out_ref, spectrum_ref):
    own = (first_ref, second_ref)
    keep(out_ref, filtered_of(own, own, table_ref, spectrum_ref, out_ref.shape[1]))


def other_kernel(matchings_ref, table_ref, filtered_own_ref, first_ref, second_ref, *refs):
    out_ref, match_ref, result_ref, spectrum_ref, sems = refs[-5:]
    match_count, _, _, lines, _ = out_ref.shape
    date = lax.axis_index("date")
    dates = match_ref.shape[1]
    fetch = pltpu.make_async_copy(matchings_ref, match_ref, sems.at[match_count])
    fetch.start()

    def copy_of(match, source_ref):
        return pltpu.make_async_copy(source_ref, out_ref.at[match, :, 0], sems.at[match])

    def send(slot, source_ref):
        for match in range(match_count):
            wanted = lax.rem(match_ref[match, date] - date + dates, dates)

            @pl.when(wanted == slot)
            def _():
                copy_of(match, source_ref).start()

    def meanwhile():
        fetch.wait()
        send(0, filtered_own_ref)

    for slot in range(1, dates):
        result = filtered_of(
            (first_ref, second_ref),
            refs[2 * slot - 2 : 2 * slot],
            table_ref,
            spectrum_ref,
            lines,
            meanwhile if slot == 1 else None,
        )
        keep(result_ref.at[slot - 1], result)
        send(slot, result_ref.at[slot - 1])
    for match in range(match_count):
        copy_of(match, filtered_own_ref).wait()


def all_tables(row_patches):
    forward = fourier_table(1.0, 1.0)
    inverse = fourier_table(-1.0, 1.0 / PATCH)
    back = inverse.reshape(2, PATCH, 2, PATCH).transpose(2, 3, 0, 1).reshape(2 * PATCH, 2 * PATCH)
    window = window_table()[:PATCH, :PATCH]
    splits = []
    for _ in range(3):
        splits.append(window.astype(jnp.bfloat16).astype(np.float32))
        window = window - splits[-1]
    natural = np.arange((row_patches + 1) * HALF)
    wide = len(natural)
    inner = natural[REACH : wide - REACH]
    orders = [
        np.concatenate([natural[:REACH], inner, natural[wide - REACH :]]),
        np.concatenate([natural[wide - REACH :], inner, natural[:REACH]]),
    ]
    lines = line_table(forward, row_patches).reshape(-1, 2, wide)
    rows = [lines[:, :, order].reshape(-1, 2 * wide) for order in orders] + [
        paired(forward),
        paired(inverse),
        np.concatenate([back, ring_table()], axis=1),
        np.concatenate([*splits, np.zeros_like(window)], axis=1),
    ]
    return np.concatenate(rows, axis=0).astype(jnp.bfloat16)


def split_tables(table_ref, row_patches):
    size = row_patches * 2 * PATCH
    start = pl.multiple_of(jnp.where(is_above(0), 0, size), size)
    line_table_of = table_ref[pl.ds(start, size), :]
    at = 2 * size
    forward = table_ref[at : at + 4 * PATCH, :]
    at += 4 * PATCH
    inverse = table_ref[at : at + 4 * PATCH, :]
    at += 4 * PATCH
    back = table_ref[at : at + LANES, :LANES]
    ring = table_ref[at : at + LANES, LANES:]
    at += LANES
    splits = table_ref[at : at + PATCH, :].astype(jnp.float32)
    window = splits[:, :PATCH] + splits[:, PATCH : 2 * PATCH] + splits[:, 2 * PATCH : 3 * PATCH]
    window = jnp.concatenate([window, window], axis=1)
    window = jnp.concatenate([window, window], axis=0)
    return line_table_of, forward, inverse, back, ring, window


def per_device(image_stack, tap_weights, offsets, matchings):
    _, _, lines, width = image_stack.shape
    match_count = matchings.shape[0]
    other = lax.ppermute(image_stack, "rg", [(0, 1), (1, 0)]).reshape(2, lines, width)
    arguments = (
        image_stack.reshape(2, lines, width),
        tap_weights.reshape(TAPS, lines),
        offsets,
    )
    raw = pl.pallas_call(
        load_kernel,
        out_shape=tuple(pltpu.VMEM(a.shape, a.dtype) for a in arguments),
        in_specs=[HBM] * 3,
        out_specs=(VMEM,) * 3,
        scratch_shapes=[pltpu.SemaphoreType.DMA((3,))],
        compiler_params=PARAMS,
        name="load",
    )(*(pltpu.with_memory_space_constraint(a, pltpu.HBM) for a in arguments))
    raw = (raw[0], other, *raw[1:])
    message = jax.ShapeDtypeStruct((2 * REACH + STEP, width), jnp.bfloat16)
    messages = pl.pallas_call(
        pack_kernel,
        out_shape=(message, message),
        in_specs=[VMEM] * 4,
        out_specs=(VMEM, VMEM),
        compiler_params=PARAMS,
        name="pack",
    )(*raw)
    peers = lax.axis_size("az")

    def swapped(value, start):
        paired_with = {i: i + 1 for i in range(start, peers - 1, 2)}
        paired_with.update({j: i for i, j in paired_with.items()})
        pairs = [
            (2 * i + core, 2 * paired_with[i] + core if i in paired_with else 2 * i + 1 - core)
            for i in range(peers)
            for core in range(2)
        ]
        return lax.ppermute(value, ("az", "rg"), pairs)

    messages = [swapped(messages[turn], turn) for turn in range(2)]
    inner = pl.pallas_call(
        inner_kernel,
        out_shape=jax.ShapeDtypeStruct((2, lines - 2 * RIM, width + HALF), jnp.float32),
        in_specs=[VMEM] * 4,
        out_specs=VMEM,
        compiler_params=PARAMS,
        name="inner",
    )(*raw)
    own = []
    for turn in range(2):
        count = REACH + (0 if turn else lines - 2 * RIM)
        call = pl.pallas_call(
            functools.partial(side_kernel, turn),
            out_shape=jax.ShapeDtypeStruct((2 * count + STEP, width), jnp.bfloat16),
            in_specs=[VMEM] * (6 + len(own)),
            out_specs=VMEM,
            compiler_params=PARAMS,
            name="side_" + "ab"[turn],
        )
        own.append(call(*raw, messages[turn], inner, *own))
    dates = lax.axis_size("date")

    def from_date(piece, slot):
        return lax.ppermute(piece, "date", [((i + slot) % dates, i) for i in range(dates)])

    others = [from_date(piece, slot) for slot in range(1, dates) for piece in own]
    row_patches = lines // HALF + 1
    chunks = (width + width + LANES) // LANES
    tables = jnp.asarray(all_tables(row_patches))
    spectrum = pltpu.VMEM((row_patches * chunks * PATCH, 2 * LANES), jnp.float32)
    filtered_own = pl.pallas_call(
        own_kernel,
        out_shape=jax.ShapeDtypeStruct((2, lines, width), jnp.float32),
        in_specs=[VMEM] * 3,
        out_specs=VMEM,
        scratch_shapes=[spectrum],
        compiler_params=PARAMS,
        name="filter_own",
    )(tables, *own)
    return pl.pallas_call(
        other_kernel,
        out_shape=jax.ShapeDtypeStruct((match_count, 2, 1, lines, width), jnp.float32),
        in_specs=[HBM] + [VMEM] * (4 + len(others)),
        out_specs=HBM,
        scratch_shapes=[
            pltpu.SMEM(matchings.shape, jnp.int32),
            pltpu.VMEM((dates - 1, 2, lines, width), jnp.float32),
            spectrum,
            pltpu.SemaphoreType.DMA((match_count + 1,)),
        ],
        compiler_params=PARAMS,
        name="filter_other",
    )(pltpu.with_memory_space_constraint(matchings, pltpu.HBM), tables, filtered_own, *own, *others)


def solution(mesh):
    placed = (
        P(None, ("parts", "date"), "az", "rg"),
        P(None, ("parts", "date"), "az"),
        P(("parts", "date"), "az"),
        P(),
    )
    return jax.shard_map(
        per_device,
        mesh=mesh,
        in_specs=placed,
        out_specs=P(None, None, ("parts", "date"), "az", "rg"),
        check_vma=False,
    )
```

```python
import functools
import math

import jax
import jax.numpy as jnp
import numpy as np
from jax import lax
from jax.experimental import pallas as pl
from jax.experimental.pallas import tpu as pltpu
from jax.sharding import PartitionSpec as P

TAPS = 8
SHIFT_MAX = 12
PATCH = 64
HALF = PATCH // 2
RIM = SHIFT_MAX + TAPS // 2
REACH = HALF + RIM
LANES = 128
STEP = 16
VMEM_LIMIT = 48 * 1024 * 1024

VMEM = pl.BlockSpec(memory_space=pltpu.VMEM)
SMEM = pl.BlockSpec(memory_space=pltpu.SMEM)
HBM = pl.BlockSpec(memory_space=pltpu.HBM)
PARAMS = pltpu.CompilerParams(vmem_limit_bytes=VMEM_LIMIT)


def fourier_table(sine_sign, table_scale):
    freq_ids = np.arange(PATCH)
    phase_ids = (freq_ids[:, None] * freq_ids[None, :]) % PATCH
    angles = phase_ids * (2.0 * math.pi / PATCH)
    cosine = np.cos(angles) * table_scale
    sine_part = np.sin(angles) * (sine_sign * table_scale)
    top = np.concatenate([cosine, -sine_part], axis=1)
    bottom = np.concatenate([sine_part, cosine], axis=1)
    return np.concatenate([top, bottom], axis=0).astype(np.float32)


def paired(table):
    split = table.reshape(2, PATCH, 2, PATCH)
    wide = np.zeros((2, 2, PATCH, 2, 2, PATCH), np.float32)
    for slot in range(2):
        wide[:, slot, :, :, slot, :] = split
    return wide.reshape(4 * PATCH, 4 * PATCH)


def line_table(forward, row_patches):
    wide_lines = (row_patches + 1) * HALF
    table = np.zeros((row_patches, 2 * PATCH, 2, wide_lines), np.float32)
    transposed = forward.T.reshape(2 * PATCH, 2, PATCH)
    for row in range(row_patches):
        table[row, :, :, row * HALF : row * HALF + PATCH] = transposed
    return table.reshape(row_patches * 2 * PATCH, 2 * wide_lines)


def window_table():
    window = np.sin(math.pi * (np.arange(PATCH) + 0.5) / PATCH) ** 2
    return np.tile(np.outer(window, window), (2, 2)).astype(np.float32)


def ring_table():
    ring = np.zeros((LANES, LANES), np.float32)
    for lane in range(LANES):
        base = lane // PATCH * PATCH
        for step in (-1, 0, 1):
            ring[base + (lane + step) % PATCH, lane] = 1.0
    return ring


def edge_of(other_ref, part, side, lines):
    width = other_ref.shape[2]
    return jnp.where(
        side == 0, other_ref[part, lines, :HALF], other_ref[part, lines, width - HALF :]
    )


def side_by_side(values):
    values = jnp.concatenate(values, axis=0)
    return jnp.concatenate([values[i : i + STEP] for i in range(0, values.shape[0], STEP)], axis=1)


def one_below(block, first, last):
    return jnp.concatenate([block[:, i * HALF : (i + 1) * HALF] for i in range(first, last)], axis=0)


def load_kernel(*refs):
    count = (len(refs) - 1) // 2
    copies = [
        pltpu.make_async_copy(refs[i], refs[count + i], refs[-1].at[i]) for i in range(count)
    ]
    for copy in copies:
        copy.start()
    for copy in copies:
        copy.wait()


def pack_kernel(image_ref, other_ref, taps_ref, offsets_ref, even_ref, odd_ref):
    lines = image_ref.shape[1]
    side = lax.axis_index("rg")
    taps = taps_ref[...]
    taps_high = taps.astype(jnp.bfloat16).astype(jnp.float32)
    taps = jnp.concatenate([taps_high, taps - taps_high], axis=0)
    shifts = jnp.broadcast_to(offsets_ref[...].astype(jnp.float32), taps.shape)

    def write(out_ref, line_start, tap_start):
        rows = slice(line_start, line_start + REACH)
        for part in range(2):
            cut = slice(part * REACH, (part + 1) * REACH)
            out_ref[cut, :] = image_ref[part, rows, :].astype(jnp.bfloat16)
        edges = [edge_of(other_ref, part, side, rows) for part in range(2)]
        cut = slice(tap_start, tap_start + HALF)
        block = side_by_side([*edges, taps[:, cut], shifts[:, cut]])
        out_ref[2 * REACH :, :] = block.astype(jnp.bfloat16)

    parity = lax.rem(lax.axis_index("az"), 2)

    @pl.when(parity == 0)
    def _():
        write(even_ref, lines - REACH, lines - HALF)
        write(odd_ref, 0, 0)

    @pl.when(parity == 1)
    def _():
        write(even_ref, 0, 0)
        write(odd_ref, lines - REACH, lines - HALF)


def is_above(turn):
    return lax.rem(lax.axis_index("az") + turn, 2) == 1


def band(taps, shift, first_line, source):
    count, lines = source.shape
    tap_ids = source - (lax.broadcasted_iota(jnp.int32, (count, lines), 1) + first_line)
    tap_ids = tap_ids - shift + (TAPS // 2 - 1)
    total = jnp.zeros((count, lines), jnp.float32)
    for tap in range(TAPS):
        total = jnp.where(tap_ids == tap, taps[tap : tap + 1, :], total)
    return total


def high_low(value):
    high = value.astype(jnp.bfloat16)
    low = (value - high.astype(jnp.float32)).astype(jnp.bfloat16)
    return jnp.concatenate([high, low], axis=0)


def apply_band(weights, rows):
    over_rows = (((0,), (0,)), ((), ()))
    rows = jnp.concatenate([rows, rows], axis=0)
    return lax.dot_general(high_low(weights), rows, over_rows, preferred_element_type=jnp.float32)


def write_piece(out_ref, parts, width):
    lines = parts[0].shape[0]
    for part, value in enumerate(parts):
        out_ref[part * lines : (part + 1) * lines, :] = value[:, :width].astype(jnp.bfloat16)
    edges = side_by_side([value[:, width:] for value in parts])
    out_ref[2 * lines :, :] = edges.astype(jnp.bfloat16)


def read_piece(ref):
    lines = (ref.shape[0] - STEP) // 2
    tiles = ref[: 2 * lines, :].astype(jnp.float32)
    edges = one_below(ref[2 * lines :, :].astype(jnp.float32), 0, 2 * lines // STEP)
    return [(v[:lines], v[lines:]) for v in (tiles, edges)]


def inner_kernel(image_ref, other_ref, taps_ref, offsets_ref, out_ref):
    lines = image_ref.shape[1]
    width = image_ref.shape[2]
    side = lax.axis_index("rg")
    cut = slice(RIM, lines - RIM)
    source = lax.broadcasted_iota(jnp.int32, (lines, lines - 2 * RIM), 0)
    weights = band(taps_ref[:, cut], offsets_ref[:, cut], RIM, source)
    weights = jnp.concatenate([weights, weights], axis=0)
    for part in range(2):
        edge = edge_of(other_ref, part, side, slice(0, lines))
        rows = high_low(jnp.concatenate([image_ref[part], edge], axis=1))
        out_ref[part] = apply_band(weights, rows)


def side_kernel(
    turn, image_ref, other_ref, taps_ref, offsets_ref, message_ref, inner_ref, *refs
):
    out_ref = refs[-1]
    lines = image_ref.shape[1]
    width = image_ref.shape[2]
    side = lax.axis_index("rg")
    place = lax.axis_index("az")
    above = is_above(turn)
    alone = jnp.where(above, place == 0, place == lax.axis_size("az") - 1)
    message = message_ref[...]
    message = jnp.where(alone, jnp.zeros_like(message), message)
    block = message[2 * REACH :, :].astype(jnp.float32)
    steps = 2 * REACH // STEP
    rim_edges = one_below(block, 0, steps).astype(jnp.bfloat16)
    rim_taps = one_below(block, steps, steps + 1)
    rim_taps = rim_taps[:TAPS] + rim_taps[TAPS:]
    rim_shift = one_below(block, steps + 1, steps + 2)[:1]

    def per_line(own, rim):
        upper = jnp.concatenate([rim, own[:, :RIM]], axis=1)
        lower = jnp.concatenate([own[:, lines - RIM :], rim], axis=1)
        return jnp.where(above, upper, lower)

    taps = per_line(taps_ref[...], rim_taps)
    shift = per_line(offsets_ref[...].astype(jnp.float32), rim_shift).astype(jnp.int32)
    first_line = jnp.where(above, -HALF, lines - RIM)
    near = 2 * RIM
    first_own = jnp.where(above, 0, lines - near)
    first_rim = jnp.where(above, -REACH, lines)
    source = lax.broadcasted_iota(jnp.int32, (REACH + near, REACH), 0)
    source = jnp.where(source < REACH, source + first_rim, source - REACH + first_own)
    weights = band(taps, shift, first_line, source)
    weights = jnp.concatenate([weights, weights[REACH:]], axis=0)
    parts = []
    for part in range(2):
        upper, lower = slice(0, near), slice(lines - near, lines)
        edge = jnp.where(
            above, edge_of(other_ref, part, side, upper), edge_of(other_ref, part, side, lower)
        )
        own = jnp.where(above, image_ref[part, upper, :], image_ref[part, lower, :])
        own = high_low(jnp.concatenate([own, edge], axis=1))
        cut = slice(part * REACH, (part + 1) * REACH)
        rim = jnp.concatenate([message[cut, :], rim_edges[cut]], axis=1)
        total = apply_band(weights, jnp.concatenate([rim, own], axis=0))
        between = inner_ref.shape[1] // 2
        upper = jnp.concatenate([total, inner_ref[part, :between]], axis=0)
        lower = jnp.concatenate([inner_ref[part, between:], total], axis=0)
        parts.append(jnp.where(above, upper, lower))
    write_piece(out_ref, parts, width)


def cross(own_parts, other_parts):
    own_real, own_imag = own_parts
    other_real, other_imag = other_parts
    real = own_real * other_real + own_imag * other_imag
    imag = own_imag * other_real - own_real * other_imag
    return real, imag


def interferogram(own_ref, other_ref):
    side = lax.axis_index("rg")
    own_tile, own_edge = read_piece(own_ref)
    other_tile, other_edge = read_piece(other_ref)
    mid = jnp.concatenate(cross(own_tile, other_tile), axis=0)
    rim = jnp.concatenate(cross(own_edge, other_edge), axis=0)
    before = jnp.where(side == 0, 0.0, rim)
    after = jnp.where(side == 0, rim, 0.0)
    filler = jnp.zeros((mid.shape[0], LANES - 2 * HALF), jnp.float32)
    shifted = jnp.concatenate([before, mid, after, filler], axis=1).astype(jnp.bfloat16)
    return jnp.concatenate([mid.astype(jnp.bfloat16), shifted], axis=1)


def line_sum(turn, tables, own_ref, other_ref):
    both = interferogram(own_ref, other_ref)
    return jnp.dot(tables.lines(turn), both, preferred_element_type=jnp.float32)


def filtered_of(line_spectra, tables, spectrum_ref, row_patches, width):
    line_spectra = line_spectra.astype(jnp.bfloat16)
    chunks = line_spectra.shape[1] // LANES
    forward, inverse, back, ring, window = tables.core()
    pieces = []
    for row in range(row_patches):
        top = row * 2 * PATCH
        for chunk in range(chunks):
            cut = slice(chunk * LANES, (chunk + 1) * LANES)
            real = line_spectra[top : top + PATCH, cut]
            imag = line_spectra[top + PATCH : top + 2 * PATCH, cut]
            pieces.append(jnp.concatenate([real, imag], axis=1))
    patches = jnp.concatenate(pieces, axis=0)
    spectrum_ref[...] = jnp.dot(patches, forward, preferred_element_type=jnp.float32)
    powers = []
    for block in range(row_patches * chunks):
        rows = slice(block * PATCH, (block + 1) * PATCH)
        real = spectrum_ref[rows, :LANES]
        imag = spectrum_ref[rows, LANES:]
        power = real * real + imag * imag
        power = power + pltpu.roll(power, 1, 0) + pltpu.roll(power, PATCH - 1, 0)
        powers.append(power.astype(jnp.bfloat16))
    smooth = jnp.dot(jnp.concatenate(powers, axis=0), ring, preferred_element_type=jnp.float32)
    gain = lax.rsqrt(lax.rsqrt(smooth * (1.0 / (9.0 * PATCH * PATCH)) + 1.0))
    shaped = jnp.concatenate(
        [spectrum_ref[:, :LANES] * gain, spectrum_ref[:, LANES:] * gain], axis=1
    ).astype(jnp.bfloat16)
    range_back = jnp.dot(shaped, inverse, preferred_element_type=jnp.float32)
    range_back = range_back.astype(jnp.bfloat16)
    window = jnp.concatenate([window] * chunks, axis=1)
    totals = [[None] * (row_patches - 1) for _ in range(2)]
    for row in range(row_patches):
        stacked = []
        for chunk in range(chunks):
            top = (row * chunks + chunk) * PATCH
            block = range_back[top : top + PATCH]
            stacked.append(jnp.concatenate([block[:, :LANES], block[:, LANES:]], axis=0))
        stacked = jnp.concatenate(stacked, axis=1)
        patch_out = jnp.dot(back, stacked, preferred_element_type=jnp.float32) * window
        for part in range(2):
            upper = patch_out[part * PATCH : part * PATCH + HALF]
            lower = patch_out[part * PATCH + HALF : (part + 1) * PATCH]
            if row > 0:
                totals[part][row - 1] = totals[part][row - 1] + upper
            if row < row_patches - 1:
                totals[part][row] = lower
    total = jnp.concatenate([block for part in totals for block in part], axis=0)
    return total[:, :width] + total[:, width + HALF : 2 * width + HALF]


def keep(ref, result):
    lines = ref.shape[1]
    for part in range(2):
        ref[part] = result[part * lines : (part + 1) * lines]


def own_kernel(table_ref, first_ref, second_ref, out_ref, spectrum_ref):
    _, lines, width = out_ref.shape
    row_patches = lines // HALF + 1
    tables = Tables(table_ref, row_patches)
    both = [interferogram(ref, ref) for ref in (first_ref, second_ref)]
    weights = jnp.concatenate([tables.lines(turn) for turn in range(2)], axis=1)
    total = jnp.dot(weights, jnp.concatenate(both, axis=0), preferred_element_type=jnp.float32)
    keep(out_ref, filtered_of(total, tables, spectrum_ref, row_patches, width))


def first_kernel(row_patches, table_ref, own_ref, other_ref, out_ref):
    out_ref[...] = line_sum(0, Tables(table_ref, row_patches), own_ref, other_ref)


def other_kernel(match_ref, table_ref, filtered_own_ref, own_ref, *refs):
    out_ref, result_ref, spectrum_ref, sems = refs[-4:]
    match_count, _, _, lines, width = out_ref.shape
    row_patches = lines // HALF + 1
    date = lax.axis_index("date")
    dates = match_ref.shape[1]
    tables = Tables(table_ref, row_patches)

    def copy_of(match, source_ref):
        return pltpu.make_async_copy(source_ref, out_ref.at[match, :, 0], sems.at[match])

    def send(slot, source_ref):
        for match in range(match_count):
            wanted = lax.rem(match_ref[match, date] - date + dates, dates)

            @pl.when(wanted == slot)
            def _():
                copy_of(match, source_ref).start()

    send(0, filtered_own_ref)
    for slot in range(1, dates):
        first_ref, other_ref = refs[2 * slot - 2 : 2 * slot]
        total = first_ref[...] + line_sum(1, tables, own_ref, other_ref)
        result = filtered_of(total, tables, spectrum_ref, row_patches, width)
        keep(result_ref.at[slot - 1], result)
        send(slot, result_ref.at[slot - 1])
    for match in range(match_count):
        copy_of(match, filtered_own_ref).wait()


def all_tables(row_patches):
    forward = fourier_table(1.0, 1.0)
    inverse = fourier_table(-1.0, 1.0 / PATCH)
    back = inverse.reshape(2, PATCH, 2, PATCH).transpose(2, 3, 0, 1).reshape(2 * PATCH, 2 * PATCH)
    window = window_table()[:PATCH, :PATCH]
    splits = []
    for _ in range(3):
        splits.append(window.astype(jnp.bfloat16).astype(np.float32))
        window = window - splits[-1]
    half = (row_patches + 1) * HALF // 2
    lines = line_table(forward, row_patches).reshape(-1, 2, 2, half)
    halves = [lines[:, :, at].reshape(-1, 2 * half) for at in range(2)]
    rows = [np.concatenate([value, np.zeros_like(value)], axis=1) for value in halves] + [
        paired(forward),
        paired(inverse),
        np.concatenate([back, ring_table()], axis=1),
        np.concatenate([*splits, np.zeros_like(window)], axis=1),
    ]
    return np.concatenate(rows, axis=0).astype(jnp.bfloat16)


class Tables:
    def __init__(self, ref, row_patches):
        self.ref = ref
        self.size = row_patches * 2 * PATCH

    def lines(self, turn):
        start = pl.multiple_of(jnp.where(is_above(turn), 0, self.size), self.size)
        return self.ref[pl.ds(start, self.size), :LANES]

    def core(self):
        ref, at = self.ref, 2 * self.size
        forward = ref[at : at + 4 * PATCH, :]
        at += 4 * PATCH
        inverse = ref[at : at + 4 * PATCH, :]
        at += 4 * PATCH
        back = ref[at : at + LANES, :LANES]
        ring = ref[at : at + LANES, LANES:]
        at += LANES
        splits = ref[at : at + PATCH, :].astype(jnp.float32)
        window = splits[:, :PATCH] + splits[:, PATCH : 2 * PATCH] + splits[:, 2 * PATCH : 3 * PATCH]
        window = jnp.concatenate([window, window], axis=1)
        window = jnp.concatenate([window, window], axis=0)
        return forward, inverse, back, ring, window


def per_device(image_stack, tap_weights, offsets, matchings):
    _, _, lines, width = image_stack.shape
    match_count = matchings.shape[0]
    other = lax.ppermute(image_stack, "rg", [(0, 1), (1, 0)]).reshape(2, lines, width)
    arguments = (
        image_stack.reshape(2, lines, width),
        tap_weights.reshape(TAPS, lines),
        offsets,
    )
    raw = pl.pallas_call(
        load_kernel,
        out_shape=tuple(pltpu.VMEM(a.shape, a.dtype) for a in arguments),
        in_specs=[HBM] * 3,
        out_specs=(VMEM,) * 3,
        scratch_shapes=[pltpu.SemaphoreType.DMA((3,))],
        compiler_params=PARAMS,
        name="load",
    )(*(pltpu.with_memory_space_constraint(a, pltpu.HBM) for a in arguments))
    raw = (raw[0], other, *raw[1:])
    message = jax.ShapeDtypeStruct((2 * REACH + STEP, width), jnp.bfloat16)
    messages = pl.pallas_call(
        pack_kernel,
        out_shape=(message, message),
        in_specs=[VMEM] * 4,
        out_specs=(VMEM, VMEM),
        compiler_params=PARAMS,
        name="pack",
    )(*raw)
    peers = lax.axis_size("az")

    def swapped(value, start):
        paired_with = {i: i + 1 for i in range(start, peers - 1, 2)}
        paired_with.update({j: i for i, j in paired_with.items()})
        pairs = [
            (2 * i + core, 2 * paired_with[i] + core if i in paired_with else 2 * i + 1 - core)
            for i in range(peers)
            for core in range(2)
        ]
        return lax.ppermute(value, ("az", "rg"), pairs)

    messages = [swapped(messages[turn], turn) for turn in range(2)]
    inner = pl.pallas_call(
        inner_kernel,
        out_shape=jax.ShapeDtypeStruct((2, lines - 2 * RIM, width + HALF), jnp.float32),
        in_specs=[VMEM] * 4,
        out_specs=VMEM,
        compiler_params=PARAMS,
        name="inner",
    )(*raw)
    own = []
    for turn in range(2):
        count = lines // 2 + HALF
        call = pl.pallas_call(
            functools.partial(side_kernel, turn),
            out_shape=jax.ShapeDtypeStruct((2 * count + STEP, width), jnp.bfloat16),
            in_specs=[VMEM] * (6 + len(own)),
            out_specs=VMEM,
            compiler_params=PARAMS,
            name="side_" + "ab"[turn],
        )
        own.append(call(*raw, messages[turn], inner, *own))
    dates = lax.axis_size("date")

    def from_date(piece, slot):
        return lax.ppermute(piece, "date", [((i + slot) % dates, i) for i in range(dates)])

    others = [from_date(piece, slot) for slot in range(1, dates) for piece in own]
    row_patches = lines // HALF + 1
    chunks = (width + width + LANES) // LANES
    tables = jnp.asarray(all_tables(row_patches))
    spectrum = pltpu.VMEM((row_patches * chunks * PATCH, 2 * LANES), jnp.float32)
    filtered_own = pl.pallas_call(
        own_kernel,
        out_shape=jax.ShapeDtypeStruct((2, lines, width), jnp.float32),
        in_specs=[VMEM] * 3,
        out_specs=VMEM,
        scratch_shapes=[spectrum],
        compiler_params=PARAMS,
        name="filter_own",
    )(tables, *own)
    pieces = []
    for first, second in zip(others[::2], others[1::2]):
        total = pl.pallas_call(
            functools.partial(first_kernel, row_patches),
            out_shape=jax.ShapeDtypeStruct((row_patches * 2 * PATCH, chunks * LANES), jnp.float32),
            in_specs=[VMEM] * 3,
            out_specs=VMEM,
            compiler_params=PARAMS,
            name="filter_first",
        )(tables, own[0], first)
        pieces += [total, second]
    return pl.pallas_call(
        other_kernel,
        out_shape=jax.ShapeDtypeStruct((match_count, 2, 1, lines, width), jnp.float32),
        in_specs=[SMEM] + [VMEM] * (3 + len(pieces)),
        out_specs=HBM,
        scratch_shapes=[
            pltpu.VMEM((dates - 1, 2, lines, width), jnp.float32),
            spectrum,
            pltpu.SemaphoreType.DMA((match_count,)),
        ],
        compiler_params=PARAMS,
        name="filter_other",
    )(matchings, tables, filtered_own, own[1], *pieces)


def solution(mesh):
    placed = (
        P(None, ("parts", "date"), "az", "rg"),
        P(None, ("parts", "date"), "az"),
        P(("parts", "date"), "az"),
        P(),
    )
    return jax.shard_map(
        per_device,
        mesh=mesh,
        in_specs=placed,
        out_specs=P(None, None, ("parts", "date"), "az", "rg"),
        check_vma=False,
    )
```

```python
import functools
import math

import jax
import jax.numpy as jnp
import numpy as np
from jax import lax
from jax.experimental import pallas as pl
from jax.experimental.pallas import tpu as pltpu
from jax.sharding import PartitionSpec as P

TAPS = 8
SHIFT_MAX = 12
PATCH = 64
HALF = PATCH // 2
RIM = SHIFT_MAX + TAPS // 2
REACH = HALF + RIM
LANES = 128
STEP = 16
VMEM_LIMIT = 48 * 1024 * 1024

VMEM = pl.BlockSpec(memory_space=pltpu.VMEM)
SMEM = pl.BlockSpec(memory_space=pltpu.SMEM)
HBM = pl.BlockSpec(memory_space=pltpu.HBM)
PARAMS = pltpu.CompilerParams(vmem_limit_bytes=VMEM_LIMIT)


def fourier_table(sine_sign, table_scale):
    freq_ids = np.arange(PATCH)
    phase_ids = (freq_ids[:, None] * freq_ids[None, :]) % PATCH
    angles = phase_ids * (2.0 * math.pi / PATCH)
    cosine = np.cos(angles) * table_scale
    sine_part = np.sin(angles) * (sine_sign * table_scale)
    top = np.concatenate([cosine, -sine_part], axis=1)
    bottom = np.concatenate([sine_part, cosine], axis=1)
    return np.concatenate([top, bottom], axis=0).astype(np.float32)


def paired(table):
    split = table.reshape(2, PATCH, 2, PATCH)
    wide = np.zeros((2, 2, PATCH, 2, 2, PATCH), np.float32)
    for slot in range(2):
        wide[:, slot, :, :, slot, :] = split
    return wide.reshape(4 * PATCH, 4 * PATCH)


def line_table(forward, row_patches):
    wide_lines = (row_patches + 1) * HALF
    table = np.zeros((row_patches, 2 * PATCH, 2, wide_lines), np.float32)
    transposed = forward.T.reshape(2 * PATCH, 2, PATCH)
    for row in range(row_patches):
        table[row, :, :, row * HALF : row * HALF + PATCH] = transposed
    return table.reshape(row_patches * 2 * PATCH, 2 * wide_lines)


def window_table():
    window = np.sin(math.pi * (np.arange(PATCH) + 0.5) / PATCH) ** 2
    return np.tile(np.outer(window, window), (2, 2)).astype(np.float32)


def ring_table():
    ring = np.zeros((LANES, LANES), np.float32)
    for lane in range(LANES):
        base = lane // PATCH * PATCH
        for step in (-1, 0, 1):
            ring[base + (lane + step) % PATCH, lane] = 1.0
    return ring


def edge_of(other_ref, part, side, lines):
    width = other_ref.shape[2]
    return jnp.where(
        side == 0, other_ref[part, lines, :HALF], other_ref[part, lines, width - HALF :]
    )


def side_by_side(values):
    values = jnp.concatenate(values, axis=0)
    return jnp.concatenate([values[i : i + STEP] for i in range(0, values.shape[0], STEP)], axis=1)


def one_below(block, first, last):
    return jnp.concatenate([block[:, i * HALF : (i + 1) * HALF] for i in range(first, last)], axis=0)


def load_kernel(*refs):
    count = (len(refs) - 1) // 2
    copies = [
        pltpu.make_async_copy(refs[i], refs[count + i], refs[-1].at[i]) for i in range(count)
    ]
    for copy in copies:
        copy.start()
    for copy in copies:
        copy.wait()


def pack_kernel(image_ref, other_ref, taps_ref, offsets_ref, even_ref, odd_ref):
    lines = image_ref.shape[1]
    side = lax.axis_index("rg")
    taps = taps_ref[...]
    taps_high = taps.astype(jnp.bfloat16).astype(jnp.float32)
    taps = jnp.concatenate([taps_high, taps - taps_high], axis=0)
    shifts = jnp.broadcast_to(offsets_ref[...].astype(jnp.float32), taps.shape)

    def write(out_ref, line_start, tap_start):
        rows = slice(line_start, line_start + REACH)
        for part in range(2):
            cut = slice(part * REACH, (part + 1) * REACH)
            out_ref[cut, :] = image_ref[part, rows, :].astype(jnp.bfloat16)
        edges = [edge_of(other_ref, part, side, rows) for part in range(2)]
        cut = slice(tap_start, tap_start + HALF)
        block = side_by_side([*edges, taps[:, cut], shifts[:, cut]])
        out_ref[2 * REACH :, :] = block.astype(jnp.bfloat16)

    parity = lax.rem(lax.axis_index("az"), 2)

    @pl.when(parity == 0)
    def _():
        write(even_ref, lines - REACH, lines - HALF)
        write(odd_ref, 0, 0)

    @pl.when(parity == 1)
    def _():
        write(even_ref, 0, 0)
        write(odd_ref, lines - REACH, lines - HALF)


def is_above(turn):
    return lax.rem(lax.axis_index("az") + turn, 2) == 1


def band(taps, shift, first_line, source):
    count, lines = source.shape
    tap_ids = source - (lax.broadcasted_iota(jnp.int32, (count, lines), 1) + first_line)
    tap_ids = tap_ids - shift + (TAPS // 2 - 1)
    total = jnp.zeros((count, lines), jnp.float32)
    for tap in range(TAPS):
        total = jnp.where(tap_ids == tap, taps[tap : tap + 1, :], total)
    return total


def high_low(value):
    high = value.astype(jnp.bfloat16)
    low = (value - high.astype(jnp.float32)).astype(jnp.bfloat16)
    return jnp.concatenate([high, low], axis=0)


def apply_band(weights, rows):
    over_rows = (((0,), (0,)), ((), ()))
    rows = jnp.concatenate([rows, rows], axis=0)
    return lax.dot_general(high_low(weights), rows, over_rows, preferred_element_type=jnp.float32)


def write_piece(out_ref, parts, width):
    lines = parts[0].shape[0]
    for part, value in enumerate(parts):
        out_ref[part * lines : (part + 1) * lines, :] = value[:, :width].astype(jnp.bfloat16)
    filler = jnp.zeros((STEP * width // HALF - 2 * lines, HALF), jnp.float32)
    edges = [value[:, width:] for value in parts]
    edges = side_by_side(edges + [filler] if filler.shape[0] else edges)
    out_ref[2 * lines :, :] = edges.astype(jnp.bfloat16)


def read_piece(ref):
    lines = (ref.shape[0] - STEP) // 2
    tiles = ref[: 2 * lines, :].astype(jnp.float32)
    edges = one_below(ref[2 * lines :, :].astype(jnp.float32), 0, 2 * lines // STEP)
    return [(v[:lines], v[lines:]) for v in (tiles, edges)]


def inner_kernel(image_ref, other_ref, taps_ref, offsets_ref, out_ref):
    lines = image_ref.shape[1]
    width = image_ref.shape[2]
    side = lax.axis_index("rg")
    cut = slice(RIM, lines - RIM)
    source = lax.broadcasted_iota(jnp.int32, (lines, lines - 2 * RIM), 0)
    weights = band(taps_ref[:, cut], offsets_ref[:, cut], RIM, source)
    weights = jnp.concatenate([weights, weights], axis=0)
    parts = []
    for part in range(2):
        edge = edge_of(other_ref, part, side, slice(0, lines))
        rows = high_low(jnp.concatenate([image_ref[part], edge], axis=1))
        parts.append(apply_band(weights, rows))
    write_piece(out_ref, parts, width)


def side_kernel(
    turn, image_ref, other_ref, taps_ref, offsets_ref, message_ref, inner_ref, *refs
):
    out_ref = refs[-1]
    lines = image_ref.shape[1]
    width = image_ref.shape[2]
    side = lax.axis_index("rg")
    place = lax.axis_index("az")
    above = is_above(turn)
    alone = jnp.where(above, place == 0, place == lax.axis_size("az") - 1)
    message = message_ref[...]
    message = jnp.where(alone, jnp.zeros_like(message), message)
    block = message[2 * REACH :, :].astype(jnp.float32)
    steps = 2 * REACH // STEP
    rim_edges = one_below(block, 0, steps).astype(jnp.bfloat16)
    rim_taps = one_below(block, steps, steps + 1)
    rim_taps = rim_taps[:TAPS] + rim_taps[TAPS:]
    rim_shift = one_below(block, steps + 1, steps + 2)[:1]

    def per_line(own, rim):
        upper = jnp.concatenate([rim, own[:, :RIM]], axis=1)
        lower = jnp.concatenate([own[:, lines - RIM :], rim], axis=1)
        return jnp.where(above, upper, lower)

    taps = per_line(taps_ref[...], rim_taps)
    shift = per_line(offsets_ref[...].astype(jnp.float32), rim_shift).astype(jnp.int32)
    first_line = jnp.where(above, -HALF, lines - RIM)
    near = 2 * RIM
    first_own = jnp.where(above, 0, lines - near)
    first_rim = jnp.where(above, -REACH, lines)
    source = lax.broadcasted_iota(jnp.int32, (REACH + near, REACH), 0)
    source = jnp.where(source < REACH, source + first_rim, source - REACH + first_own)
    weights = band(taps, shift, first_line, source)
    weights = jnp.concatenate([weights, weights[REACH:]], axis=0)
    parts = []
    for part in range(2):
        upper, lower = slice(0, near), slice(lines - near, lines)
        edge = jnp.where(
            above, edge_of(other_ref, part, side, upper), edge_of(other_ref, part, side, lower)
        )
        own = jnp.where(above, image_ref[part, upper, :], image_ref[part, lower, :])
        own = high_low(jnp.concatenate([own, edge], axis=1))
        cut = slice(part * REACH, (part + 1) * REACH)
        rim = jnp.concatenate([message[cut, :], rim_edges[cut]], axis=1)
        parts.append(apply_band(weights, jnp.concatenate([rim, own], axis=0)))
    write_piece(out_ref, parts, width)


def pass_kernel(piece_ref, *refs):
    refs[-1][...] = piece_ref[...]


def cross(own_parts, other_parts):
    own_real, own_imag = own_parts
    other_real, other_imag = other_parts
    real = own_real * other_real + own_imag * other_imag
    imag = own_imag * other_real - own_real * other_imag
    return real, imag


def interferogram(own_ref, other_ref):
    side = lax.axis_index("rg")
    own_tile, own_edge = read_piece(own_ref)
    other_tile, other_edge = read_piece(other_ref)
    mid = jnp.concatenate(cross(own_tile, other_tile), axis=0)
    rim = jnp.concatenate(cross(own_edge, other_edge), axis=0)
    before = jnp.where(side == 0, 0.0, rim)
    after = jnp.where(side == 0, rim, 0.0)
    filler = jnp.zeros((mid.shape[0], LANES - 2 * HALF), jnp.float32)
    shifted = jnp.concatenate([before, mid, after, filler], axis=1).astype(jnp.bfloat16)
    return jnp.concatenate([mid.astype(jnp.bfloat16), shifted], axis=1)


def first_sum(tables, own_refs, other_refs):
    both = [interferogram(own, other) for own, other in zip(own_refs, other_refs)]
    both = jnp.concatenate(both, axis=0)
    return jnp.dot(tables.first(), both, preferred_element_type=jnp.float32)


def second_sum(tables, own_ref, other_ref):
    both = interferogram(own_ref, other_ref)
    return jnp.dot(tables.second(), both, preferred_element_type=jnp.float32)


def filtered_of(line_spectra, tables, spectrum_ref, row_patches, width):
    line_spectra = line_spectra.astype(jnp.bfloat16)
    chunks = line_spectra.shape[1] // LANES
    forward, inverse, back, ring, window = tables.core()
    pieces = []
    for row in range(row_patches):
        top = row * 2 * PATCH
        for chunk in range(chunks):
            cut = slice(chunk * LANES, (chunk + 1) * LANES)
            real = line_spectra[top : top + PATCH, cut]
            imag = line_spectra[top + PATCH : top + 2 * PATCH, cut]
            pieces.append(jnp.concatenate([real, imag], axis=1))
    patches = jnp.concatenate(pieces, axis=0)
    spectrum_ref[...] = jnp.dot(patches, forward, preferred_element_type=jnp.float32)
    powers = []
    for block in range(row_patches * chunks):
        rows = slice(block * PATCH, (block + 1) * PATCH)
        real = spectrum_ref[rows, :LANES]
        imag = spectrum_ref[rows, LANES:]
        power = real * real + imag * imag
        power = power + pltpu.roll(power, 1, 0) + pltpu.roll(power, PATCH - 1, 0)
        powers.append(power.astype(jnp.bfloat16))
    smooth = jnp.dot(jnp.concatenate(powers, axis=0), ring, preferred_element_type=jnp.float32)
    gain = lax.rsqrt(lax.rsqrt(smooth * (1.0 / (9.0 * PATCH * PATCH)) + 1.0))
    shaped = jnp.concatenate(
        [spectrum_ref[:, :LANES] * gain, spectrum_ref[:, LANES:] * gain], axis=1
    ).astype(jnp.bfloat16)
    range_back = jnp.dot(shaped, inverse, preferred_element_type=jnp.float32)
    range_back = range_back.astype(jnp.bfloat16)
    window = jnp.concatenate([window] * chunks, axis=1)
    totals = [[None] * (row_patches - 1) for _ in range(2)]
    for row in range(row_patches):
        stacked = []
        for chunk in range(chunks):
            top = (row * chunks + chunk) * PATCH
            block = range_back[top : top + PATCH]
            stacked.append(jnp.concatenate([block[:, :LANES], block[:, LANES:]], axis=0))
        stacked = jnp.concatenate(stacked, axis=1)
        patch_out = jnp.dot(back, stacked, preferred_element_type=jnp.float32) * window
        for part in range(2):
            upper = patch_out[part * PATCH : part * PATCH + HALF]
            lower = patch_out[part * PATCH + HALF : (part + 1) * PATCH]
            if row > 0:
                totals[part][row - 1] = totals[part][row - 1] + upper
            if row < row_patches - 1:
                totals[part][row] = lower
    total = jnp.concatenate([block for part in totals for block in part], axis=0)
    return total[:, :width] + total[:, width + HALF : 2 * width + HALF]


def keep(ref, result):
    lines = ref.shape[1]
    for part in range(2):
        ref[part] = result[part * lines : (part + 1) * lines]


def own_kernel(table_ref, first_ref, inner_ref, second_ref, out_ref, spectrum_ref):
    _, lines, width = out_ref.shape
    row_patches = lines // HALF + 1
    tables = Tables(table_ref, row_patches)
    first = (first_ref, inner_ref)
    total = first_sum(tables, first, first) + second_sum(tables, second_ref, second_ref)
    keep(out_ref, filtered_of(total, tables, spectrum_ref, row_patches, width))


def first_kernel(row_patches, table_ref, first_ref, inner_ref, other_ref, middle_ref, out_ref):
    tables = Tables(table_ref, row_patches)
    out_ref[...] = first_sum(tables, (first_ref, inner_ref), (other_ref, middle_ref))


def other_kernel(match_ref, table_ref, filtered_own_ref, own_ref, *refs):
    out_ref, result_ref, spectrum_ref, sems = refs[-4:]
    match_count, _, _, lines, width = out_ref.shape
    row_patches = lines // HALF + 1
    date = lax.axis_index("date")
    dates = match_ref.shape[1]
    tables = Tables(table_ref, row_patches)

    def copy_of(match, source_ref):
        return pltpu.make_async_copy(source_ref, out_ref.at[match, :, 0], sems.at[match])

    def send(slot, source_ref):
        for match in range(match_count):
            wanted = lax.rem(match_ref[match, date] - date + dates, dates)

            @pl.when(wanted == slot)
            def _():
                copy_of(match, source_ref).start(priority=match % 2)

    send(0, filtered_own_ref)
    for slot in range(1, dates):
        first_ref, other_ref = refs[2 * slot - 2 : 2 * slot]
        total = first_ref[...] + second_sum(tables, own_ref, other_ref)
        result = filtered_of(total, tables, spectrum_ref, row_patches, width)
        keep(result_ref.at[slot - 1], result)
        send(slot, result_ref.at[slot - 1])
    for match in range(match_count):
        copy_of(match, filtered_own_ref).wait()


def all_tables(row_patches):
    forward = fourier_table(1.0, 1.0)
    inverse = fourier_table(-1.0, 1.0 / PATCH)
    back = inverse.reshape(2, PATCH, 2, PATCH).transpose(2, 3, 0, 1).reshape(2 * PATCH, 2 * PATCH)
    window = window_table()[:PATCH, :PATCH]
    splits = []
    for _ in range(3):
        splits.append(window.astype(jnp.bfloat16).astype(np.float32))
        window = window - splits[-1]
    wide = (row_patches + 1) * HALF
    natural = np.arange(wide)
    upper, inner, lower = natural[:REACH], natural[REACH : wide - REACH], natural[wide - REACH :]
    lines = line_table(forward, row_patches).reshape(-1, 2, wide)

    def columns(*orders):
        cut = [lines[:, :, order].reshape(len(lines), -1) for order in orders]
        cut = np.concatenate(cut, axis=1)
        return np.pad(cut, ((0, 0), (0, 4 * PATCH - cut.shape[1])))

    rows = [columns(upper, inner), columns(lower, inner), columns(lower), columns(upper)] + [
        paired(forward),
        paired(inverse),
        np.concatenate([back, ring_table()], axis=1),
        np.concatenate([*splits, np.zeros_like(window)], axis=1),
    ]
    return np.concatenate(rows, axis=0).astype(jnp.bfloat16)


class Tables:
    def __init__(self, ref, row_patches):
        self.ref = ref
        self.size = row_patches * 2 * PATCH

    def first(self):
        inner = self.size // (2 * PATCH) * HALF + HALF - 2 * REACH
        return self.of_side(0)[:, : 2 * (REACH + inner)]

    def second(self):
        return self.of_side(2)[:, : 2 * REACH]

    def of_side(self, block):
        start = jnp.where(is_above(0), block * self.size, (block + 1) * self.size)
        return self.ref[pl.ds(pl.multiple_of(start, self.size), self.size), :]

    def core(self):
        ref, at = self.ref, 4 * self.size
        forward = ref[at : at + 4 * PATCH, :]
        at += 4 * PATCH
        inverse = ref[at : at + 4 * PATCH, :]
        at += 4 * PATCH
        back = ref[at : at + LANES, :LANES]
        ring = ref[at : at + LANES, LANES:]
        at += LANES
        splits = ref[at : at + PATCH, :].astype(jnp.float32)
        window = splits[:, :PATCH] + splits[:, PATCH : 2 * PATCH] + splits[:, 2 * PATCH : 3 * PATCH]
        window = jnp.concatenate([window, window], axis=1)
        window = jnp.concatenate([window, window], axis=0)
        return forward, inverse, back, ring, window


def per_device(image_stack, tap_weights, offsets, matchings):
    _, _, lines, width = image_stack.shape
    match_count = matchings.shape[0]
    other = lax.ppermute(image_stack, "rg", [(0, 1), (1, 0)]).reshape(2, lines, width)
    arguments = (
        image_stack.reshape(2, lines, width),
        tap_weights.reshape(TAPS, lines),
        offsets,
    )
    raw = pl.pallas_call(
        load_kernel,
        out_shape=tuple(pltpu.VMEM(a.shape, a.dtype) for a in arguments),
        in_specs=[HBM] * 3,
        out_specs=(VMEM,) * 3,
        scratch_shapes=[pltpu.SemaphoreType.DMA((3,))],
        compiler_params=PARAMS,
        name="load",
    )(*(pltpu.with_memory_space_constraint(a, pltpu.HBM) for a in arguments))
    raw = (raw[0], other, *raw[1:])
    message = jax.ShapeDtypeStruct((2 * REACH + STEP, width), jnp.bfloat16)
    messages = pl.pallas_call(
        pack_kernel,
        out_shape=(message, message),
        in_specs=[VMEM] * 4,
        out_specs=(VMEM, VMEM),
        compiler_params=PARAMS,
        name="pack",
    )(*raw)
    peers = lax.axis_size("az")

    def swapped(value, start):
        paired_with = {i: i + 1 for i in range(start, peers - 1, 2)}
        paired_with.update({j: i for i, j in paired_with.items()})
        pairs = [
            (2 * i + core, 2 * paired_with[i] + core if i in paired_with else 2 * i + 1 - core)
            for i in range(peers)
            for core in range(2)
        ]
        return lax.ppermute(value, ("az", "rg"), pairs)

    messages = [swapped(messages[turn], turn) for turn in range(2)]
    def piece_of(count):
        return jax.ShapeDtypeStruct((2 * count + STEP, width), jnp.bfloat16)

    inner = pl.pallas_call(
        inner_kernel,
        out_shape=piece_of(lines - 2 * RIM),
        in_specs=[VMEM] * 4,
        out_specs=VMEM,
        compiler_params=PARAMS,
        name="inner",
    )(*raw)
    sides = []
    for turn in range(2):
        call = pl.pallas_call(
            functools.partial(side_kernel, turn),
            out_shape=piece_of(REACH),
            in_specs=[VMEM] * (6 + len(sides)),
            out_specs=VMEM,
            compiler_params=PARAMS,
            name="side_" + "ab"[turn],
        )
        sides.append(call(*raw, messages[turn], inner, *sides))
    own = (sides[0], inner, sides[1])
    dates = lax.axis_size("date")

    def from_date(piece, slot):
        return lax.ppermute(piece, "date", [((i + slot) % dates, i) for i in range(dates)])

    slots = range(1, dates)
    middles = [from_date(inner, slot) for slot in slots]
    firsts = [from_date(sides[0], slot) for slot in slots]
    last = pl.pallas_call(
        pass_kernel,
        out_shape=piece_of(REACH),
        in_specs=[VMEM] * (1 + len(middles)),
        out_specs=VMEM,
        compiler_params=PARAMS,
        name="pass",
    )(sides[1], *middles)
    seconds = [from_date(last, slot) for slot in slots]
    row_patches = lines // HALF + 1
    chunks = (width + width + LANES) // LANES
    tables = jnp.asarray(all_tables(row_patches))
    spectrum = pltpu.VMEM((row_patches * chunks * PATCH, 2 * LANES), jnp.float32)
    filtered_own = pl.pallas_call(
        own_kernel,
        out_shape=jax.ShapeDtypeStruct((2, lines, width), jnp.float32),
        in_specs=[VMEM] * 4,
        out_specs=VMEM,
        scratch_shapes=[spectrum],
        compiler_params=PARAMS,
        name="filter_own",
    )(tables, *own)
    pieces = []
    for first, middle, second in zip(firsts, middles, seconds):
        total = pl.pallas_call(
            functools.partial(first_kernel, row_patches),
            out_shape=jax.ShapeDtypeStruct((row_patches * 2 * PATCH, chunks * LANES), jnp.float32),
            in_specs=[VMEM] * 5,
            out_specs=VMEM,
            compiler_params=PARAMS,
            name="filter_first",
        )(tables, *own[:2], first, middle)
        pieces += [total, second]
    return pl.pallas_call(
        other_kernel,
        out_shape=jax.ShapeDtypeStruct((match_count, 2, 1, lines, width), jnp.float32),
        in_specs=[SMEM] + [VMEM] * (3 + len(pieces)),
        out_specs=HBM,
        scratch_shapes=[
            pltpu.VMEM((dates - 1, 2, lines, width), jnp.float32),
            spectrum,
            pltpu.SemaphoreType.DMA((match_count,)),
        ],
        compiler_params=PARAMS,
        name="filter_other",
    )(matchings, tables, filtered_own, own[2], *pieces)


def solution(mesh):
    placed = (
        P(None, ("parts", "date"), "az", "rg"),
        P(None, ("parts", "date"), "az"),
        P(("parts", "date"), "az"),
        P(),
    )
    return jax.shard_map(
        per_device,
        mesh=mesh,
        in_specs=placed,
        out_specs=P(None, None, ("parts", "date"), "az", "rg"),
        check_vma=False,
    )
```

```python
import functools
import math

import jax
import jax.numpy as jnp
import numpy as np
from jax import lax
from jax.experimental import pallas as pl
from jax.experimental.pallas import tpu as pltpu
from jax.sharding import PartitionSpec as P

TAPS = 8
SHIFT_MAX = 12
PATCH = 64
HALF = PATCH // 2
RIM = SHIFT_MAX + TAPS // 2
REACH = HALF + RIM
LANES = 128
STEP = 16
VMEM_LIMIT = 48 * 1024 * 1024

VMEM = pl.BlockSpec(memory_space=pltpu.VMEM)
SMEM = pl.BlockSpec(memory_space=pltpu.SMEM)
HBM = pl.BlockSpec(memory_space=pltpu.HBM)
PARAMS = pltpu.CompilerParams(vmem_limit_bytes=VMEM_LIMIT)


def fourier_table(sine_sign, table_scale):
    freq_ids = np.arange(PATCH)
    phase_ids = (freq_ids[:, None] * freq_ids[None, :]) % PATCH
    angles = phase_ids * (2.0 * math.pi / PATCH)
    cosine = np.cos(angles) * table_scale
    sine_part = np.sin(angles) * (sine_sign * table_scale)
    top = np.concatenate([cosine, -sine_part], axis=1)
    bottom = np.concatenate([sine_part, cosine], axis=1)
    return np.concatenate([top, bottom], axis=0).astype(np.float32)


def paired(table):
    split = table.reshape(2, PATCH, 2, PATCH)
    wide = np.zeros((2, 2, PATCH, 2, 2, PATCH), np.float32)
    for slot in range(2):
        wide[:, slot, :, :, slot, :] = split
    return wide.reshape(4 * PATCH, 4 * PATCH)


def line_table(forward, row_patches):
    wide_lines = (row_patches + 1) * HALF
    table = np.zeros((row_patches, 2 * PATCH, 2, wide_lines), np.float32)
    transposed = forward.T.reshape(2 * PATCH, 2, PATCH)
    for row in range(row_patches):
        table[row, :, :, row * HALF : row * HALF + PATCH] = transposed
    return table.reshape(row_patches * 2 * PATCH, 2 * wide_lines)


def window_table():
    window = np.sin(math.pi * (np.arange(PATCH) + 0.5) / PATCH) ** 2
    return np.tile(np.outer(window, window), (2, 2)).astype(np.float32)


def ring_table():
    ring = np.zeros((LANES, LANES), np.float32)
    for lane in range(LANES):
        base = lane // PATCH * PATCH
        for step in (-1, 0, 1):
            ring[base + (lane + step) % PATCH, lane] = 1.0
    return ring


def edge_of(other_ref, part, side, lines):
    width = other_ref.shape[2]
    return jnp.where(
        side == 0, other_ref[part, lines, :HALF], other_ref[part, lines, width - HALF :]
    )


def side_by_side(values):
    values = jnp.concatenate(values, axis=0)
    return jnp.concatenate([values[i : i + STEP] for i in range(0, values.shape[0], STEP)], axis=1)


def one_below(block, first, last):
    return jnp.concatenate([block[:, i * HALF : (i + 1) * HALF] for i in range(first, last)], axis=0)


def load_kernel(*refs):
    count = (len(refs) - 1) // 2
    copies = [
        pltpu.make_async_copy(refs[i], refs[count + i], refs[-1].at[i]) for i in range(count)
    ]
    for copy in copies:
        copy.start()
    for copy in copies:
        copy.wait()


def pack_kernel(image_ref, other_ref, taps_ref, offsets_ref, even_ref, odd_ref):
    lines = image_ref.shape[1]
    side = lax.axis_index("rg")
    taps = taps_ref[...]
    taps_high = taps.astype(jnp.bfloat16).astype(jnp.float32)
    taps = jnp.concatenate([taps_high, taps - taps_high], axis=0)
    shifts = jnp.broadcast_to(offsets_ref[...].astype(jnp.float32), taps.shape)

    def write(out_ref, line_start, tap_start):
        rows = slice(line_start, line_start + REACH)
        for part in range(2):
            cut = slice(part * REACH, (part + 1) * REACH)
            out_ref[cut, :] = image_ref[part, rows, :].astype(jnp.bfloat16)
        edges = [edge_of(other_ref, part, side, rows) for part in range(2)]
        cut = slice(tap_start, tap_start + HALF)
        block = side_by_side([*edges, taps[:, cut], shifts[:, cut]])
        out_ref[2 * REACH :, :] = block.astype(jnp.bfloat16)

    parity = lax.rem(lax.axis_index("az"), 2)

    @pl.when(parity == 0)
    def _():
        write(even_ref, lines - REACH, lines - HALF)
        write(odd_ref, 0, 0)

    @pl.when(parity == 1)
    def _():
        write(even_ref, 0, 0)
        write(odd_ref, lines - REACH, lines - HALF)


def is_above(turn):
    return lax.rem(lax.axis_index("az") + turn, 2) == 1


def band(taps, shift, first_line, source):
    count, lines = source.shape
    tap_ids = source - (lax.broadcasted_iota(jnp.int32, (count, lines), 1) + first_line)
    tap_ids = tap_ids - shift + (TAPS // 2 - 1)
    total = jnp.zeros((count, lines), jnp.float32)
    for tap in range(TAPS):
        total = jnp.where(tap_ids == tap, taps[tap : tap + 1, :], total)
    return total


def high_low(value):
    high = value.astype(jnp.bfloat16)
    low = (value - high.astype(jnp.float32)).astype(jnp.bfloat16)
    return jnp.concatenate([high, low], axis=0)


def apply_band(weights, rows):
    over_rows = (((0,), (0,)), ((), ()))
    rows = jnp.concatenate([rows, rows], axis=0)
    return lax.dot_general(high_low(weights), rows, over_rows, preferred_element_type=jnp.float32)


def write_piece(out_ref, parts, width):
    lines = parts[0].shape[0]
    for part, value in enumerate(parts):
        out_ref[part * lines : (part + 1) * lines, :] = value[:, :width].astype(jnp.bfloat16)
    edges = side_by_side([value[:, width:] for value in parts])
    out_ref[2 * lines :, :] = edges.astype(jnp.bfloat16)


def read_piece(ref, first, count):
    lines = (count - STEP) // 2
    middle = first + 2 * lines
    tiles = ref[first:middle, :].astype(jnp.float32)
    edges = one_below(ref[middle : first + count, :].astype(jnp.float32), 0, 2 * lines // STEP)
    return [(v[:lines], v[lines:]) for v in (tiles, edges)]


def inner_kernel(image_ref, other_ref, taps_ref, offsets_ref, out_ref):
    lines = image_ref.shape[1]
    width = image_ref.shape[2]
    side = lax.axis_index("rg")
    source = lax.broadcasted_iota(jnp.int32, (lines, lines), 0)
    weights = band(taps_ref[...], offsets_ref[...], 0, source)
    weights = jnp.concatenate([weights, weights], axis=0)
    for part in range(2):
        edge = edge_of(other_ref, part, side, slice(0, lines))
        rows = high_low(jnp.concatenate([image_ref[part], edge], axis=1))
        out_ref[part] = apply_band(weights, rows)


def side_lines(turn, image_ref, other_ref, taps_ref, offsets_ref, message_ref):
    lines = image_ref.shape[1]
    side = lax.axis_index("rg")
    above = is_above(turn)
    message = message_ref[...]
    block = message[2 * REACH :, :].astype(jnp.float32)
    steps = 2 * REACH // STEP
    rim_edges = one_below(block, 0, steps).astype(jnp.bfloat16)
    rim_taps = one_below(block, steps, steps + 1)
    rim_taps = rim_taps[:TAPS] + rim_taps[TAPS:]
    rim_shift = one_below(block, steps + 1, steps + 2)[:1]

    def per_line(own, rim):
        upper = jnp.concatenate([rim, own[:, :RIM]], axis=1)
        lower = jnp.concatenate([own[:, lines - RIM :], rim], axis=1)
        return jnp.where(above, upper, lower)

    taps = per_line(taps_ref[...], rim_taps)
    shift = per_line(offsets_ref[...].astype(jnp.float32), rim_shift).astype(jnp.int32)
    first_line = jnp.where(above, -HALF, lines - RIM)
    near = 2 * RIM
    first_own = jnp.where(above, 0, lines - near)
    first_rim = jnp.where(above, -REACH, lines)
    source = lax.broadcasted_iota(jnp.int32, (REACH + near, REACH), 0)
    source = jnp.where(source < REACH, source + first_rim, source - REACH + first_own)
    weights = band(taps, shift, first_line, source)
    weights = jnp.concatenate([weights, weights[REACH:]], axis=0)
    parts = []
    for part in range(2):
        upper, lower = slice(0, near), slice(lines - near, lines)
        edge = jnp.where(
            above, edge_of(other_ref, part, side, upper), edge_of(other_ref, part, side, lower)
        )
        own = jnp.where(above, image_ref[part, upper, :], image_ref[part, lower, :])
        own = high_low(jnp.concatenate([own, edge], axis=1))
        cut = slice(part * REACH, (part + 1) * REACH)
        rim = jnp.concatenate([message[cut, :], rim_edges[cut]], axis=1)
        parts.append(apply_band(weights, jnp.concatenate([rim, own], axis=0)))
    return parts


def side_kernel(turn, *refs):
    image_ref, other_ref, taps_ref, offsets_ref, message_ref, inner_ref = refs[:6]
    out_ref = refs[-1]
    width = image_ref.shape[2]
    place = lax.axis_index("az")
    above = is_above(turn)
    alone = jnp.where(above, place == 0, place == lax.axis_size("az") - 1)
    if turn == 1:
        count = refs[6].shape[0]
        out_ref[:count, :] = refs[6][...]
        out_ref = out_ref.at[count:]

    lines = inner_ref.shape[1]
    half = lines // 2 + HALF

    @pl.when(alone)
    def _():
        halves = []
        for part in range(2):
            blank = jnp.zeros((HALF, inner_ref.shape[2]), jnp.float32)
            upper = jnp.concatenate([blank, inner_ref[part, : half - HALF]], axis=0)
            lower = jnp.concatenate([inner_ref[part, lines - half + HALF :], blank], axis=0)
            halves.append(jnp.where(above, upper, lower))
        write_piece(out_ref, halves, width)

    @pl.when(jnp.logical_not(alone))
    def _():
        halves = []
        for part, total in enumerate(side_lines(turn, *refs[:5])):
            near = inner_ref[part, RIM : half - HALF]
            upper = jnp.concatenate([total, near], axis=0)
            near = inner_ref[part, lines - half + HALF : lines - RIM]
            lower = jnp.concatenate([near, total], axis=0)
            halves.append(jnp.where(above, upper, lower))
        write_piece(out_ref, halves, width)


def cross(own_parts, other_parts):
    own_real, own_imag = own_parts
    other_real, other_imag = other_parts
    real = own_real * other_real + own_imag * other_imag
    imag = own_imag * other_real - own_real * other_imag
    return real, imag


def interferogram(own_ref, other_ref, first, count):
    side = lax.axis_index("rg")
    own_tile, own_edge = read_piece(own_ref, first, count)
    other_tile, other_edge = read_piece(other_ref, first, count)
    mid = jnp.concatenate(cross(own_tile, other_tile), axis=0)
    rim = jnp.concatenate(cross(own_edge, other_edge), axis=0)
    before = jnp.where(side == 0, 0.0, rim)
    after = jnp.where(side == 0, rim, 0.0)
    filler = jnp.zeros((mid.shape[0], LANES - 2 * HALF), jnp.float32)
    shifted = jnp.concatenate([before, mid, after, filler], axis=1).astype(jnp.bfloat16)
    return jnp.concatenate([mid.astype(jnp.bfloat16), shifted], axis=1)


def line_sum(tables, own_ref, other_ref):
    count = own_ref.shape[0] // 2
    both = [interferogram(own_ref, other_ref, turn * count, count) for turn in range(2)]
    weights = jnp.concatenate([tables.lines(turn) for turn in range(2)], axis=1)
    both = jnp.concatenate(both, axis=0)
    return jnp.dot(weights, both, preferred_element_type=jnp.float32)


def filtered_of(line_spectra, tables, spectrum_ref, row_patches, width):
    line_spectra = line_spectra.astype(jnp.bfloat16)
    chunks = line_spectra.shape[1] // LANES
    forward, inverse, back, ring, window = tables.core()
    pieces = []
    for row in range(row_patches):
        top = row * 2 * PATCH
        for chunk in range(chunks):
            cut = slice(chunk * LANES, (chunk + 1) * LANES)
            real = line_spectra[top : top + PATCH, cut]
            imag = line_spectra[top + PATCH : top + 2 * PATCH, cut]
            pieces.append(jnp.concatenate([real, imag], axis=1))
    patches = jnp.concatenate(pieces, axis=0)
    spectrum_ref[...] = jnp.dot(patches, forward, preferred_element_type=jnp.float32)
    powers = []
    for block in range(row_patches * chunks):
        rows = slice(block * PATCH, (block + 1) * PATCH)
        real = spectrum_ref[rows, :LANES]
        imag = spectrum_ref[rows, LANES:]
        power = real * real + imag * imag
        power = power + pltpu.roll(power, 1, 0) + pltpu.roll(power, PATCH - 1, 0)
        powers.append(power.astype(jnp.bfloat16))
    smooth = jnp.dot(jnp.concatenate(powers, axis=0), ring, preferred_element_type=jnp.float32)
    gain = lax.rsqrt(lax.rsqrt(smooth * (1.0 / (9.0 * PATCH * PATCH)) + 1.0))
    shaped = jnp.concatenate(
        [spectrum_ref[:, :LANES] * gain, spectrum_ref[:, LANES:] * gain], axis=1
    ).astype(jnp.bfloat16)
    range_back = jnp.dot(shaped, inverse, preferred_element_type=jnp.float32)
    range_back = range_back.astype(jnp.bfloat16)
    window = jnp.concatenate([window] * chunks, axis=1)
    totals = [[None] * (row_patches - 1) for _ in range(2)]
    for row in range(row_patches):
        stacked = []
        for chunk in range(chunks):
            top = (row * chunks + chunk) * PATCH
            block = range_back[top : top + PATCH]
            stacked.append(jnp.concatenate([block[:, :LANES], block[:, LANES:]], axis=0))
        stacked = jnp.concatenate(stacked, axis=1)
        patch_out = jnp.dot(back, stacked, preferred_element_type=jnp.float32) * window
        for part in range(2):
            upper = patch_out[part * PATCH : part * PATCH + HALF]
            lower = patch_out[part * PATCH + HALF : (part + 1) * PATCH]
            if row > 0:
                totals[part][row - 1] = totals[part][row - 1] + upper
            if row < row_patches - 1:
                totals[part][row] = lower
    total = jnp.concatenate([block for part in totals for block in part], axis=0)
    return total[:, :width] + total[:, width + HALF : 2 * width + HALF]


def keep(ref, result):
    lines = ref.shape[1]
    for part in range(2):
        ref[part] = result[part * lines : (part + 1) * lines]


def own_kernel(table_ref, own_ref, out_ref, spectrum_ref):
    _, lines, width = out_ref.shape
    row_patches = lines // HALF + 1
    tables = Tables(table_ref, row_patches)
    total = line_sum(tables, own_ref, own_ref)
    keep(out_ref, filtered_of(total, tables, spectrum_ref, row_patches, width))


def other_kernel(match_ref, table_ref, filtered_own_ref, own_ref, *refs):
    out_ref, result_ref, spectrum_ref, sems = refs[-4:]
    match_count, _, _, lines, width = out_ref.shape
    row_patches = lines // HALF + 1
    date = lax.axis_index("date")
    dates = match_ref.shape[1]
    tables = Tables(table_ref, row_patches)

    def copy_of(match, source_ref):
        return pltpu.make_async_copy(source_ref, out_ref.at[match, :, 0], sems.at[match])

    def send(slot, source_ref):
        for match in range(match_count):
            wanted = lax.rem(match_ref[match, date] - date + dates, dates)

            @pl.when(wanted == slot)
            def _():
                copy_of(match, source_ref).start()

    send(0, filtered_own_ref)
    for slot in range(1, dates):
        total = line_sum(tables, own_ref, refs[slot - 1])
        result = filtered_of(total, tables, spectrum_ref, row_patches, width)
        keep(result_ref.at[slot - 1], result)
        send(slot, result_ref.at[slot - 1])
    for match in range(match_count):
        copy_of(match, filtered_own_ref).wait()


def all_tables(row_patches):
    forward = fourier_table(1.0, 1.0)
    inverse = fourier_table(-1.0, 1.0 / PATCH)
    back = inverse.reshape(2, PATCH, 2, PATCH).transpose(2, 3, 0, 1).reshape(2 * PATCH, 2 * PATCH)
    window = window_table()[:PATCH, :PATCH]
    splits = []
    for _ in range(3):
        splits.append(window.astype(jnp.bfloat16).astype(np.float32))
        window = window - splits[-1]
    half = (row_patches + 1) * HALF // 2
    lines = line_table(forward, row_patches).reshape(-1, 2, 2, half)
    halves = [lines[:, :, at].reshape(-1, 2 * half) for at in range(2)]
    rows = [np.concatenate([value, np.zeros_like(value)], axis=1) for value in halves] + [
        paired(forward),
        paired(inverse),
        np.concatenate([back, ring_table()], axis=1),
        np.concatenate([*splits, np.zeros_like(window)], axis=1),
    ]
    return np.concatenate(rows, axis=0).astype(jnp.bfloat16)


class Tables:
    def __init__(self, ref, row_patches):
        self.ref = ref
        self.size = row_patches * 2 * PATCH

    def lines(self, turn):
        start = pl.multiple_of(jnp.where(is_above(turn), 0, self.size), self.size)
        return self.ref[pl.ds(start, self.size), :LANES]

    def core(self):
        ref, at = self.ref, 2 * self.size
        forward = ref[at : at + 4 * PATCH, :]
        at += 4 * PATCH
        inverse = ref[at : at + 4 * PATCH, :]
        at += 4 * PATCH
        back = ref[at : at + LANES, :LANES]
        ring = ref[at : at + LANES, LANES:]
        at += LANES
        splits = ref[at : at + PATCH, :].astype(jnp.float32)
        window = splits[:, :PATCH] + splits[:, PATCH : 2 * PATCH] + splits[:, 2 * PATCH : 3 * PATCH]
        window = jnp.concatenate([window, window], axis=1)
        window = jnp.concatenate([window, window], axis=0)
        return forward, inverse, back, ring, window


def per_device(image_stack, tap_weights, offsets, matchings):
    _, _, lines, width = image_stack.shape
    match_count = matchings.shape[0]
    other = lax.ppermute(image_stack, "rg", [(0, 1), (1, 0)]).reshape(2, lines, width)
    arguments = (
        image_stack.reshape(2, lines, width),
        tap_weights.reshape(TAPS, lines),
        offsets,
    )
    raw = pl.pallas_call(
        load_kernel,
        out_shape=tuple(pltpu.VMEM(a.shape, a.dtype) for a in arguments),
        in_specs=[HBM] * 3,
        out_specs=(VMEM,) * 3,
        scratch_shapes=[pltpu.SemaphoreType.DMA((3,))],
        compiler_params=PARAMS,
        name="load",
    )(*(pltpu.with_memory_space_constraint(a, pltpu.HBM) for a in arguments))
    raw = (raw[0], other, *raw[1:])
    message = jax.ShapeDtypeStruct((2 * REACH + STEP, width), jnp.bfloat16)
    messages = pl.pallas_call(
        pack_kernel,
        out_shape=(message, message),
        in_specs=[VMEM] * 4,
        out_specs=(VMEM, VMEM),
        compiler_params=PARAMS,
        name="pack",
    )(*raw)
    peers = lax.axis_size("az")

    def swapped(value, start):
        paired_with = {i: i + 1 for i in range(start, peers - 1, 2)}
        paired_with.update({j: i for i, j in paired_with.items()})
        pairs = [
            (2 * i + core, 2 * paired_with[i] + core if i in paired_with else 2 * i + 1 - core)
            for i in range(peers)
            for core in range(2)
        ]
        return lax.ppermute(value, ("az", "rg"), pairs)

    messages = [swapped(messages[turn], turn) for turn in range(2)]
    inner = pl.pallas_call(
        inner_kernel,
        out_shape=jax.ShapeDtypeStruct((2, lines, width + HALF), jnp.float32),
        in_specs=[VMEM] * 4,
        out_specs=VMEM,
        compiler_params=PARAMS,
        name="inner",
    )(*raw)
    pieces = []
    count = 2 * (lines // 2 + HALF) + STEP
    for turn in range(2):
        call = pl.pallas_call(
            functools.partial(side_kernel, turn),
            out_shape=jax.ShapeDtypeStruct(((turn + 1) * count, width), jnp.bfloat16),
            in_specs=[VMEM] * (6 + turn),
            out_specs=VMEM,
            compiler_params=PARAMS,
            name="side_" + "ab"[turn],
        )
        pieces.append(call(*raw, messages[turn], inner, *pieces))
    own = pieces[1]
    dates = lax.axis_size("date")

    def from_date(piece, slot):
        return lax.ppermute(piece, "date", [((i + slot) % dates, i) for i in range(dates)])

    others = [from_date(own, slot) for slot in range(1, dates)]
    row_patches = lines // HALF + 1
    chunks = (width + width + LANES) // LANES
    tables = jnp.asarray(all_tables(row_patches))
    spectrum = pltpu.VMEM((row_patches * chunks * PATCH, 2 * LANES), jnp.float32)
    filtered_own = pl.pallas_call(
        own_kernel,
        out_shape=jax.ShapeDtypeStruct((2, lines, width), jnp.float32),
        in_specs=[VMEM] * 2,
        out_specs=VMEM,
        scratch_shapes=[spectrum],
        compiler_params=PARAMS,
        name="filter_own",
    )(tables, own)
    return pl.pallas_call(
        other_kernel,
        out_shape=jax.ShapeDtypeStruct((match_count, 2, 1, lines, width), jnp.float32),
        in_specs=[SMEM] + [VMEM] * (3 + len(others)),
        out_specs=HBM,
        scratch_shapes=[
            pltpu.VMEM((dates - 1, 2, lines, width), jnp.float32),
            spectrum,
            pltpu.SemaphoreType.DMA((match_count,)),
        ],
        compiler_params=PARAMS,
        name="filter_other",
    )(matchings, tables, filtered_own, own, *others)


def solution(mesh):
    placed = (
        P(None, ("parts", "date"), "az", "rg"),
        P(None, ("parts", "date"), "az"),
        P(("parts", "date"), "az"),
        P(),
    )
    return jax.shard_map(
        per_device,
        mesh=mesh,
        in_specs=placed,
        out_specs=P(None, None, ("parts", "date"), "az", "rg"),
        check_vma=False,
    )
```

```python
import functools
import math

import jax
import jax.numpy as jnp
import numpy as np
from jax import lax
from jax.experimental import pallas as pl
from jax.experimental.pallas import tpu as pltpu
from jax.sharding import PartitionSpec as P

TAPS = 8
SHIFT_MAX = 12
PATCH = 64
HALF = PATCH // 2
RIM = SHIFT_MAX + TAPS // 2
REACH = HALF + RIM
LANES = 128
STEP = 16
VMEM_LIMIT = 48 * 1024 * 1024

VMEM = pl.BlockSpec(memory_space=pltpu.VMEM)
SMEM = pl.BlockSpec(memory_space=pltpu.SMEM)
HBM = pl.BlockSpec(memory_space=pltpu.HBM)
PARAMS = pltpu.CompilerParams(vmem_limit_bytes=VMEM_LIMIT)


def fourier_table(sine_sign, table_scale):
    freq_ids = np.arange(PATCH)
    phase_ids = (freq_ids[:, None] * freq_ids[None, :]) % PATCH
    angles = phase_ids * (2.0 * math.pi / PATCH)
    cosine = np.cos(angles) * table_scale
    sine_part = np.sin(angles) * (sine_sign * table_scale)
    top = np.concatenate([cosine, -sine_part], axis=1)
    bottom = np.concatenate([sine_part, cosine], axis=1)
    return np.concatenate([top, bottom], axis=0).astype(np.float32)


def paired(table):
    split = table.reshape(2, PATCH, 2, PATCH)
    wide = np.zeros((2, 2, PATCH, 2, 2, PATCH), np.float32)
    for slot in range(2):
        wide[:, slot, :, :, slot, :] = split
    return wide.reshape(4 * PATCH, 4 * PATCH)


def line_table(forward, row_patches):
    wide_lines = (row_patches + 1) * HALF
    table = np.zeros((row_patches, 2 * PATCH, 2, wide_lines), np.float32)
    transposed = forward.T.reshape(2 * PATCH, 2, PATCH)
    for row in range(row_patches):
        table[row, :, :, row * HALF : row * HALF + PATCH] = transposed
    return table.reshape(row_patches * 2 * PATCH, 2 * wide_lines)


def window_table():
    window = np.sin(math.pi * (np.arange(PATCH) + 0.5) / PATCH) ** 2
    return np.tile(np.outer(window, window), (2, 2)).astype(np.float32)


def ring_table():
    ring = np.zeros((LANES, LANES), np.float32)
    for lane in range(LANES):
        base = lane // PATCH * PATCH
        for step in (-1, 0, 1):
            ring[base + (lane + step) % PATCH, lane] = 1.0
    return ring


def edge_of(other_ref, part, side, lines):
    width = other_ref.shape[2]
    return jnp.where(
        side == 0, other_ref[part, lines, :HALF], other_ref[part, lines, width - HALF :]
    )


def side_by_side(values):
    values = jnp.concatenate(values, axis=0)
    return jnp.concatenate([values[i : i + STEP] for i in range(0, values.shape[0], STEP)], axis=1)


def one_below(block, first, last):
    return jnp.concatenate([block[:, i * HALF : (i + 1) * HALF] for i in range(first, last)], axis=0)


def load_kernel(*refs):
    count = (len(refs) - 1) // 2
    copies = [
        pltpu.make_async_copy(refs[i], refs[count + i], refs[-1].at[i]) for i in range(count)
    ]
    for copy in copies:
        copy.start()
    for copy in copies:
        copy.wait()


def pack_kernel(image_ref, other_ref, taps_ref, offsets_ref, even_ref, odd_ref):
    lines = image_ref.shape[1]
    side = lax.axis_index("rg")
    taps = taps_ref[...]
    taps_high = taps.astype(jnp.bfloat16).astype(jnp.float32)
    taps = jnp.concatenate([taps_high, taps - taps_high], axis=0)
    shifts = jnp.broadcast_to(offsets_ref[...].astype(jnp.float32), taps.shape)

    def write(out_ref, line_start, tap_start):
        rows = slice(line_start, line_start + REACH)
        for part in range(2):
            cut = slice(part * REACH, (part + 1) * REACH)
            out_ref[cut, :] = image_ref[part, rows, :].astype(jnp.bfloat16)
        edges = [edge_of(other_ref, part, side, rows) for part in range(2)]
        cut = slice(tap_start, tap_start + HALF)
        block = side_by_side([*edges, taps[:, cut], shifts[:, cut]])
        out_ref[2 * REACH :, :] = block.astype(jnp.bfloat16)

    parity = lax.rem(lax.axis_index("az"), 2)

    @pl.when(parity == 0)
    def _():
        write(even_ref, lines - REACH, lines - HALF)
        write(odd_ref, 0, 0)

    @pl.when(parity == 1)
    def _():
        write(even_ref, 0, 0)
        write(odd_ref, lines - REACH, lines - HALF)


def is_above(turn):
    return lax.rem(lax.axis_index("az") + turn, 2) == 1


def band(taps, shift, first_line, source):
    count, lines = source.shape
    tap_ids = source - (lax.broadcasted_iota(jnp.int32, (count, lines), 1) + first_line)
    tap_ids = tap_ids - shift + (TAPS // 2 - 1)
    total = jnp.zeros((count, lines), jnp.float32)
    for tap in range(TAPS):
        total = jnp.where(tap_ids == tap, taps[tap : tap + 1, :], total)
    return total


def high_low(value):
    high = value.astype(jnp.bfloat16)
    low = (value - high.astype(jnp.float32)).astype(jnp.bfloat16)
    return jnp.concatenate([high, low], axis=0)


def apply_band(weights, rows):
    over_rows = (((0,), (0,)), ((), ()))
    rows = jnp.concatenate([rows, rows], axis=0)
    return lax.dot_general(high_low(weights), rows, over_rows, preferred_element_type=jnp.float32)


def write_piece(out_ref, parts, width):
    lines = parts[0].shape[0]
    for part, value in enumerate(parts):
        out_ref[part * lines : (part + 1) * lines, :] = value[:, :width].astype(jnp.bfloat16)
    edges = side_by_side([value[:, width:] for value in parts])
    out_ref[2 * lines :, :] = edges.astype(jnp.bfloat16)


def read_piece(ref, first, count):
    lines = (count - STEP) // 2
    middle = first + 2 * lines
    tiles = ref[first:middle, :].astype(jnp.float32)
    edges = one_below(ref[middle : first + count, :].astype(jnp.float32), 0, 2 * lines // STEP)
    return [(v[:lines], v[lines:]) for v in (tiles, edges)]


def inner_kernel(image_ref, other_ref, taps_ref, offsets_ref, out_ref):
    lines = image_ref.shape[1]
    width = image_ref.shape[2]
    side = lax.axis_index("rg")
    source = lax.broadcasted_iota(jnp.int32, (lines, lines), 0)
    weights = band(taps_ref[...], offsets_ref[...], 0, source)
    weights = jnp.concatenate([weights, weights], axis=0)
    for part in range(2):
        edge = edge_of(other_ref, part, side, slice(0, lines))
        rows = high_low(jnp.concatenate([image_ref[part], edge], axis=1))
        out_ref[part] = apply_band(weights, rows)


def side_lines(turn, image_ref, other_ref, taps_ref, offsets_ref, message_ref):
    lines = image_ref.shape[1]
    side = lax.axis_index("rg")
    above = is_above(turn)
    message = message_ref[...]
    block = message[2 * REACH :, :].astype(jnp.float32)
    steps = 2 * REACH // STEP
    rim_edges = one_below(block, 0, steps).astype(jnp.bfloat16)
    rim_taps = one_below(block, steps, steps + 1)
    rim_taps = rim_taps[:TAPS] + rim_taps[TAPS:]
    rim_shift = one_below(block, steps + 1, steps + 2)[:1]

    def per_line(own, rim):
        upper = jnp.concatenate([rim, own[:, :RIM]], axis=1)
        lower = jnp.concatenate([own[:, lines - RIM :], rim], axis=1)
        return jnp.where(above, upper, lower)

    taps = per_line(taps_ref[...], rim_taps)
    shift = per_line(offsets_ref[...].astype(jnp.float32), rim_shift).astype(jnp.int32)
    first_line = jnp.where(above, -HALF, lines - RIM)
    near = 2 * RIM
    first_own = jnp.where(above, 0, lines - near)
    first_rim = jnp.where(above, -REACH, lines)
    source = lax.broadcasted_iota(jnp.int32, (REACH + near, REACH), 0)
    source = jnp.where(source < REACH, source + first_rim, source - REACH + first_own)
    weights = band(taps, shift, first_line, source)
    weights = jnp.concatenate([weights, weights[REACH:]], axis=0)
    parts = []
    for part in range(2):
        upper, lower = slice(0, near), slice(lines - near, lines)
        edge = jnp.where(
            above, edge_of(other_ref, part, side, upper), edge_of(other_ref, part, side, lower)
        )
        own = jnp.where(above, image_ref[part, upper, :], image_ref[part, lower, :])
        own = high_low(jnp.concatenate([own, edge], axis=1))
        cut = slice(part * REACH, (part + 1) * REACH)
        rim = jnp.concatenate([message[cut, :], rim_edges[cut]], axis=1)
        parts.append(apply_band(weights, jnp.concatenate([rim, own], axis=0)))
    return parts


def side_kernel(turn, *refs):
    image_ref, other_ref, taps_ref, offsets_ref, message_ref, inner_ref = refs[:6]
    out_ref = refs[-1]
    width = image_ref.shape[2]
    place = lax.axis_index("az")
    above = is_above(turn)
    alone = jnp.where(above, place == 0, place == lax.axis_size("az") - 1)
    if turn == 1:
        count = refs[6].shape[0]
        out_ref[:count, :] = refs[6][...]
        out_ref = out_ref.at[count:]

    lines = inner_ref.shape[1]
    half = lines // 2 + HALF

    @pl.when(alone)
    def _():
        halves = []
        for part in range(2):
            blank = jnp.zeros((HALF, inner_ref.shape[2]), jnp.float32)
            upper = jnp.concatenate([blank, inner_ref[part, : half - HALF]], axis=0)
            lower = jnp.concatenate([inner_ref[part, lines - half + HALF :], blank], axis=0)
            halves.append(jnp.where(above, upper, lower))
        write_piece(out_ref, halves, width)

    @pl.when(jnp.logical_not(alone))
    def _():
        halves = []
        for part, total in enumerate(side_lines(turn, *refs[:5])):
            near = inner_ref[part, RIM : half - HALF]
            upper = jnp.concatenate([total, near], axis=0)
            near = inner_ref[part, lines - half + HALF : lines - RIM]
            lower = jnp.concatenate([near, total], axis=0)
            halves.append(jnp.where(above, upper, lower))
        write_piece(out_ref, halves, width)


def cross(own_parts, other_parts):
    own_real, own_imag = own_parts
    other_real, other_imag = other_parts
    real = own_real * other_real + own_imag * other_imag
    imag = own_imag * other_real - own_real * other_imag
    return real, imag


def interferogram(own_ref, other_ref, first, count):
    side = lax.axis_index("rg")
    own_tile, own_edge = read_piece(own_ref, first, count)
    other_tile, other_edge = read_piece(other_ref, first, count)
    mid = jnp.concatenate(cross(own_tile, other_tile), axis=0)
    rim = jnp.concatenate(cross(own_edge, other_edge), axis=0)
    before = jnp.where(side == 0, 0.0, rim)
    after = jnp.where(side == 0, rim, 0.0)
    filler = jnp.zeros((mid.shape[0], LANES - 2 * HALF), jnp.float32)
    shifted = jnp.concatenate([before, mid, after, filler], axis=1).astype(jnp.bfloat16)
    return jnp.concatenate([mid.astype(jnp.bfloat16), shifted], axis=1)


def line_sum(tables, own_ref, other_ref):
    count = own_ref.shape[0] // 2
    both = [interferogram(own_ref, other_ref, turn * count, count) for turn in range(2)]
    weights = jnp.concatenate([tables.lines(turn) for turn in range(2)], axis=1)
    both = jnp.concatenate(both, axis=0)
    return jnp.dot(weights, both, preferred_element_type=jnp.float32)


def filtered_of(line_spectra, tables, spectrum_ref, row_patches, width):
    line_spectra = line_spectra.astype(jnp.bfloat16)
    chunks = line_spectra.shape[1] // LANES
    forward, inverse, back, ring, window = tables.core()
    step = chunks * PATCH
    spans = [slice(row * step, (row + 1) * step) for row in range(row_patches)]
    for row, span in enumerate(spans):
        top = row * 2 * PATCH
        pieces = []
        for chunk in range(chunks):
            cut = slice(chunk * LANES, (chunk + 1) * LANES)
            real = line_spectra[top : top + PATCH, cut]
            imag = line_spectra[top + PATCH : top + 2 * PATCH, cut]
            pieces.append(jnp.concatenate([real, imag], axis=1))
        patches = jnp.concatenate(pieces, axis=0)
        spectrum_ref[span, :] = jnp.dot(patches, forward, preferred_element_type=jnp.float32)
    smooths = []
    for span in spans:
        powers = []
        for start in range(span.start, span.stop, PATCH):
            real = spectrum_ref[start : start + PATCH, :LANES]
            imag = spectrum_ref[start : start + PATCH, LANES:]
            power = real * real + imag * imag
            power = power + pltpu.roll(power, 1, 0) + pltpu.roll(power, PATCH - 1, 0)
            powers.append(power.astype(jnp.bfloat16))
        powers = jnp.concatenate(powers, axis=0)
        smooths.append(jnp.dot(powers, ring, preferred_element_type=jnp.float32))
    range_backs = []
    for span, smooth in zip(spans, smooths):
        gain = lax.rsqrt(lax.rsqrt(smooth * (1.0 / (9.0 * PATCH * PATCH)) + 1.0))
        shaped = jnp.concatenate(
            [spectrum_ref[span, :LANES] * gain, spectrum_ref[span, LANES:] * gain], axis=1
        ).astype(jnp.bfloat16)
        range_back = jnp.dot(shaped, inverse, preferred_element_type=jnp.float32)
        range_backs.append(range_back.astype(jnp.bfloat16))
    window = jnp.concatenate([window] * chunks, axis=1)
    totals = [[None] * (row_patches - 1) for _ in range(2)]
    for row in range(row_patches):
        stacked = []
        for chunk in range(chunks):
            block = range_backs[row][chunk * PATCH : (chunk + 1) * PATCH]
            stacked.append(jnp.concatenate([block[:, :LANES], block[:, LANES:]], axis=0))
        stacked = jnp.concatenate(stacked, axis=1)
        patch_out = jnp.dot(back, stacked, preferred_element_type=jnp.float32) * window
        for part in range(2):
            upper = patch_out[part * PATCH : part * PATCH + HALF]
            lower = patch_out[part * PATCH + HALF : (part + 1) * PATCH]
            if row > 0:
                totals[part][row - 1] = totals[part][row - 1] + upper
            if row < row_patches - 1:
                totals[part][row] = lower
    total = jnp.concatenate([block for part in totals for block in part], axis=0)
    return total[:, :width] + total[:, width + HALF : 2 * width + HALF]


def keep(ref, result):
    lines = ref.shape[1]
    for part in range(2):
        ref[part] = result[part * lines : (part + 1) * lines]


def own_kernel(table_ref, own_ref, out_ref, spectrum_ref):
    _, lines, width = out_ref.shape
    row_patches = lines // HALF + 1
    tables = Tables(table_ref, row_patches)
    total = line_sum(tables, own_ref, own_ref)
    keep(out_ref, filtered_of(total, tables, spectrum_ref, row_patches, width))


def other_kernel(match_ref, table_ref, filtered_own_ref, own_ref, *refs):
    out_ref, result_ref, spectrum_ref, sems = refs[-4:]
    match_count, _, _, lines, width = out_ref.shape
    row_patches = lines // HALF + 1
    date = lax.axis_index("date")
    dates = match_ref.shape[1]
    tables = Tables(table_ref, row_patches)

    def copy_of(match, source_ref):
        return pltpu.make_async_copy(source_ref, out_ref.at[match, :, 0], sems.at[match])

    def send(slot, source_ref):
        for match in range(match_count):
            wanted = lax.rem(match_ref[match, date] - date + dates, dates)

            @pl.when(wanted == slot)
            def _():
                copy_of(match, source_ref).start()

    send(0, filtered_own_ref)
    for slot in range(1, dates):
        total = line_sum(tables, own_ref, refs[slot - 1])
        result = filtered_of(total, tables, spectrum_ref, row_patches, width)
        keep(result_ref.at[slot - 1], result)
        send(slot, result_ref.at[slot - 1])
    for match in range(match_count):
        copy_of(match, filtered_own_ref).wait()


def all_tables(row_patches):
    forward = fourier_table(1.0, 1.0)
    inverse = fourier_table(-1.0, 1.0 / PATCH)
    back = inverse.reshape(2, PATCH, 2, PATCH).transpose(2, 3, 0, 1).reshape(2 * PATCH, 2 * PATCH)
    window = window_table()[:PATCH, :PATCH]
    splits = []
    for _ in range(3):
        splits.append(window.astype(jnp.bfloat16).astype(np.float32))
        window = window - splits[-1]
    half = (row_patches + 1) * HALF // 2
    lines = line_table(forward, row_patches).reshape(-1, 2, 2, half)
    halves = [lines[:, :, at].reshape(-1, 2 * half) for at in range(2)]
    rows = [np.concatenate([value, np.zeros_like(value)], axis=1) for value in halves] + [
        paired(forward),
        paired(inverse),
        np.concatenate([back, ring_table()], axis=1),
        np.concatenate([*splits, np.zeros_like(window)], axis=1),
    ]
    return np.concatenate(rows, axis=0).astype(jnp.bfloat16)


class Tables:
    def __init__(self, ref, row_patches):
        self.ref = ref
        self.size = row_patches * 2 * PATCH

    def lines(self, turn):
        start = pl.multiple_of(jnp.where(is_above(turn), 0, self.size), self.size)
        return self.ref[pl.ds(start, self.size), :LANES]

    def core(self):
        ref, at = self.ref, 2 * self.size
        forward = ref[at : at + 4 * PATCH, :]
        at += 4 * PATCH
        inverse = ref[at : at + 4 * PATCH, :]
        at += 4 * PATCH
        back = ref[at : at + LANES, :LANES]
        ring = ref[at : at + LANES, LANES:]
        at += LANES
        splits = ref[at : at + PATCH, :].astype(jnp.float32)
        window = splits[:, :PATCH] + splits[:, PATCH : 2 * PATCH] + splits[:, 2 * PATCH : 3 * PATCH]
        window = jnp.concatenate([window, window], axis=1)
        window = jnp.concatenate([window, window], axis=0)
        return forward, inverse, back, ring, window


def per_device(image_stack, tap_weights, offsets, matchings):
    _, _, lines, width = image_stack.shape
    match_count = matchings.shape[0]
    other = lax.ppermute(image_stack, "rg", [(0, 1), (1, 0)]).reshape(2, lines, width)
    arguments = (
        image_stack.reshape(2, lines, width),
        tap_weights.reshape(TAPS, lines),
        offsets,
    )
    raw = pl.pallas_call(
        load_kernel,
        out_shape=tuple(pltpu.VMEM(a.shape, a.dtype) for a in arguments),
        in_specs=[HBM] * 3,
        out_specs=(VMEM,) * 3,
        scratch_shapes=[pltpu.SemaphoreType.DMA((3,))],
        compiler_params=PARAMS,
        name="load",
    )(*(pltpu.with_memory_space_constraint(a, pltpu.HBM) for a in arguments))
    raw = (raw[0], other, *raw[1:])
    message = jax.ShapeDtypeStruct((2 * REACH + STEP, width), jnp.bfloat16)
    messages = pl.pallas_call(
        pack_kernel,
        out_shape=(message, message),
        in_specs=[VMEM] * 4,
        out_specs=(VMEM, VMEM),
        compiler_params=PARAMS,
        name="pack",
    )(*raw)
    peers = lax.axis_size("az")

    def swapped(value, start):
        paired_with = {i: i + 1 for i in range(start, peers - 1, 2)}
        paired_with.update({j: i for i, j in paired_with.items()})
        pairs = [
            (2 * i + core, 2 * paired_with[i] + core if i in paired_with else 2 * i + 1 - core)
            for i in range(peers)
            for core in range(2)
        ]
        return lax.ppermute(value, ("az", "rg"), pairs)

    messages = [swapped(messages[turn], turn) for turn in range(2)]
    inner = pl.pallas_call(
        inner_kernel,
        out_shape=jax.ShapeDtypeStruct((2, lines, width + HALF), jnp.float32),
        in_specs=[VMEM] * 4,
        out_specs=VMEM,
        compiler_params=PARAMS,
        name="inner",
    )(*raw)
    pieces = []
    count = 2 * (lines // 2 + HALF) + STEP
    for turn in range(2):
        call = pl.pallas_call(
            functools.partial(side_kernel, turn),
            out_shape=jax.ShapeDtypeStruct(((turn + 1) * count, width), jnp.bfloat16),
            in_specs=[VMEM] * (6 + turn),
            out_specs=VMEM,
            compiler_params=PARAMS,
            name="side_" + "ab"[turn],
        )
        pieces.append(call(*raw, messages[turn], inner, *pieces))
    own = pieces[1]
    dates = lax.axis_size("date")

    def from_date(piece, slot):
        return lax.ppermute(piece, "date", [((i + slot) % dates, i) for i in range(dates)])

    others = [from_date(own, slot) for slot in range(1, dates)]
    row_patches = lines // HALF + 1
    chunks = (width + width + LANES) // LANES
    tables = jnp.asarray(all_tables(row_patches))
    spectrum = pltpu.VMEM((row_patches * chunks * PATCH, 2 * LANES), jnp.float32)
    filtered_own = pl.pallas_call(
        own_kernel,
        out_shape=jax.ShapeDtypeStruct((2, lines, width), jnp.float32),
        in_specs=[VMEM] * 2,
        out_specs=VMEM,
        scratch_shapes=[spectrum],
        compiler_params=PARAMS,
        name="filter_own",
    )(tables, own)
    return pl.pallas_call(
        other_kernel,
        out_shape=jax.ShapeDtypeStruct((match_count, 2, 1, lines, width), jnp.float32),
        in_specs=[SMEM] + [VMEM] * (3 + len(others)),
        out_specs=HBM,
        scratch_shapes=[
            pltpu.VMEM((dates - 1, 2, lines, width), jnp.float32),
            spectrum,
            pltpu.SemaphoreType.DMA((match_count,)),
        ],
        compiler_params=PARAMS,
        name="filter_other",
    )(matchings, tables, filtered_own, own, *others)


def solution(mesh):
    placed = (
        P(None, ("parts", "date"), "az", "rg"),
        P(None, ("parts", "date"), "az"),
        P(("parts", "date"), "az"),
        P(),
    )
    return jax.shard_map(
        per_device,
        mesh=mesh,
        in_specs=placed,
        out_specs=P(None, None, ("parts", "date"), "az", "rg"),
        check_vma=False,
    )
```

```python
import functools
import math

import jax
import jax.numpy as jnp
import numpy as np
from jax import lax
from jax.experimental import pallas as pl
from jax.experimental.pallas import tpu as pltpu
from jax.sharding import PartitionSpec as P

TAPS = 8
SHIFT_MAX = 12
PATCH = 64
HALF = PATCH // 2
RIM = SHIFT_MAX + TAPS // 2
REACH = HALF + RIM
LANES = 128
STEP = 16
VMEM_LIMIT = 48 * 1024 * 1024

VMEM = pl.BlockSpec(memory_space=pltpu.VMEM)
SMEM = pl.BlockSpec(memory_space=pltpu.SMEM)
HBM = pl.BlockSpec(memory_space=pltpu.HBM)
PARAMS = pltpu.CompilerParams(vmem_limit_bytes=VMEM_LIMIT)


def fourier_table(sine_sign, table_scale):
    freq_ids = np.arange(PATCH)
    phase_ids = (freq_ids[:, None] * freq_ids[None, :]) % PATCH
    angles = phase_ids * (2.0 * math.pi / PATCH)
    cosine = np.cos(angles) * table_scale
    sine_part = np.sin(angles) * (sine_sign * table_scale)
    top = np.concatenate([cosine, -sine_part], axis=1)
    bottom = np.concatenate([sine_part, cosine], axis=1)
    return np.concatenate([top, bottom], axis=0).astype(np.float32)


def paired(table):
    split = table.reshape(2, PATCH, 2, PATCH)
    wide = np.zeros((2, 2, PATCH, 2, 2, PATCH), np.float32)
    for slot in range(2):
        wide[:, slot, :, :, slot, :] = split
    return wide.reshape(4 * PATCH, 4 * PATCH)


def line_table(forward, row_patches):
    wide_lines = (row_patches + 1) * HALF
    table = np.zeros((row_patches, 2 * PATCH, 2, wide_lines), np.float32)
    transposed = forward.T.reshape(2 * PATCH, 2, PATCH)
    for row in range(row_patches):
        table[row, :, :, row * HALF : row * HALF + PATCH] = transposed
    return table.reshape(row_patches * 2 * PATCH, 2 * wide_lines)


def window_table():
    window = np.sin(math.pi * (np.arange(PATCH) + 0.5) / PATCH) ** 2
    return np.tile(np.outer(window, window), (2, 2)).astype(np.float32)


def ring_table():
    ring = np.zeros((LANES, LANES), np.float32)
    for lane in range(LANES):
        base = lane // PATCH * PATCH
        for step in (-1, 0, 1):
            ring[base + (lane + step) % PATCH, lane] = 1.0
    return ring


def edge_of(other_ref, part, side, lines):
    width = other_ref.shape[2]
    return jnp.where(
        side == 0, other_ref[part, lines, :HALF], other_ref[part, lines, width - HALF :]
    )


def side_by_side(values):
    values = jnp.concatenate(values, axis=0)
    return jnp.concatenate([values[i : i + STEP] for i in range(0, values.shape[0], STEP)], axis=1)


def one_below(block, first, last):
    return jnp.concatenate([block[:, i * HALF : (i + 1) * HALF] for i in range(first, last)], axis=0)


def load_kernel(*refs):
    count = (len(refs) - 1) // 2
    copies = [
        pltpu.make_async_copy(refs[i], refs[count + i], refs[-1].at[i]) for i in range(count)
    ]
    for copy in copies:
        copy.start()
    for copy in copies:
        copy.wait()


def pack_kernel(image_ref, other_ref, taps_ref, offsets_ref, even_ref, odd_ref):
    lines = image_ref.shape[1]
    side = lax.axis_index("rg")
    taps = taps_ref[...]
    taps_high = taps.astype(jnp.bfloat16).astype(jnp.float32)
    taps = jnp.concatenate([taps_high, taps - taps_high], axis=0)
    shifts = jnp.broadcast_to(offsets_ref[...].astype(jnp.float32), taps.shape)

    def write(out_ref, line_start, tap_start):
        rows = slice(line_start, line_start + REACH)
        for part in range(2):
            cut = slice(part * REACH, (part + 1) * REACH)
            out_ref[cut, :] = image_ref[part, rows, :].astype(jnp.bfloat16)
        edges = [edge_of(other_ref, part, side, rows) for part in range(2)]
        cut = slice(tap_start, tap_start + HALF)
        block = side_by_side([*edges, taps[:, cut], shifts[:, cut]])
        out_ref[2 * REACH :, :] = block.astype(jnp.bfloat16)

    parity = lax.rem(lax.axis_index("az"), 2)

    @pl.when(parity == 0)
    def _():
        write(even_ref, lines - REACH, lines - HALF)
        write(odd_ref, 0, 0)

    @pl.when(parity == 1)
    def _():
        write(even_ref, 0, 0)
        write(odd_ref, lines - REACH, lines - HALF)


def is_above(turn):
    return lax.rem(lax.axis_index("az") + turn, 2) == 1


def band(taps, shift, first_line, source):
    count, lines = source.shape
    tap_ids = source - (lax.broadcasted_iota(jnp.int32, (count, lines), 1) + first_line)
    tap_ids = tap_ids - shift + (TAPS // 2 - 1)
    total = jnp.zeros((count, lines), jnp.float32)
    for tap in range(TAPS):
        total = jnp.where(tap_ids == tap, taps[tap : tap + 1, :], total)
    return total


def high_low(value):
    high = value.astype(jnp.bfloat16)
    low = (value - high.astype(jnp.float32)).astype(jnp.bfloat16)
    return jnp.concatenate([high, low], axis=0)


def apply_band(weights, rows):
    over_rows = (((0,), (0,)), ((), ()))
    rows = jnp.concatenate([rows, rows], axis=0)
    return lax.dot_general(high_low(weights), rows, over_rows, preferred_element_type=jnp.float32)


def write_piece(out_ref, parts, width):
    lines = parts[0].shape[0]
    for part, value in enumerate(parts):
        out_ref[part * lines : (part + 1) * lines, :] = value[:, :width].astype(jnp.bfloat16)
    edges = side_by_side([value[:, width:] for value in parts])
    out_ref[2 * lines :, :] = edges.astype(jnp.bfloat16)


def read_piece(ref, first, count):
    lines = (count - STEP) // 2
    middle = first + 2 * lines
    tiles = ref[first:middle, :].astype(jnp.float32)
    edges = one_below(ref[middle : first + count, :].astype(jnp.float32), 0, 2 * lines // STEP)
    return [(v[:lines], v[lines:]) for v in (tiles, edges)]


def inner_kernel(image_ref, other_ref, taps_ref, offsets_ref, out_ref):
    lines = image_ref.shape[1]
    width = image_ref.shape[2]
    side = lax.axis_index("rg")
    source = lax.broadcasted_iota(jnp.int32, (lines, lines), 0)
    weights = band(taps_ref[...], offsets_ref[...], 0, source)
    weights = jnp.concatenate([weights, weights], axis=0)
    for part in range(2):
        edge = edge_of(other_ref, part, side, slice(0, lines))
        rows = high_low(jnp.concatenate([image_ref[part], edge], axis=1))
        out_ref[part] = apply_band(weights, rows)


def side_lines(turn, image_ref, other_ref, taps_ref, offsets_ref, message_ref):
    lines = image_ref.shape[1]
    side = lax.axis_index("rg")
    above = is_above(turn)
    message = message_ref[...]
    block = message[2 * REACH :, :].astype(jnp.float32)
    steps = 2 * REACH // STEP
    rim_edges = one_below(block, 0, steps).astype(jnp.bfloat16)
    rim_taps = one_below(block, steps, steps + 1)
    rim_taps = rim_taps[:TAPS] + rim_taps[TAPS:]
    rim_shift = one_below(block, steps + 1, steps + 2)[:1]

    def per_line(own, rim):
        upper = jnp.concatenate([rim, own[:, :RIM]], axis=1)
        lower = jnp.concatenate([own[:, lines - RIM :], rim], axis=1)
        return jnp.where(above, upper, lower)

    taps = per_line(taps_ref[...], rim_taps)
    shift = per_line(offsets_ref[...].astype(jnp.float32), rim_shift).astype(jnp.int32)
    first_line = jnp.where(above, -HALF, lines - RIM)
    near = 2 * RIM
    first_own = jnp.where(above, 0, lines - near)
    first_rim = jnp.where(above, -REACH, lines)
    source = lax.broadcasted_iota(jnp.int32, (REACH + near, REACH), 0)
    source = jnp.where(source < REACH, source + first_rim, source - REACH + first_own)
    weights = band(taps, shift, first_line, source)
    weights = jnp.concatenate([weights, weights[REACH:]], axis=0)
    parts = []
    for part in range(2):
        upper, lower = slice(0, near), slice(lines - near, lines)
        edge = jnp.where(
            above, edge_of(other_ref, part, side, upper), edge_of(other_ref, part, side, lower)
        )
        own = jnp.where(above, image_ref[part, upper, :], image_ref[part, lower, :])
        own = high_low(jnp.concatenate([own, edge], axis=1))
        cut = slice(part * REACH, (part + 1) * REACH)
        rim = jnp.concatenate([message[cut, :], rim_edges[cut]], axis=1)
        parts.append(apply_band(weights, jnp.concatenate([rim, own], axis=0)))
    return parts


def side_kernel(turn, *refs):
    image_ref, other_ref, taps_ref, offsets_ref, message_ref, inner_ref = refs[:6]
    out_ref = refs[-1]
    width = image_ref.shape[2]
    place = lax.axis_index("az")
    above = is_above(turn)
    alone = jnp.where(above, place == 0, place == lax.axis_size("az") - 1)
    if turn == 1:
        count = refs[6].shape[0]
        out_ref[:count, :] = refs[6][...]
        out_ref = out_ref.at[count:]

    lines = inner_ref.shape[1]
    half = lines // 2 + HALF

    @pl.when(alone)
    def _():
        halves = []
        for part in range(2):
            blank = jnp.zeros((HALF, inner_ref.shape[2]), jnp.float32)
            upper = jnp.concatenate([blank, inner_ref[part, : half - HALF]], axis=0)
            lower = jnp.concatenate([inner_ref[part, lines - half + HALF :], blank], axis=0)
            halves.append(jnp.where(above, upper, lower))
        write_piece(out_ref, halves, width)

    @pl.when(jnp.logical_not(alone))
    def _():
        halves = []
        for part, total in enumerate(side_lines(turn, *refs[:5])):
            near = inner_ref[part, RIM : half - HALF]
            upper = jnp.concatenate([total, near], axis=0)
            near = inner_ref[part, lines - half + HALF : lines - RIM]
            lower = jnp.concatenate([near, total], axis=0)
            halves.append(jnp.where(above, upper, lower))
        write_piece(out_ref, halves, width)


def cross(own_parts, other_parts):
    own_real, own_imag = own_parts
    other_real, other_imag = other_parts
    real = own_real * other_real + own_imag * other_imag
    imag = own_imag * other_real - own_real * other_imag
    return real, imag


def both_halves(ref):
    count = ref.shape[0] // 2
    return [read_piece(ref, turn * count, count) for turn in range(2)]


def interferogram(own, other):
    side = lax.axis_index("rg")
    own_tile, own_edge = own
    other_tile, other_edge = other
    mid = jnp.concatenate(cross(own_tile, other_tile), axis=0)
    rim = jnp.concatenate(cross(own_edge, other_edge), axis=0)
    before = jnp.where(side == 0, 0.0, rim)
    after = jnp.where(side == 0, rim, 0.0)
    filler = jnp.zeros((mid.shape[0], LANES - 2 * HALF), jnp.float32)
    shifted = jnp.concatenate([before, mid, after, filler], axis=1).astype(jnp.bfloat16)
    return jnp.concatenate([mid.astype(jnp.bfloat16), shifted], axis=1)


def line_sum(tables, own, other):
    both = [interferogram(*halves) for halves in zip(own, other)]
    weights = jnp.concatenate([tables.lines(turn) for turn in range(2)], axis=1)
    both = jnp.concatenate(both, axis=0)
    return jnp.dot(weights, both, preferred_element_type=jnp.float32)


def filtered_of(line_spectra, tables, spectrum_ref, row_patches, width):
    line_spectra = line_spectra.astype(jnp.bfloat16)
    chunks = line_spectra.shape[1] // LANES
    forward, inverse, back, ring, window = tables.core()
    step = chunks * PATCH
    spans = [slice(row * step, (row + 1) * step) for row in range(row_patches)]
    for row, span in enumerate(spans):
        top = row * 2 * PATCH
        pieces = []
        for chunk in range(chunks):
            cut = slice(chunk * LANES, (chunk + 1) * LANES)
            real = line_spectra[top : top + PATCH, cut]
            imag = line_spectra[top + PATCH : top + 2 * PATCH, cut]
            pieces.append(jnp.concatenate([real, imag], axis=1))
        patches = jnp.concatenate(pieces, axis=0)
        spectrum_ref[span, :] = jnp.dot(patches, forward, preferred_element_type=jnp.float32)
    smooths = []
    for span in spans:
        powers = []
        for start in range(span.start, span.stop, PATCH):
            real = spectrum_ref[start : start + PATCH, :LANES]
            imag = spectrum_ref[start : start + PATCH, LANES:]
            power = real * real + imag * imag
            power = power + pltpu.roll(power, 1, 0) + pltpu.roll(power, PATCH - 1, 0)
            powers.append(power.astype(jnp.bfloat16))
        powers = jnp.concatenate(powers, axis=0)
        smooths.append(jnp.dot(powers, ring, preferred_element_type=jnp.float32))
    range_backs = []
    for span, smooth in zip(spans, smooths):
        gain = lax.rsqrt(lax.rsqrt(smooth * (1.0 / (9.0 * PATCH * PATCH)) + 1.0))
        shaped = jnp.concatenate(
            [spectrum_ref[span, :LANES] * gain, spectrum_ref[span, LANES:] * gain], axis=1
        ).astype(jnp.bfloat16)
        range_back = jnp.dot(shaped, inverse, preferred_element_type=jnp.float32)
        range_backs.append(range_back.astype(jnp.bfloat16))
    window = jnp.concatenate([window] * chunks, axis=1)
    totals = [[None] * (row_patches - 1) for _ in range(2)]
    for row in range(row_patches):
        stacked = []
        for chunk in range(chunks):
            block = range_backs[row][chunk * PATCH : (chunk + 1) * PATCH]
            stacked.append(jnp.concatenate([block[:, :LANES], block[:, LANES:]], axis=0))
        stacked = jnp.concatenate(stacked, axis=1)
        patch_out = jnp.dot(back, stacked, preferred_element_type=jnp.float32) * window
        for part in range(2):
            upper = patch_out[part * PATCH : part * PATCH + HALF]
            lower = patch_out[part * PATCH + HALF : (part + 1) * PATCH]
            if row > 0:
                totals[part][row - 1] = totals[part][row - 1] + upper
            if row < row_patches - 1:
                totals[part][row] = lower
    total = jnp.concatenate([block for part in totals for block in part], axis=0)
    return total[:, :width] + total[:, width + HALF : 2 * width + HALF]


def keep(ref, result):
    lines = ref.shape[1]
    for part in range(2):
        ref[part] = result[part * lines : (part + 1) * lines]


def own_kernel(table_ref, own_ref, out_ref, tile_ref, edge_ref, spectrum_ref):
    _, lines, width = out_ref.shape
    row_patches = lines // HALF + 1
    tables = Tables(table_ref, row_patches)
    own = both_halves(own_ref)
    for turn, (tile, edge) in enumerate(own):
        for part in range(2):
            tile_ref[turn, part] = tile[part]
            edge_ref[turn, part] = edge[part]
    total = line_sum(tables, own, own)
    keep(out_ref, filtered_of(total, tables, spectrum_ref, row_patches, width))


def other_kernel(match_ref, table_ref, filtered_own_ref, tile_ref, edge_ref, *refs):
    out_ref, result_ref, spectrum_ref, sems = refs[-4:]
    match_count, _, _, lines, width = out_ref.shape
    row_patches = lines // HALF + 1
    date = lax.axis_index("date")
    dates = match_ref.shape[1]
    tables = Tables(table_ref, row_patches)

    def copy_of(match, source_ref):
        return pltpu.make_async_copy(source_ref, out_ref.at[match, :, 0], sems.at[match])

    def send(slot, source_ref):
        for match in range(match_count):
            wanted = lax.rem(match_ref[match, date] - date + dates, dates)

            @pl.when(wanted == slot)
            def _():
                copy_of(match, source_ref).start()

    send(0, filtered_own_ref)
    own = [
        [(ref[turn, 0], ref[turn, 1]) for ref in (tile_ref, edge_ref)] for turn in range(2)
    ]
    for slot in range(1, dates):
        total = line_sum(tables, own, both_halves(refs[slot - 1]))
        result = filtered_of(total, tables, spectrum_ref, row_patches, width)
        keep(result_ref.at[slot - 1], result)
        send(slot, result_ref.at[slot - 1])
    for match in range(match_count):
        copy_of(match, filtered_own_ref).wait()


def all_tables(row_patches):
    forward = fourier_table(1.0, 1.0)
    inverse = fourier_table(-1.0, 1.0 / PATCH)
    back = inverse.reshape(2, PATCH, 2, PATCH).transpose(2, 3, 0, 1).reshape(2 * PATCH, 2 * PATCH)
    window = window_table()[:PATCH, :PATCH]
    splits = []
    for _ in range(3):
        splits.append(window.astype(jnp.bfloat16).astype(np.float32))
        window = window - splits[-1]
    half = (row_patches + 1) * HALF // 2
    lines = line_table(forward, row_patches).reshape(-1, 2, 2, half)
    halves = [lines[:, :, at].reshape(-1, 2 * half) for at in range(2)]
    rows = [np.concatenate([value, np.zeros_like(value)], axis=1) for value in halves] + [
        paired(forward),
        paired(inverse),
        np.concatenate([back, ring_table()], axis=1),
        np.concatenate([*splits, np.zeros_like(window)], axis=1),
    ]
    return np.concatenate(rows, axis=0).astype(jnp.bfloat16)


class Tables:
    def __init__(self, ref, row_patches):
        self.ref = ref
        self.size = row_patches * 2 * PATCH

    def lines(self, turn):
        start = pl.multiple_of(jnp.where(is_above(turn), 0, self.size), self.size)
        return self.ref[pl.ds(start, self.size), :LANES]

    def core(self):
        ref, at = self.ref, 2 * self.size
        forward = ref[at : at + 4 * PATCH, :]
        at += 4 * PATCH
        inverse = ref[at : at + 4 * PATCH, :]
        at += 4 * PATCH
        back = ref[at : at + LANES, :LANES]
        ring = ref[at : at + LANES, LANES:]
        at += LANES
        splits = ref[at : at + PATCH, :].astype(jnp.float32)
        window = splits[:, :PATCH] + splits[:, PATCH : 2 * PATCH] + splits[:, 2 * PATCH : 3 * PATCH]
        window = jnp.concatenate([window, window], axis=1)
        window = jnp.concatenate([window, window], axis=0)
        return forward, inverse, back, ring, window


def per_device(image_stack, tap_weights, offsets, matchings):
    _, _, lines, width = image_stack.shape
    match_count = matchings.shape[0]
    other = lax.ppermute(image_stack, "rg", [(0, 1), (1, 0)]).reshape(2, lines, width)
    arguments = (
        image_stack.reshape(2, lines, width),
        tap_weights.reshape(TAPS, lines),
        offsets,
    )
    raw = pl.pallas_call(
        load_kernel,
        out_shape=tuple(pltpu.VMEM(a.shape, a.dtype) for a in arguments),
        in_specs=[HBM] * 3,
        out_specs=(VMEM,) * 3,
        scratch_shapes=[pltpu.SemaphoreType.DMA((3,))],
        compiler_params=PARAMS,
        name="load",
    )(*(pltpu.with_memory_space_constraint(a, pltpu.HBM) for a in arguments))
    raw = (raw[0], other, *raw[1:])
    message = jax.ShapeDtypeStruct((2 * REACH + STEP, width), jnp.bfloat16)
    messages = pl.pallas_call(
        pack_kernel,
        out_shape=(message, message),
        in_specs=[VMEM] * 4,
        out_specs=(VMEM, VMEM),
        compiler_params=PARAMS,
        name="pack",
    )(*raw)
    peers = lax.axis_size("az")

    def swapped(value, start):
        paired_with = {i: i + 1 for i in range(start, peers - 1, 2)}
        paired_with.update({j: i for i, j in paired_with.items()})
        pairs = [
            (2 * i + core, 2 * paired_with[i] + core if i in paired_with else 2 * i + 1 - core)
            for i in range(peers)
            for core in range(2)
        ]
        return lax.ppermute(value, ("az", "rg"), pairs)

    messages = [swapped(messages[turn], turn) for turn in range(2)]
    inner = pl.pallas_call(
        inner_kernel,
        out_shape=jax.ShapeDtypeStruct((2, lines, width + HALF), jnp.float32),
        in_specs=[VMEM] * 4,
        out_specs=VMEM,
        compiler_params=PARAMS,
        name="inner",
    )(*raw)
    pieces = []
    count = 2 * (lines // 2 + HALF) + STEP
    for turn in range(2):
        call = pl.pallas_call(
            functools.partial(side_kernel, turn),
            out_shape=jax.ShapeDtypeStruct(((turn + 1) * count, width), jnp.bfloat16),
            in_specs=[VMEM] * (6 + turn),
            out_specs=VMEM,
            compiler_params=PARAMS,
            name="side_" + "ab"[turn],
        )
        pieces.append(call(*raw, messages[turn], inner, *pieces))
    own = pieces[1]
    dates = lax.axis_size("date")

    def from_date(piece, slot):
        return lax.ppermute(piece, "date", [((i + slot) % dates, i) for i in range(dates)])

    others = [from_date(own, slot) for slot in range(1, dates)]
    row_patches = lines // HALF + 1
    chunks = (width + width + LANES) // LANES
    tables = jnp.asarray(all_tables(row_patches))
    spectrum = pltpu.VMEM((row_patches * chunks * PATCH, 2 * LANES), jnp.float32)
    half = lines // 2 + HALF
    filtered_own, *own_parts = pl.pallas_call(
        own_kernel,
        out_shape=(
            jax.ShapeDtypeStruct((2, lines, width), jnp.float32),
            jax.ShapeDtypeStruct((2, 2, half, width), jnp.float32),
            jax.ShapeDtypeStruct((2, 2, half, HALF), jnp.float32),
        ),
        in_specs=[VMEM] * 2,
        out_specs=(VMEM,) * 3,
        scratch_shapes=[spectrum],
        compiler_params=PARAMS,
        name="filter_own",
    )(tables, own)
    return pl.pallas_call(
        other_kernel,
        out_shape=jax.ShapeDtypeStruct((match_count, 2, 1, lines, width), jnp.float32),
        in_specs=[SMEM] + [VMEM] * (4 + len(others)),
        out_specs=HBM,
        scratch_shapes=[
            pltpu.VMEM((dates - 1, 2, lines, width), jnp.float32),
            spectrum,
            pltpu.SemaphoreType.DMA((match_count,)),
        ],
        compiler_params=PARAMS,
        name="filter_other",
    )(matchings, tables, filtered_own, *own_parts, *others)


def solution(mesh):
    placed = (
        P(None, ("parts", "date"), "az", "rg"),
        P(None, ("parts", "date"), "az"),
        P(("parts", "date"), "az"),
        P(),
    )
    return jax.shard_map(
        per_device,
        mesh=mesh,
        in_specs=placed,
        out_specs=P(None, None, ("parts", "date"), "az", "rg"),
        check_vma=False,
    )
```

```python
import functools
import math

import jax
import jax.numpy as jnp
import numpy as np
from jax import lax
from jax.experimental import pallas as pl
from jax.experimental.pallas import tpu as pltpu
from jax.sharding import PartitionSpec as P

TAPS = 8
SHIFT_MAX = 12
PATCH = 64
HALF = PATCH // 2
RIM = SHIFT_MAX + TAPS // 2
REACH = HALF + RIM
LANES = 128
STEP = 16
VMEM_LIMIT = 48 * 1024 * 1024

VMEM = pl.BlockSpec(memory_space=pltpu.VMEM)
SMEM = pl.BlockSpec(memory_space=pltpu.SMEM)
HBM = pl.BlockSpec(memory_space=pltpu.HBM)
PARAMS = pltpu.CompilerParams(vmem_limit_bytes=VMEM_LIMIT)


def fourier_table(sine_sign, table_scale):
    freq_ids = np.arange(PATCH)
    phase_ids = (freq_ids[:, None] * freq_ids[None, :]) % PATCH
    angles = phase_ids * (2.0 * math.pi / PATCH)
    cosine = np.cos(angles) * table_scale
    sine_part = np.sin(angles) * (sine_sign * table_scale)
    top = np.concatenate([cosine, -sine_part], axis=1)
    bottom = np.concatenate([sine_part, cosine], axis=1)
    return np.concatenate([top, bottom], axis=0).astype(np.float32)


def paired(table):
    split = table.reshape(2, PATCH, 2, PATCH)
    wide = np.zeros((2, 2, PATCH, 2, 2, PATCH), np.float32)
    for slot in range(2):
        wide[:, slot, :, :, slot, :] = split
    return wide.reshape(4 * PATCH, 4 * PATCH)


def line_table(forward, row_patches):
    wide_lines = (row_patches + 1) * HALF
    table = np.zeros((row_patches, 2 * PATCH, 2, wide_lines), np.float32)
    transposed = forward.T.reshape(2 * PATCH, 2, PATCH)
    for row in range(row_patches):
        table[row, :, :, row * HALF : row * HALF + PATCH] = transposed
    return table.reshape(row_patches * 2 * PATCH, 2 * wide_lines)


def window_table():
    window = np.sin(math.pi * (np.arange(PATCH) + 0.5) / PATCH) ** 2
    return np.tile(np.outer(window, window), (2, 2)).astype(np.float32)


def ring_table():
    ring = np.zeros((LANES, LANES), np.float32)
    for lane in range(LANES):
        base = lane // PATCH * PATCH
        for step in (-1, 0, 1):
            ring[base + (lane + step) % PATCH, lane] = 1.0
    return ring


def edge_of(other_ref, part, side, lines):
    width = other_ref.shape[2]
    return jnp.where(
        side == 0, other_ref[part, lines, :HALF], other_ref[part, lines, width - HALF :]
    )


def side_by_side(values):
    values = jnp.concatenate(values, axis=0)
    return jnp.concatenate([values[i : i + STEP] for i in range(0, values.shape[0], STEP)], axis=1)


def one_below(block, first, last):
    return jnp.concatenate([block[:, i * HALF : (i + 1) * HALF] for i in range(first, last)], axis=0)


def load_kernel(*refs):
    count = (len(refs) - 1) // 2
    copies = [
        pltpu.make_async_copy(refs[i], refs[count + i], refs[-1].at[i]) for i in range(count)
    ]
    for copy in copies:
        copy.start()
    for copy in copies:
        copy.wait()


def pack_kernel(image_ref, other_ref, taps_ref, offsets_ref, even_ref, odd_ref):
    lines = image_ref.shape[1]
    side = lax.axis_index("rg")
    taps = taps_ref[...]
    taps_high = taps.astype(jnp.bfloat16).astype(jnp.float32)
    taps = jnp.concatenate([taps_high, taps - taps_high], axis=0)
    shifts = jnp.broadcast_to(offsets_ref[...].astype(jnp.float32), taps.shape)

    def write(out_ref, line_start, tap_start):
        rows = slice(line_start, line_start + REACH)
        for part in range(2):
            cut = slice(part * REACH, (part + 1) * REACH)
            out_ref[cut, :] = image_ref[part, rows, :].astype(jnp.bfloat16)
        edges = [edge_of(other_ref, part, side, rows) for part in range(2)]
        cut = slice(tap_start, tap_start + HALF)
        block = side_by_side([*edges, taps[:, cut], shifts[:, cut]])
        out_ref[2 * REACH :, :] = block.astype(jnp.bfloat16)

    parity = lax.rem(lax.axis_index("az"), 2)

    @pl.when(parity == 0)
    def _():
        write(even_ref, lines - REACH, lines - HALF)
        write(odd_ref, 0, 0)

    @pl.when(parity == 1)
    def _():
        write(even_ref, 0, 0)
        write(odd_ref, lines - REACH, lines - HALF)


def is_above(turn):
    return lax.rem(lax.axis_index("az") + turn, 2) == 1


def band(taps, shift, first_line, source):
    count, lines = source.shape
    tap_ids = source - (lax.broadcasted_iota(jnp.int32, (count, lines), 1) + first_line)
    tap_ids = tap_ids - shift + (TAPS // 2 - 1)
    total = jnp.zeros((count, lines), jnp.float32)
    for tap in range(TAPS):
        total = jnp.where(tap_ids == tap, taps[tap : tap + 1, :], total)
    return total


def high_low(value):
    high = value.astype(jnp.bfloat16)
    low = (value - high.astype(jnp.float32)).astype(jnp.bfloat16)
    return jnp.concatenate([high, low], axis=0)


def apply_band(weights, rows):
    over_rows = (((0,), (0,)), ((), ()))
    rows = jnp.concatenate([rows, rows], axis=0)
    return lax.dot_general(high_low(weights), rows, over_rows, preferred_element_type=jnp.float32)


def write_piece(out_ref, parts, width):
    lines = parts[0].shape[0]
    for part, value in enumerate(parts):
        out_ref[part * lines : (part + 1) * lines, :] = value[:, :width].astype(jnp.bfloat16)
    edges = side_by_side([value[:, width:] for value in parts])
    out_ref[2 * lines :, :] = edges.astype(jnp.bfloat16)


def read_piece(ref, first, count):
    lines = (count - STEP) // 2
    middle = first + 2 * lines
    tiles = ref[first:middle, :].astype(jnp.float32)
    edges = one_below(ref[middle : first + count, :].astype(jnp.float32), 0, 2 * lines // STEP)
    return [(v[:lines], v[lines:]) for v in (tiles, edges)]


def inner_kernel(image_ref, other_ref, taps_ref, offsets_ref, out_ref):
    lines = image_ref.shape[1]
    width = image_ref.shape[2]
    side = lax.axis_index("rg")
    source = lax.broadcasted_iota(jnp.int32, (lines, lines), 0)
    weights = band(taps_ref[...], offsets_ref[...], 0, source)
    weights = jnp.concatenate([weights, weights], axis=0)
    for part in range(2):
        edge = edge_of(other_ref, part, side, slice(0, lines))
        rows = high_low(jnp.concatenate([image_ref[part], edge], axis=1))
        out_ref[part] = apply_band(weights, rows)


def side_lines(turn, image_ref, other_ref, taps_ref, offsets_ref, message_ref):
    lines = image_ref.shape[1]
    side = lax.axis_index("rg")
    above = is_above(turn)
    message = message_ref[...]
    block = message[2 * REACH :, :].astype(jnp.float32)
    steps = 2 * REACH // STEP
    rim_edges = one_below(block, 0, steps).astype(jnp.bfloat16)
    rim_taps = one_below(block, steps, steps + 1)
    rim_taps = rim_taps[:TAPS] + rim_taps[TAPS:]
    rim_shift = one_below(block, steps + 1, steps + 2)[:1]

    def per_line(own, rim):
        upper = jnp.concatenate([rim, own[:, :RIM]], axis=1)
        lower = jnp.concatenate([own[:, lines - RIM :], rim], axis=1)
        return jnp.where(above, upper, lower)

    taps = per_line(taps_ref[...], rim_taps)
    shift = per_line(offsets_ref[...].astype(jnp.float32), rim_shift).astype(jnp.int32)
    first_line = jnp.where(above, -HALF, lines - RIM)
    near = 2 * RIM
    first_own = jnp.where(above, 0, lines - near)
    first_rim = jnp.where(above, -REACH, lines)
    source = lax.broadcasted_iota(jnp.int32, (REACH + near, REACH), 0)
    source = jnp.where(source < REACH, source + first_rim, source - REACH + first_own)
    weights = band(taps, shift, first_line, source)
    weights = jnp.concatenate([weights, weights[REACH:]], axis=0)
    parts = []
    for part in range(2):
        upper, lower = slice(0, near), slice(lines - near, lines)
        edge = jnp.where(
            above, edge_of(other_ref, part, side, upper), edge_of(other_ref, part, side, lower)
        )
        own = jnp.where(above, image_ref[part, upper, :], image_ref[part, lower, :])
        own = high_low(jnp.concatenate([own, edge], axis=1))
        cut = slice(part * REACH, (part + 1) * REACH)
        rim = jnp.concatenate([message[cut, :], rim_edges[cut]], axis=1)
        parts.append(apply_band(weights, jnp.concatenate([rim, own], axis=0)))
    return parts


def side_kernel(turn, *refs):
    image_ref, other_ref, taps_ref, offsets_ref, message_ref, inner_ref = refs[:6]
    out_ref = refs[-1]
    width = image_ref.shape[2]
    place = lax.axis_index("az")
    above = is_above(turn)
    alone = jnp.where(above, place == 0, place == lax.axis_size("az") - 1)
    if turn == 1:
        count = refs[6].shape[0]
        out_ref[:count, :] = refs[6][...]
        out_ref = out_ref.at[count:]

    lines = inner_ref.shape[1]
    half = lines // 2 + HALF

    @pl.when(alone)
    def _():
        halves = []
        for part in range(2):
            blank = jnp.zeros((HALF, inner_ref.shape[2]), jnp.float32)
            upper = jnp.concatenate([blank, inner_ref[part, : half - HALF]], axis=0)
            lower = jnp.concatenate([inner_ref[part, lines - half + HALF :], blank], axis=0)
            halves.append(jnp.where(above, upper, lower))
        write_piece(out_ref, halves, width)

    @pl.when(jnp.logical_not(alone))
    def _():
        halves = []
        for part, total in enumerate(side_lines(turn, *refs[:5])):
            near = inner_ref[part, RIM : half - HALF]
            upper = jnp.concatenate([total, near], axis=0)
            near = inner_ref[part, lines - half + HALF : lines - RIM]
            lower = jnp.concatenate([near, total], axis=0)
            halves.append(jnp.where(above, upper, lower))
        write_piece(out_ref, halves, width)


def cross(own_parts, other_parts):
    own_real, own_imag = own_parts
    other_real, other_imag = other_parts
    real = own_real * other_real + own_imag * other_imag
    imag = own_imag * other_real - own_real * other_imag
    return real, imag


def both_halves(ref):
    count = ref.shape[0] // 2
    return [read_piece(ref, turn * count, count) for turn in range(2)]


def interferogram(own, other):
    side = lax.axis_index("rg")
    own_tile, own_edge = own
    other_tile, other_edge = other
    mid = jnp.concatenate(cross(own_tile, other_tile), axis=0)
    rim = jnp.concatenate(cross(own_edge, other_edge), axis=0)
    before = jnp.where(side == 0, 0.0, rim)
    after = jnp.where(side == 0, rim, 0.0)
    filler = jnp.zeros((mid.shape[0], LANES - 2 * HALF), jnp.float32)
    shifted = jnp.concatenate([before, mid, after, filler], axis=1).astype(jnp.bfloat16)
    return jnp.concatenate([mid.astype(jnp.bfloat16), shifted], axis=1)


def line_sum(tables, own, other):
    both = [interferogram(*halves) for halves in zip(own, other)]
    weights = jnp.concatenate([tables.lines(turn) for turn in range(2)], axis=1)
    both = jnp.concatenate(both, axis=0)
    return jnp.dot(weights, both, preferred_element_type=jnp.float32)


def filtered_of(line_spectra, tables, spectrum_ref, row_patches, width, emit):
    line_spectra = line_spectra.astype(jnp.bfloat16)
    chunks = line_spectra.shape[1] // LANES
    forward, inverse, back, ring, window = tables.core()
    step = chunks * PATCH
    spans = [slice(row * step, (row + 1) * step) for row in range(row_patches)]
    for row, span in enumerate(spans):
        top = row * 2 * PATCH
        pieces = []
        for chunk in range(chunks):
            cut = slice(chunk * LANES, (chunk + 1) * LANES)
            real = line_spectra[top : top + PATCH, cut]
            imag = line_spectra[top + PATCH : top + 2 * PATCH, cut]
            pieces.append(jnp.concatenate([real, imag], axis=1))
        patches = jnp.concatenate(pieces, axis=0)
        spectrum_ref[span, :] = jnp.dot(patches, forward, preferred_element_type=jnp.float32)
    smooths = []
    for span in spans:
        powers = []
        for start in range(span.start, span.stop, PATCH):
            real = spectrum_ref[start : start + PATCH, :LANES]
            imag = spectrum_ref[start : start + PATCH, LANES:]
            power = real * real + imag * imag
            power = power + pltpu.roll(power, 1, 0) + pltpu.roll(power, PATCH - 1, 0)
            powers.append(power.astype(jnp.bfloat16))
        powers = jnp.concatenate(powers, axis=0)
        smooths.append(jnp.dot(powers, ring, preferred_element_type=jnp.float32))
    range_backs = []
    for span, smooth in zip(spans, smooths):
        gain = lax.rsqrt(lax.rsqrt(smooth * (1.0 / (9.0 * PATCH * PATCH)) + 1.0))
        shaped = jnp.concatenate(
            [spectrum_ref[span, :LANES] * gain, spectrum_ref[span, LANES:] * gain], axis=1
        ).astype(jnp.bfloat16)
        range_back = jnp.dot(shaped, inverse, preferred_element_type=jnp.float32)
        range_backs.append(range_back.astype(jnp.bfloat16))
    window = jnp.concatenate([window] * chunks, axis=1)
    earlier = None
    for row in range(row_patches):
        stacked = []
        for chunk in range(chunks):
            block = range_backs[row][chunk * PATCH : (chunk + 1) * PATCH]
            stacked.append(jnp.concatenate([block[:, :LANES], block[:, LANES:]], axis=0))
        stacked = jnp.concatenate(stacked, axis=1)
        patch_out = jnp.dot(back, stacked, preferred_element_type=jnp.float32) * window
        uppers = [patch_out[part * PATCH : part * PATCH + HALF] for part in range(2)]
        if row > 0:
            total = jnp.concatenate(uppers, axis=0) + earlier
            emit(row - 1, total[:, :width] + total[:, width + HALF : 2 * width + HALF])
        lowers = [patch_out[part * PATCH + HALF : (part + 1) * PATCH] for part in range(2)]
        earlier = jnp.concatenate(lowers, axis=0)


def keep(ref, row, total):
    for part in range(2):
        ref[part, row * HALF : (row + 1) * HALF] = total[part * HALF : (part + 1) * HALF]


def own_kernel(table_ref, own_ref, out_ref, tile_ref, edge_ref, spectrum_ref):
    _, lines, width = out_ref.shape
    row_patches = lines // HALF + 1
    tables = Tables(table_ref, row_patches)
    own = both_halves(own_ref)
    for turn, (tile, edge) in enumerate(own):
        for part in range(2):
            tile_ref[turn, part] = tile[part]
            edge_ref[turn, part] = edge[part]
    total = line_sum(tables, own, own)
    emit = functools.partial(keep, out_ref)
    filtered_of(total, tables, spectrum_ref, row_patches, width, emit)


def other_kernel(match_ref, table_ref, filtered_own_ref, tile_ref, edge_ref, *refs):
    out_ref, result_ref, spectrum_ref, sems = refs[-4:]
    match_count, _, _, lines, width = out_ref.shape
    row_patches = lines // HALF + 1
    date = lax.axis_index("date")
    dates = match_ref.shape[1]
    tables = Tables(table_ref, row_patches)

    rows = lines // HALF

    def copy_of(match, row, source_ref):
        cut = slice(row * HALF, (row + 1) * HALF)
        target = out_ref.at[match, :, 0, cut]
        return pltpu.make_async_copy(source_ref.at[:, cut], target, sems.at[match, row])

    def send(slot, row, source_ref):
        for match in range(match_count):
            wanted = lax.rem(match_ref[match, date] - date + dates, dates)

            @pl.when(wanted == slot)
            def _():
                copy_of(match, row, source_ref).start()

    for row in range(rows):
        send(0, row, filtered_own_ref)
    own = [
        [(ref[turn, 0], ref[turn, 1]) for ref in (tile_ref, edge_ref)] for turn in range(2)
    ]
    for slot in range(1, dates):
        total = line_sum(tables, own, both_halves(refs[slot - 1]))
        target_ref = result_ref.at[slot - 1]

        def emit(row, total):
            keep(target_ref, row, total)
            send(slot, row, target_ref)

        filtered_of(total, tables, spectrum_ref, row_patches, width, emit)
    for match in range(match_count):
        for row in range(rows):
            copy_of(match, row, filtered_own_ref).wait()


def all_tables(row_patches):
    forward = fourier_table(1.0, 1.0)
    inverse = fourier_table(-1.0, 1.0 / PATCH)
    back = inverse.reshape(2, PATCH, 2, PATCH).transpose(2, 3, 0, 1).reshape(2 * PATCH, 2 * PATCH)
    window = window_table()[:PATCH, :PATCH]
    splits = []
    for _ in range(3):
        splits.append(window.astype(jnp.bfloat16).astype(np.float32))
        window = window - splits[-1]
    half = (row_patches + 1) * HALF // 2
    lines = line_table(forward, row_patches).reshape(-1, 2, 2, half)
    halves = [lines[:, :, at].reshape(-1, 2 * half) for at in range(2)]
    rows = [np.concatenate([value, np.zeros_like(value)], axis=1) for value in halves] + [
        paired(forward),
        paired(inverse),
        np.concatenate([back, ring_table()], axis=1),
        np.concatenate([*splits, np.zeros_like(window)], axis=1),
    ]
    return np.concatenate(rows, axis=0).astype(jnp.bfloat16)


class Tables:
    def __init__(self, ref, row_patches):
        self.ref = ref
        self.size = row_patches * 2 * PATCH

    def lines(self, turn):
        start = pl.multiple_of(jnp.where(is_above(turn), 0, self.size), self.size)
        return self.ref[pl.ds(start, self.size), :LANES]

    def core(self):
        ref, at = self.ref, 2 * self.size
        forward = ref[at : at + 4 * PATCH, :]
        at += 4 * PATCH
        inverse = ref[at : at + 4 * PATCH, :]
        at += 4 * PATCH
        back = ref[at : at + LANES, :LANES]
        ring = ref[at : at + LANES, LANES:]
        at += LANES
        splits = ref[at : at + PATCH, :].astype(jnp.float32)
        window = splits[:, :PATCH] + splits[:, PATCH : 2 * PATCH] + splits[:, 2 * PATCH : 3 * PATCH]
        window = jnp.concatenate([window, window], axis=1)
        window = jnp.concatenate([window, window], axis=0)
        return forward, inverse, back, ring, window


def per_device(image_stack, tap_weights, offsets, matchings):
    _, _, lines, width = image_stack.shape
    match_count = matchings.shape[0]
    other = lax.ppermute(image_stack, "rg", [(0, 1), (1, 0)]).reshape(2, lines, width)
    arguments = (
        image_stack.reshape(2, lines, width),
        tap_weights.reshape(TAPS, lines),
        offsets,
    )
    raw = pl.pallas_call(
        load_kernel,
        out_shape=tuple(pltpu.VMEM(a.shape, a.dtype) for a in arguments),
        in_specs=[HBM] * 3,
        out_specs=(VMEM,) * 3,
        scratch_shapes=[pltpu.SemaphoreType.DMA((3,))],
        compiler_params=PARAMS,
        name="load",
    )(*(pltpu.with_memory_space_constraint(a, pltpu.HBM) for a in arguments))
    raw = (raw[0], other, *raw[1:])
    message = jax.ShapeDtypeStruct((2 * REACH + STEP, width), jnp.bfloat16)
    messages = pl.pallas_call(
        pack_kernel,
        out_shape=(message, message),
        in_specs=[VMEM] * 4,
        out_specs=(VMEM, VMEM),
        compiler_params=PARAMS,
        name="pack",
    )(*raw)
    peers = lax.axis_size("az")

    def swapped(value, start):
        paired_with = {i: i + 1 for i in range(start, peers - 1, 2)}
        paired_with.update({j: i for i, j in paired_with.items()})
        pairs = [
            (2 * i + core, 2 * paired_with[i] + core if i in paired_with else 2 * i + 1 - core)
            for i in range(peers)
            for core in range(2)
        ]
        return lax.ppermute(value, ("az", "rg"), pairs)

    messages = [swapped(messages[turn], turn) for turn in range(2)]
    inner = pl.pallas_call(
        inner_kernel,
        out_shape=jax.ShapeDtypeStruct((2, lines, width + HALF), jnp.float32),
        in_specs=[VMEM] * 4,
        out_specs=VMEM,
        compiler_params=PARAMS,
        name="inner",
    )(*raw)
    pieces = []
    count = 2 * (lines // 2 + HALF) + STEP
    for turn in range(2):
        call = pl.pallas_call(
            functools.partial(side_kernel, turn),
            out_shape=jax.ShapeDtypeStruct(((turn + 1) * count, width), jnp.bfloat16),
            in_specs=[VMEM] * (6 + turn),
            out_specs=VMEM,
            compiler_params=PARAMS,
            name="side_" + "ab"[turn],
        )
        pieces.append(call(*raw, messages[turn], inner, *pieces))
    own = pieces[1]
    dates = lax.axis_size("date")

    def from_date(piece, slot):
        return lax.ppermute(piece, "date", [((i + slot) % dates, i) for i in range(dates)])

    others = [from_date(own, slot) for slot in range(1, dates)]
    row_patches = lines // HALF + 1
    chunks = (width + width + LANES) // LANES
    tables = jnp.asarray(all_tables(row_patches))
    spectrum = pltpu.VMEM((row_patches * chunks * PATCH, 2 * LANES), jnp.float32)
    half = lines // 2 + HALF
    filtered_own, *own_parts = pl.pallas_call(
        own_kernel,
        out_shape=(
            jax.ShapeDtypeStruct((2, lines, width), jnp.float32),
            jax.ShapeDtypeStruct((2, 2, half, width), jnp.float32),
            jax.ShapeDtypeStruct((2, 2, half, HALF), jnp.float32),
        ),
        in_specs=[VMEM] * 2,
        out_specs=(VMEM,) * 3,
        scratch_shapes=[spectrum],
        compiler_params=PARAMS,
        name="filter_own",
    )(tables, own)
    return pl.pallas_call(
        other_kernel,
        out_shape=jax.ShapeDtypeStruct((match_count, 2, 1, lines, width), jnp.float32),
        in_specs=[SMEM] + [VMEM] * (4 + len(others)),
        out_specs=HBM,
        scratch_shapes=[
            pltpu.VMEM((dates - 1, 2, lines, width), jnp.float32),
            spectrum,
            pltpu.SemaphoreType.DMA((match_count, lines // HALF)),
        ],
        compiler_params=PARAMS,
        name="filter_other",
    )(matchings, tables, filtered_own, *own_parts, *others)


def solution(mesh):
    placed = (
        P(None, ("parts", "date"), "az", "rg"),
        P(None, ("parts", "date"), "az"),
        P(("parts", "date"), "az"),
        P(),
    )
    return jax.shard_map(
        per_device,
        mesh=mesh,
        in_specs=placed,
        out_specs=P(None, None, ("parts", "date"), "az", "rg"),
        check_vma=False,
    )
```

```python
import functools
import math

import jax
import jax.numpy as jnp
import numpy as np
from jax import lax
from jax.experimental import pallas as pl
from jax.experimental.pallas import tpu as pltpu
from jax.sharding import PartitionSpec as P

TAPS = 8
SHIFT_MAX = 12
PATCH = 64
HALF = PATCH // 2
RIM = SHIFT_MAX + TAPS // 2
REACH = HALF + RIM
LANES = 128
STEP = 16
VMEM_LIMIT = 48 * 1024 * 1024

VMEM = pl.BlockSpec(memory_space=pltpu.VMEM)
SMEM = pl.BlockSpec(memory_space=pltpu.SMEM)
HBM = pl.BlockSpec(memory_space=pltpu.HBM)
PARAMS = pltpu.CompilerParams(vmem_limit_bytes=VMEM_LIMIT)


def fourier_table(sine_sign, table_scale):
    freq_ids = np.arange(PATCH)
    phase_ids = (freq_ids[:, None] * freq_ids[None, :]) % PATCH
    angles = phase_ids * (2.0 * math.pi / PATCH)
    cosine = np.cos(angles) * table_scale
    sine_part = np.sin(angles) * (sine_sign * table_scale)
    top = np.concatenate([cosine, -sine_part], axis=1)
    bottom = np.concatenate([sine_part, cosine], axis=1)
    return np.concatenate([top, bottom], axis=0).astype(np.float32)


def paired(table):
    split = table.reshape(2, PATCH, 2, PATCH)
    wide = np.zeros((2, 2, PATCH, 2, 2, PATCH), np.float32)
    for slot in range(2):
        wide[:, slot, :, :, slot, :] = split
    return wide.reshape(4 * PATCH, 4 * PATCH)


def line_table(forward, row_patches):
    wide_lines = (row_patches + 1) * HALF
    table = np.zeros((row_patches, 2 * PATCH, 2, wide_lines), np.float32)
    transposed = forward.T.reshape(2 * PATCH, 2, PATCH)
    for row in range(row_patches):
        table[row, :, :, row * HALF : row * HALF + PATCH] = transposed
    return table.reshape(row_patches * 2 * PATCH, 2 * wide_lines)


def window_table():
    window = np.sin(math.pi * (np.arange(PATCH) + 0.5) / PATCH) ** 2
    return np.tile(np.outer(window, window), (2, 2)).astype(np.float32)


def ring_table():
    ring = np.zeros((LANES, LANES), np.float32)
    for lane in range(LANES):
        base = lane // PATCH * PATCH
        for step in (-1, 0, 1):
            ring[base + (lane + step) % PATCH, lane] = 1.0
    return ring


def edge_of(other_ref, part, side, lines):
    width = other_ref.shape[2]
    return jnp.where(
        side == 0, other_ref[part, lines, :HALF], other_ref[part, lines, width - HALF :]
    )


def side_by_side(values):
    values = jnp.concatenate(values, axis=0)
    return jnp.concatenate([values[i : i + STEP] for i in range(0, values.shape[0], STEP)], axis=1)


def one_below(block, first, last):
    return jnp.concatenate([block[:, i * HALF : (i + 1) * HALF] for i in range(first, last)], axis=0)


def load_kernel(*refs):
    count = (len(refs) - 1) // 2
    copies = [
        pltpu.make_async_copy(refs[i], refs[count + i], refs[-1].at[i]) for i in range(count)
    ]
    for copy in copies:
        copy.start()
    for copy in copies:
        copy.wait()


def pack_kernel(image_ref, other_ref, taps_ref, offsets_ref, even_ref, odd_ref):
    lines = image_ref.shape[1]
    side = lax.axis_index("rg")
    taps = taps_ref[...]
    taps_high = taps.astype(jnp.bfloat16).astype(jnp.float32)
    taps = jnp.concatenate([taps_high, taps - taps_high], axis=0)
    shifts = jnp.broadcast_to(offsets_ref[...].astype(jnp.float32), taps.shape)

    def write(out_ref, line_start, tap_start):
        rows = slice(line_start, line_start + REACH)
        for part in range(2):
            cut = slice(part * REACH, (part + 1) * REACH)
            out_ref[cut, :] = image_ref[part, rows, :].astype(jnp.bfloat16)
        edges = [edge_of(other_ref, part, side, rows) for part in range(2)]
        cut = slice(tap_start, tap_start + HALF)
        block = side_by_side([*edges, taps[:, cut], shifts[:, cut]])
        out_ref[2 * REACH :, :] = block.astype(jnp.bfloat16)

    parity = lax.rem(lax.axis_index("az"), 2)

    @pl.when(parity == 0)
    def _():
        write(even_ref, lines - REACH, lines - HALF)
        write(odd_ref, 0, 0)

    @pl.when(parity == 1)
    def _():
        write(even_ref, 0, 0)
        write(odd_ref, lines - REACH, lines - HALF)


def is_above(turn):
    return lax.rem(lax.axis_index("az") + turn, 2) == 1


def band(taps, shift, first_line, source):
    count, lines = source.shape
    tap_ids = source - (lax.broadcasted_iota(jnp.int32, (count, lines), 1) + first_line)
    tap_ids = tap_ids - shift + (TAPS // 2 - 1)
    total = jnp.zeros((count, lines), jnp.float32)
    for tap in range(TAPS):
        total = jnp.where(tap_ids == tap, taps[tap : tap + 1, :], total)
    return total


def high_low(value):
    high = value.astype(jnp.bfloat16)
    low = (value - high.astype(jnp.float32)).astype(jnp.bfloat16)
    return jnp.concatenate([high, low], axis=0)


def apply_band(weights, rows):
    over_rows = (((0,), (0,)), ((), ()))
    rows = jnp.concatenate([rows, rows], axis=0)
    return lax.dot_general(high_low(weights), rows, over_rows, preferred_element_type=jnp.float32)


def write_piece(out_ref, parts, width):
    lines = parts[0].shape[0]
    for part, value in enumerate(parts):
        out_ref[part * lines : (part + 1) * lines, :] = value[:, :width].astype(jnp.bfloat16)
    edges = side_by_side([value[:, width:] for value in parts])
    out_ref[2 * lines :, :] = edges.astype(jnp.bfloat16)


def read_piece(ref, first, count):
    lines = (count - STEP) // 2
    middle = first + 2 * lines
    tiles = ref[first:middle, :].astype(jnp.float32)
    edges = one_below(ref[middle : first + count, :].astype(jnp.float32), 0, 2 * lines // STEP)
    return [(v[:lines], v[lines:]) for v in (tiles, edges)]


def inner_kernel(image_ref, other_ref, taps_ref, offsets_ref, out_ref):
    lines = image_ref.shape[1]
    width = image_ref.shape[2]
    side = lax.axis_index("rg")
    source = lax.broadcasted_iota(jnp.int32, (lines, lines), 0)
    weights = band(taps_ref[...], offsets_ref[...], 0, source)
    weights = jnp.concatenate([weights, weights], axis=0)
    for part in range(2):
        edge = edge_of(other_ref, part, side, slice(0, lines))
        rows = high_low(jnp.concatenate([image_ref[part], edge], axis=1))
        out_ref[part] = apply_band(weights, rows)


def side_lines(turn, image_ref, other_ref, taps_ref, offsets_ref, message_ref):
    lines = image_ref.shape[1]
    side = lax.axis_index("rg")
    above = is_above(turn)
    message = message_ref[...]
    block = message[2 * REACH :, :].astype(jnp.float32)
    steps = 2 * REACH // STEP
    rim_edges = one_below(block, 0, steps).astype(jnp.bfloat16)
    rim_taps = one_below(block, steps, steps + 1)
    rim_taps = rim_taps[:TAPS] + rim_taps[TAPS:]
    rim_shift = one_below(block, steps + 1, steps + 2)[:1]

    def per_line(own, rim):
        upper = jnp.concatenate([rim, own[:, :RIM]], axis=1)
        lower = jnp.concatenate([own[:, lines - RIM :], rim], axis=1)
        return jnp.where(above, upper, lower)

    taps = per_line(taps_ref[...], rim_taps)
    shift = per_line(offsets_ref[...].astype(jnp.float32), rim_shift).astype(jnp.int32)
    first_line = jnp.where(above, -HALF, lines - RIM)
    near = 2 * RIM
    first_own = jnp.where(above, 0, lines - near)
    first_rim = jnp.where(above, -REACH, lines)
    source = lax.broadcasted_iota(jnp.int32, (REACH + near, REACH), 0)
    source = jnp.where(source < REACH, source + first_rim, source - REACH + first_own)
    weights = band(taps, shift, first_line, source)
    weights = jnp.concatenate([weights, weights[REACH:]], axis=0)
    parts = []
    for part in range(2):
        upper, lower = slice(0, near), slice(lines - near, lines)
        edge = jnp.where(
            above, edge_of(other_ref, part, side, upper), edge_of(other_ref, part, side, lower)
        )
        own = jnp.where(above, image_ref[part, upper, :], image_ref[part, lower, :])
        own = high_low(jnp.concatenate([own, edge], axis=1))
        cut = slice(part * REACH, (part + 1) * REACH)
        rim = jnp.concatenate([message[cut, :], rim_edges[cut]], axis=1)
        parts.append(apply_band(weights, jnp.concatenate([rim, own], axis=0)))
    return parts


def side_kernel(turn, *refs):
    image_ref, other_ref, taps_ref, offsets_ref, message_ref, inner_ref = refs[:6]
    out_ref = refs[-1]
    width = image_ref.shape[2]
    place = lax.axis_index("az")
    above = is_above(turn)
    alone = jnp.where(above, place == 0, place == lax.axis_size("az") - 1)
    if turn == 1:
        count = refs[6].shape[0]
        out_ref[:count, :] = refs[6][...]
        out_ref = out_ref.at[count:]

    lines = inner_ref.shape[1]
    half = lines // 2 + HALF

    @pl.when(alone)
    def _():
        halves = []
        for part in range(2):
            blank = jnp.zeros((HALF, inner_ref.shape[2]), jnp.float32)
            upper = jnp.concatenate([blank, inner_ref[part, : half - HALF]], axis=0)
            lower = jnp.concatenate([inner_ref[part, lines - half + HALF :], blank], axis=0)
            halves.append(jnp.where(above, upper, lower))
        write_piece(out_ref, halves, width)

    @pl.when(jnp.logical_not(alone))
    def _():
        halves = []
        for part, total in enumerate(side_lines(turn, *refs[:5])):
            near = inner_ref[part, RIM : half - HALF]
            upper = jnp.concatenate([total, near], axis=0)
            near = inner_ref[part, lines - half + HALF : lines - RIM]
            lower = jnp.concatenate([near, total], axis=0)
            halves.append(jnp.where(above, upper, lower))
        write_piece(out_ref, halves, width)


def cross(own_parts, other_parts):
    own_real, own_imag = own_parts
    other_real, other_imag = other_parts
    real = own_real * other_real + own_imag * other_imag
    imag = own_imag * other_real - own_real * other_imag
    return real, imag


def both_halves(ref):
    count = ref.shape[0] // 2
    return [read_piece(ref, turn * count, count) for turn in range(2)]


def interferogram(own, other):
    side = lax.axis_index("rg")
    own_tile, own_edge = own
    other_tile, other_edge = other
    mid = jnp.concatenate(cross(own_tile, other_tile), axis=0)
    rim = jnp.concatenate(cross(own_edge, other_edge), axis=0)
    before = jnp.where(side == 0, 0.0, rim)
    after = jnp.where(side == 0, rim, 0.0)
    filler = jnp.zeros((mid.shape[0], LANES - 2 * HALF), jnp.float32)
    shifted = jnp.concatenate([before, mid, after, filler], axis=1).astype(jnp.bfloat16)
    return jnp.concatenate([mid.astype(jnp.bfloat16), shifted], axis=1)


def line_sum(tables, own, other):
    both = [interferogram(*halves) for halves in zip(own, other)]
    weights = jnp.concatenate([tables.lines(turn) for turn in range(2)], axis=1)
    both = jnp.concatenate(both, axis=0)
    return jnp.dot(weights, both, preferred_element_type=jnp.float32)


def filtered_of(line_spectra, tables, spectrum_ref, row_patches, width, emit):
    line_spectra = line_spectra.astype(jnp.bfloat16)
    chunks = line_spectra.shape[1] // LANES
    forward, inverse, back, ring, window = tables.core()
    step = chunks * PATCH
    spans = [slice(row * step, (row + 1) * step) for row in range(row_patches)]
    for row, span in enumerate(spans):
        top = row * 2 * PATCH
        pieces = []
        for chunk in range(chunks):
            cut = slice(chunk * LANES, (chunk + 1) * LANES)
            real = line_spectra[top : top + PATCH, cut]
            imag = line_spectra[top + PATCH : top + 2 * PATCH, cut]
            pieces.append(jnp.concatenate([real, imag], axis=1))
        patches = jnp.concatenate(pieces, axis=0)
        spectrum_ref[span, :] = jnp.dot(patches, forward, preferred_element_type=jnp.float32)
    window = jnp.concatenate([window] * chunks, axis=1)
    earlier, range_backs = None, []
    for group in (spans[:-1], spans[-1:]):
        smooths = []
        for span in group:
            powers = []
            for start in range(span.start, span.stop, PATCH):
                real = spectrum_ref[start : start + PATCH, :LANES]
                imag = spectrum_ref[start : start + PATCH, LANES:]
                power = real * real + imag * imag
                power = power + pltpu.roll(power, 1, 0) + pltpu.roll(power, PATCH - 1, 0)
                powers.append(power.astype(jnp.bfloat16))
            powers = jnp.concatenate(powers, axis=0)
            smooths.append(jnp.dot(powers, ring, preferred_element_type=jnp.float32))
        for span, smooth in zip(group, smooths):
            gain = lax.rsqrt(lax.rsqrt(smooth * (1.0 / (9.0 * PATCH * PATCH)) + 1.0))
            shaped = jnp.concatenate(
                [spectrum_ref[span, :LANES] * gain, spectrum_ref[span, LANES:] * gain], axis=1
            ).astype(jnp.bfloat16)
            range_back = jnp.dot(shaped, inverse, preferred_element_type=jnp.float32)
            range_backs.append(range_back.astype(jnp.bfloat16))
        for row in range(len(range_backs) - len(group), len(range_backs)):
            stacked = []
            for chunk in range(chunks):
                block = range_backs[row][chunk * PATCH : (chunk + 1) * PATCH]
                stacked.append(jnp.concatenate([block[:, :LANES], block[:, LANES:]], axis=0))
            stacked = jnp.concatenate(stacked, axis=1)
            patch_out = jnp.dot(back, stacked, preferred_element_type=jnp.float32) * window
            uppers = [patch_out[part * PATCH : part * PATCH + HALF] for part in range(2)]
            if row > 0:
                total = jnp.concatenate(uppers, axis=0) + earlier
                emit(row - 1, total[:, :width] + total[:, width + HALF : 2 * width + HALF])
            lowers = [patch_out[part * PATCH + HALF : (part + 1) * PATCH] for part in range(2)]
            earlier = jnp.concatenate(lowers, axis=0)


def keep(ref, row, total):
    for part in range(2):
        ref[part, row * HALF : (row + 1) * HALF] = total[part * HALF : (part + 1) * HALF]


def own_kernel(table_ref, own_ref, out_ref, tile_ref, edge_ref, spectrum_ref):
    _, lines, width = out_ref.shape
    row_patches = lines // HALF + 1
    tables = Tables(table_ref, row_patches)
    own = both_halves(own_ref)
    for turn, (tile, edge) in enumerate(own):
        for part in range(2):
            tile_ref[turn, part] = tile[part]
            edge_ref[turn, part] = edge[part]
    total = line_sum(tables, own, own)
    emit = functools.partial(keep, out_ref)
    filtered_of(total, tables, spectrum_ref, row_patches, width, emit)


def other_kernel(match_ref, table_ref, filtered_own_ref, tile_ref, edge_ref, *refs):
    out_ref, result_ref, spectrum_ref, sems = refs[-4:]
    match_count, _, _, lines, width = out_ref.shape
    row_patches = lines // HALF + 1
    date = lax.axis_index("date")
    dates = match_ref.shape[1]
    tables = Tables(table_ref, row_patches)

    rows = lines // HALF

    def copy_of(match, row, source_ref):
        cut = slice(row * HALF, (row + 1) * HALF)
        target = out_ref.at[match, :, 0, cut]
        return pltpu.make_async_copy(source_ref.at[:, cut], target, sems.at[match, row])

    def send(slot, row, source_ref):
        for match in range(match_count):
            wanted = lax.rem(match_ref[match, date] - date + dates, dates)

            @pl.when(wanted == slot)
            def _():
                copy_of(match, row, source_ref).start()

    for row in range(rows):
        send(0, row, filtered_own_ref)
    own = [
        [(ref[turn, 0], ref[turn, 1]) for ref in (tile_ref, edge_ref)] for turn in range(2)
    ]
    for slot in range(1, dates):
        total = line_sum(tables, own, both_halves(refs[slot - 1]))
        target_ref = result_ref.at[slot - 1]

        def emit(row, total):
            keep(target_ref, row, total)
            send(slot, row, target_ref)

        filtered_of(total, tables, spectrum_ref, row_patches, width, emit)
    for match in range(match_count):
        for row in range(rows):
            copy_of(match, row, filtered_own_ref).wait()


def all_tables(row_patches):
    forward = fourier_table(1.0, 1.0)
    inverse = fourier_table(-1.0, 1.0 / PATCH)
    back = inverse.reshape(2, PATCH, 2, PATCH).transpose(2, 3, 0, 1).reshape(2 * PATCH, 2 * PATCH)
    window = window_table()[:PATCH, :PATCH]
    splits = []
    for _ in range(3):
        splits.append(window.astype(jnp.bfloat16).astype(np.float32))
        window = window - splits[-1]
    half = (row_patches + 1) * HALF // 2
    lines = line_table(forward, row_patches).reshape(-1, 2, 2, half)
    halves = [lines[:, :, at].reshape(-1, 2 * half) for at in range(2)]
    rows = [np.concatenate([value, np.zeros_like(value)], axis=1) for value in halves] + [
        paired(forward),
        paired(inverse),
        np.concatenate([back, ring_table()], axis=1),
        np.concatenate([*splits, np.zeros_like(window)], axis=1),
    ]
    return np.concatenate(rows, axis=0).astype(jnp.bfloat16)


class Tables:
    def __init__(self, ref, row_patches):
        self.ref = ref
        self.size = row_patches * 2 * PATCH

    def lines(self, turn):
        start = pl.multiple_of(jnp.where(is_above(turn), 0, self.size), self.size)
        return self.ref[pl.ds(start, self.size), :LANES]

    def core(self):
        ref, at = self.ref, 2 * self.size
        forward = ref[at : at + 4 * PATCH, :]
        at += 4 * PATCH
        inverse = ref[at : at + 4 * PATCH, :]
        at += 4 * PATCH
        back = ref[at : at + LANES, :LANES]
        ring = ref[at : at + LANES, LANES:]
        at += LANES
        splits = ref[at : at + PATCH, :].astype(jnp.float32)
        window = splits[:, :PATCH] + splits[:, PATCH : 2 * PATCH] + splits[:, 2 * PATCH : 3 * PATCH]
        window = jnp.concatenate([window, window], axis=1)
        window = jnp.concatenate([window, window], axis=0)
        return forward, inverse, back, ring, window


def per_device(image_stack, tap_weights, offsets, matchings):
    _, _, lines, width = image_stack.shape
    match_count = matchings.shape[0]
    other = lax.ppermute(image_stack, "rg", [(0, 1), (1, 0)]).reshape(2, lines, width)
    arguments = (
        image_stack.reshape(2, lines, width),
        tap_weights.reshape(TAPS, lines),
        offsets,
    )
    raw = pl.pallas_call(
        load_kernel,
        out_shape=tuple(pltpu.VMEM(a.shape, a.dtype) for a in arguments),
        in_specs=[HBM] * 3,
        out_specs=(VMEM,) * 3,
        scratch_shapes=[pltpu.SemaphoreType.DMA((3,))],
        compiler_params=PARAMS,
        name="load",
    )(*(pltpu.with_memory_space_constraint(a, pltpu.HBM) for a in arguments))
    raw = (raw[0], other, *raw[1:])
    message = jax.ShapeDtypeStruct((2 * REACH + STEP, width), jnp.bfloat16)
    messages = pl.pallas_call(
        pack_kernel,
        out_shape=(message, message),
        in_specs=[VMEM] * 4,
        out_specs=(VMEM, VMEM),
        compiler_params=PARAMS,
        name="pack",
    )(*raw)
    peers = lax.axis_size("az")

    def swapped(value, start):
        paired_with = {i: i + 1 for i in range(start, peers - 1, 2)}
        paired_with.update({j: i for i, j in paired_with.items()})
        pairs = [
            (2 * i + core, 2 * paired_with[i] + core if i in paired_with else 2 * i + 1 - core)
            for i in range(peers)
            for core in range(2)
        ]
        return lax.ppermute(value, ("az", "rg"), pairs)

    messages = [swapped(messages[turn], turn) for turn in range(2)]
    inner = pl.pallas_call(
        inner_kernel,
        out_shape=jax.ShapeDtypeStruct((2, lines, width + HALF), jnp.float32),
        in_specs=[VMEM] * 4,
        out_specs=VMEM,
        compiler_params=PARAMS,
        name="inner",
    )(*raw)
    pieces = []
    count = 2 * (lines // 2 + HALF) + STEP
    for turn in range(2):
        call = pl.pallas_call(
            functools.partial(side_kernel, turn),
            out_shape=jax.ShapeDtypeStruct(((turn + 1) * count, width), jnp.bfloat16),
            in_specs=[VMEM] * (6 + turn),
            out_specs=VMEM,
            compiler_params=PARAMS,
            name="side_" + "ab"[turn],
        )
        pieces.append(call(*raw, messages[turn], inner, *pieces))
    own = pieces[1]
    dates = lax.axis_size("date")

    def from_date(piece, slot):
        return lax.ppermute(piece, "date", [((i + slot) % dates, i) for i in range(dates)])

    others = [from_date(own, slot) for slot in range(1, dates)]
    row_patches = lines // HALF + 1
    chunks = (width + width + LANES) // LANES
    tables = jnp.asarray(all_tables(row_patches))
    spectrum = pltpu.VMEM((row_patches * chunks * PATCH, 2 * LANES), jnp.float32)
    half = lines // 2 + HALF
    filtered_own, *own_parts = pl.pallas_call(
        own_kernel,
        out_shape=(
            jax.ShapeDtypeStruct((2, lines, width), jnp.float32),
            jax.ShapeDtypeStruct((2, 2, half, width), jnp.float32),
            jax.ShapeDtypeStruct((2, 2, half, HALF), jnp.float32),
        ),
        in_specs=[VMEM] * 2,
        out_specs=(VMEM,) * 3,
        scratch_shapes=[spectrum],
        compiler_params=PARAMS,
        name="filter_own",
    )(tables, own)
    return pl.pallas_call(
        other_kernel,
        out_shape=jax.ShapeDtypeStruct((match_count, 2, 1, lines, width), jnp.float32),
        in_specs=[SMEM] + [VMEM] * (4 + len(others)),
        out_specs=HBM,
        scratch_shapes=[
            pltpu.VMEM((dates - 1, 2, lines, width), jnp.float32),
            spectrum,
            pltpu.SemaphoreType.DMA((match_count, lines // HALF)),
        ],
        compiler_params=PARAMS,
        name="filter_other",
    )(matchings, tables, filtered_own, *own_parts, *others)


def solution(mesh):
    placed = (
        P(None, ("parts", "date"), "az", "rg"),
        P(None, ("parts", "date"), "az"),
        P(("parts", "date"), "az"),
        P(),
    )
    return jax.shard_map(
        per_device,
        mesh=mesh,
        in_specs=placed,
        out_specs=P(None, None, ("parts", "date"), "az", "rg"),
        check_vma=False,
    )
```

```python
import functools
import math

import jax
import jax.numpy as jnp
import numpy as np
from jax import lax
from jax.experimental import pallas as pl
from jax.experimental.pallas import tpu as pltpu
from jax.sharding import PartitionSpec as P

TAPS = 8
SHIFT_MAX = 12
PATCH = 64
HALF = PATCH // 2
RIM = SHIFT_MAX + TAPS // 2
REACH = HALF + RIM
LANES = 128
STEP = 16
VMEM_LIMIT = 48 * 1024 * 1024

VMEM = pl.BlockSpec(memory_space=pltpu.VMEM)
SMEM = pl.BlockSpec(memory_space=pltpu.SMEM)
HBM = pl.BlockSpec(memory_space=pltpu.HBM)
PARAMS = pltpu.CompilerParams(vmem_limit_bytes=VMEM_LIMIT)


def fourier_table(sine_sign, table_scale):
    freq_ids = np.arange(PATCH)
    phase_ids = (freq_ids[:, None] * freq_ids[None, :]) % PATCH
    angles = phase_ids * (2.0 * math.pi / PATCH)
    cosine = np.cos(angles) * table_scale
    sine_part = np.sin(angles) * (sine_sign * table_scale)
    top = np.concatenate([cosine, -sine_part], axis=1)
    bottom = np.concatenate([sine_part, cosine], axis=1)
    return np.concatenate([top, bottom], axis=0).astype(np.float32)


def paired(table):
    split = table.reshape(2, PATCH, 2, PATCH)
    wide = np.zeros((2, 2, PATCH, 2, 2, PATCH), np.float32)
    for slot in range(2):
        wide[:, slot, :, :, slot, :] = split
    return wide.reshape(4 * PATCH, 4 * PATCH)


def line_table(forward, row_patches):
    wide_lines = (row_patches + 1) * HALF
    table = np.zeros((row_patches, 2 * PATCH, 2, wide_lines), np.float32)
    transposed = forward.T.reshape(2 * PATCH, 2, PATCH)
    for row in range(row_patches):
        table[row, :, :, row * HALF : row * HALF + PATCH] = transposed
    return table.reshape(row_patches * 2 * PATCH, 2 * wide_lines)


def window_table():
    window = np.sin(math.pi * (np.arange(PATCH) + 0.5) / PATCH) ** 2
    return np.tile(np.outer(window, window), (2, 2)).astype(np.float32)


def ring_table():
    ring = np.zeros((LANES, LANES), np.float32)
    for lane in range(LANES):
        base = lane // PATCH * PATCH
        for step in (-1, 0, 1):
            ring[base + (lane + step) % PATCH, lane] = 1.0
    return ring


def edge_of(other_ref, part, side, lines):
    width = other_ref.shape[2]
    return jnp.where(
        side == 0, other_ref[part, lines, :HALF], other_ref[part, lines, width - HALF :]
    )


def side_by_side(values):
    values = jnp.concatenate(values, axis=0)
    return jnp.concatenate([values[i : i + STEP] for i in range(0, values.shape[0], STEP)], axis=1)


def one_below(block, first, last):
    return jnp.concatenate([block[:, i * HALF : (i + 1) * HALF] for i in range(first, last)], axis=0)


def load_kernel(*refs):
    count = (len(refs) - 1) // 2
    copies = [
        pltpu.make_async_copy(refs[i], refs[count + i], refs[-1].at[i]) for i in range(count)
    ]
    for copy in copies:
        copy.start()
    for copy in copies:
        copy.wait()


def pack_kernel(turn, image_ref, other_ref, taps_ref, offsets_ref, out_ref):
    lines = image_ref.shape[1]
    side = lax.axis_index("rg")
    taps = taps_ref[...]
    taps_high = taps.astype(jnp.bfloat16).astype(jnp.float32)
    taps = jnp.concatenate([taps_high, taps - taps_high], axis=0)
    shifts = jnp.broadcast_to(offsets_ref[...].astype(jnp.float32), taps.shape)

    def write(out_ref, line_start, tap_start):
        rows = slice(line_start, line_start + REACH)
        for part in range(2):
            cut = slice(part * REACH, (part + 1) * REACH)
            out_ref[cut, :] = image_ref[part, rows, :].astype(jnp.bfloat16)
        edges = [edge_of(other_ref, part, side, rows) for part in range(2)]
        cut = slice(tap_start, tap_start + HALF)
        block = side_by_side([*edges, taps[:, cut], shifts[:, cut]])
        out_ref[2 * REACH :, :] = block.astype(jnp.bfloat16)

    above = is_above(turn)

    @pl.when(above)
    def _():
        write(out_ref, 0, 0)

    @pl.when(jnp.logical_not(above))
    def _():
        write(out_ref, lines - REACH, lines - HALF)


def is_above(turn):
    return lax.rem(lax.axis_index("az") + turn, 2) == 1


def band(taps, shift, first_line, source):
    count, lines = source.shape
    tap_ids = source - (lax.broadcasted_iota(jnp.int32, (count, lines), 1) + first_line)
    tap_ids = tap_ids - shift + (TAPS // 2 - 1)
    total = jnp.zeros((count, lines), jnp.float32)
    for tap in range(TAPS):
        total = jnp.where(tap_ids == tap, taps[tap : tap + 1, :], total)
    return total


def high_low(value):
    high = value.astype(jnp.bfloat16)
    low = (value - high.astype(jnp.float32)).astype(jnp.bfloat16)
    return jnp.concatenate([high, low], axis=0)


def apply_band(weights, rows):
    over_rows = (((0,), (0,)), ((), ()))
    rows = jnp.concatenate([rows, rows], axis=0)
    return lax.dot_general(high_low(weights), rows, over_rows, preferred_element_type=jnp.float32)


def write_piece(out_ref, parts, width):
    lines = parts[0].shape[0]
    for part, value in enumerate(parts):
        out_ref[part * lines : (part + 1) * lines, :] = value[:, :width].astype(jnp.bfloat16)
    edges = side_by_side([value[:, width:] for value in parts])
    out_ref[2 * lines :, :] = edges.astype(jnp.bfloat16)


def read_piece(ref, first, count):
    lines = (count - STEP) // 2
    middle = first + 2 * lines
    tiles = ref[first:middle, :].astype(jnp.float32)
    edges = one_below(ref[middle : first + count, :].astype(jnp.float32), 0, 2 * lines // STEP)
    return [(v[:lines], v[lines:]) for v in (tiles, edges)]


def inner_kernel(image_ref, other_ref, taps_ref, offsets_ref, out_ref):
    lines = image_ref.shape[1]
    width = image_ref.shape[2]
    side = lax.axis_index("rg")
    source = lax.broadcasted_iota(jnp.int32, (lines, lines), 0)
    weights = band(taps_ref[...], offsets_ref[...], 0, source)
    weights = jnp.concatenate([weights, weights], axis=0)
    for part in range(2):
        edge = edge_of(other_ref, part, side, slice(0, lines))
        rows = high_low(jnp.concatenate([image_ref[part], edge], axis=1))
        out_ref[part] = apply_band(weights, rows)


def side_lines(turn, image_ref, other_ref, taps_ref, offsets_ref, message_ref):
    lines = image_ref.shape[1]
    side = lax.axis_index("rg")
    above = is_above(turn)
    message = message_ref[...]
    block = message[2 * REACH :, :].astype(jnp.float32)
    steps = 2 * REACH // STEP
    rim_edges = one_below(block, 0, steps).astype(jnp.bfloat16)
    rim_taps = one_below(block, steps, steps + 1)
    rim_taps = rim_taps[:TAPS] + rim_taps[TAPS:]
    rim_shift = one_below(block, steps + 1, steps + 2)[:1]

    def per_line(own, rim):
        upper = jnp.concatenate([rim, own[:, :RIM]], axis=1)
        lower = jnp.concatenate([own[:, lines - RIM :], rim], axis=1)
        return jnp.where(above, upper, lower)

    taps = per_line(taps_ref[...], rim_taps)
    shift = per_line(offsets_ref[...].astype(jnp.float32), rim_shift).astype(jnp.int32)
    first_line = jnp.where(above, -HALF, lines - RIM)
    near = 2 * RIM
    first_own = jnp.where(above, 0, lines - near)
    first_rim = jnp.where(above, -REACH, lines)
    source = lax.broadcasted_iota(jnp.int32, (REACH + near, REACH), 0)
    source = jnp.where(source < REACH, source + first_rim, source - REACH + first_own)
    weights = band(taps, shift, first_line, source)
    weights = jnp.concatenate([weights, weights[REACH:]], axis=0)
    parts = []
    for part in range(2):
        upper, lower = slice(0, near), slice(lines - near, lines)
        edge = jnp.where(
            above, edge_of(other_ref, part, side, upper), edge_of(other_ref, part, side, lower)
        )
        own = jnp.where(above, image_ref[part, upper, :], image_ref[part, lower, :])
        own = high_low(jnp.concatenate([own, edge], axis=1))
        cut = slice(part * REACH, (part + 1) * REACH)
        rim = jnp.concatenate([message[cut, :], rim_edges[cut]], axis=1)
        parts.append(apply_band(weights, jnp.concatenate([rim, own], axis=0)))
    return parts


def side_kernel(turn, *refs):
    image_ref, other_ref, taps_ref, offsets_ref, message_ref, inner_ref = refs[:6]
    out_ref = refs[-1]
    width = image_ref.shape[2]
    place = lax.axis_index("az")
    above = is_above(turn)
    alone = jnp.where(above, place == 0, place == lax.axis_size("az") - 1)
    if turn == 1:
        count = refs[6].shape[0]
        out_ref[:count, :] = refs[6][...]
        out_ref = out_ref.at[count:]

    lines = inner_ref.shape[1]
    half = lines // 2 + HALF

    @pl.when(alone)
    def _():
        halves = []
        for part in range(2):
            blank = jnp.zeros((HALF, inner_ref.shape[2]), jnp.float32)
            upper = jnp.concatenate([blank, inner_ref[part, : half - HALF]], axis=0)
            lower = jnp.concatenate([inner_ref[part, lines - half + HALF :], blank], axis=0)
            halves.append(jnp.where(above, upper, lower))
        write_piece(out_ref, halves, width)

    @pl.when(jnp.logical_not(alone))
    def _():
        halves = []
        for part, total in enumerate(side_lines(turn, *refs[:5])):
            near = inner_ref[part, RIM : half - HALF]
            upper = jnp.concatenate([total, near], axis=0)
            near = inner_ref[part, lines - half + HALF : lines - RIM]
            lower = jnp.concatenate([near, total], axis=0)
            halves.append(jnp.where(above, upper, lower))
        write_piece(out_ref, halves, width)


def cross(own_parts, other_parts):
    own_real, own_imag = own_parts
    other_real, other_imag = other_parts
    real = own_real * other_real + own_imag * other_imag
    imag = own_imag * other_real - own_real * other_imag
    return real, imag


def both_halves(ref):
    count = ref.shape[0] // 2
    return [read_piece(ref, turn * count, count) for turn in range(2)]


def interferogram(own, other):
    side = lax.axis_index("rg")
    own_tile, own_edge = own
    other_tile, other_edge = other
    mid = jnp.concatenate(cross(own_tile, other_tile), axis=0)
    rim = jnp.concatenate(cross(own_edge, other_edge), axis=0)
    before = jnp.where(side == 0, 0.0, rim)
    after = jnp.where(side == 0, rim, 0.0)
    filler = jnp.zeros((mid.shape[0], LANES - 2 * HALF), jnp.float32)
    shifted = jnp.concatenate([before, mid, after, filler], axis=1).astype(jnp.bfloat16)
    return jnp.concatenate([mid.astype(jnp.bfloat16), shifted], axis=1)


def line_sum(tables, own, other):
    both = [interferogram(*halves) for halves in zip(own, other)]
    weights = jnp.concatenate([tables.lines(turn) for turn in range(2)], axis=1)
    both = jnp.concatenate(both, axis=0)
    return jnp.dot(weights, both, preferred_element_type=jnp.float32)


def filtered_of(line_spectra, tables, spectrum_ref, row_patches, width, emit):
    line_spectra = line_spectra.astype(jnp.bfloat16)
    chunks = line_spectra.shape[1] // LANES
    forward, inverse, back, ring, window = tables.core()
    step = chunks * PATCH
    spans = [slice(row * step, (row + 1) * step) for row in range(row_patches)]
    for row, span in enumerate(spans):
        top = row * 2 * PATCH
        pieces = []
        for chunk in range(chunks):
            cut = slice(chunk * LANES, (chunk + 1) * LANES)
            real = line_spectra[top : top + PATCH, cut]
            imag = line_spectra[top + PATCH : top + 2 * PATCH, cut]
            pieces.append(jnp.concatenate([real, imag], axis=1))
        patches = jnp.concatenate(pieces, axis=0)
        spectrum_ref[span, :] = jnp.dot(patches, forward, preferred_element_type=jnp.float32)
    smooths = []
    for span in spans:
        powers = []
        for start in range(span.start, span.stop, PATCH):
            real = spectrum_ref[start : start + PATCH, :LANES]
            imag = spectrum_ref[start : start + PATCH, LANES:]
            power = real * real + imag * imag
            power = power + pltpu.roll(power, 1, 0) + pltpu.roll(power, PATCH - 1, 0)
            powers.append(power.astype(jnp.bfloat16))
        powers = jnp.concatenate(powers, axis=0)
        smooths.append(jnp.dot(powers, ring, preferred_element_type=jnp.float32))
    range_backs = []
    for span, smooth in zip(spans, smooths):
        gain = lax.rsqrt(lax.rsqrt(smooth * (1.0 / (9.0 * PATCH * PATCH)) + 1.0))
        shaped = jnp.concatenate(
            [spectrum_ref[span, :LANES] * gain, spectrum_ref[span, LANES:] * gain], axis=1
        ).astype(jnp.bfloat16)
        range_back = jnp.dot(shaped, inverse, preferred_element_type=jnp.float32)
        range_backs.append(range_back.astype(jnp.bfloat16))
    window = jnp.concatenate([window] * chunks, axis=1)
    earlier = None
    for row in range(row_patches):
        stacked = []
        for chunk in range(chunks):
            block = range_backs[row][chunk * PATCH : (chunk + 1) * PATCH]
            stacked.append(jnp.concatenate([block[:, :LANES], block[:, LANES:]], axis=0))
        stacked = jnp.concatenate(stacked, axis=1)
        patch_out = jnp.dot(back, stacked, preferred_element_type=jnp.float32) * window
        uppers = [patch_out[part * PATCH : part * PATCH + HALF] for part in range(2)]
        if row > 0:
            total = jnp.concatenate(uppers, axis=0) + earlier
            emit(row - 1, total[:, :width] + total[:, width + HALF : 2 * width + HALF])
        lowers = [patch_out[part * PATCH + HALF : (part + 1) * PATCH] for part in range(2)]
        earlier = jnp.concatenate(lowers, axis=0)


def keep(ref, row, total):
    for part in range(2):
        ref[part, row * HALF : (row + 1) * HALF] = total[part * HALF : (part + 1) * HALF]


def own_kernel(table_ref, own_ref, out_ref, tile_ref, edge_ref, spectrum_ref):
    _, lines, width = out_ref.shape
    row_patches = lines // HALF + 1
    tables = Tables(table_ref, row_patches)
    own = both_halves(own_ref)
    for turn, (tile, edge) in enumerate(own):
        for part in range(2):
            tile_ref[turn, part] = tile[part]
            edge_ref[turn, part] = edge[part]
    total = line_sum(tables, own, own)
    emit = functools.partial(keep, out_ref)
    filtered_of(total, tables, spectrum_ref, row_patches, width, emit)


def other_kernel(match_ref, table_ref, filtered_own_ref, tile_ref, edge_ref, *refs):
    out_ref, result_ref, spectrum_ref, sems = refs[-4:]
    match_count, _, _, lines, width = out_ref.shape
    row_patches = lines // HALF + 1
    date = lax.axis_index("date")
    dates = match_ref.shape[1]
    tables = Tables(table_ref, row_patches)

    rows = lines // HALF

    def copy_of(match, row, source_ref):
        cut = slice(row * HALF, (row + 1) * HALF)
        target = out_ref.at[match, :, 0, cut]
        return pltpu.make_async_copy(source_ref.at[:, cut], target, sems.at[match, row])

    def send(slot, row, source_ref):
        for match in range(match_count):
            wanted = lax.rem(match_ref[match, date] - date + dates, dates)

            @pl.when(wanted == slot)
            def _():
                copy_of(match, row, source_ref).start()

    for row in range(rows):
        send(0, row, filtered_own_ref)
    own = [
        [(ref[turn, 0], ref[turn, 1]) for ref in (tile_ref, edge_ref)] for turn in range(2)
    ]
    for slot in range(1, dates):
        total = line_sum(tables, own, both_halves(refs[slot - 1]))
        target_ref = result_ref.at[slot - 1]

        def emit(row, total):
            keep(target_ref, row, total)
            send(slot, row, target_ref)

        filtered_of(total, tables, spectrum_ref, row_patches, width, emit)
    for match in range(match_count):
        for row in range(rows):
            copy_of(match, row, filtered_own_ref).wait()


def all_tables(row_patches):
    forward = fourier_table(1.0, 1.0)
    inverse = fourier_table(-1.0, 1.0 / PATCH)
    back = inverse.reshape(2, PATCH, 2, PATCH).transpose(2, 3, 0, 1).reshape(2 * PATCH, 2 * PATCH)
    window = window_table()[:PATCH, :PATCH]
    splits = []
    for _ in range(3):
        splits.append(window.astype(jnp.bfloat16).astype(np.float32))
        window = window - splits[-1]
    half = (row_patches + 1) * HALF // 2
    lines = line_table(forward, row_patches).reshape(-1, 2, 2, half)
    halves = [lines[:, :, at].reshape(-1, 2 * half) for at in range(2)]
    rows = [np.concatenate([value, np.zeros_like(value)], axis=1) for value in halves] + [
        paired(forward),
        paired(inverse),
        np.concatenate([back, ring_table()], axis=1),
        np.concatenate([*splits, np.zeros_like(window)], axis=1),
    ]
    return np.concatenate(rows, axis=0).astype(jnp.bfloat16)


class Tables:
    def __init__(self, ref, row_patches):
        self.ref = ref
        self.size = row_patches * 2 * PATCH

    def lines(self, turn):
        start = pl.multiple_of(jnp.where(is_above(turn), 0, self.size), self.size)
        return self.ref[pl.ds(start, self.size), :LANES]

    def core(self):
        ref, at = self.ref, 2 * self.size
        forward = ref[at : at + 4 * PATCH, :]
        at += 4 * PATCH
        inverse = ref[at : at + 4 * PATCH, :]
        at += 4 * PATCH
        back = ref[at : at + LANES, :LANES]
        ring = ref[at : at + LANES, LANES:]
        at += LANES
        splits = ref[at : at + PATCH, :].astype(jnp.float32)
        window = splits[:, :PATCH] + splits[:, PATCH : 2 * PATCH] + splits[:, 2 * PATCH : 3 * PATCH]
        window = jnp.concatenate([window, window], axis=1)
        window = jnp.concatenate([window, window], axis=0)
        return forward, inverse, back, ring, window


def per_device(image_stack, tap_weights, offsets, matchings):
    _, _, lines, width = image_stack.shape
    match_count = matchings.shape[0]
    other = lax.ppermute(image_stack, "rg", [(0, 1), (1, 0)]).reshape(2, lines, width)
    arguments = (
        image_stack.reshape(2, lines, width),
        tap_weights.reshape(TAPS, lines),
        offsets,
    )
    raw = pl.pallas_call(
        load_kernel,
        out_shape=tuple(pltpu.VMEM(a.shape, a.dtype) for a in arguments),
        in_specs=[HBM] * 3,
        out_specs=(VMEM,) * 3,
        scratch_shapes=[pltpu.SemaphoreType.DMA((3,))],
        compiler_params=PARAMS,
        name="load",
    )(*(pltpu.with_memory_space_constraint(a, pltpu.HBM) for a in arguments))
    raw = (raw[0], other, *raw[1:])
    message = jax.ShapeDtypeStruct((2 * REACH + STEP, width), jnp.bfloat16)
    messages = [
        pl.pallas_call(
            functools.partial(pack_kernel, turn),
            out_shape=message,
            in_specs=[VMEM] * 4,
            out_specs=VMEM,
            compiler_params=PARAMS,
            name="pack_" + "ab"[turn],
        )(*raw)
        for turn in range(2)
    ]
    peers = lax.axis_size("az")

    def swapped(value, start):
        paired_with = {i: i + 1 for i in range(start, peers - 1, 2)}
        paired_with.update({j: i for i, j in paired_with.items()})
        pairs = [
            (2 * i + core, 2 * paired_with[i] + core if i in paired_with else 2 * i + 1 - core)
            for i in range(peers)
            for core in range(2)
        ]
        return lax.ppermute(value, ("az", "rg"), pairs)

    messages = [swapped(messages[turn], turn) for turn in range(2)]
    inner = pl.pallas_call(
        inner_kernel,
        out_shape=jax.ShapeDtypeStruct((2, lines, width + HALF), jnp.float32),
        in_specs=[VMEM] * 4,
        out_specs=VMEM,
        compiler_params=PARAMS,
        name="inner",
    )(*raw)
    pieces = []
    count = 2 * (lines // 2 + HALF) + STEP
    for turn in range(2):
        call = pl.pallas_call(
            functools.partial(side_kernel, turn),
            out_shape=jax.ShapeDtypeStruct(((turn + 1) * count, width), jnp.bfloat16),
            in_specs=[VMEM] * (6 + turn),
            out_specs=VMEM,
            compiler_params=PARAMS,
            name="side_" + "ab"[turn],
        )
        pieces.append(call(*raw, messages[turn], inner, *pieces))
    own = pieces[1]
    dates = lax.axis_size("date")

    def from_date(piece, slot):
        return lax.ppermute(piece, "date", [((i + slot) % dates, i) for i in range(dates)])

    others = [from_date(own, slot) for slot in range(1, dates)]
    row_patches = lines // HALF + 1
    chunks = (width + width + LANES) // LANES
    tables = jnp.asarray(all_tables(row_patches))
    spectrum = pltpu.VMEM((row_patches * chunks * PATCH, 2 * LANES), jnp.float32)
    half = lines // 2 + HALF
    filtered_own, *own_parts = pl.pallas_call(
        own_kernel,
        out_shape=(
            jax.ShapeDtypeStruct((2, lines, width), jnp.float32),
            jax.ShapeDtypeStruct((2, 2, half, width), jnp.float32),
            jax.ShapeDtypeStruct((2, 2, half, HALF), jnp.float32),
        ),
        in_specs=[VMEM] * 2,
        out_specs=(VMEM,) * 3,
        scratch_shapes=[spectrum],
        compiler_params=PARAMS,
        name="filter_own",
    )(tables, own)
    return pl.pallas_call(
        other_kernel,
        out_shape=jax.ShapeDtypeStruct((match_count, 2, 1, lines, width), jnp.float32),
        in_specs=[SMEM] + [VMEM] * (4 + len(others)),
        out_specs=HBM,
        scratch_shapes=[
            pltpu.VMEM((dates - 1, 2, lines, width), jnp.float32),
            spectrum,
            pltpu.SemaphoreType.DMA((match_count, lines // HALF)),
        ],
        compiler_params=PARAMS,
        name="filter_other",
    )(matchings, tables, filtered_own, *own_parts, *others)


def solution(mesh):
    placed = (
        P(None, ("parts", "date"), "az", "rg"),
        P(None, ("parts", "date"), "az"),
        P(("parts", "date"), "az"),
        P(),
    )
    return jax.shard_map(
        per_device,
        mesh=mesh,
        in_specs=placed,
        out_specs=P(None, None, ("parts", "date"), "az", "rg"),
        check_vma=False,
    )
```
